32 devices in a mesh: dp: 8 (over z, x), seq: 4 (over y, core).
Axes of the slice: x: 2, y: 2, z: 4, core: 2. Of those that a mesh axis runs over, the one named last changes fastest.
Arguments:
- stream: int32 [65536], replicated, may hold values from 0 to 255
- offsets: int32 [16], replicated, may hold values from 0 to 64383
- embed: float32 [256, 512], P(('dp', 'seq')), may hold values from -6 to 6
- head: float32 [512, 256], P(('dp', 'seq')), may hold values from -0.25 to 0.25
- attn_in: float32 [2, 512, 1536], P(None, ('dp', 'seq')), may hold values from -0.25 to 0.25
- attn_out: float32 [2, 512, 512], P(None, ('dp', 'seq')), may hold values from -1 to 1
- ffn_in: float32 [2, 512, 2048], P(None, ('dp', 'seq')), may hold values from -0.25 to 0.25
- ffn_out: float32 [2, 2048, 512], P(None, ('dp', 'seq')), may hold values from -0.125 to 0.125
- gains: float32 [5, 512], P(None, ('dp', 'seq')), may hold values from 0.5 to 1.5
- embed_row: float32 [256], P(('dp', 'seq')), may hold values from 8.138021e-08 to 8.138021e-07
- embed_col: float32 [512], replicated, may hold values from 8.138021e-08 to 8.138021e-07
- head_row: float32 [512], P(('dp', 'seq')), may hold values from 8.138021e-08 to 8.138021e-07
- head_col: float32 [256], replicated, may hold values from 8.138021e-08 to 8.138021e-07
- in_row: float32 [2, 512], P(None, ('dp', 'seq')), may hold values from 8.138021e-08 to 8.138021e-07
- in_col: float32 [2, 1536], replicated, may hold values from 8.138021e-08 to 8.138021e-07
- out_row: float32 [2, 512], P(None, ('dp', 'seq')), may hold values from 8.138021e-08 to 8.138021e-07
- out_col: float32 [2, 512], replicated, may hold values from 8.138021e-08 to 8.138021e-07
- up_row: float32 [2, 512], P(None, ('dp', 'seq')), may hold values from 8.138021e-08 to 8.138021e-07
- up_col: float32 [2, 2048], replicated, may hold values from 8.138021e-08 to 8.138021e-07
- down_row: float32 [2, 2048], P(None, ('dp', 'seq')), may hold values from 8.138021e-08 to 8.138021e-07
- down_col: float32 [2, 512], replicated, may hold values from 8.138021e-08 to 8.138021e-07
- gains_sq: float32 [5, 512], P(None, ('dp', 'seq')), may hold values from 2.0345053e-07 to 2.0345053e-06
Outputs:
- loss_sum: float32 [], replicated
- count_real: float32 [], replicated
- embed_grad: float32 [256, 512], P(('dp', 'seq'))
- embed_row_new: float32 [256], P(('dp', 'seq'))
- embed_col_new: float32 [512], replicated
- embed_new: float32 [256, 512], P(('dp', 'seq'))
- head_grad: float32 [512, 256], P(('dp', 'seq'))
- head_row_new: float32 [512], P(('dp', 'seq'))
- head_col_new: float32 [256], replicated
- head_new: float32 [512, 256], P(('dp', 'seq'))
- attn_in_grad: float32 [2, 512, 1536], P(None, ('dp', 'seq'))
- in_row_new: float32 [2, 512], P(None, ('dp', 'seq'))
- in_col_new: float32 [2, 1536], replicated
- attn_in_new: float32 [2, 512, 1536], P(None, ('dp', 'seq'))
- attn_out_grad: float32 [2, 512, 512], P(None, ('dp', 'seq'))
- out_row_new: float32 [2, 512], P(None, ('dp', 'seq'))
- out_col_new: float32 [2, 512], replicated
- attn_out_new: float32 [2, 512, 512], P(None, ('dp', 'seq'))
- ffn_in_grad: float32 [2, 512, 2048], P(None, ('dp', 'seq'))
- up_row_new: float32 [2, 512], P(None, ('dp', 'seq'))
- up_col_new: float32 [2, 2048], replicated
- ffn_in_new: float32 [2, 512, 2048], P(None, ('dp', 'seq'))
- ffn_out_grad: float32 [2, 2048, 512], P(None, ('dp', 'seq'))
- down_row_new: float32 [2, 2048], P(None, ('dp', 'seq'))
- down_col_new: float32 [2, 512], replicated
- ffn_out_new: float32 [2, 2048, 512], P(None, ('dp', 'seq'))
- gains_grad: float32 [5, 512], P(None, ('dp', 'seq'))
- gains_sq_new: float32 [5, 512], P(None, ('dp', 'seq'))
- gains_new: float32 [5, 512], P(None, ('dp', 'seq'))
The draws below stay inside these ranges and needn't reach their ends.
Inputs may be any that keep to these rules, and one draw needn't show every extreme that they name: `offsets`: window starts; a window may run past the end of the stream by up to 384 bytes.
All inputs are finite; a program needn't handle non-finite values.
Results may differ from the reference program's by a relative error of at most 0.0045.
The reference program's roundings to bfloat16 on the way count: a program that leaves them out, or rounds other values in their place, can miss the bound.
Values may be sent and summed in bfloat16 or wider, within the bound.
No kernel may reach another device: no remote copies, remote signals or barrier semaphores. Data moves between devices by JAX's collectives and lax.ppermute only.
A program may use at most 192 MiB of HBM per device.

```python
import math
from functools import partial
import jax
import jax.numpy as jnp
import numpy as np
from jax import lax

D = 512
HEADS = 8
FF = 2048
VOCAB = 256
SHORT = 3
HD = 64
STREAM = 65536
STEP = 10
LEN = 1536
LOSS = 768
WINDOWS = 16


def with_ends(entries, key, low, top_value):
    longest = entries.shape.index(max(entries.shape))
    spots = []
    for shift in (0, 1):
        where = [jax.random.randint(jax.random.fold_in(key, axis), (), 0, length) for axis, length in enumerate(entries.shape)]
        where[longest] = (where[longest] + shift) % entries.shape[longest]
        spots.append(tuple(where))
    return entries.at[spots[0]].set(low).at[spots[1]].set(top_value)


def levels(key, dims, cuts, smallest, high):
    loudness = 1.0
    for dim, parts in cuts:
        steps = jax.random.uniform(jax.random.fold_in(jax.random.fold_in(key, 6), dim), (parts,), jnp.float32, smallest / len(cuts), high / len(cuts))
        loudness = loudness * jnp.repeat(jnp.exp(steps), dims[dim] // parts).reshape((-1,) + (1,) * (len(dims) - 1 - dim))
    return loudness


def rank_table(count, skew):
    weights = [(1 << 20) // math.isqrt(standing ** skew) + 1 for standing in range(1, count + 1)]
    spread = 1 + sum(weights) // (1 << 30)
    return np.cumsum(np.array([max(1, weight // spread) for weight in weights]))


def skewed_ids(rng, shape, number_of, skew):
    listing = rank_table(number_of, skew)
    pick = jax.random.randint(jax.random.fold_in(rng, 1), shape, 0, int(listing[number_of - 1]))
    grade = jnp.searchsorted(jnp.asarray(listing, jnp.int32), pick, side="right")
    return jax.random.permutation(jax.random.fold_in(rng, 2), number_of)[grade].astype(jnp.int32)


def normal_values(key, extent, spread, reach, cuts=(), kind=jnp.bfloat16):
    entries = spread * jax.random.normal(key, extent, jnp.float32)
    if cuts:
        entries = entries * levels(key, extent, cuts, -0.22, 0.18)
    return jnp.clip(entries, -reach, reach).astype(kind)


def setup_inputs(seed: int = 0) -> dict:
    keys = jax.random.split(jax.random.key(seed), 23)
    return {
        "stream": with_ends(skewed_ids(keys[0], (STREAM,), VOCAB, 2), jax.random.fold_in(keys[0], 3), 0, VOCAB - 1).astype(jnp.int32),
        "offsets": with_ends(jax.random.randint(keys[1], (WINDOWS,), 0, STREAM - LEN + LEN // 4), jax.random.fold_in(keys[1], 1), 0, (STREAM - LEN + LEN // 4) - 1).astype(jnp.int32),
        "embed": normal_values(keys[2], (VOCAB, D), 1.0, 6.0, ((0, 32),), jnp.float32),
        "head": normal_values(keys[3], (D, VOCAB), D ** -0.5, 0.25, ((0, 32),), jnp.float32),
        "attn_in": normal_values(keys[4], (2, D, 3 * D), D ** -0.5, 0.25, ((1, 32),), jnp.float32),
        "attn_out": normal_values(keys[5], (2, D, D), (D // 16) ** -0.5, 1.0, ((1, 32),), jnp.float32),
        "ffn_in": normal_values(keys[6], (2, D, FF), D ** -0.5, 0.25, ((1, 32),), jnp.float32),
        "ffn_out": normal_values(keys[7], (2, FF, D), FF ** -0.5, 0.125, ((1, 32),), jnp.float32),
        "gains": jnp.clip(1.0 + 0.1 * jax.random.normal(keys[8], (5, D), jnp.float32), 0.5, 1.5),
        "embed_row": jnp.clip(jnp.exp(math.log(8.138021030390519e-07) - 2.3025851 * jax.random.uniform(keys[9], (VOCAB,), jnp.float32) ** levels(keys[9], (VOCAB,), ((0, 32),), -0.2, 0.2)), 8.138020746173424e-08, 8.138021030390519e-07),
        "embed_col": jnp.clip(jnp.exp(jax.random.uniform(keys[10], (D,), jnp.float32, math.log(8.138020746173424e-08), math.log(8.138021030390519e-07))), 8.138020746173424e-08, 8.138021030390519e-07),
        "head_row": jnp.clip(jnp.exp(math.log(8.138021030390519e-07) - 2.3025851 * jax.random.uniform(keys[11], (D,), jnp.float32) ** levels(keys[11], (D,), ((0, 32),), -0.2, 0.2)), 8.138020746173424e-08, 8.138021030390519e-07),
        "head_col": jnp.clip(jnp.exp(jax.random.uniform(keys[12], (VOCAB,), jnp.float32, math.log(8.138020746173424e-08), math.log(8.138021030390519e-07))), 8.138020746173424e-08, 8.138021030390519e-07),
        "in_row": jnp.clip(jnp.exp(math.log(8.138021030390519e-07) - 2.3025851 * jax.random.uniform(keys[13], (2, D), jnp.float32) ** levels(keys[13], (2, D), ((1, 32),), -0.2, 0.2)), 8.138020746173424e-08, 8.138021030390519e-07),
        "in_col": jnp.clip(jnp.exp(jax.random.uniform(keys[14], (2, 3 * D), jnp.float32, math.log(8.138020746173424e-08), math.log(8.138021030390519e-07))), 8.138020746173424e-08, 8.138021030390519e-07),
        "out_row": jnp.clip(jnp.exp(math.log(8.138021030390519e-07) - 2.3025851 * jax.random.uniform(keys[15], (2, D), jnp.float32) ** levels(keys[15], (2, D), ((1, 32),), -0.2, 0.2)), 8.138020746173424e-08, 8.138021030390519e-07),
        "out_col": jnp.clip(jnp.exp(jax.random.uniform(keys[16], (2, D), jnp.float32, math.log(8.138020746173424e-08), math.log(8.138021030390519e-07))), 8.138020746173424e-08, 8.138021030390519e-07),
        "up_row": jnp.clip(jnp.exp(math.log(8.138021030390519e-07) - 2.3025851 * jax.random.uniform(keys[17], (2, D), jnp.float32) ** levels(keys[17], (2, D), ((1, 32),), -0.2, 0.2)), 8.138020746173424e-08, 8.138021030390519e-07),
        "up_col": jnp.clip(jnp.exp(jax.random.uniform(keys[18], (2, FF), jnp.float32, math.log(8.138020746173424e-08), math.log(8.138021030390519e-07))), 8.138020746173424e-08, 8.138021030390519e-07),
        "down_row": jnp.clip(jnp.exp(math.log(8.138021030390519e-07) - 2.3025851 * jax.random.uniform(keys[19], (2, FF), jnp.float32) ** levels(keys[19], (2, FF), ((1, 32),), -0.2, 0.2)), 8.138020746173424e-08, 8.138021030390519e-07),
        "down_col": jnp.clip(jnp.exp(jax.random.uniform(keys[20], (2, D), jnp.float32, math.log(8.138020746173424e-08), math.log(8.138021030390519e-07))), 8.138020746173424e-08, 8.138021030390519e-07),
        "gains_sq": jnp.clip(jnp.exp(math.log(2.0345053144410485e-06) - 2.3025851 * jax.random.uniform(keys[21], (5, D), jnp.float32) ** levels(keys[21], (5, D), ((1, 32),), -0.2, 0.2)), 2.0345052575976297e-07, 2.0345053144410485e-06),
    }


@jax.custom_vjp
def low(v):
    return lax.optimization_barrier(v.astype(jnp.bfloat16)).astype(jnp.float32)

@jax.custom_vjp
def low_back(v):
    return v

def low_keep(v):
    return (low(v), None)

def low_pass(kept, grad):
    return (grad,)

def back_keep(v):
    return (v, None)

def back_low(kept, grad):
    return (low(grad),)
low.defvjp(low_keep, low_pass)
low_back.defvjp(back_keep, back_low)
EPSILON = 1e-05
RATE_SCALE = 0.5
LOG_TWO = math.log(2.0)

def product(left, right):
    return jnp.dot(left, right, precision=lax.Precision.HIGHEST, preferred_element_type=jnp.float32)

def layer_norm(values, gain_row):
    center = values - lax.optimization_barrier(jnp.mean(values, -1, keepdims=True))
    return center * lax.rsqrt(lax.optimization_barrier(jnp.mean(center * center, -1, keepdims=True)) + EPSILON) * gain_row

def rotate(values, positions):
    half_size = values.shape[-1] // 2
    frequency = 10000.0 ** (-jnp.arange(half_size, dtype=jnp.float32) / half_size)
    angles = positions.astype(jnp.float32)[:, None] * frequency[None, :]
    cosine = jnp.cos(angles)[:, None, :]
    sine_table = jnp.sin(angles)[:, None, :]
    first_half = values[..., :half_size]
    second_half = values[..., half_size:]
    return jnp.concatenate([first_half * cosine - second_half * sine_table, second_half * cosine + first_half * sine_table], -1)

def attend(queries, key_rows, value_rows, positions):

    def single(pieces):
        scores = low_back(product(pieces[0], pieces[1].T))
        scores = jnp.where(positions[:, None] >= positions[None, :], scores, -1e+30)
        attn_prob = low(jax.nn.softmax(scores, -1))
        return product(attn_prob, pieces[2])
    head_out = lax.map(jax.checkpoint(single), (queries.transpose(1, 0, 2), key_rows.transpose(1, 0, 2), value_rows.transpose(1, 0, 2)))
    return head_out.transpose(1, 0, 2)

def layer(values, positions, w_in, w_out, w_up, w_down, gain_attn, gain_ffn):
    row_count = values.shape[0]
    normed = low(layer_norm(values, gain_attn))
    mixed = low_back(product(normed, w_in)).reshape(row_count, 3, HEADS, HD)
    queries = low(rotate(mixed[:, 0], positions) * 0.125)
    key_rows = low(rotate(mixed[:, 1], positions))
    value_rows = low(mixed[:, 2])
    attended = low(low_back(attend(queries, key_rows, value_rows, positions))).reshape(row_count, D)
    middle = values + low_back(product(attended, w_out))
    hidden = low(jax.nn.gelu(low_back(product(low(layer_norm(middle, gain_ffn)), w_up))))
    return middle + low_back(product(hidden, w_down))

def window_loss(weights, window_start, stream):
    embed_low, head_low, in_low, out_low, up_low, down_low, gain_rows = weights
    positions = jnp.arange(LEN, dtype=jnp.int32)
    stream_index = window_start + positions
    tokens_in = stream[jnp.minimum(stream_index, STREAM - 1)]
    targets = stream[jnp.minimum(stream_index + 1, STREAM - 1)]
    counted = ((positions >= LEN - LOSS) & (stream_index + 1 < STREAM)).astype(jnp.float32)
    first_res = layer(low_back(embed_low[tokens_in]), positions, in_low[0], out_low[0], up_low[0], down_low[0], gain_rows[0], gain_rows[1])
    shifted = jnp.concatenate([jnp.zeros((SHORT - 1, D), jnp.float32), first_res[:LEN - SHORT + 1]], 0)
    pooled = lax.optimization_barrier(jnp.mean(shifted.reshape(LEN // SHORT, SHORT, D), 1))
    coarse = layer(pooled, jnp.arange(LEN // SHORT, dtype=jnp.int32), in_low[1], out_low[1], up_low[1], down_low[1], gain_rows[2], gain_rows[3])
    joined = first_res + jnp.repeat(coarse, SHORT, axis=0)
    logits = low_back(product(low(layer_norm(joined, gain_rows[4])), head_low))
    log_total = jax.scipy.special.logsumexp(logits, -1)
    target_logit = jnp.take_along_axis(logits, targets[:, None], 1)[:, 0]
    return jnp.sum((log_total - target_logit) * counted) / LOG_TWO

def factored(gradient, row_state, col_state, weight, decay_rate):
    row_count = gradient.shape[-2]
    col_count = gradient.shape[-1]
    square = gradient * gradient
    new_row = decay_rate * row_state + (1.0 - decay_rate) * lax.optimization_barrier(jnp.mean(square, -1))
    new_col = decay_rate * col_state + (1.0 - decay_rate) * lax.optimization_barrier(jnp.sum(square, -2)) / row_count
    mean_row = lax.optimization_barrier(jnp.sum(new_row, -1)) / row_count
    update = gradient / jnp.sqrt(new_row[..., :, None] * new_col[..., None, :] / mean_row[..., None, None])
    size_all = row_count * col_count
    rms_update = jnp.sqrt(lax.optimization_barrier(jnp.sum(update * update, (-2, -1))) / size_all)
    rms_weight = jnp.sqrt(lax.optimization_barrier(jnp.sum(weight * weight, (-2, -1))) / size_all)
    step_rate = RATE_SCALE * rms_weight / jnp.maximum(1.0, rms_update)
    return (new_row, new_col, weight - step_rate[..., None, None] * update)

def reference(stream, offsets, embed, head, attn_in, attn_out, ffn_in, ffn_out, gains, embed_row, embed_col, head_row, head_col, in_row, in_col, out_row, out_col, up_row, up_col, down_row, down_col, gains_sq):
    decay_rate = 1.0 - STEP ** (-0.8)
    positions = jnp.arange(LEN, dtype=jnp.int32)
    stream_index = offsets[:, None] + positions[None, :]
    count_real = jnp.sum(((positions[None, :] >= LEN - LOSS) & (stream_index + 1 < STREAM)).astype(jnp.float32))
    weights = (embed, head, attn_in, attn_out, ffn_in, ffn_out, gains)

    def objective(params):
        lowered = jax.tree.map(low, params)

        def add_window(running_total, window_start):
            return (running_total + jax.checkpoint(partial(window_loss, stream=stream))(lowered, window_start), None)
        loss_sum, _ = lax.scan(add_window, jnp.zeros((), jnp.float32), offsets)
        return (loss_sum / count_real, loss_sum)
    _, pull, loss_sum = jax.vjp(objective, weights, has_aux=True)
    gradients = pull(jnp.ones((), jnp.float32))[0]
    embed_r, embed_c, embed_w = factored(gradients[0], embed_row, embed_col, embed, decay_rate)
    head_r, head_c, head_w = factored(gradients[1], head_row, head_col, head, decay_rate)
    in_r, in_c, in_w = factored(gradients[2], in_row, in_col, attn_in, decay_rate)
    out_r, out_c, out_w = factored(gradients[3], out_row, out_col, attn_out, decay_rate)
    up_r, up_c, up_w = factored(gradients[4], up_row, up_col, ffn_in, decay_rate)
    down_r, down_c, down_w = factored(gradients[5], down_row, down_col, ffn_out, decay_rate)
    gain_grad = gradients[6]
    new_sq = decay_rate * gains_sq + (1.0 - decay_rate) * gain_grad * gain_grad
    gain_update = gain_grad / jnp.sqrt(new_sq)
    rms_update = jnp.sqrt(lax.optimization_barrier(jnp.sum(gain_update * gain_update, -1)) / D)
    rms_weight = jnp.sqrt(lax.optimization_barrier(jnp.sum(gains * gains, -1)) / D)
    step_rate = RATE_SCALE * rms_weight / jnp.maximum(1.0, rms_update)
    gains_next = gains - step_rate[:, None] * gain_update
    return (loss_sum, count_real, gradients[0], embed_r, embed_c, embed_w, gradients[1], head_r, head_c, head_w, gradients[2], in_r, in_c, in_w, gradients[3], out_r, out_c, out_w, gradients[4], up_r, up_c, up_w, gradients[5], down_r, down_c, down_w, gain_grad, new_sq, gains_next)
```

```python
from functools import partial
import math

import jax
import jax.numpy as jnp
from jax import lax
from jax.experimental import pallas as pl
from jax.experimental.pallas import tpu as pltpu
from jax.sharding import PartitionSpec as P

D = 512
HEADS = 8
FF = 2048
VOCAB = 256
SHORT = 3
HD = 64
SPAN = 384
CSPAN = SPAN // SHORT
STREAM = 65536
STEP = 10
SHARDS = 32
TILE = 16

EPSILON = 1e-05
RATE_SCALE = 0.5
LOG_TWO = math.log(2.0)
MASKED = -1e30
GELU_A = math.sqrt(2.0 / math.pi)
GELU_B = 0.044715
BOTH = ("dp", "seq")
F32 = jnp.float32
BF16 = jnp.bfloat16
VMEM_LIMIT = 56 * 2**20


def nn(left, right):
    return jnp.dot(left, right, preferred_element_type=F32)


def nt(left, right):
    return lax.dot_general(left, right, (((1,), (1,)), ((), ())), preferred_element_type=F32)


def call(body, name, outs, ins, flops, grid=(), in_specs=None, out_specs=None, scratch=(), prefetch=0):
    moved = sum(math.prod(o.shape) * o.dtype.itemsize for o in outs)
    moved += sum(math.prod(i.shape) * i.dtype.itemsize for i in ins)
    spec = pltpu.PrefetchScalarGridSpec(
        num_scalar_prefetch=prefetch,
        grid=grid,
        in_specs=in_specs or [pl.BlockSpec(memory_space=pltpu.VMEM)] * (len(ins) - prefetch),
        out_specs=out_specs or [pl.BlockSpec(memory_space=pltpu.VMEM)] * len(outs),
        scratch_shapes=list(scratch),
    )
    return pl.pallas_call(
        body,
        grid_spec=spec,
        out_shape=list(outs),
        compiler_params=pltpu.CompilerParams(vmem_limit_bytes=VMEM_LIMIT),
        cost_estimate=pl.CostEstimate(flops=flops, bytes_accessed=moved, transcendentals=0),
        name=name,
    )(*ins)


def shape(dims, kind=F32):
    return jax.ShapeDtypeStruct(dims, kind)


def norm_parts(values):
    center = values - jnp.mean(values, -1, keepdims=True)
    scale = lax.rsqrt(jnp.mean(center * center, -1, keepdims=True) + EPSILON)
    return center * scale, scale


def norm_pull(hat, scale, gain, cotangent):
    pulled = cotangent * gain
    inner = pulled - jnp.mean(pulled, -1, keepdims=True) - hat * jnp.mean(pulled * hat, -1, keepdims=True)
    return scale * inner, jnp.sum(cotangent * hat, 0, keepdims=True)


def swap_halves(values):
    lane = lax.broadcasted_iota(jnp.int32, values.shape, 1)
    return jnp.where(lane % HD < HD // 2, pltpu.roll(values, 128 - HD // 2, 1), pltpu.roll(values, HD // 2, 1))


def rope(values, cosine, sine):
    pieces = []
    for start in range(0, D, 128):
        piece = values[:, start : start + 128]
        pieces.append(piece * cosine + swap_halves(piece) * sine)
    return jnp.concatenate(pieces, 1)


def rope_pull(values, cosine, sine):
    pieces = []
    for start in range(0, D, 128):
        piece = values[:, start : start + 128]
        pieces.append(piece * cosine + swap_halves(piece * sine))
    return jnp.concatenate(pieces, 1)


def gelu_parts(values):
    inner = GELU_A * (values + GELU_B * (values * values * values))
    wave = jnp.tanh(inner)
    return wave, 0.5 * (1.0 + wave)


def tile_of(ref, index):
    return ref[:, TILE * index : TILE * index + TILE, :].reshape(D, ref.shape[-1])


def project_body(full, token_ref, x_ref, w_ref, gain_ref, cos_ref, sin_ref, *outs):
    if full:
        h_ref, q_ref, k_ref, v_ref = outs
        token = token_ref[...]
        row = (token // 8) * TILE + token % 8
        hot = (row == lax.broadcasted_iota(jnp.int32, (token.shape[0], D), 1)).astype(BF16)
        values = nn(hot, tile_of(w_ref, 3))
        h_ref[...] = values.astype(BF16)
        gain = gain_ref[0:1, :]
    else:
        q_ref, k_ref, v_ref = outs
        values = x_ref[...]
        gain = gain_ref[2:3, :]
    normed = (norm_parts(values)[0] * gain).astype(BF16)
    cosine, sine = cos_ref[...], sin_ref[...]
    rows = q_ref.shape[0]
    skip = normed.shape[0] - rows
    query = nn(normed[skip:], tile_of(w_ref, 0))
    q_ref[...] = (rope(query, cosine[skip:], sine[skip:]) * 0.125).astype(BF16)
    k_ref[...] = rope(nn(normed, tile_of(w_ref, 1)), cosine, sine).astype(BF16)
    v_ref[...] = nn(normed, tile_of(w_ref, 2)).astype(BF16)


def project(token, x, packed, gains, cosine, sine, full):
    rows = cosine.shape[0]
    q_rows = rows if full else rows // 2
    outs = [shape((q_rows, D), BF16), shape((rows, D), BF16), shape((rows, D), BF16)]
    if full:
        outs = [shape((rows, D), BF16)] + outs
    whole = pl.BlockSpec(memory_space=pltpu.VMEM)
    tiles = 4 if full else 3
    return call(
        partial(project_body, full),
        "project_full" if full else "project_short",
        outs,
        [token, x, packed, gains, cosine, sine],
        2 * rows * D * D * 4,
        grid=(1,),
        in_specs=[
            pl.BlockSpec(token.shape, lambda i: (0, 0)),
            pl.BlockSpec(x.shape, lambda i: (0, 0)),
            pl.BlockSpec((SHARDS, TILE * tiles, D), lambda i: (0, 0, 0)),
            pl.BlockSpec(gains.shape, lambda i: (0, 0)),
            pl.BlockSpec(cosine.shape, lambda i: (0, 0)),
            pl.BlockSpec(sine.shape, lambda i: (0, 0)),
        ],
        out_specs=[pl.BlockSpec(o.shape, lambda i: (0, 0)) for o in outs],
    )


def attend_body(count, block, step, nk_ref, q_ref, k_ref, v_ref, out_ref, lse_ref, s_scr, p_scr):
    nk = nk_ref[pl.program_id(0)]
    lane = lax.broadcasted_iota(jnp.int32, (1, 256), 1)
    column = lax.broadcasted_iota(jnp.int32, (step, 128), 1)
    zero = jnp.zeros((), BF16)

    def variant(blocks):
        width = blocks * block

        def head(j):
            mine = lane // HD == j
            query = jnp.where(mine, q_ref[0], zero)
            s_scr[:, :width] = nt(query, k_ref[:width, :])

            def rows(i):
                part = pl.ds(i * step if isinstance(i, int) else pl.multiple_of(i * step, step), step)
                score = s_scr[part, :width]
                row = i * step + lax.broadcasted_iota(jnp.int32, (step, block), 0)
                key = lax.broadcasted_iota(jnp.int32, (step, block), 1)
                edge = jnp.where(row >= key, score[:, width - block :], MASKED)
                score = jnp.concatenate([score[:, : width - block], edge], 1) if blocks > 1 else edge
                top = jnp.max(score, -1, keepdims=True)
                raised = jnp.exp(score - top)
                total = jnp.sum(raised, -1, keepdims=True)
                p_scr[part, :width] = (raised * (1.0 / total)).astype(BF16)
                lse_ref[0, 0, part, :] = jnp.where(column == j, top + jnp.log(total), lse_ref[0, 0, part, :])

            each_rows(rows, block // step, count)
            found = nn(p_scr[:, :width], v_ref[:width, :]).astype(BF16)
            out_ref[0] = found if j == 0 else jnp.where(mine, found, out_ref[0])

        for j in range(4):
            head(j)

    for blocks in range(1, count + 1):
        pl.when(nk == blocks)(partial(variant, blocks))


def each_rows(rows, steps, count):
    if count <= 4:
        for i in range(steps):
            rows(i)
    else:
        lax.fori_loop(0, steps, lambda i, carry: (rows(i), carry)[1], 0)


def attend(nk, q, k, v, block):
    slots = q.shape[0] // block
    keys = k.shape[0]
    count = keys // block
    out, lse = call(
        partial(attend_body, count, block, 64),
        "attend",
        [shape((slots, block, D), BF16), shape((slots, 2, block, 128))],
        [nk, q.reshape(slots, block, D), k, v],
        slots * block * keys * D * 4,
        grid=(slots, 2),
        in_specs=[
            pl.BlockSpec((1, block, 256), lambda s, h, _: (s, 0, h)),
            pl.BlockSpec((keys, 256), lambda s, h, _: (0, h)),
            pl.BlockSpec((keys, 256), lambda s, h, _: (0, h)),
        ],
        out_specs=[
            pl.BlockSpec((1, block, 256), lambda s, h, _: (s, 0, h)),
            pl.BlockSpec((1, 1, block, 128), lambda s, h, _: (s, h, 0, 0)),
        ],
        scratch=[pltpu.VMEM((block, keys), F32), pltpu.VMEM((block, keys), BF16)],
        prefetch=1,
    )
    return out.reshape(slots * block, D), lse


def attend_back_body(
    count, block, step, nk_ref, q_ref, k_ref, v_ref, back_ref, lse_ref, dq_ref, dkv_ref, s_scr, dp_scr, p_scr, ds_scr, dk_scr, dv_scr
):
    slot = pl.program_id(1)
    nk = nk_ref[slot]
    lane = lax.broadcasted_iota(jnp.int32, (1, 256), 1)
    column = lax.broadcasted_iota(jnp.int32, (step, 128), 1)
    zero = jnp.zeros((), BF16)

    @pl.when(slot == 0)
    def _():
        dk_scr[...] = jnp.zeros_like(dk_scr)
        dv_scr[...] = jnp.zeros_like(dv_scr)

    def variant(blocks):
        width = blocks * block
        query_t = q_ref[0].T
        back_t = back_ref[0].T

        def head(j):
            mine = lane // HD == j
            query = jnp.where(mine, q_ref[0], zero)
            back = jnp.where(mine, back_ref[0], zero)
            s_scr[:, :width] = nt(query, k_ref[:width, :])
            dp_scr[:, :width] = nt(back, v_ref[:width, :])

            def rows(i):
                part = pl.ds(i * step if isinstance(i, int) else pl.multiple_of(i * step, step), step)
                score = s_scr[part, :width]
                row = i * step + lax.broadcasted_iota(jnp.int32, (step, block), 0)
                key = lax.broadcasted_iota(jnp.int32, (step, block), 1)
                edge = jnp.where(row >= key, score[:, width - block :], MASKED)
                score = jnp.concatenate([score[:, : width - block], edge], 1) if blocks > 1 else edge
                lse = jnp.sum(jnp.where(column == j, lse_ref[0, 0, part, :], 0.0), -1, keepdims=True)
                prob = jnp.exp(score - lse)
                p_scr[part, :width] = prob.astype(BF16)
                prob_back = dp_scr[part, :width]
                delta = jnp.sum(prob * prob_back, -1, keepdims=True)
                ds_scr[part, :width] = (prob * (prob_back - delta)).astype(BF16)

            each_rows(rows, block // step, count)
            found = nn(ds_scr[:, :width], k_ref[:width, :])
            dq_ref[0] = found if j == 0 else jnp.where(mine, found, dq_ref[0])
            own = slice(HD * j, HD * j + HD)
            dk_scr[own, :width] += nn(query_t[own], ds_scr[:, :width])
            dv_scr[own, :width] += nn(back_t[own], p_scr[:, :width])

        for j in range(4):
            head(j)

    for blocks in range(1, count + 1):
        pl.when(nk == blocks)(partial(variant, blocks))

    @pl.when(slot == pl.num_programs(1) - 1)
    def _():
        for owner in range(count // 2):
            for place, at in enumerate((owner, count - 1 - owner)):
                dkv_ref[owner, 0, :, place * block : place * block + block] = dk_scr[:, at * block : at * block + block]
                dkv_ref[owner, 1, :, place * block : place * block + block] = dv_scr[:, at * block : at * block + block]


def attend_back(nk, q, k, v, back, lse, block):
    slots = q.shape[0] // block
    keys = k.shape[0]
    count = keys // block
    dq, dkv = call(
        partial(attend_back_body, count, block, 64),
        "attend_back",
        [shape((slots, block, D)), shape((count // 2, 2, D, 2 * block))],
        [nk, q.reshape(slots, block, D), k, v, back.reshape(slots, block, D), lse],
        slots * block * keys * D * 10,
        grid=(2, slots),
        in_specs=[
            pl.BlockSpec((1, block, 256), lambda h, s, _: (s, 0, h)),
            pl.BlockSpec((keys, 256), lambda h, s, _: (0, h)),
            pl.BlockSpec((keys, 256), lambda h, s, _: (0, h)),
            pl.BlockSpec((1, block, 256), lambda h, s, _: (s, 0, h)),
            pl.BlockSpec((1, 1, block, 128), lambda h, s, _: (s, h, 0, 0)),
        ],
        out_specs=[
            pl.BlockSpec((1, block, 256), lambda h, s, _: (s, 0, h)),
            pl.BlockSpec((count // 2, 2, 256, 2 * block), lambda h, s, _: (0, 0, h, 0)),
        ],
        scratch=[
            pltpu.VMEM((block, keys), F32),
            pltpu.VMEM((block, keys), F32),
            pltpu.VMEM((block, keys), BF16),
            pltpu.VMEM((block, keys), BF16),
            pltpu.VMEM((256, keys), F32),
            pltpu.VMEM((256, keys), F32),
        ],
        prefetch=1,
    )
    return dq.reshape(slots * block, D), dkv


def branch_body(gain_row, x_ref, a_ref, out_w, up_w, down_w, gain_ref, mid_ref, res_ref):
    middle = x_ref[...].astype(F32) + nn(a_ref[...], tile_of(out_w, 0))
    mid_ref[...] = middle
    normed = (norm_parts(middle)[0] * gain_ref[gain_row : gain_row + 1, :]).astype(BF16)
    total = middle
    for chunk in range(FF // D):
        up = nn(normed, tile_of(up_w, chunk))
        hidden = (up * gelu_parts(up)[1]).astype(BF16)
        total = total + nn(hidden, down_w[8 * chunk : 8 * chunk + 8].reshape(D, D))
    res_ref[...] = total


def branch(x, a, out_w, up_w, down_w, gains, gain_row):
    rows = a.shape[0]
    step = min(rows, SPAN)
    return call(
        partial(branch_body, gain_row),
        "branch",
        [shape((rows, D)), shape((rows, D))],
        [x, a, out_w[0], up_w[0], down_w[0], gains],
        2 * rows * D * D * 9,
        grid=(rows // step,),
        in_specs=[
            pl.BlockSpec((step, D), lambda i: (i, 0)),
            pl.BlockSpec((step, D), lambda i: (i, 0)),
            out_w[1](1),
            up_w[1](1),
            down_w[1](1),
            pl.BlockSpec(gains.shape, lambda i: (0, 0)),
        ],
        out_specs=[pl.BlockSpec((step, D), lambda i: (i, 0)), pl.BlockSpec((step, D), lambda i: (i, 0))],
    )


def branch_back_body(
    gain_row, cot_ref, mid_ref, a_ref, out_w, up_w, down_w, gain_ref, dmid_ref, da_ref, dout_ref, dup_ref, ddown_ref, dgain_ref,
    norm_scr, normt_scr, cot_scr, acc_scr,
):
    chunk = pl.program_id(0)

    @pl.when(chunk == 0)
    def _():
        hat, _ = norm_parts(mid_ref[...])
        normed = (hat * gain_ref[gain_row : gain_row + 1, :]).astype(BF16)
        norm_scr[...] = normed
        normt_scr[...] = normed.T
        cot_scr[...] = cot_ref[...].astype(BF16)

    down_in = cot_scr[...]
    up_tile = up_w[...].reshape(D, D)
    up = nn(norm_scr[...], up_tile)
    wave, gate = gelu_parts(up)
    hidden = (up * gate).astype(BF16)
    slope = gate + 0.5 * up * (1.0 - wave * wave) * (GELU_A * (1.0 + 3.0 * GELU_B * up * up))
    up_in = (nt(down_in, down_w[...].reshape(D, D)) * slope).astype(BF16)
    ddown_ref[...] = nn(hidden.T, down_in).reshape(ddown_ref.shape)
    dup_ref[...] = nn(normt_scr[...], up_in).reshape(dup_ref.shape)
    part = nt(up_in, up_tile)

    @pl.when(chunk == 0)
    def _():
        acc_scr[...] = part

    @pl.when(chunk > 0)
    def _():
        acc_scr[...] += part

    @pl.when(chunk == FF // D - 1)
    def _():
        hat, scale = norm_parts(mid_ref[...])
        pulled, dgain = norm_pull(hat, scale, gain_ref[gain_row : gain_row + 1, :], acc_scr[...])
        dgain_ref[...] = dgain
        dmid = cot_ref[...] + pulled
        dmid_ref[...] = dmid
        out_in = dmid.astype(BF16)
        dout_ref[...] = nn(a_ref[...].T, out_in).reshape(dout_ref.shape)
        da_ref[...] = nt(out_in, tile_of(out_w, 0)).astype(BF16)


def branch_back(cot, mid, a, out_w, up_w, down_w, gains, gain_row):
    rows = a.shape[0]
    whole = pl.BlockSpec((rows, D), lambda i: (0, 0))
    return call(
        partial(branch_back_body, gain_row),
        "branch_back",
        [
            shape((rows, D)),
            shape((rows, D), BF16),
            shape((SHARDS, TILE, D)),
            shape((SHARDS, 4 * TILE, D)),
            shape((SHARDS, 4 * TILE, D)),
            shape((1, D)),
        ],
        [cot, mid, a, out_w[0], up_w[0], down_w[0], gains],
        2 * rows * D * D * 22,
        grid=(FF // D,),
        in_specs=[whole, whole, whole, out_w[1](1), up_w[2], down_w[2], pl.BlockSpec(gains.shape, lambda i: (0, 0))],
        out_specs=[
            whole,
            whole,
            pl.BlockSpec((SHARDS, TILE, D), lambda i: (0, 0, 0)),
            pl.BlockSpec((SHARDS, TILE, D), lambda i: (0, i, 0)),
            pl.BlockSpec((8, 4 * TILE, D), lambda i: (i, 0, 0)),
            pl.BlockSpec((1, D), lambda i: (0, 0)),
        ],
        scratch=[
            pltpu.VMEM((rows, D), BF16),
            pltpu.VMEM((D, rows), BF16),
            pltpu.VMEM((rows, D), BF16),
            pltpu.VMEM((rows, D), F32),
        ],
    )


def project_back_body(full, dq_ref, keep_ref, recv_ref, dmid_ref, x_ref, token_ref, w_ref, gain_ref, cos_ref, sin_ref, dw_ref, dgain_ref, dx_ref):
    gain_row = 0 if full else 2
    gain = gain_ref[gain_row : gain_row + 1, :]
    values = x_ref[...].astype(F32)
    hat, scale = norm_parts(values)
    normed_t = (hat * gain).astype(BF16).T
    cosine, sine = cos_ref[...], sin_ref[...]
    rows = values.shape[0]
    skip = rows - dq_ref.shape[0]
    total = jnp.zeros((rows, D), F32)
    for kind in range(3):
        if kind == 0:
            grad = (rope_pull(dq_ref[...] * 0.125, cosine[skip:], sine[skip:])).astype(BF16)
            dw = nn(normed_t[:, skip:], grad)
        else:
            grad = (keep_ref[kind - 1] + recv_ref[kind - 1].astype(F32)).T
            grad = (rope_pull(grad, cosine, sine) if kind == 1 else grad).astype(BF16)
            dw = nn(normed_t, grad)
        dw_ref[:, TILE * kind : TILE * kind + TILE, :] = dw.reshape(SHARDS, TILE, D)
        back = nt(grad, tile_of(w_ref, kind))
        if kind == 0 and skip:
            back = jnp.concatenate([jnp.zeros((skip, D), F32), back], 0)
        total = total + back
    pulled, dgain = norm_pull(hat, scale, gain, total)
    dgain_ref[...] = dgain
    if full:
        back = (dmid_ref[...] + pulled).astype(BF16)
        hot = (token_ref[...] == lax.broadcasted_iota(jnp.int32, (VOCAB, rows), 0)).astype(BF16)
        dx_ref[...] = nn(hot, back)
    else:
        dx_ref[:skip, :] = pulled[:skip]
        dx_ref[skip:, :] = dmid_ref[...] + pulled[skip:]


def project_back(dq, keep, recv, dmid, x, token, packed, gains, cosine, sine, full):
    rows = cosine.shape[0]
    outs = [shape((SHARDS, 3 * TILE, D)), shape((1, D)), shape((VOCAB, D) if full else (rows, D))]
    ins = [dq, keep, recv, dmid, x, token, packed, gains, cosine, sine]
    specs = [pl.BlockSpec(i.shape, lambda s, r=len(i.shape): (0,) * r) for i in ins]
    specs[6] = pl.BlockSpec((SHARDS, 3 * TILE, D), lambda i: (0, 0, 0))
    return call(
        partial(project_back_body, full),
        "project_back",
        outs,
        ins,
        2 * rows * D * D * 6,
        grid=(1,),
        in_specs=specs,
        out_specs=[pl.BlockSpec(o.shape, lambda s, r=len(o.shape): (0,) * r) for o in outs],
    )


def thirds(ref, lead, start):
    found = ref[(*lead, pl.ds(start, CSPAN, stride=SHORT), slice(None))]
    for shift in range(1, SHORT):
        found = found + ref[(*lead, pl.ds(start + shift, CSPAN, stride=SHORT), slice(None))]
    return found


def spread(ref, lead, value):
    for shift in range(SHORT):
        ref[(*lead, pl.ds(shift, CSPAN, stride=SHORT), slice(None))] = value


def pool_body(h_ref, halo_ref, z_ref, scr):
    for slot in range(2):
        for piece in range(D // 128):
            lanes = slice(128 * piece, 128 * piece + 128)
            scr[slot, piece, 6:8, :] = halo_ref[2 * slot : 2 * slot + 2, lanes]
            scr[slot, piece, 8:, :] = h_ref[SPAN * slot : SPAN * slot + SPAN, lanes]
            total = thirds(scr, (slot, piece), 6)
            z_ref[CSPAN * slot : CSPAN * slot + CSPAN, lanes] = total * (1.0 / SHORT)


def pool(h, halo):
    return call(
        pool_body, "pool", [shape((2 * CSPAN, D))], [h, halo], 4 * h.size, scratch=[pltpu.VMEM((2, D // 128, SPAN + 8, 128), F32)]
    )[0]


def head_body(h_ref, z_ref, w_ref, gain_ref, target_ref, counted_ref, rate_ref, loss_ref, dhead_ref, dgain_ref, dh_ref, dz_ref, up_scr):
    pieces = [slice(128 * piece, 128 * piece + 128) for piece in range(D // 128)]
    for piece, lanes in enumerate(pieces):
        spread(up_scr, (piece,), z_ref[:, lanes])
    gain = gain_ref[4:5, :]
    hat, scale = norm_parts(h_ref[...] + jnp.concatenate([up_scr[piece] for piece in range(len(pieces))], 1))
    normed = (hat * gain).astype(BF16)
    head = w_ref[...].reshape(D, VOCAB)
    logits = nn(normed, head)
    top = jnp.max(logits, -1, keepdims=True)
    raised = jnp.exp(logits - top)
    total = jnp.sum(raised, -1, keepdims=True)
    log_total = top + jnp.log(total)
    hot = target_ref[...] == lax.broadcasted_iota(jnp.int32, logits.shape, 1)
    picked = jnp.sum(jnp.where(hot, logits, 0.0), -1, keepdims=True)
    counted = counted_ref[...]
    loss = jnp.sum((log_total - picked) * counted, 0, keepdims=True) * (1.0 / LOG_TWO)
    loss_ref[...] = jnp.broadcast_to(loss, (1, 128))
    grad = ((jnp.exp(logits - log_total) - jnp.where(hot, 1.0, 0.0)) * (counted * rate_ref[0, 0])).astype(BF16)
    dhead_ref[...] = nn(normed.T, grad).reshape(dhead_ref.shape)
    pulled, dgain = norm_pull(hat, scale, gain, nt(grad, head))
    dgain_ref[...] = dgain
    dh_ref[...] = pulled
    for piece, lanes in enumerate(pieces):
        up_scr[piece] = pulled[:, lanes]
        dz_ref[:, lanes] = thirds(up_scr, (piece,), 0)


def head_loss(h, z, head_w, gains, target, counted, rate):
    ins = [h, z, head_w[0], gains, target, counted, rate]
    outs = [shape((1, 128)), shape((SHARDS, TILE, VOCAB)), shape((1, D)), shape((SPAN, D)), shape((CSPAN, D))]
    specs = [pl.BlockSpec(i.shape, lambda s, r=len(i.shape): (0,) * r) for i in ins]
    specs[0] = pl.BlockSpec((SPAN, D), lambda i: (1, 0))
    specs[2] = head_w[1]
    return call(
        head_body,
        "head_loss",
        outs,
        ins,
        6 * SPAN * D * VOCAB,
        grid=(1,),
        in_specs=specs,
        out_specs=[pl.BlockSpec(o.shape, lambda s, r=len(o.shape): (0,) * r) for o in outs],
        scratch=[pltpu.VMEM((D // 128, SPAN, 128), F32)],
    )


def unpool_body(dz_ref, halo_ref, dh_ref, out_ref, scr):
    for slot in range(2):
        for piece in range(D // 128):
            lanes = slice(128 * piece, 128 * piece + 128)
            spread(scr, (slot, piece), dz_ref[CSPAN * slot : CSPAN * slot + CSPAN, lanes] * (1.0 / SHORT))
            edge = halo_ref[slot : slot + 1, lanes] * (1.0 / SHORT)
            scr[slot, piece, SPAN:, :] = jnp.broadcast_to(edge, (8, 128))
            found = scr[slot, piece, 2 : SPAN + 2, :]
            if slot == 1:
                found = found + dh_ref[:, lanes]
            out_ref[SPAN * slot : SPAN * slot + SPAN, lanes] = found


def unpool(dz, halo, dh):
    return call(
        unpool_body, "unpool", [shape((2 * SPAN, D))], [dz, halo, dh], 4 * dz.size, scratch=[pltpu.VMEM((2, D // 128, SPAN + 8, 128), F32)]
    )[0]


def flat_index():
    return lax.axis_index("dp") * lax.axis_size("seq") + lax.axis_index("seq")


def flat_count():
    return lax.axis_size("dp") * lax.axis_size("seq")


def swapped(value, bit):
    return lax.ppermute(value, BOTH, [(i, i ^ (1 << bit)) for i in range(flat_count())])


def bit_of(bit):
    return (flat_index() >> bit) & 1


GATHER_ORDERS = ((4, 3, 2, 1, 0), (4, 3, 1, 2, 0))
REDUCE_ORDERS = ((2, 1, 3, 4), (1, 2, 3, 4))


def gather_tree(part, order):
    bits = len(order)
    value = part.reshape((1,) * bits + part.shape)
    for bit in order:
        axis = bits - 1 - bit
        other = swapped(value, bit)
        value = jnp.where(
            bit_of(bit) == 1, jnp.concatenate([other, value], axis), jnp.concatenate([value, other], axis)
        )
    return value.reshape((2**bits,) + part.shape)


def gather_packed(part):
    half = part.shape[0] // (2 * TILE) * TILE
    return jnp.concatenate(
        [gather_tree(part[:half], GATHER_ORDERS[0]), gather_tree(part[half:], GATHER_ORDERS[1])], 1
    )


def reduce_step(value, bit, bits):
    axis = bits - 1 - bit
    mine = bit_of(bit)
    keep = lax.dynamic_index_in_dim(value, mine, axis, True)
    send = lax.dynamic_index_in_dim(value, 1 - mine, axis, True).astype(BF16)
    return keep + swapped(send, bit).astype(F32)


def reduce_tree(pieces):
    bits = 5
    value = jnp.concatenate(pieces, 1) if len(pieces) > 1 else pieces[0]
    rows = value.shape[1]
    value = reduce_step(value.reshape((2,) * bits + value.shape[1:]), 0, bits)
    half = rows // (2 * TILE) * TILE
    found = []
    for part, order in zip((value[..., :half, :], value[..., half:, :]), REDUCE_ORDERS):
        for bit in order:
            part = reduce_step(part, bit, bits)
        found.append(part.reshape(part.shape[-2:]))
    return jnp.concatenate(found, 0)


def group_perm(ways, links):
    count = lax.axis_size("seq")
    return [(base + a, base + b) for base in range(0, count, ways) for a, b in links]


def gather_group(value, ways):
    rank = lax.axis_index("seq") % ways
    if ways == 2:
        other = lax.ppermute(value, "seq", group_perm(2, ((0, 1), (1, 0))))
        return jnp.where(rank == 0, jnp.stack([value, other]), jnp.stack([other, value]))
    groups = [list(range(base, base + ways)) for base in range(0, lax.axis_size("seq"), ways)]
    return lax.all_gather(value, "seq", axis=0, tiled=False, axis_index_groups=groups)


def in_order(value):
    ways, rows = value.shape[0], value.shape[1] // 2
    blocks = [value[w, :rows] for w in range(ways)] + [value[w, rows:] for w in reversed(range(ways))]
    return jnp.concatenate(blocks, 0)


def scatter_group(value, ways):
    rank = lax.axis_index("seq") % ways
    if ways == 2:
        keep = lax.dynamic_index_in_dim(value, rank, 0, False)
        send = lax.dynamic_index_in_dim(value, 1 - rank, 0, False).astype(BF16)
        return keep, lax.ppermute(send, "seq", group_perm(2, ((0, 1), (1, 0))))
    groups = [list(range(base, base + ways)) for base in range(0, lax.axis_size("seq"), ways)]
    total = lax.psum_scatter(value, "seq", scatter_dimension=0, tiled=False, axis_index_groups=groups)
    return total, jnp.zeros(total.shape, BF16)


def halo_down(first, second, ways):
    rank = lax.axis_index("seq") % ways
    from_low = lax.ppermute(first, "seq", group_perm(ways, [(i, i + 1) for i in range(ways - 1)]))
    from_high = lax.ppermute(second, "seq", group_perm(ways, [(i + 1, i) for i in range(ways - 1)]))
    return from_low, jnp.where(rank == ways - 1, first, from_high)


def halo_up(first, second, ways):
    rank = lax.axis_index("seq") % ways
    from_high = lax.ppermute(first, "seq", group_perm(ways, [(i + 1, i) for i in range(ways - 1)]))
    from_low = lax.ppermute(second, "seq", group_perm(ways, [(i, i + 1) for i in range(ways - 1)]))
    return jnp.where(rank == ways - 1, second, from_high), from_low


def sum_all(value):
    count = flat_count()
    for bit in range(count.bit_length() - 1):
        value = value + swapped(value, bit)
    return value


def tiles(weight):
    rows = weight.shape[0]
    return [weight[:, start : start + D] for start in range(0, weight.shape[1], D)] if rows else []


def pack_edge(embed, gains):
    rows = embed.shape[-2]
    pad = jnp.zeros((8, D - gains.shape[1]), gains.dtype)
    side = jnp.concatenate([jnp.concatenate([gains, jnp.zeros((3, gains.shape[1]), gains.dtype)], 0), pad], 1)
    return jnp.concatenate([embed, side], 0)


def gather_weights(embed, head, attn_in, attn_out, ffn_in, ffn_out, gains):
    if flat_count() == SHARDS:
        head_tile = jnp.concatenate([head, jnp.zeros_like(head)], 1)
        first = jnp.concatenate(tiles(attn_in[0]) + [pack_edge(embed, gains)], 0)
        second = jnp.concatenate(tiles(ffn_in[0]) + [ffn_out[0], attn_out[0]], 0)
        third = jnp.concatenate(tiles(ffn_in[1]) + [ffn_out[1]] + tiles(attn_in[1]) + [attn_out[1], head_tile], 0)
        first = gather_packed(first)
        second = gather_packed(second)
        third = lax.all_gather(third, BOTH, axis=0, tiled=False)
        return first, second, third
    full = [
        lax.all_gather(weight, BOTH, axis=axis, tiled=True)
        for weight, axis in ((embed, 0), (head, 0), (attn_in, 1), (attn_out, 1), (ffn_in, 1), (ffn_out, 1), (gains, 1))
    ]
    embed, head, attn_in, attn_out, ffn_in, ffn_out, gains = full
    fold = lambda weight: weight.reshape(SHARDS, TILE, D)
    edge = jnp.zeros((SHARDS, TILE, D), BF16).at[:, :8].set(embed.reshape(SHARDS, 8, D))
    edge = edge.at[:, 8:13, :TILE].set(gains.reshape(5, SHARDS, TILE).transpose(1, 0, 2))
    head_tile = jnp.zeros((SHARDS, TILE, D), BF16).at[:, :, :VOCAB].set(head.reshape(SHARDS, TILE, VOCAB))
    down = ffn_out.reshape(2, SHARDS, 4 * TILE, D)
    first = jnp.concatenate([fold(t) for t in tiles(attn_in[0])] + [edge], 1)
    second = jnp.concatenate([fold(t) for t in tiles(ffn_in[0])] + [down[0], fold(attn_out[0])], 1)
    third = jnp.concatenate(
        [fold(t) for t in tiles(ffn_in[1])]
        + [down[1]]
        + [fold(t) for t in tiles(attn_in[1])]
        + [fold(attn_out[1]), head_tile],
        1,
    )
    return first, second, third


def reduce_natural(grad, axis):
    return lax.psum_scatter(grad, BOTH, scatter_dimension=axis, tiled=True)


def unfold(packed):
    parts = packed.shape[1] // TILE
    return jnp.concatenate([packed[:, TILE * i : TILE * i + TILE].reshape(D, D) for i in range(parts)], 1)


def local(
    stream, offsets, embed, head, attn_in, attn_out, ffn_in, ffn_out, gains,
    embed_row, embed_col, head_row, head_col, in_row, in_col, out_row, out_col, up_row, up_col, down_row, down_col, gains_sq,
):
    seq_rank = lax.axis_index("seq")
    dp_rank = lax.axis_index("dp")
    seq_count = lax.axis_size("seq")
    per_group = offsets.shape[0] // lax.axis_size("dp")
    ways = seq_count // per_group
    blocks = 2 * ways
    length = SPAN * blocks
    rank = seq_rank % ways
    window_start = offsets[dp_rank * per_group + seq_rank // ways]

    first, second, third = gather_weights(*[w.astype(BF16) for w in (embed, head, attn_in, attn_out, ffn_in, ffn_out, gains)])
    gain_rows = first[:, 3 * TILE + 8 : 3 * TILE + 13, :TILE].transpose(1, 0, 2).reshape(5, D).astype(F32)
    gain_rows = jnp.concatenate([gain_rows, jnp.zeros((3, D), F32)], 0)

    def part(packed, rows, at):
        return (
            packed,
            lambda rank: pl.BlockSpec((SHARDS, rows, D), lambda *i: (0, at // rows, 0)),
            pl.BlockSpec((SHARDS, TILE, D), lambda i: (0, at // TILE + i, 0)),
        )

    def part_down(packed, at):
        return (
            packed,
            lambda rank: pl.BlockSpec((SHARDS, 4 * TILE, D), lambda *i: (0, at // (4 * TILE), 0)),
            pl.BlockSpec((8, 4 * TILE, D), lambda i: (i, at // (4 * TILE), 0)),
        )

    up_0, down_0, out_0 = part(second, 4 * TILE, 0), part_down(second, 4 * TILE), part(second, TILE, 8 * TILE)
    up_1, down_1, out_1 = part(third, 4 * TILE, 0), part_down(third, 4 * TILE), part(third, TILE, 11 * TILE)
    in_1 = third[:, 8 * TILE : 11 * TILE]
    head_w = (third, pl.BlockSpec((SHARDS, TILE, VOCAB), lambda i: (0, 12, 0)))

    limits = jnp.minimum(length, STREAM - 1 - offsets) - (length - length // 2)
    count_real = jnp.sum(jnp.maximum(limits, 0)).astype(F32)
    own_blocks = jnp.stack([rank, blocks - 1 - rank])
    positions = (own_blocks[:, None] * SPAN + jnp.arange(SPAN, dtype=jnp.int32)[None]).reshape(-1)
    coarse_pos = (own_blocks[:, None] * CSPAN + jnp.arange(CSPAN, dtype=jnp.int32)[None]).reshape(-1)
    reach = own_blocks + 1
    starts = window_start + own_blocks * SPAN
    padded = jnp.concatenate([stream, jnp.broadcast_to(stream[-1:], (length,))], 0)
    tokens = jnp.concatenate([lax.dynamic_slice_in_dim(padded, starts[s], SPAN, 0) for s in range(2)], 0)
    target = lax.dynamic_slice_in_dim(padded, starts[1] + 1, SPAN, 0)
    counted = (window_start + positions[SPAN:] + 1 < STREAM).astype(F32)
    rate = (1.0 / (LOG_TWO * count_real)).reshape(1, 1)

    def tables(at):
        frequency = 10000.0 ** (-jnp.arange(HD // 2, dtype=F32) / (HD // 2))
        angles = at.astype(F32)[:, None] * frequency[None, :]
        cosine, sine = jnp.cos(angles), jnp.sin(angles)
        return (jnp.concatenate([cosine] * 4, 1), jnp.concatenate([-sine, sine] * 2, 1))

    cos_0, sin_0 = tables(positions)
    cos_1, sin_1 = tables(coarse_pos)

    h_0, q_0, k_0, v_0 = project(tokens[:, None], jnp.zeros((8, 128), F32), first, gain_rows, cos_0, sin_0, True)
    kv_0 = in_order(gather_group(jnp.concatenate([k_0, v_0], 1), ways))
    k_all_0, v_all_0 = kv_0[:, :D], kv_0[:, D:]
    a_0, lse_0 = attend(reach, q_0, k_all_0, v_all_0, SPAN)
    m_0, h_1 = branch(h_0, a_0, out_0, up_0, down_0, gain_rows, 1)

    halo = halo_down(h_1[SPAN - 2 : SPAN], h_1[2 * SPAN - 2 :], ways)
    z_0 = pool(h_1, jnp.concatenate(halo, 0))
    q_1, k_1, v_1 = project(jnp.zeros((8, 128), jnp.int32), z_0, in_1, gain_rows, cos_1, sin_1, False)
    kv_1 = in_order(gather_group(jnp.concatenate([k_1, v_1], 1), ways))
    k_all_1, v_all_1 = kv_1[:, :D], kv_1[:, D:]
    a_1, lse_1 = attend(reach[1:], q_1, k_all_1, v_all_1, CSPAN)
    m_1, z_1 = branch(z_0[CSPAN:], a_1, out_1, up_1, down_1, gain_rows, 3)
    loss, d_head, dg_4, d_h2, d_z1 = head_loss(h_1, z_1, head_w, gain_rows, target[:, None], counted[:, None], rate)

    d_m1, d_a1, d_out_1, d_up_1, d_down_1, dg_3 = branch_back(d_z1, m_1, a_1, out_1, up_1, down_1, gain_rows, 3)
    d_q1, d_kv1 = attend_back(reach[1:], q_1, k_all_1, v_all_1, d_a1, lse_1, CSPAN)
    keep, recv = scatter_group(d_kv1, ways)
    d_in_1, dg_2, d_z0 = project_back(
        d_q1, keep, recv, d_m1, z_0, jnp.zeros((8, 128), jnp.int32), in_1, gain_rows, cos_1, sin_1, False
    )
    halo = halo_up(d_z0[:1], d_z0[CSPAN : CSPAN + 1], ways)
    d_h1 = unpool(d_z0, jnp.concatenate(halo, 0), d_h2)

    d_m0, d_a0, d_out_0, d_up_0, d_down_0, dg_1 = branch_back(d_h1, m_0, a_0, out_0, up_0, down_0, gain_rows, 1)
    d_q0, d_kv0 = attend_back(reach, q_0, k_all_0, v_all_0, d_a0, lse_0, SPAN)
    keep, recv = scatter_group(d_kv0, ways)
    d_in_0, dg_0, d_embed = project_back(
        d_q0, keep, recv, d_m0, h_0, tokens[None, :], first, gain_rows, cos_0, sin_0, True
    )
    d_gains = jnp.concatenate([dg_0, dg_1, dg_2, dg_3, dg_4], 0)

    if flat_count() == SHARDS:
        head_tile = jnp.concatenate([d_head, jnp.zeros_like(d_head)], 2)
        edge = jnp.concatenate(
            [
                d_embed.reshape(SHARDS, 8, D),
                jnp.pad(d_gains.reshape(5, SHARDS, TILE).transpose(1, 0, 2), ((0, 0), (0, 3), (0, D - TILE))),
            ],
            1,
        )
        late = reduce_tree([d_up_1, d_down_1, d_in_1, d_out_1, head_tile])
        middle = reduce_tree([d_up_0, d_down_0])
        early = reduce_tree([d_in_0, d_out_0, edge])

        def columns(packed, count):
            return jnp.concatenate([packed[TILE * i : TILE * i + TILE] for i in range(count)], 1)

        g_embed = early[4 * TILE : 4 * TILE + 8]
        gain_grad = early[4 * TILE + 8 : 4 * TILE + 13, :TILE]
        g_head = late[12 * TILE :, :VOCAB]
        g_in = jnp.stack([columns(early, 3), columns(late[8 * TILE :], 3)])
        g_out = jnp.stack([early[3 * TILE : 4 * TILE], late[11 * TILE : 12 * TILE]])
        g_up = jnp.stack([columns(middle, 4), columns(late, 4)])
        g_down = jnp.stack([middle[4 * TILE :], late[4 * TILE : 8 * TILE]])
    else:
        g_embed = reduce_natural(d_embed, 0)
        g_head = reduce_natural(d_head.reshape(D, VOCAB), 0)
        g_in = reduce_natural(jnp.stack([unfold(d_in_0), unfold(d_in_1)]), 1)
        g_out = reduce_natural(jnp.stack([unfold(d_out_0), unfold(d_out_1)]), 1)
        g_up = reduce_natural(jnp.stack([unfold(d_up_0), unfold(d_up_1)]), 1)
        g_down = reduce_natural(jnp.stack([d_down_0.reshape(FF, D), d_down_1.reshape(FF, D)]), 1)
        gain_grad = reduce_natural(d_gains, 1)

    decay = 1.0 - STEP ** (-0.8)
    matrices = [
        (g_embed, embed_row, embed_col, embed, VOCAB),
        (g_head, head_row, head_col, head, D),
        (g_in, in_row, in_col, attn_in, D),
        (g_out, out_row, out_col, attn_out, D),
        (g_up, up_row, up_col, ffn_in, D),
        (g_down, down_row, down_col, ffn_out, FF),
    ]
    new_rows, sums = [], []
    for grad, row, _, weight, _ in matrices:
        square = grad * grad
        new_row = decay * row + (1.0 - decay) * jnp.mean(square, -1)
        new_rows.append(new_row)
        sums += [
            jnp.sum(square, -2),
            jnp.sum(square / new_row[..., None], -2),
            jnp.sum(new_row, -1),
            jnp.sum(weight * weight, (-2, -1)),
        ]
    new_sq = decay * gains_sq + (1.0 - decay) * gain_grad * gain_grad
    gain_update = gain_grad / jnp.sqrt(new_sq)
    sums += [jnp.sum(gain_update * gain_update, -1), jnp.sum(gains * gains, -1), loss[0, :1]]
    flat = jnp.concatenate([s.reshape(-1) for s in sums], 0)
    size = flat.shape[0]
    flat = jnp.pad(flat, (0, -size % 1024)).reshape(-1, 128)
    flat = sum_all(flat).reshape(-1)
    totals, at = [], 0
    for s in sums:
        totals.append(flat[at : at + s.size].reshape(s.shape))
        at += s.size
    outputs = [totals[-1].reshape(()), count_real]
    for index, (grad, _, col, weight, full_rows) in enumerate(matrices):
        col_sum, ratio_sum, row_sum, weight_sum = totals[4 * index : 4 * index + 4]
        new_row = new_rows[index]
        new_col = decay * col + (1.0 - decay) * col_sum / full_rows
        mean_row = row_sum / full_rows
        size_all = full_rows * grad.shape[-1]
        update_sum = mean_row * jnp.sum(ratio_sum / new_col, -1)
        rate_now = RATE_SCALE * jnp.sqrt(weight_sum / size_all) / jnp.maximum(1.0, jnp.sqrt(update_sum / size_all))
        update = grad / jnp.sqrt(new_row[..., :, None] * new_col[..., None, :] / mean_row[..., None, None])
        outputs += [grad, new_row, new_col, weight - rate_now[..., None, None] * update]
    gain_rate = RATE_SCALE * jnp.sqrt(totals[-2] / D) / jnp.maximum(1.0, jnp.sqrt(totals[-3] / D))
    outputs += [gain_grad, new_sq, gains - gain_rate[:, None] * gain_update]
    return tuple(outputs)


def solution(mesh):
    row = P(BOTH, None)
    mid = P(None, BOTH, None)
    vec = P(BOTH)
    vec2 = P(None, BOTH)
    state = (vec, P(), vec, P(), vec2, P(), vec2, P(), vec2, P(), vec2, P(), vec2)
    return jax.shard_map(
        local,
        mesh=mesh,
        in_specs=(P(), P(), row, row, mid, mid, mid, mid, vec2) + state,
        out_specs=(P(), P())
        + (row, vec, P(), row) * 2
        + (mid, vec2, P(), mid) * 4
        + (vec2, vec2, vec2),
        check_vma=False,
    )
```

```python
from functools import partial
import math

import jax
import jax.numpy as jnp
from jax import lax
from jax.experimental import pallas as pl
from jax.experimental.pallas import tpu as pltpu
from jax.sharding import PartitionSpec as P

D = 512
HEADS = 8
FF = 2048
VOCAB = 256
SHORT = 3
HD = 64
SPAN = 384
CSPAN = SPAN // SHORT
STREAM = 65536
STEP = 10
SHARDS = 32
TILE = 16

EPSILON = 1e-05
RATE_SCALE = 0.5
LOG_TWO = math.log(2.0)
MASKED = -1e30
GELU_A = math.sqrt(2.0 / math.pi)
GELU_B = 0.044715
BOTH = ("dp", "seq")
F32 = jnp.float32
BF16 = jnp.bfloat16
VMEM_LIMIT = 56 * 2**20


def nn(left, right):
    return jnp.dot(left, right, preferred_element_type=F32)


def nt(left, right):
    return lax.dot_general(left, right, (((1,), (1,)), ((), ())), preferred_element_type=F32)


def call(body, name, outs, ins, us, grid=(1,), in_specs=None, out_specs=None, scratch=(), prefetch=1):
    spec = pltpu.PrefetchScalarGridSpec(
        num_scalar_prefetch=prefetch,
        grid=grid,
        in_specs=in_specs or [whole(i.shape) for i in ins[prefetch:]],
        out_specs=out_specs or [whole(o.shape) for o in outs],
        scratch_shapes=list(scratch),
    )
    return pl.pallas_call(
        body,
        grid_spec=spec,
        out_shape=list(outs),
        compiler_params=pltpu.CompilerParams(vmem_limit_bytes=VMEM_LIMIT),
        cost_estimate=pl.CostEstimate(flops=int(us * 2e10), bytes_accessed=1 << 20, transcendentals=0),
        name=name,
    )(*ins)


def whole(dims):
    return pl.BlockSpec(dims, lambda *_: (0,) * len(dims))


def shape(dims, kind=F32):
    return jax.ShapeDtypeStruct(dims, kind)


RANK, CORE, BITS, CHIP = 2, 3, 4, 9
WEIGHT_PARTS = 4


def norm_parts(values):
    center = values - jnp.mean(values, -1, keepdims=True)
    scale = lax.rsqrt(jnp.mean(center * center, -1, keepdims=True) + EPSILON)
    return center * scale, scale


def norm_pull(hat, scale, gain, cotangent):
    pulled = cotangent * gain
    inner = pulled - jnp.mean(pulled, -1, keepdims=True) - hat * jnp.mean(pulled * hat, -1, keepdims=True)
    return scale * inner, jnp.sum(cotangent * hat, 0, keepdims=True)


def swap_halves(values):
    lane = lax.broadcasted_iota(jnp.int32, values.shape, 1)
    return jnp.where(lane % HD < HD // 2, pltpu.roll(values, 128 - HD // 2, 1), pltpu.roll(values, HD // 2, 1))


def rope(values, cosine, sine):
    pieces = []
    for start in range(0, D, 128):
        piece = values[:, start : start + 128]
        pieces.append(piece * cosine + swap_halves(piece) * sine)
    return jnp.concatenate(pieces, 1)


def rope_pull(values, cosine, sine):
    pieces = []
    for start in range(0, D, 128):
        piece = values[:, start : start + 128]
        pieces.append(piece * cosine + swap_halves(piece * sine))
    return jnp.concatenate(pieces, 1)


def gelu_parts(values):
    inner = GELU_A * (values + GELU_B * (values * values * values))
    wave = jnp.tanh(inner)
    return wave, 0.5 * (1.0 + wave)


def gelu_slope(values, wave, gate):
    return gate + 0.5 * values * (1.0 - wave * wave) * (GELU_A * (1.0 + 3.0 * GELU_B * values * values))


def tile_of(ref, index):
    return ref[:, TILE * index : TILE * index + TILE, :].reshape(D, ref.shape[-1])


def settle(refs, scr, info, second):
    if len(refs) == 1:
        return refs[0]
    last, next_last = (1, 0) if second else (0, 1)

    def place(r, carry):
        mask = ((r & 1) << 3) | (((r >> 1) & 1) << 2) | (((r >> 2) & 1) << next_last)
        for far in range(2):
            chip = info[CHIP] ^ (mask | (far << last))
            scr[2 * chip + info[CORE]] = refs[far][r]
            scr[2 * chip + 1 - info[CORE]] = refs[2 + far][r]
        return carry

    lax.fori_loop(0, SHARDS // 4, place, 0)
    return scr


def front(bundle, rows):
    return [pl.BlockSpec((value.shape[0], rows, D), lambda *_: (0, 0, 0)) for value in bundle]


def bundle_scratch(*bundles):
    return [pltpu.VMEM((SHARDS, *bundle[0].shape[1:]), BF16) for bundle in bundles if len(bundle) > 1]


def thirds(ref, lead, start):
    found = ref[(*lead, pl.ds(start, CSPAN, stride=SHORT), slice(None))]
    for shift in range(1, SHORT):
        found = found + ref[(*lead, pl.ds(start + shift, CSPAN, stride=SHORT), slice(None))]
    return found


def spread(ref, lead, value):
    for shift in range(SHORT):
        ref[(*lead, pl.ds(shift, CSPAN, stride=SHORT), slice(None))] = value


LANES = [slice(start, start + 128) for start in range(0, D, 128)]


def grad_shapes(rows, split):
    if split:
        return [shape((SHARDS // 2, rows, D)), shape((SHARDS // 2, rows, D), BF16)]
    return [shape((SHARDS, rows, D))]


def grad_specs(rows, split, index, shards=SHARDS):
    if split:
        return [pl.BlockSpec((shards // 2, rows, D), index)] * 2
    return [pl.BlockSpec((shards, rows, D), index)]


def put(refs, core, value, at=0, rows=TILE, chunk=0):
    width = value.shape[-1]
    part = pl.ds(at, rows)
    shards = D // rows
    if len(refs) == 2:
        pairs = value.reshape(shards // 2, 2, rows, width)
        low, high = pairs[:, 0], pairs[:, 1]
        where = pl.ds(chunk * (shards // 2), shards // 2)
        refs[0][where, part, :width] = jnp.where(core == 0, low, high)
        refs[1][where, part, :width] = jnp.where(core == 0, high, low).astype(BF16)
    else:
        refs[0][pl.ds(chunk * shards, shards), part, :width] = value.reshape(shards, rows, width).astype(refs[0].dtype)


def project_body(info, token_ref, *rest, each):
    wa_refs, wb_refs = rest[:each], rest[each : 2 * each]
    cos_ref, sin_ref, h_ref, q_ref, k_ref, v_ref, gain_ref = rest[2 * each : 2 * each + 7]
    scr = rest[2 * each + 7 :]
    wa_ref, wb_ref = scr if each > 1 else (wa_refs[0], wb_refs[0])

    @pl.when(pl.program_id(0) == 0)
    def _():
        settle(wa_refs, scr and scr[0], info, False)
        settle(wb_refs, scr and scr[1], info, True)
        lane = lax.broadcasted_iota(jnp.int32, (8, D), 1)
        found = jnp.zeros((8, D), F32)
        for shard in range(SHARDS):
            side = wb_ref[shard, TILE : 2 * TILE, :].astype(F32)[8:]
            side = side if shard == 0 else pltpu.roll(side, TILE * shard, 1)
            found = jnp.where(lane // TILE == shard, side, found)
        gain_ref[...] = found

    token = token_ref[...]
    row = (token // 8) * TILE + token % 8
    hot = (row == lax.broadcasted_iota(jnp.int32, (token.shape[0], D), 1)).astype(BF16)
    values = nn(hot, tile_of(wb_ref, 1))
    h_ref[...] = values.astype(BF16)
    normed = (norm_parts(values)[0] * gain_ref[0:1, :]).astype(BF16)
    cosine, sine = cos_ref[...], sin_ref[...]
    q_ref[...] = (rope(nn(normed, tile_of(wa_ref, 0)), cosine, sine) * 0.125).astype(BF16)
    k_ref[...] = rope(nn(normed, tile_of(wa_ref, 1)), cosine, sine).astype(BF16)
    v_ref[...] = nn(normed, tile_of(wb_ref, 0)).astype(BF16)


def project(info, token, bundles, cosine, sine):
    rows = cosine.shape[0]
    step = SPAN
    weights = [*bundles[0], *bundles[1]]
    return call(
        partial(project_body, each=len(bundles[0])),
        "project",
        [shape((rows, D), BF16)] * 4 + [shape((8, D))],
        [info, token, *weights, cosine, sine],
        5,
        grid=(rows // step,),
        in_specs=[pl.BlockSpec((step, 1), lambda i, _: (i, 0))]
        + [whole(w.shape) for w in weights]
        + [pl.BlockSpec((step, 128), lambda i, _: (i, 0))] * 2,
        out_specs=[pl.BlockSpec((step, D), lambda i, _: (i, 0))] * 4 + [whole((8, D))],
        scratch=bundle_scratch(*bundles),
    )


def project_short_body(
    info, h_ref, tail_ref, low_ref, high_ref, w_ref, gain_ref, cos_ref, sin_ref, z_ref, q_ref, k_ref, v_ref, scr, *, ways
):
    for slot in range(2):
        if slot == 0:
            halo = low_ref[...]
        else:
            halo = jnp.where(info[RANK] == ways - 1, tail_ref[0], high_ref[...])
        for piece, lanes in enumerate(LANES):
            scr[slot, piece, :8, :] = halo[:, lanes]
            scr[slot, piece, 8:, :] = h_ref[SPAN * slot : SPAN * slot + SPAN, lanes]
            total = thirds(scr, (slot, piece), 6)
            z_ref[CSPAN * slot : CSPAN * slot + CSPAN, lanes] = total * (1.0 / SHORT)
    normed = (norm_parts(z_ref[...])[0] * gain_ref[2:3, :]).astype(BF16)
    cosine, sine = cos_ref[...], sin_ref[...]
    query = nn(normed[CSPAN:], tile_of(w_ref, 0))
    q_ref[...] = (rope(query, cosine[CSPAN:], sine[CSPAN:]) * 0.125).astype(BF16)
    k_ref[...] = rope(nn(normed, tile_of(w_ref, 1)), cosine, sine).astype(BF16)
    v_ref[...] = nn(normed, tile_of(w_ref, 2)).astype(BF16)


def project_short(info, h, tail, low, high, packed, gains, cosine, sine, ways):
    outs = [shape((2 * CSPAN, D)), shape((CSPAN, D), BF16), shape((2 * CSPAN, D), BF16), shape((2 * CSPAN, D), BF16)]
    ins = [info, h, tail, low, high, packed, gains, cosine, sine]
    specs = [whole(i.shape) for i in ins[1:]]
    specs[4:5] = front([packed], 3 * TILE)
    return call(
        partial(project_short_body, ways=ways),
        "project_short",
        outs,
        ins,
        4,
        in_specs=specs,
        scratch=[pltpu.VMEM((2, D // 128, SPAN + 8, 128), F32)],
    )


def order_keys(info, own, other, found, block, count):
    for at in range(count):
        owner = min(at, count - 1 - at)
        place = 0 if owner == at else 1
        part = slice(place * block, place * block + block)
        found[at * block : at * block + block, :] = jnp.where(info[RANK] == owner, own[part, :], other[part, :])


def each_rows(rows, steps, count):
    if count <= 4:
        for i in range(steps):
            rows(i)
    else:
        lax.fori_loop(0, steps, lambda i, carry: (rows(i), carry)[1], 0)


def each_head(head, together):
    if together == 4:
        for j in range(4):
            head(j)
        return

    def some(i, carry):
        for j in range(together):
            head(i * together + j)
        return carry

    lax.fori_loop(0, 4 // together, some, 0)


def masked_rows(s_scr, part, start, step, block, width):
    score = s_scr[part, :width]
    row = start + lax.broadcasted_iota(jnp.int32, (step, block), 0)
    key = lax.broadcasted_iota(jnp.int32, (step, block), 1)
    edge = jnp.where(row >= key, score[:, width - block :], MASKED)
    return jnp.concatenate([score[:, : width - block], edge], 1) if width > block else edge


def rows_part(i, step):
    return pl.ds(i * step if isinstance(i, int) else pl.multiple_of(i * step, step), step)


def attend_body(info, q_ref, *rest, count, block, step, pair, base):
    if pair:
        k_own, k_other, v_own, v_other, out_ref, lse_ref, s_scr, p_scr, k_ref, v_ref = rest
    else:
        k_ref, v_ref, out_ref, lse_ref, s_scr, p_scr = rest
    slot = pl.program_id(1)
    nk = info[slot + base]
    lane = lax.broadcasted_iota(jnp.int32, (1, 256), 1)
    column = lax.broadcasted_iota(jnp.int32, (step, 128), 1)
    zero = jnp.zeros((), BF16)
    if pair:

        @pl.when(slot == 0)
        def _():
            order_keys(info, k_own, k_other, k_ref, block, count)
            order_keys(info, v_own, v_other, v_ref, block, count)

    def variant(blocks):
        width = blocks * block

        def head(j):
            mine = lane // HD == j
            s_scr[:, :width] = nt(jnp.where(mine, q_ref[...], zero), k_ref[:width, :])

            def rows(i):
                part = rows_part(i, step)
                score = masked_rows(s_scr, part, i * step, step, block, width)
                top = jnp.max(score, -1, keepdims=True)
                raised = jnp.exp(score - top)
                total = jnp.sum(raised, -1, keepdims=True)
                p_scr[part, :width] = (raised * (1.0 / total)).astype(BF16)
                lse_ref[0, 0, part, :] = jnp.where(column == j, top + jnp.log(total), lse_ref[0, 0, part, :])

            each_rows(rows, block // step, count)
            found = nn(p_scr[:, :width], v_ref[:width, :]).astype(BF16)
            out_ref[...] = jnp.where(mine, found, out_ref[...])

        each_head(head, 4 if count <= 4 else 1)

    for blocks in range(1, count + 1):
        pl.when(nk == blocks)(partial(variant, blocks))


def attend(info, q, keys, block, first, groups):
    slots = q.shape[0] // block
    pair = len(keys) == 4
    total = keys[0].shape[0] * (2 if pair else 1)
    count = total // block
    scratch = [pltpu.VMEM((block, total), F32), pltpu.VMEM((block, total), BF16)]
    if pair:
        scratch += [pltpu.VMEM((total, 256), BF16)] * 2
    return call(
        partial(attend_body, count=count, block=block, step=64, pair=pair, base=2 - slots),
        "attend",
        [shape((slots * block, 256 * groups), BF16), shape((groups, slots, block, 128))],
        [info, q, *keys],
        8 if block == SPAN else 4,
        grid=(groups, slots),
        in_specs=[pl.BlockSpec((block, 256), lambda h, s, _: (s, h + first))]
        + [pl.BlockSpec((key.shape[0], 256), lambda h, s, _: (0, h + first)) for key in keys],
        out_specs=[
            pl.BlockSpec((block, 256), lambda h, s, _: (s, h)),
            pl.BlockSpec((1, 1, block, 128), lambda h, s, _: (h, s, 0, 0)),
        ],
        scratch=scratch,
    )


def attend_back_body(info, q_ref, *rest, count, block, step, pair, base):
    if pair:
        k_own, k_other, v_own, v_other, back_ref, lse_ref, dq_ref, keep_ref, send_ref = rest[:9]
        s_scr, dp_scr, p_scr, ds_scr, dk_scr, dv_scr, qt_scr, bt_scr, k_ref, v_ref = rest[9:]
    else:
        k_ref, v_ref, back_ref, lse_ref, dq_ref, keep_ref = rest[:6]
        s_scr, dp_scr, p_scr, ds_scr, dk_scr, dv_scr, qt_scr, bt_scr = rest[6:]
    slot = pl.program_id(1)
    nk = info[slot + base]
    lane = lax.broadcasted_iota(jnp.int32, (1, 256), 1)
    column = lax.broadcasted_iota(jnp.int32, (step, 128), 1)
    zero = jnp.zeros((), BF16)

    qt_scr[...] = q_ref[...].T
    bt_scr[...] = back_ref[...].T

    @pl.when(slot == 0)
    def _():
        dk_scr[...] = jnp.zeros_like(dk_scr)
        dv_scr[...] = jnp.zeros_like(dv_scr)
        if pair:
            order_keys(info, k_own, k_other, k_ref, block, count)
            order_keys(info, v_own, v_other, v_ref, block, count)

    def variant(blocks):
        width = blocks * block

        def head(j):
            mine = lane // HD == j
            s_scr[:, :width] = nt(jnp.where(mine, q_ref[...], zero), k_ref[:width, :])
            dp_scr[:, :width] = nt(jnp.where(mine, back_ref[...], zero), v_ref[:width, :])

            def rows(i):
                part = rows_part(i, step)
                score = masked_rows(s_scr, part, i * step, step, block, width)
                lse = jnp.sum(jnp.where(column == j, lse_ref[0, 0, part, :], 0.0), -1, keepdims=True)
                prob = jnp.exp(score - lse)
                p_scr[part, :width] = prob.astype(BF16)
                prob_back = dp_scr[part, :width]
                delta = jnp.sum(prob * prob_back, -1, keepdims=True)
                ds_scr[part, :width] = (prob * (prob_back - delta)).astype(BF16)

            each_rows(rows, block // step, count)
            found = nn(ds_scr[:, :width], k_ref[:width, :])
            dq_ref[...] = jnp.where(mine, found, dq_ref[...])
            own = pl.ds(HD * j if isinstance(j, int) else pl.multiple_of(HD * j, HD), HD)
            dk_scr[own, :width] += nn(qt_scr[own, :], ds_scr[:, :width])
            dv_scr[own, :width] += nn(bt_scr[own, :], p_scr[:, :width])

        each_head(head, 2 if count <= 4 else 1)

    for blocks in range(1, count + 1):
        pl.when(nk == blocks)(partial(variant, blocks))

    @pl.when(slot == pl.num_programs(1) - 1)
    def _():
        for kind, scr in enumerate((dk_scr, dv_scr)):
            for place in range(2):
                to = slice(place * block, place * block + block)

                def from_owner(owner):
                    at = owner if place == 0 else count - 1 - owner
                    return scr[:, at * block : at * block + block]

                if pair:
                    low, high = from_owner(0), from_owner(1)
                    keep_ref[kind, :, to] = jnp.where(info[RANK] == 0, low, high)
                    send_ref[kind, :, to] = jnp.where(info[RANK] == 0, high, low).astype(BF16)
                else:
                    for owner in range(count // 2):
                        keep_ref[owner, kind, :, to] = from_owner(owner)


def attend_back(info, q, keys, back, lse, block, first, groups):
    slots = q.shape[0] // block
    pair = len(keys) == 4
    total = keys[0].shape[0] * (2 if pair else 1)
    count = total // block
    outs = [shape((slots * block, 256 * groups))]
    out_specs = [pl.BlockSpec((block, 256), lambda h, s, _: (s, h))]
    if pair:
        outs += [shape((2, 256 * groups, 2 * block)), shape((2, 256 * groups, 2 * block), BF16)]
        out_specs += [pl.BlockSpec((2, 256, 2 * block), lambda h, s, _: (0, h, 0))] * 2
    else:
        outs += [shape((count // 2, 2, 256 * groups, 2 * block))]
        out_specs += [pl.BlockSpec((count // 2, 2, 256, 2 * block), lambda h, s, _: (0, 0, h, 0))]
    scratch = [
        pltpu.VMEM((block, total), F32),
        pltpu.VMEM((block, total), F32),
        pltpu.VMEM((block, total), BF16),
        pltpu.VMEM((block, total), BF16),
        pltpu.VMEM((256, total), F32),
        pltpu.VMEM((256, total), F32),
        pltpu.VMEM((256, block), BF16),
        pltpu.VMEM((256, block), BF16),
    ]
    if pair:
        scratch += [pltpu.VMEM((total, 256), BF16)] * 2
    return call(
        partial(attend_back_body, count=count, block=block, step=64, pair=pair, base=2 - slots),
        "attend_back",
        outs,
        [info, q, *keys, back, lse],
        13 if block == SPAN else 7,
        grid=(groups, slots),
        in_specs=[pl.BlockSpec((block, 256), lambda h, s, _: (s, h + first))]
        + [pl.BlockSpec((key.shape[0], 256), lambda h, s, _: (0, h + first)) for key in keys]
        + [
            pl.BlockSpec((block, 256), lambda h, s, _: (s, h)),
            pl.BlockSpec((1, 1, block, 128), lambda h, s, _: (h, s, 0, 0)),
        ],
        out_specs=out_specs,
        scratch=scratch,
    )


def branch_body(info, x_ref, a0_ref, a1_ref, *rest, each):
    up_refs, down_refs = rest[:each], rest[each : 2 * each]
    gain_ref, mid_ref, res_ref, tail_ref = rest[2 * each : 2 * each + 4]
    scr = rest[2 * each + 4 :]
    up_w, down_w = scr if each > 1 else (up_refs[0], down_refs[0])

    @pl.when(pl.program_id(0) == 0)
    def _():
        settle(up_refs, scr and scr[0], info, False)
        settle(down_refs, scr and scr[1], info, True)

    out_tile = tile_of(down_w, 4)
    middle = x_ref[...].astype(F32) + nn(a0_ref[...], out_tile[:256]) + nn(a1_ref[...], out_tile[256:])
    mid_ref[...] = middle
    normed = (norm_parts(middle)[0] * gain_ref[1:2, :]).astype(BF16)
    total = mid_ref[...]
    for chunk in range(FF // D):
        up = nn(normed, tile_of(up_w, chunk))
        hidden = (up * gelu_parts(up)[1]).astype(BF16)
        total = total + nn(hidden, down_w[8 * chunk : 8 * chunk + 8, : 4 * TILE, :].reshape(D, D))
    res_ref[...] = total
    tail_ref[0] = total[total.shape[0] - 8 :]


def branch(info, x, parts, bundles, gains):
    rows = x.shape[0]
    row = lambda width: pl.BlockSpec((SPAN, width), lambda i, _: (i, 0))
    weights = [*bundles[0], *bundles[1]]
    return call(
        partial(branch_body, each=len(bundles[0])),
        "branch",
        [shape((rows, D)), shape((rows, D)), shape((2, 8, D))],
        [info, x, *parts, *weights, gains],
        9,
        grid=(rows // SPAN,),
        in_specs=[row(D), row(256), row(256), *[whole(w.shape) for w in weights], whole(gains.shape)],
        out_specs=[row(D), row(D), pl.BlockSpec((1, 8, D), lambda i, _: (i, 0, 0))],
        scratch=bundle_scratch(*bundles),
    )


def branch_back_body(info, dz_ref, edge_ref, high_ref, low_ref, dh_ref, mid_ref, a0_ref, a1_ref, *rest, ways, split):
    each = 2 if split else 1
    parts = WEIGHT_PARTS if split else 1
    uw_refs, dw_refs, gain_ref = rest[:parts], rest[parts : 2 * parts], rest[2 * parts]
    rest = rest[2 * parts + 1 :]
    dmid_ref, da0_ref, da1_ref, dgain_ref = rest[:4]
    up_refs, down_refs = rest[4 : 4 + each], rest[4 + each : 4 + 2 * each]
    norm_scr, normt_scr, cot_scr, cotb_scr, acc_scr, pool_scr = rest[4 + 2 * each : 10 + 2 * each]
    w_scr = rest[10 + 2 * each :]
    up_w, down_w = w_scr if split else (uw_refs[0], dw_refs[0])
    chunk = pl.program_id(0)
    core = info[CORE]

    @pl.when(chunk == 0)
    def _():
        settle(uw_refs, w_scr and w_scr[0], info, False)
        settle(dw_refs, w_scr and w_scr[1], info, True)
        for slot in range(2):
            if slot == 0:
                edge = jnp.where(info[RANK] == ways - 1, edge_ref[1], high_ref[...])
            else:
                edge = low_ref[...]
            for piece, lanes in enumerate(LANES):
                spread(pool_scr, (slot, piece), dz_ref[CSPAN * slot : CSPAN * slot + CSPAN, lanes] * (1.0 / SHORT))
                pool_scr[slot, piece, SPAN:, :] = jnp.broadcast_to(edge[0:1, lanes] * (1.0 / SHORT), (8, 128))
                found = pool_scr[slot, piece, 2 : SPAN + 2, :]
                if slot == 1:
                    found = found + dh_ref[:, lanes]
                cot_scr[SPAN * slot : SPAN * slot + SPAN, lanes] = found
        cotb_scr[...] = cot_scr[...].astype(BF16)
        normed = (norm_parts(mid_ref[...])[0] * gain_ref[1:2, :]).astype(BF16)
        norm_scr[...] = normed
        normt_scr[...] = normed.T
        acc_scr[...] = jnp.zeros_like(acc_scr)

    down_in = cotb_scr[...]
    up_tile = up_w[:, pl.ds(pl.multiple_of(chunk * TILE, TILE), TILE), :].reshape(D, D)
    down_tile = down_w[pl.ds(chunk * 8, 8), : 4 * TILE, :].reshape(D, D)
    up = nn(norm_scr[...], up_tile)
    wave, gate = gelu_parts(up)
    hidden = (up * gate).astype(BF16)
    up_in = (nt(down_in, down_tile) * gelu_slope(up, wave, gate)).astype(BF16)
    put(down_refs, core, nn(hidden.T, down_in), rows=4 * TILE, chunk=chunk)
    put(up_refs, core, nn(normt_scr[...], up_in))
    acc_scr[...] += nt(up_in, up_tile)

    @pl.when(chunk == FF // D - 1)
    def _():
        hat, scale = norm_parts(mid_ref[...])
        pulled, dgain = norm_pull(hat, scale, gain_ref[1:2, :], acc_scr[...])
        dgain_ref[...] = dgain
        dmid = cot_scr[...] + pulled
        dmid_ref[...] = dmid
        out_in = dmid.astype(BF16)
        out_tile = tile_of(down_w, 4)
        put(down_refs, core, jnp.concatenate([nn(a0_ref[...].T, out_in), nn(a1_ref[...].T, out_in)], 0), at=4 * TILE)
        da0_ref[...] = nt(out_in, out_tile[:256]).astype(BF16)
        da1_ref[...] = nt(out_in, out_tile[256:]).astype(BF16)


def branch_back(info, dz, edge, high, low, dh, mid, parts, bundles, gains, ways, split):
    rows = mid.shape[0]
    ins = [info, dz, edge, high, low, dh, mid, *parts, *bundles[0], *bundles[1], gains]
    specs = [whole(i.shape) for i in ins[1:]]
    return call(
        partial(branch_back_body, ways=ways, split=split),
        "branch_back",
        [shape((rows, D)), shape((rows, 256), BF16), shape((rows, 256), BF16), shape((1, D))]
        + grad_shapes(4 * TILE, split)
        + grad_shapes(5 * TILE, split),
        ins,
        18,
        grid=(FF // D,),
        in_specs=specs,
        out_specs=[whole((rows, D)), whole((rows, 256)), whole((rows, 256)), whole((1, D))]
        + grad_specs(TILE, split, lambda i, _: (0, i, 0))
        + grad_specs(5 * TILE, split, lambda i, _: (0, 0, 0)),
        scratch=[
            pltpu.VMEM((rows, D), BF16),
            pltpu.VMEM((D, rows), BF16),
            pltpu.VMEM((rows, D), F32),
            pltpu.VMEM((rows, D), BF16),
            pltpu.VMEM((rows, D), F32),
            pltpu.VMEM((2, D // 128, SPAN + 8, 128), F32),
            *bundle_scratch(*bundles),
        ],
    )


def short_body(info, x_ref, a_ref, h_ref, *rest, split):
    each = 2 if split else 1
    w_ref, gain_ref, target_ref, counted_ref, rate_ref = rest[:5]
    rest = rest[5:]
    loss_ref, dg4_ref, dg3_ref, dh_ref, dmid_ref, da_ref = rest[:6]
    up_refs, down_refs, head_refs = [rest[6 + each * i : 6 + each * i + each] for i in range(3)]
    mid_scr, norm_scr, normt_scr, cot_scr, acc_scr, up_scr = rest[6 + 3 * each :]
    down_rows = slice(7 * TILE, 11 * TILE)
    step = pl.program_id(0)
    core = info[CORE]

    @pl.when(step == 0)
    def _():
        middle = x_ref[...] + nn(a_ref[...], tile_of(w_ref, 11))
        mid_scr[...] = middle
        normed = (norm_parts(middle)[0] * gain_ref[3:4, :]).astype(BF16)
        norm_scr[...] = normed
        normt_scr[...] = normed.T
        total = mid_scr[...]
        for chunk in range(FF // D):
            up = nn(normed, tile_of(w_ref, 3 + chunk))
            hidden = (up * gelu_parts(up)[1]).astype(BF16)
            total = total + nn(hidden, w_ref[8 * chunk : 8 * chunk + 8, down_rows, :].reshape(D, D))
        for piece, lanes in enumerate(LANES):
            spread(up_scr, (piece,), total[:, lanes])
        gain = gain_ref[4:5, :]
        hat, scale = norm_parts(h_ref[...] + jnp.concatenate([up_scr[piece] for piece in range(len(LANES))], 1))
        final = (hat * gain).astype(BF16)
        head = tile_of(w_ref, 12)[:, :VOCAB]
        logits = nn(final, head)
        top = jnp.max(logits, -1, keepdims=True)
        log_total = top + jnp.log(jnp.sum(jnp.exp(logits - top), -1, keepdims=True))
        hot = target_ref[...] == lax.broadcasted_iota(jnp.int32, logits.shape, 1)
        picked = jnp.sum(jnp.where(hot, logits, 0.0), -1, keepdims=True)
        counted = counted_ref[...]
        loss = jnp.sum((log_total - picked) * counted, 0, keepdims=True) * (1.0 / LOG_TWO)
        loss_ref[...] = jnp.broadcast_to(loss, (1, 128))
        grad = ((jnp.exp(logits - log_total) - jnp.where(hot, 1.0, 0.0)) * (counted * rate_ref[0, 0])).astype(BF16)
        dhead = nn(final.T, grad)
        put(head_refs, core, jnp.concatenate([dhead, jnp.zeros((D, D - VOCAB), F32)], 1))
        pulled, dgain = norm_pull(hat, scale, gain, nt(grad, head))
        dg4_ref[...] = dgain
        dh_ref[...] = pulled
        for piece, lanes in enumerate(LANES):
            up_scr[piece] = pulled[:, lanes]
            cot_scr[:, lanes] = thirds(up_scr, (piece,), 0)
        acc_scr[...] = jnp.zeros_like(acc_scr)

    @pl.when(step > 0)
    def _():
        chunk = step - 1
        down_in = cot_scr[...].astype(BF16)
        up_tile = w_ref[:, pl.ds(pl.multiple_of((chunk + 3) * TILE, TILE), TILE), :].reshape(D, D)
        up = nn(norm_scr[...], up_tile)
        wave, gate = gelu_parts(up)
        hidden = (up * gate).astype(BF16)
        up_in = (nt(down_in, w_ref[pl.ds(chunk * 8, 8), down_rows, :].reshape(D, D)) * gelu_slope(up, wave, gate)).astype(BF16)
        put(down_refs, core, nn(hidden.T, down_in), rows=4 * TILE, chunk=chunk)
        put(up_refs, core, nn(normt_scr[...], up_in))
        acc_scr[...] += nt(up_in, up_tile)

    @pl.when(step == FF // D)
    def _():
        hat, scale = norm_parts(mid_scr[...])
        pulled, dgain = norm_pull(hat, scale, gain_ref[3:4, :], acc_scr[...])
        dg3_ref[...] = dgain
        dmid = cot_scr[...] + pulled
        dmid_ref[...] = dmid
        out_in = dmid.astype(BF16)
        put(down_refs, core, nn(a_ref[...].T, out_in), at=4 * TILE)
        da_ref[...] = nt(out_in, tile_of(w_ref, 11)).astype(BF16)


def short_rest(info, z, a, h, packed, gains, target, counted, rate, split):
    ins = [info, z, a, h, packed, gains, target, counted, rate]
    specs = [whole(i.shape) for i in ins[1:]]
    specs[0] = pl.BlockSpec((CSPAN, D), lambda *_: (1, 0))
    specs[2] = pl.BlockSpec((SPAN, D), lambda *_: (1, 0))
    specs[-1] = pl.BlockSpec(memory_space=pltpu.SMEM)
    return call(
        partial(short_body, split=split),
        "short_rest",
        [shape((1, 128)), shape((1, D)), shape((1, D)), shape((SPAN, D)), shape((CSPAN, D)), shape((CSPAN, D), BF16)]
        + grad_shapes(4 * TILE, split)
        + grad_shapes(5 * TILE, split)
        + grad_shapes(TILE, split),
        ins,
        12,
        grid=(FF // D + 1,),
        in_specs=specs,
        out_specs=[whole((1, 128)), whole((1, D)), whole((1, D)), whole((SPAN, D)), whole((CSPAN, D)), whole((CSPAN, D))]
        + grad_specs(TILE, split, lambda i, _: (0, jnp.maximum(i - 1, 0), 0))
        + grad_specs(5 * TILE, split, lambda i, _: (0, 0, 0))
        + grad_specs(TILE, split, lambda i, _: (0, 0, 0)),
        scratch=[
            pltpu.VMEM((CSPAN, D), F32),
            pltpu.VMEM((CSPAN, D), BF16),
            pltpu.VMEM((D, CSPAN), BF16),
            pltpu.VMEM((CSPAN, D), F32),
            pltpu.VMEM((CSPAN, D), F32),
            pltpu.VMEM((D // 128, SPAN, 128), F32),
        ],
    )


def project_back_body(info, *refs, full, split, groups):
    refs = list(refs)
    take = lambda n: [refs.pop(0) for _ in range(n)]
    dqs, keeps, recvs = take(groups), take(groups), take(groups)
    dmid_ref, x_ref = take(2)
    if full:
        (token_ref,) = take(1)
        wa_refs, wb_refs = [take(WEIGHT_PARTS if split else 1) for _ in range(2)]
        dg_refs = take(4)
        wa_ref = settle(wa_refs, refs[-2], info, False)
        wb_ref = settle(wb_refs, refs[-1], info, True)
        weight = [tile_of(wa_ref, 0), tile_of(wa_ref, 1), tile_of(wb_ref, 0)]
    else:
        (w_ref,) = take(1)
        weight = [tile_of(w_ref, kind) for kind in range(3)]
    gain_ref, cos_ref, sin_ref = take(3)
    each = 2 if split else 1
    first_refs = take(each)
    if full:
        second_refs = take(each)
    if not full or not split:
        dgain_ref, dx_ref = take(2)
    if not full:
        (edge_ref,) = take(1)
    core = info[CORE]
    gain = gain_ref[0:1, :] if full else gain_ref[2:3, :]
    hat, scale = norm_parts(x_ref[...].astype(F32))
    normed_t = (hat * gain).astype(BF16).T
    cosine, sine = cos_ref[...], sin_ref[...]
    rows = hat.shape[0]
    skip = rows - dqs[0].shape[0]
    total = jnp.zeros((rows, D), F32)
    for kind in range(3):
        if kind == 0:
            grad = jnp.concatenate([dq[...] for dq in dqs], 1) if groups > 1 else dqs[0][...]
            grad = rope_pull(grad * 0.125, cosine[skip:], sine[skip:]).astype(BF16)
            found = nn(normed_t[:, skip:], grad)
        else:
            both = [(keep[kind - 1] + recv[kind - 1].astype(F32)).T for keep, recv in zip(keeps, recvs)]
            grad = jnp.concatenate(both, 1) if groups > 1 else both[0]
            grad = (rope_pull(grad, cosine, sine) if kind == 1 else grad).astype(BF16)
            found = nn(normed_t, grad)
        if full and kind == 2:
            put(second_refs, core, found)
        else:
            put(first_refs, core, found, at=TILE * kind)
        back = nt(grad, weight[kind])
        if kind == 0 and skip:
            back = jnp.concatenate([jnp.zeros((skip, D), F32), back], 0)
        total = total + back
    pulled, dgain = norm_pull(hat, scale, gain, total)
    if not full:
        dgain_ref[...] = dgain
        dx = jnp.concatenate([pulled[:skip], dmid_ref[...] + pulled[skip:]], 0)
        dx_ref[...] = dx
        for slot in range(2):
            edge_ref[slot] = dx[CSPAN * slot : CSPAN * slot + 8]
        return
    back = (dmid_ref[...] + pulled).astype(BF16)
    hot = (token_ref[...] == lax.broadcasted_iota(jnp.int32, (VOCAB, rows), 0)).astype(BF16)
    dembed = nn(hot, back)
    if not split:
        dgain_ref[...] = dgain
        dx_ref[...] = dembed
        return
    dgains = jnp.concatenate([dgain] + [ref[...] for ref in dg_refs] + [jnp.zeros((3, D), F32)], 0)
    lane = lax.broadcasted_iota(jnp.int32, (8, D), 1)
    sides = [
        jnp.where(lane < TILE, dgains if j == 0 else pltpu.roll(dgains, D - TILE * j, 1), 0.0) for j in range(SHARDS)
    ]
    embeds = dembed.reshape(SHARDS, 8, D)
    for chip in range(SHARDS // 2):
        for part, values in ((slice(TILE, TILE + 8), embeds), (slice(TILE + 8, 2 * TILE), sides)):
            low, high = values[2 * chip], values[2 * chip + 1]
            second_refs[0][chip, part, :] = jnp.where(core == 0, low, high)
    second_refs[1][:, TILE:, :] = jnp.stack(
        [
            jnp.where(
                core == 0,
                jnp.concatenate([embeds[2 * chip + 1], sides[2 * chip + 1]], 0),
                jnp.concatenate([embeds[2 * chip], sides[2 * chip]], 0),
            ).astype(BF16)
            for chip in range(SHARDS // 2)
        ],
        0,
    )


def project_back(info, dqs, keeps, recvs, dmid, x, extra, bundles, dgs, gains, cosine, sine, full, split):
    groups = len(dqs)
    rows = cosine.shape[0]
    weights = [value for bundle in bundles for value in bundle]
    ins = [info, *dqs, *keeps, *recvs, dmid, x, *extra, *weights, *dgs, gains, cosine, sine]
    specs = [whole(i.shape) for i in ins[1:]]
    scratch = [pltpu.VMEM((SHARDS, 2 * TILE, D), BF16) for _ in bundles] if full else []
    if full:
        outs = grad_shapes(2 * TILE, split)
        outs += grad_shapes(2 * TILE if split else TILE, split)
        if not split:
            outs += [shape((1, D)), shape((VOCAB, D))]
    else:
        at = 3 * groups + 2
        specs[at : at + len(weights)] = front(weights, 3 * TILE)
        outs = grad_shapes(3 * TILE, split) + [shape((1, D)), shape((rows, D)), shape((2, 8, D))]
    return call(
        partial(project_back_body, full=full, split=split, groups=groups),
        "project_back",
        outs,
        ins,
        10 if full else 5,
        in_specs=specs,
        scratch=scratch,
    )


def fold_body(info, *refs, layout):
    refs = list(refs)
    outs = refs[4 * sum(len(rows) for rows in layout) :]
    for order, rows in enumerate(layout):
        at = 0
        for count in rows:
            keep, far, recv, far_recv = [refs.pop(0) for _ in range(4)]
            lead = outs[2 * order].shape[0]
            part = slice(at, at + count)
            flat = lambda ref: ref[...].reshape(lead, count, D)
            outs[2 * order][:, part, :] = flat(keep) + flat(recv).astype(F32)
            outs[2 * order + 1][:, part, :] = (flat(far) + flat(far_recv).astype(F32)).astype(BF16)
            at += count


def fold(info, orders, steps, us):
    ins, specs, outs, out_specs, layout = [info], [], [], [], []
    for sources, pre, post, bit in orders:
        layout.append([keep.shape[-2] for keep, _ in sources])
        for keep, recv in sources:
            dims = (pre, 2, post, keep.shape[-2], D)
            for value in (keep, recv):
                for other in (0, 1):
                    ins.append(value.reshape(dims))
                    specs.append(
                        pl.BlockSpec(
                            (pre // steps, 1, post, keep.shape[-2], D),
                            lambda i, info, other=other, bit=bit: (i, jnp.abs(info[BITS + bit] - other), 0, 0, 0),
                        )
                    )
        total = sum(layout[-1])
        for kind in (F32, BF16):
            outs.append(shape((pre * post, total, D), kind))
            out_specs.append(pl.BlockSpec((pre * post // steps, total, D), lambda i, _: (i, 0, 0)))
    found = call(
        partial(fold_body, layout=layout), "fold", outs, ins, us, grid=(steps,), in_specs=specs, out_specs=out_specs
    )
    return [(found[2 * i], found[2 * i + 1]) for i in range(len(orders))]


CORE_BIT, Y_BIT, X_BIT, Z0_BIT, Z1_BIT = range(5)


class Scatter:
    def __init__(self, info, firsts, seconds):
        self.info = info
        self.values = [
            [(keep, swapped(send, CORE_BIT)) for keep, send in sources] for sources in (firsts, seconds)
        ]
        self.stage = 0

    def plan(self):
        first, second, steps = (
            ((X_BIT, 4, 2), (Y_BIT, 8, 1), 4),
            ((Y_BIT, 4, 1), (X_BIT, 4, 1), 4),
            ((Z0_BIT, 2, 1), (Z0_BIT, 2, 1), 2),
            ((Z1_BIT, 1, 1), (Z1_BIT, 1, 1), 1),
        )[self.stage]
        orders = [(sources, pre, post, bit) for sources, (bit, pre, post) in zip(self.values, (first, second))]
        return orders, steps

    def folded(self, found, bits):
        self.values = [[(keep, swapped(send, bit))] for (keep, send), bit in zip(found, bits)]
        self.stage += 1

    def joined(self, other):
        found = Scatter(self.info, [], [])
        found.values = [mine + more for mine, more in zip(self.values, other.values)]
        found.stage = self.stage
        return found

    def kept(self):
        return [keep for sources in self.values for keep, _ in sources]

    def result(self):
        return [keep.reshape(-1, D) + recv.reshape(-1, D).astype(F32) for ((keep, recv),) in self.values]


def step_all(info, *needed):
    def step(*scatters):
        plans = [scatter.plan() for scatter in scatters]
        orders = [order for plan, _ in plans for order in plan]
        found = fold(after(info, needed) if needed else info, orders, min(steps for _, steps in plans), 4)
        for index, scatter in enumerate(scatters):
            part = slice(2 * index, 2 * index + 2)
            scatter.folded(found[part], [bit for *_, bit in orders[part]])

    return step


def after(value, *needed):
    leaves = jax.tree.leaves(needed)
    return lax.optimization_barrier((value, *leaves))[0]


def flat_index():
    return lax.axis_index("dp") * lax.axis_size("seq") + lax.axis_index("seq")


def flat_count():
    return lax.axis_size("dp") * lax.axis_size("seq")


def swapped(value, bit):
    return lax.ppermute(value, BOTH, [(i, i ^ (1 << bit)) for i in range(flat_count())])


def bit_of(bit):
    return (flat_index() >> bit) & 1


class Gather:
    def __init__(self, packed):
        self.values = [packed[None]]

    def send(self, *bits, needed=()):
        if needed:
            self.values = [after(value, *needed) for value in self.values]
        self.coming = [swapped(value, bit) for value, bit in zip(self.values, bits)]
        return self

    def pairs(self, needed):
        pairs = list(zip(self.values, self.coming))
        return lax.optimization_barrier((pairs, list(needed)))[0]

    def join(self, split=None, needed=()):
        pairs = self.pairs(needed)
        if split is not None:
            ((here, there),) = pairs
            pairs = [(here[:, :split], there[:, :split]), (here[:, split:], there[:, split:])]
        self.values = [jnp.concatenate(pair, 0) for pair in pairs]
        return self

    def send_last(self, *bits, needed=()):
        self.send(*bits, needed=needed)
        self.near = [swapped(value, CORE_BIT) for value in self.values]
        return self

    def last(self, needed=()):
        self.values = self.pairs(needed)
        return [
            (here, there, near, swapped(there, CORE_BIT)) for (here, there), near in zip(self.values, self.near)
        ]


def group_perm(ways, links):
    count = lax.axis_size("seq")
    return [(base + a, base + b) for base in range(0, count, ways) for a, b in links]


def window_keys(k, v, ways):
    if ways == 2:
        swap = group_perm(2, ((0, 1), (1, 0)))
        return [k, lax.ppermute(k, "seq", swap), v, lax.ppermute(v, "seq", swap)]
    groups = [list(range(base, base + ways)) for base in range(0, lax.axis_size("seq"), ways)]
    found = []
    for value in (k, v):
        every = lax.all_gather(value, "seq", axis=0, tiled=False, axis_index_groups=groups)
        rows = every.shape[1] // 2
        blocks = [every[w, :rows] for w in range(ways)] + [every[w, rows:] for w in reversed(range(ways))]
        found.append(jnp.concatenate(blocks, 0))
    return found


def window_sum(grads, ways):
    if ways == 2:
        keep, send = grads
        return keep, lax.ppermute(send, "seq", group_perm(2, ((0, 1), (1, 0))))
    groups = [list(range(base, base + ways)) for base in range(0, lax.axis_size("seq"), ways)]
    total = lax.psum_scatter(grads[0], "seq", scatter_dimension=0, tiled=False, axis_index_groups=groups)
    return total, jnp.zeros(total.shape, BF16)


def up_one(value, ways):
    return lax.ppermute(value, "seq", group_perm(ways, [(i, i + 1) for i in range(ways - 1)]))


def down_one(value, ways):
    return lax.ppermute(value, "seq", group_perm(ways, [(i + 1, i) for i in range(ways - 1)]))


def sum_all(value):
    count = flat_count()
    for bit in range(count.bit_length() - 1):
        value = value + swapped(value, bit)
    return value


def tiles(weight):
    rows = weight.shape[0]
    return [weight[:, start : start + D] for start in range(0, weight.shape[1], D)] if rows else []


def pack_edge(embed, gains):
    rows = embed.shape[-2]
    pad = jnp.zeros((8, D - gains.shape[1]), gains.dtype)
    side = jnp.concatenate([jnp.concatenate([gains, jnp.zeros((3, gains.shape[1]), gains.dtype)], 0), pad], 1)
    return jnp.concatenate([embed, side], 0)


def gather_weights(embed, head, attn_in, attn_out, ffn_in, ffn_out, gains):
    full = [
        lax.all_gather(weight, BOTH, axis=axis, tiled=True)
        for weight, axis in ((embed, 0), (head, 0), (attn_in, 1), (attn_out, 1), (ffn_in, 1), (ffn_out, 1), (gains, 1))
    ]
    embed, head, attn_in, attn_out, ffn_in, ffn_out, gains = full
    fold_rows = lambda weight: weight.reshape(SHARDS, TILE, D)
    edge = jnp.zeros((SHARDS, TILE, D), BF16).at[:, :8].set(embed.reshape(SHARDS, 8, D))
    edge = edge.at[:, 8:13, :TILE].set(gains.reshape(5, SHARDS, TILE).transpose(1, 0, 2))
    head_tile = jnp.zeros((SHARDS, TILE, D), BF16).at[:, :, :VOCAB].set(head.reshape(SHARDS, TILE, VOCAB))
    down = ffn_out.reshape(2, SHARDS, 4 * TILE, D)
    side = [[fold_rows(t) for t in tiles(attn_in[i])] for i in range(2)]
    up = [[fold_rows(t) for t in tiles(ffn_in[i])] for i in range(2)]
    firsts = [jnp.concatenate(side[0][:2], 1), jnp.concatenate([side[0][2], edge], 1)]
    seconds = [jnp.concatenate(up[0], 1), jnp.concatenate([down[0], fold_rows(attn_out[0])], 1)]
    third = jnp.concatenate(side[1] + up[1] + [down[1], fold_rows(attn_out[1]), head_tile], 1)
    return firsts, seconds, third


def reduce_natural(grad, axis):
    return lax.psum_scatter(grad, BOTH, scatter_dimension=axis, tiled=True)


def unfold(packed):
    parts = packed.shape[1] // TILE
    return jnp.concatenate([packed[:, TILE * i : TILE * i + TILE].reshape(D, D) for i in range(parts)], 1)


def local(
    stream, offsets, embed, head, attn_in, attn_out, ffn_in, ffn_out, gains,
    embed_row, embed_col, head_row, head_col, in_row, in_col, out_row, out_col, up_row, up_col, down_row, down_col, gains_sq,
):
    seq_rank = lax.axis_index("seq")
    dp_rank = lax.axis_index("dp")
    seq_count = lax.axis_size("seq")
    per_group = offsets.shape[0] // lax.axis_size("dp")
    ways = seq_count // per_group
    blocks = 2 * ways
    length = SPAN * blocks
    rank = seq_rank % ways
    split = flat_count() == SHARDS
    if split:
        low = lambda *values: [value.astype(BF16) for value in values]
        in_low, up_low, down_low, out_low, head_low = low(attn_in[1], ffn_in[1], ffn_out[1], attn_out[1], head)
        head_low = jnp.concatenate([head_low, jnp.zeros_like(head_low)], 1)
        third = jnp.concatenate(tiles(in_low) + tiles(up_low) + [down_low, out_low, head_low], 0)
        third = lax.all_gather(third, BOTH, axis=0, tiled=False)
        embed_low, gains_low, in_low = low(embed, gains, attn_in[0])
        one = Gather(jnp.concatenate(tiles(in_low) + [pack_edge(embed_low, gains_low)], 0))
        up_low, down_low, out_low = low(*after((ffn_in[0], ffn_out[0], attn_out[0]), one.values))
        two = Gather(jnp.concatenate(tiles(up_low) + [down_low, out_low], 0))
        one.send(Z1_BIT).join()
        two.send(Z1_BIT, needed=one.values)
        one.send(Z0_BIT).join(2 * TILE)
        offsets_then, stream_then = after((offsets, stream), *one.values)
        two.join().send(Z0_BIT, needed=one.values)
        one.send(X_BIT, Y_BIT).join()
        two.join(4 * TILE)
        one.send_last(Y_BIT, X_BIT)
        first = one.last()
        two.send(X_BIT, Y_BIT, needed=one.values)
    else:
        low = [w.astype(BF16) for w in (embed, head, attn_in, attn_out, ffn_in, ffn_out, gains)]
        first, second, third = gather_weights(*low)
        first, second = [[(value,) for value in pair] for pair in (first, second)]
        offsets_then, stream_then = offsets, stream

    window_start = offsets_then[dp_rank * per_group + seq_rank // ways]
    limits = jnp.minimum(length, STREAM - 1 - offsets_then) - (length - length // 2)
    count_real = jnp.sum(jnp.maximum(limits, 0)).astype(F32)
    own_blocks = jnp.stack([rank, blocks - 1 - rank]) + 0 * window_start
    positions = (own_blocks[:, None] * SPAN + jnp.arange(SPAN, dtype=jnp.int32)[None]).reshape(-1)
    coarse_pos = (own_blocks[:, None] * CSPAN + jnp.arange(CSPAN, dtype=jnp.int32)[None]).reshape(-1)
    reach = own_blocks + 1
    info = jnp.concatenate(
        [reach, jnp.stack([rank, flat_index() & 1] + [bit_of(bit) for bit in range(5)] + [flat_index() >> 1])], 0
    ).astype(jnp.int32)
    starts = window_start + own_blocks * SPAN
    padded = jnp.concatenate([stream_then, jnp.broadcast_to(stream_then[-1:], (length,))], 0)
    tokens = jnp.concatenate([lax.dynamic_slice_in_dim(padded, starts[s], SPAN, 0) for s in range(2)], 0)
    target = lax.dynamic_slice_in_dim(padded, starts[1] + 1, SPAN, 0)
    counted = (window_start + positions[SPAN:] + 1 < STREAM).astype(F32)
    rate = (1.0 / (LOG_TWO * count_real)).reshape(1, 1)

    def tables(at):
        frequency = 10000.0 ** (-jnp.arange(HD // 2, dtype=F32) / (HD // 2))
        angles = at.astype(F32)[:, None] * frequency[None, :]
        cosine, sine = jnp.cos(angles), jnp.sin(angles)
        return (jnp.concatenate([cosine] * 4, 1), jnp.concatenate([-sine, sine] * 2, 1))

    cos_0, sin_0 = tables(positions)
    cos_1, sin_1 = tables(coarse_pos)

    h_0, q_0, k_0, v_0, gain_rows = project(info, tokens[:, None], first, cos_0, sin_0)
    if split:
        two.join(needed=[q_0]).send_last(Y_BIT, X_BIT)
        k_0, v_0 = after((k_0, v_0), two.values)
    keys_0 = window_keys(k_0, v_0, ways)
    a_lo, lse_lo = attend(info, q_0, keys_0, SPAN, 0, 1)
    if split:
        second = two.last([a_lo])
    a_hi, lse_hi = attend(info, after(q_0, a_lo, two.values) if split else q_0, keys_0, SPAN, 1, 1)
    m_0, h_1, tail = branch(info, h_0, (a_lo, a_hi), second, gain_rows)

    z_0, q_1, k_1, v_1 = project_short(
        info, h_1, tail, up_one(tail[0], ways), down_one(tail[1], ways), third, gain_rows, cos_1, sin_1, ways
    )
    keys_1 = window_keys(k_1, v_1, ways)
    a_1, lse_1 = attend(info, q_1, keys_1, CSPAN, 0, 2)
    found = short_rest(info, z_0, a_1, h_1, third, gain_rows, target[:, None], counted[:, None], rate, split)
    loss, dg_4, dg_3, d_h2, d_m1, d_a1 = found[:6]
    each = 2 if split else 1
    d_up_1, d_down_1, d_head = [found[6 + each * i : 6 + each * i + each] for i in range(3)]
    if split:
        late = Scatter(info, [d_up_1], [d_down_1])
    d_q1, *d_kv1 = attend_back(info, q_1, keys_1, d_a1, lse_1, CSPAN, 0, 2)
    keep, recv = window_sum(d_kv1, ways)
    found = project_back(info, [d_q1], [keep], [recv], d_m1, z_0, [], [(third,)], [], gain_rows, cos_1, sin_1, False, split)
    d_in_1, (dg_2, d_z0, edge) = found[:each], found[each:]

    high, low_edge = down_one(edge[0], ways), up_one(edge[1], ways)
    found = branch_back(info, d_z0, edge, high, low_edge, d_h2, m_0, (a_lo, a_hi), second, gain_rows, ways, split)
    d_m0, da_lo, da_hi, dg_1 = found[:4]
    d_up_0, d_down_0 = [found[4 + each * i : 4 + each * i + each] for i in range(2)]
    if split:
        middle = Scatter(info, [d_up_0, d_in_1], [d_down_0, d_head])
        step_all(info, d_m0)(late)
        step_all(info, late.kept())(middle)
        both = late.joined(middle)
        da_lo = after(da_lo, both.kept())
    dq_lo, *dkv_lo = attend_back(info, q_0, keys_0, da_lo, lse_lo, SPAN, 0, 1)
    if split:
        da_hi = after(da_hi, dq_lo)
    sum_lo = window_sum(dkv_lo, ways)
    dq_hi, *dkv_hi = attend_back(info, q_0, keys_0, da_hi, lse_hi, SPAN, 1, 1)
    if split:
        step_all(info, dq_hi)(both)
        dkv_hi = after(tuple(dkv_hi), both.kept())
    sum_hi = window_sum(dkv_hi, ways)
    found = project_back(
        info, [dq_lo, dq_hi], [sum_lo[0], sum_hi[0]], [sum_lo[1], sum_hi[1]], d_m0, h_0, [tokens[None, :]], first,
        [dg_1, dg_2, dg_3, dg_4], gain_rows, cos_0, sin_0, True, split,
    )

    if split:
        early = Scatter(info, [found[:2]], [found[2:]])
        step_all(info, found[0])(both)
        step_all(info, both.kept())(early)
        step_all(info)(early)
        step_all(info)(both, early)
        step_all(info)(early)
        both.values = after(both.values, early.kept())
        both_a, both_b = both.result()
        late_a, late_b = both_a[: 4 * TILE], both_b[: 5 * TILE]
        middle_a, middle_b = both_a[4 * TILE :], both_b[5 * TILE :]
        early_a, early_b = early.result()

        def columns(packed, count):
            return jnp.concatenate([packed[TILE * i : TILE * i + TILE] for i in range(count)], 1)

        g_embed = early_b[TILE : TILE + 8]
        gain_grad = early_b[TILE + 8 : TILE + 13, :TILE]
        g_head = middle_b[5 * TILE :, :VOCAB]
        g_in = jnp.stack([jnp.concatenate([columns(early_a, 2), early_b[:TILE]], 1), columns(middle_a[4 * TILE :], 3)])
        g_out = jnp.stack([middle_b[4 * TILE : 5 * TILE], late_b[4 * TILE :]])
        g_up = jnp.stack([columns(middle_a, 4), columns(late_a, 4)])
        g_down = jnp.stack([middle_b[: 4 * TILE], late_b[: 4 * TILE]])
    else:
        d_qk, d_v, dg_0, d_embed = found
        d_in_0 = jnp.concatenate([d_qk, d_v], 1)
        g_embed = reduce_natural(d_embed, 0)
        g_head = reduce_natural(d_head[0][:, :, :VOCAB].reshape(D, VOCAB), 0)
        g_in = reduce_natural(jnp.stack([unfold(d_in_0), unfold(d_in_1[0])]), 1)
        g_out = reduce_natural(jnp.stack([unfold(d) for d in (d_down_0[0][:, 4 * TILE :], d_down_1[0][:, 4 * TILE :])]), 1)
        g_up = reduce_natural(jnp.stack([unfold(d_up_0[0]), unfold(d_up_1[0])]), 1)
        g_down = reduce_natural(jnp.stack([d.reshape(FF, D) for d in (d_down_0[0][:, : 4 * TILE], d_down_1[0][:, : 4 * TILE])]), 1)
        gain_grad = reduce_natural(jnp.concatenate([dg_0, dg_1, dg_2, dg_3, dg_4], 0), 1)

    embed, head, attn_in, attn_out, ffn_in, ffn_out = after((embed, head, attn_in, attn_out, ffn_in, ffn_out), d_q1)
    decay = 1.0 - STEP ** (-0.8)
    matrices = [
        (g_embed, embed_row, embed_col, embed, VOCAB),
        (g_head, head_row, head_col, head, D),
        (g_in, in_row, in_col, attn_in, D),
        (g_out, out_row, out_col, attn_out, D),
        (g_up, up_row, up_col, ffn_in, D),
        (g_down, down_row, down_col, ffn_out, FF),
    ]
    new_rows, sums = [], []
    for grad, row, _, weight, _ in matrices:
        square = grad * grad
        new_row = decay * row + (1.0 - decay) * jnp.mean(square, -1)
        new_rows.append(new_row)
        sums += [
            jnp.sum(square, -2),
            jnp.sum(square / new_row[..., None], -2),
            jnp.sum(new_row, -1),
            jnp.sum(weight * weight, (-2, -1)),
        ]
    new_sq = decay * gains_sq + (1.0 - decay) * gain_grad * gain_grad
    gain_update = gain_grad / jnp.sqrt(new_sq)
    sums += [jnp.sum(gain_update * gain_update, -1), jnp.sum(gains * gains, -1), loss[0, :1]]
    flat = jnp.concatenate([s.reshape(-1) for s in sums], 0)
    size = flat.shape[0]
    flat = jnp.pad(flat, (0, -size % 1024)).reshape(-1, 128)
    flat = sum_all(flat).reshape(-1)
    totals, at = [], 0
    for s in sums:
        totals.append(flat[at : at + s.size].reshape(s.shape))
        at += s.size
    outputs = [totals[-1].reshape(()), count_real]
    for index, (grad, _, col, weight, full_rows) in enumerate(matrices):
        col_sum, ratio_sum, row_sum, weight_sum = totals[4 * index : 4 * index + 4]
        new_row = new_rows[index]
        new_col = decay * col + (1.0 - decay) * col_sum / full_rows
        mean_row = row_sum / full_rows
        size_all = full_rows * grad.shape[-1]
        update_sum = mean_row * jnp.sum(ratio_sum / new_col, -1)
        rate_now = RATE_SCALE * jnp.sqrt(weight_sum / size_all) / jnp.maximum(1.0, jnp.sqrt(update_sum / size_all))
        update = grad / jnp.sqrt(new_row[..., :, None] * new_col[..., None, :] / mean_row[..., None, None])
        outputs += [grad, new_row, new_col, weight - rate_now[..., None, None] * update]
    gain_rate = RATE_SCALE * jnp.sqrt(totals[-2] / D) / jnp.maximum(1.0, jnp.sqrt(totals[-3] / D))
    outputs += [gain_grad, new_sq, gains - gain_rate[:, None] * gain_update]
    return tuple(outputs)


def solution(mesh):
    row = P(BOTH, None)
    mid = P(None, BOTH, None)
    vec = P(BOTH)
    vec2 = P(None, BOTH)
    state = (vec, P(), vec, P(), vec2, P(), vec2, P(), vec2, P(), vec2, P(), vec2)
    return jax.shard_map(
        local,
        mesh=mesh,
        in_specs=(P(), P(), row, row, mid, mid, mid, mid, vec2) + state,
        out_specs=(P(), P())
        + (row, vec, P(), row) * 2
        + (mid, vec2, P(), mid) * 4
        + (vec2, vec2, vec2),
        check_vma=False,
    )
```

```python
from functools import partial
import math

import jax
import jax.numpy as jnp
from jax import lax
from jax.experimental import pallas as pl
from jax.experimental.pallas import tpu as pltpu
from jax.sharding import PartitionSpec as P

D = 512
HEADS = 8
FF = 2048
VOCAB = 256
SHORT = 3
HD = 64
SPAN = 384
CSPAN = SPAN // SHORT
STREAM = 65536
STEP = 10
SHARDS = 32
TILE = 16

EPSILON = 1e-05
RATE_SCALE = 0.5
LOG_TWO = math.log(2.0)
MASKED = -1e30
GELU_A = math.sqrt(2.0 / math.pi)
GELU_B = 0.044715
BOTH = ("dp", "seq")
F32 = jnp.float32
BF16 = jnp.bfloat16
VMEM_LIMIT = 56 * 2**20


def nn(left, right):
    return jnp.dot(left, right, preferred_element_type=F32)


def nt(left, right):
    return lax.dot_general(left, right, (((1,), (1,)), ((), ())), preferred_element_type=F32)


def call(body, name, outs, ins, us, grid=(1,), in_specs=None, out_specs=None, scratch=(), prefetch=1):
    spec = pltpu.PrefetchScalarGridSpec(
        num_scalar_prefetch=prefetch,
        grid=grid,
        in_specs=in_specs or [whole(i.shape) for i in ins[prefetch:]],
        out_specs=out_specs or [whole(o.shape) for o in outs],
        scratch_shapes=list(scratch),
    )
    return pl.pallas_call(
        body,
        grid_spec=spec,
        out_shape=list(outs),
        compiler_params=pltpu.CompilerParams(vmem_limit_bytes=VMEM_LIMIT),
        cost_estimate=pl.CostEstimate(flops=int(us * 2e10), bytes_accessed=1 << 20, transcendentals=0),
        name=name,
    )(*ins)


def whole(dims):
    return pl.BlockSpec(dims, lambda *_: (0,) * len(dims))


def shape(dims, kind=F32):
    return jax.ShapeDtypeStruct(dims, kind)


RANK, CORE, BITS, CHIP = 2, 3, 4, 9
WEIGHT_PARTS = 4


def norm_parts(values):
    center = values - jnp.mean(values, -1, keepdims=True)
    scale = lax.rsqrt(jnp.mean(center * center, -1, keepdims=True) + EPSILON)
    return center * scale, scale


def norm_pull(hat, scale, gain, cotangent):
    pulled = cotangent * gain
    inner = pulled - jnp.mean(pulled, -1, keepdims=True) - hat * jnp.mean(pulled * hat, -1, keepdims=True)
    return scale * inner, jnp.sum(cotangent * hat, 0, keepdims=True)


def swap_halves(values):
    lane = lax.broadcasted_iota(jnp.int32, values.shape, 1)
    return jnp.where(lane % HD < HD // 2, pltpu.roll(values, 128 - HD // 2, 1), pltpu.roll(values, HD // 2, 1))


def rope(values, cosine, sine):
    pieces = []
    for start in range(0, D, 128):
        piece = values[:, start : start + 128]
        pieces.append(piece * cosine + swap_halves(piece) * sine)
    return jnp.concatenate(pieces, 1)


def rope_pull(values, cosine, sine):
    pieces = []
    for start in range(0, D, 128):
        piece = values[:, start : start + 128]
        pieces.append(piece * cosine + swap_halves(piece * sine))
    return jnp.concatenate(pieces, 1)


def gelu_parts(values):
    inner = GELU_A * (values + GELU_B * (values * values * values))
    wave = jnp.tanh(inner)
    return wave, 0.5 * (1.0 + wave)


def gelu_slope(values, wave, gate):
    return gate + 0.5 * values * (1.0 - wave * wave) * (GELU_A * (1.0 + 3.0 * GELU_B * values * values))


def tile_of(ref, index):
    return ref[:, TILE * index : TILE * index + TILE, :].reshape(D, ref.shape[-1])


def settle(refs, scr, info, second, start=0):
    if len(refs) == 1:
        return refs[0].at[:, start:]
    rows = slice(start, start + scr.shape[1])
    last, next_last = (1, 0) if second else (0, 1)

    def place(r, carry):
        mask = ((r & 1) << 3) | (((r >> 1) & 1) << 2) | (((r >> 2) & 1) << next_last)
        for far in range(2):
            chip = info[CHIP] ^ (mask | (far << last))
            scr[2 * chip + info[CORE]] = refs[far][r, rows]
            scr[2 * chip + 1 - info[CORE]] = refs[2 + far][r, rows]
        return carry

    lax.fori_loop(0, SHARDS // 4, place, 0)
    return scr


def bundle_scratch(bundles, rows):
    return [pltpu.VMEM((SHARDS, count, D), BF16) for bundle, count in zip(bundles, rows) if len(bundle) > 1]


def thirds(ref, lead, start):
    found = ref[(*lead, pl.ds(start, CSPAN, stride=SHORT), slice(None))]
    for shift in range(1, SHORT):
        found = found + ref[(*lead, pl.ds(start + shift, CSPAN, stride=SHORT), slice(None))]
    return found


def spread(ref, lead, value):
    for shift in range(SHORT):
        ref[(*lead, pl.ds(shift, CSPAN, stride=SHORT), slice(None))] = value


LANES = [slice(start, start + 128) for start in range(0, D, 128)]


def grad_shapes(rows, split):
    if split:
        return [shape((SHARDS // 2, rows, D)), shape((SHARDS // 2, rows, D), BF16)]
    return [shape((SHARDS, rows, D))]


def grad_specs(rows, split, index, shards=SHARDS):
    if split:
        return [pl.BlockSpec((shards // 2, rows, D), index)] * 2
    return [pl.BlockSpec((shards, rows, D), index)]


def put(refs, core, value, at=0, rows=TILE, chunk=0):
    width = value.shape[-1]
    part = pl.ds(at, rows)
    shards = D // rows
    if len(refs) == 2:
        pairs = value.reshape(shards // 2, 2, rows, width)
        low, high = pairs[:, 0], pairs[:, 1]
        where = pl.ds(chunk * (shards // 2), shards // 2)
        refs[0][where, part, :width] = jnp.where(core == 0, low, high)
        refs[1][where, part, :width] = jnp.where(core == 0, high, low).astype(BF16)
    else:
        refs[0][pl.ds(chunk * shards, shards), part, :width] = value.reshape(shards, rows, width).astype(refs[0].dtype)


def project_body(info, token_ref, *rest, each):
    wa_refs, wb_refs = rest[:each], rest[each : 2 * each]
    cos_ref, sin_ref, h_ref, q_ref, kv_ref, gain_ref = rest[2 * each : 2 * each + 6]
    scr = rest[2 * each + 6 :]
    wa_ref, wb_ref = scr if each > 1 else (wa_refs[0], wb_refs[0])

    @pl.when(pl.program_id(0) == 0)
    def _():
        settle(wa_refs, scr and scr[0], info, False)
        settle(wb_refs, scr and scr[1], info, True)
        lane = lax.broadcasted_iota(jnp.int32, (8, D), 1)
        found = jnp.zeros((8, D), F32)
        for shard in range(SHARDS):
            side = wb_ref[shard, TILE : 2 * TILE, :].astype(F32)[8:]
            side = side if shard == 0 else pltpu.roll(side, TILE * shard, 1)
            found = jnp.where(lane // TILE == shard, side, found)
        gain_ref[...] = found

    token = token_ref[...]
    row = (token // 8) * TILE + token % 8
    hot = (row == lax.broadcasted_iota(jnp.int32, (token.shape[0], D), 1)).astype(BF16)
    values = nn(hot, tile_of(wb_ref, 1))
    h_ref[...] = values.astype(BF16)
    normed = (norm_parts(values)[0] * gain_ref[0:1, :]).astype(BF16)
    cosine, sine = cos_ref[...], sin_ref[...]
    q_ref[...] = (rope(nn(normed, tile_of(wa_ref, 0)), cosine, sine) * 0.125).astype(BF16)
    kv_ref[0] = rope(nn(normed, tile_of(wa_ref, 1)), cosine, sine).astype(BF16)
    kv_ref[1] = nn(normed, tile_of(wb_ref, 0)).astype(BF16)


def project(info, token, bundles, cosine, sine):
    rows = cosine.shape[0]
    step = SPAN
    weights = [*bundles[0], *bundles[1]]
    return call(
        partial(project_body, each=len(bundles[0])),
        "project",
        [shape((rows, D), BF16)] * 2 + [shape((2, rows, D), BF16), shape((8, D))],
        [info, token, *weights, cosine, sine],
        5,
        grid=(rows // step,),
        in_specs=[pl.BlockSpec((step, 1), lambda i, _: (i, 0))]
        + [whole(w.shape) for w in weights]
        + [pl.BlockSpec((step, 128), lambda i, _: (i, 0))] * 2,
        out_specs=[pl.BlockSpec((step, D), lambda i, _: (i, 0))] * 2
        + [pl.BlockSpec((2, step, D), lambda i, _: (0, i, 0)), whole((8, D))],
        scratch=bundle_scratch(bundles, (2 * TILE, 2 * TILE)),
    )


def project_short_body(
    info, h_ref, tail_ref, low_ref, high_ref, *rest, ways, each
):
    wa_refs, wb_refs = rest[:each], rest[each : 2 * each]
    gain_ref, cos_ref, sin_ref, z_ref, q_ref, kv_ref, scr = rest[2 * each : 2 * each + 7]
    wa_ref = settle(wa_refs, rest[-2], info, False, 4 * TILE)
    wb_ref = settle(wb_refs, rest[-1], info, True, 5 * TILE)
    for slot in range(2):
        if slot == 0:
            halo = low_ref[...]
        else:
            halo = jnp.where(info[RANK] == ways - 1, tail_ref[0], high_ref[...])
        for piece, lanes in enumerate(LANES):
            scr[slot, piece, :8, :] = halo[:, lanes]
            scr[slot, piece, 8:, :] = h_ref[SPAN * slot : SPAN * slot + SPAN, lanes]
            total = thirds(scr, (slot, piece), 6)
            z_ref[CSPAN * slot : CSPAN * slot + CSPAN, lanes] = total * (1.0 / SHORT)
    normed = (norm_parts(z_ref[...])[0] * gain_ref[2:3, :]).astype(BF16)
    cosine, sine = cos_ref[...], sin_ref[...]
    query = nn(normed[CSPAN:], tile_of(wa_ref, 0))
    q_ref[...] = (rope(query, cosine[CSPAN:], sine[CSPAN:]) * 0.125).astype(BF16)
    kv_ref[0] = rope(nn(normed, tile_of(wa_ref, 1)), cosine, sine).astype(BF16)
    kv_ref[1] = nn(normed, tile_of(wb_ref, 0)).astype(BF16)


def project_short(info, h, tail, low, high, bundles, gains, cosine, sine, ways):
    outs = [shape((2 * CSPAN, D)), shape((CSPAN, D), BF16), shape((2, 2 * CSPAN, D), BF16)]
    ins = [info, h, tail, low, high, *bundles[0], *bundles[1], gains, cosine, sine]
    specs = [whole(i.shape) for i in ins[1:]]
    return call(
        partial(project_short_body, ways=ways, each=len(bundles[0])),
        "project_short",
        outs,
        ins,
        0.05,
        in_specs=specs,
        scratch=[pltpu.VMEM((2, D // 128, SPAN + 8, 128), F32)] + bundle_scratch(bundles, (2 * TILE, TILE)),
    )


def order_keys(info, own, other, found, block, count):
    for at in range(count):
        owner = min(at, count - 1 - at)
        place = 0 if owner == at else 1
        part = slice(place * block, place * block + block)
        for kind, keys in enumerate(found):
            keys[at * block : at * block + block, :] = jnp.where(
                info[RANK] == owner, own[kind, part, :], other[kind, part, :]
            )


def each_rows(rows, steps, count):
    if count <= 4:
        for i in range(steps):
            rows(i)
    else:
        lax.fori_loop(0, steps, lambda i, carry: (rows(i), carry)[1], 0)


def each_head(head, together):
    if together == 4:
        for j in range(4):
            head(j)
        return

    def some(i, carry):
        for j in range(together):
            head(i * together + j)
        return carry

    lax.fori_loop(0, 4 // together, some, 0)


def masked_rows(s_scr, part, start, step, block, width):
    score = s_scr[part, :width]
    row = start + lax.broadcasted_iota(jnp.int32, (step, block), 0)
    key = lax.broadcasted_iota(jnp.int32, (step, block), 1)
    edge = jnp.where(row >= key, score[:, width - block :], MASKED)
    return jnp.concatenate([score[:, : width - block], edge], 1) if width > block else edge


def rows_part(i, step):
    return pl.ds(i * step if isinstance(i, int) else pl.multiple_of(i * step, step), step)


def attend_body(info, q_ref, *rest, count, block, step, pair, base):
    if pair:
        own, other, out_ref, lse_ref, s_scr, p_scr, k_ref, v_ref = rest
    else:
        k_ref, v_ref, out_ref, lse_ref, s_scr, p_scr = rest
    slot = pl.program_id(1)
    nk = info[slot + base]
    lane = lax.broadcasted_iota(jnp.int32, (1, 256), 1)
    column = lax.broadcasted_iota(jnp.int32, (step, 128), 1)
    zero = jnp.zeros((), BF16)
    if pair:

        @pl.when(slot == 0)
        def _():
            order_keys(info, own, other, (k_ref, v_ref), block, count)

    def variant(blocks):
        width = blocks * block

        def head(j):
            mine = lane // HD == j
            s_scr[:, :width] = nt(jnp.where(mine, q_ref[...], zero), k_ref[:width, :])

            def rows(i):
                part = rows_part(i, step)
                score = masked_rows(s_scr, part, i * step, step, block, width)
                top = jnp.max(score, -1, keepdims=True)
                raised = jnp.exp(score - top)
                total = jnp.sum(raised, -1, keepdims=True)
                p_scr[part, :width] = (raised * (1.0 / total)).astype(BF16)
                lse_ref[0, 0, part, :] = jnp.where(column == j, top + jnp.log(total), lse_ref[0, 0, part, :])

            each_rows(rows, block // step, count)
            found = nn(p_scr[:, :width], v_ref[:width, :]).astype(BF16)
            out_ref[...] = jnp.where(mine, found, out_ref[...])

        each_head(head, 4 if count <= 4 else 1)

    for blocks in range(1, count + 1):
        pl.when(nk == blocks)(partial(variant, blocks))


def key_spec(key, first):
    lead = key.shape[:-1]
    return pl.BlockSpec((*lead, 256), lambda h, s, _: (0,) * len(lead) + (h + first,))


def attend(info, q, keys, block, first, groups):
    slots = q.shape[0] // block
    pair = keys[0].ndim == 3
    total = keys[0].shape[-2] * (2 if pair else 1)
    count = total // block
    scratch = [pltpu.VMEM((block, total), F32), pltpu.VMEM((block, total), BF16)]
    if pair:
        scratch += [pltpu.VMEM((total, 256), BF16)] * 2
    return call(
        partial(attend_body, count=count, block=block, step=64, pair=pair, base=2 - slots),
        "attend",
        [shape((slots * block, 256 * groups), BF16), shape((groups, slots, block, 128))],
        [info, q, *keys],
        8 if block == SPAN else 0.05,
        grid=(groups, slots),
        in_specs=[pl.BlockSpec((block, 256), lambda h, s, _: (s, h + first))]
        + [key_spec(key, first) for key in keys],
        out_specs=[
            pl.BlockSpec((block, 256), lambda h, s, _: (s, h)),
            pl.BlockSpec((1, 1, block, 128), lambda h, s, _: (h, s, 0, 0)),
        ],
        scratch=scratch,
    )


def attend_back_body(info, q_ref, *rest, count, block, step, pair, base):
    if pair:
        own, other, back_ref, lse_ref, dq_ref, keep_ref, send_ref = rest[:7]
        s_scr, dp_scr, p_scr, ds_scr, dk_scr, dv_scr, qt_scr, bt_scr, k_ref, v_ref = rest[7:]
    else:
        k_ref, v_ref, back_ref, lse_ref, dq_ref, keep_ref = rest[:6]
        s_scr, dp_scr, p_scr, ds_scr, dk_scr, dv_scr, qt_scr, bt_scr = rest[6:]
    slot = pl.program_id(1)
    nk = info[slot + base]
    lane = lax.broadcasted_iota(jnp.int32, (1, 256), 1)
    column = lax.broadcasted_iota(jnp.int32, (step, 128), 1)
    zero = jnp.zeros((), BF16)

    qt_scr[...] = q_ref[...].T
    bt_scr[...] = back_ref[...].T

    @pl.when(slot == 0)
    def _():
        dk_scr[...] = jnp.zeros_like(dk_scr)
        dv_scr[...] = jnp.zeros_like(dv_scr)
        if pair:
            order_keys(info, own, other, (k_ref, v_ref), block, count)

    def variant(blocks):
        width = blocks * block

        def head(j):
            mine = lane // HD == j
            s_scr[:, :width] = nt(jnp.where(mine, q_ref[...], zero), k_ref[:width, :])
            dp_scr[:, :width] = nt(jnp.where(mine, back_ref[...], zero), v_ref[:width, :])

            def rows(i):
                part = rows_part(i, step)
                score = masked_rows(s_scr, part, i * step, step, block, width)
                lse = jnp.sum(jnp.where(column == j, lse_ref[0, 0, part, :], 0.0), -1, keepdims=True)
                prob = jnp.exp(score - lse)
                p_scr[part, :width] = prob.astype(BF16)
                prob_back = dp_scr[part, :width]
                delta = jnp.sum(prob * prob_back, -1, keepdims=True)
                ds_scr[part, :width] = (prob * (prob_back - delta)).astype(BF16)

            each_rows(rows, block // step, count)
            found = nn(ds_scr[:, :width], k_ref[:width, :])
            dq_ref[...] = jnp.where(mine, found, dq_ref[...])
            mine_rows = pl.ds(HD * j if isinstance(j, int) else pl.multiple_of(HD * j, HD), HD)
            dk_scr[mine_rows, :width] += nn(qt_scr[mine_rows, :], ds_scr[:, :width])
            dv_scr[mine_rows, :width] += nn(bt_scr[mine_rows, :], p_scr[:, :width])

        each_head(head, 2 if count <= 4 else 1)

    for blocks in range(1, count + 1):
        pl.when(nk == blocks)(partial(variant, blocks))

    @pl.when(slot == pl.num_programs(1) - 1)
    def _():
        for kind, scr in enumerate((dk_scr, dv_scr)):
            for place in range(2):
                to = slice(place * block, place * block + block)

                def from_owner(owner):
                    at = owner if place == 0 else count - 1 - owner
                    return scr[:, at * block : at * block + block]

                if pair:
                    low, high = from_owner(0), from_owner(1)
                    keep_ref[kind, :, to] = jnp.where(info[RANK] == 0, low, high)
                    send_ref[kind, :, to] = jnp.where(info[RANK] == 0, high, low).astype(BF16)
                else:
                    for owner in range(count // 2):
                        keep_ref[owner, kind, :, to] = from_owner(owner)


def attend_back(info, q, keys, back, lse, block, first, groups):
    slots = q.shape[0] // block
    pair = keys[0].ndim == 3
    total = keys[0].shape[-2] * (2 if pair else 1)
    count = total // block
    outs = [shape((slots * block, 256 * groups))]
    out_specs = [pl.BlockSpec((block, 256), lambda h, s, _: (s, h))]
    if pair:
        outs += [shape((2, 256 * groups, 2 * block)), shape((2, 256 * groups, 2 * block), BF16)]
        out_specs += [pl.BlockSpec((2, 256, 2 * block), lambda h, s, _: (0, h, 0))] * 2
    else:
        outs += [shape((count // 2, 2, 256 * groups, 2 * block))]
        out_specs += [pl.BlockSpec((count // 2, 2, 256, 2 * block), lambda h, s, _: (0, 0, h, 0))]
    scratch = [
        pltpu.VMEM((block, total), F32),
        pltpu.VMEM((block, total), F32),
        pltpu.VMEM((block, total), BF16),
        pltpu.VMEM((block, total), BF16),
        pltpu.VMEM((256, total), F32),
        pltpu.VMEM((256, total), F32),
        pltpu.VMEM((256, block), BF16),
        pltpu.VMEM((256, block), BF16),
    ]
    if pair:
        scratch += [pltpu.VMEM((total, 256), BF16)] * 2
    return call(
        partial(attend_back_body, count=count, block=block, step=64, pair=pair, base=2 - slots),
        "attend_back",
        outs,
        [info, q, *keys, back, lse],
        13 if block == SPAN else 7,
        grid=(groups, slots),
        in_specs=[pl.BlockSpec((block, 256), lambda h, s, _: (s, h + first))]
        + [key_spec(key, first) for key in keys]
        + [
            pl.BlockSpec((block, 256), lambda h, s, _: (s, h)),
            pl.BlockSpec((1, 1, block, 128), lambda h, s, _: (h, s, 0, 0)),
        ],
        out_specs=out_specs,
        scratch=scratch,
    )


def branch_body(info, x_ref, a0_ref, a1_ref, *rest, each):
    up_refs, down_refs = rest[:each], rest[each : 2 * each]
    gain_ref, mid_ref, res_ref, tail_ref = rest[2 * each : 2 * each + 4]
    scr = rest[2 * each + 4 :]
    up_w, down_w = scr if each > 1 else (up_refs[0], down_refs[0])

    @pl.when(pl.program_id(0) == 0)
    def _():
        settle(up_refs, scr and scr[0], info, False)
        settle(down_refs, scr and scr[1], info, True)

    out_tile = tile_of(down_w, 4)
    middle = x_ref[...].astype(F32) + nn(a0_ref[...], out_tile[:256]) + nn(a1_ref[...], out_tile[256:])
    mid_ref[...] = middle
    normed = (norm_parts(middle)[0] * gain_ref[1:2, :]).astype(BF16)
    total = mid_ref[...]
    for chunk in range(FF // D):
        up = nn(normed, tile_of(up_w, chunk))
        hidden = (up * gelu_parts(up)[1]).astype(BF16)
        total = total + nn(hidden, down_w[8 * chunk : 8 * chunk + 8, : 4 * TILE, :].reshape(D, D))
    res_ref[...] = total
    tail_ref[0] = total[total.shape[0] - 8 :]


def branch(info, x, parts, bundles, gains):
    rows = x.shape[0]
    row = lambda width: pl.BlockSpec((SPAN, width), lambda i, _: (i, 0))
    weights = [*bundles[0], *bundles[1]]
    return call(
        partial(branch_body, each=len(bundles[0])),
        "branch",
        [shape((rows, D)), shape((rows, D)), shape((2, 8, D))],
        [info, x, *parts, *weights, gains],
        9,
        grid=(rows // SPAN,),
        in_specs=[row(D), row(256), row(256), *[whole(w.shape) for w in weights], whole(gains.shape)],
        out_specs=[row(D), row(D), pl.BlockSpec((1, 8, D), lambda i, _: (i, 0, 0))],
        scratch=bundle_scratch(bundles, (4 * TILE, 5 * TILE)),
    )


def branch_back_body(info, dz_ref, edge_ref, high_ref, low_ref, dh_ref, mid_ref, a0_ref, a1_ref, *rest, ways, split):
    each = 2 if split else 1
    parts = WEIGHT_PARTS if split else 1
    uw_refs, dw_refs, gain_ref = rest[:parts], rest[parts : 2 * parts], rest[2 * parts]
    rest = rest[2 * parts + 1 :]
    dmid_ref, da0_ref, da1_ref, dgain_ref = rest[:4]
    up_refs, down_refs = rest[4 : 4 + each], rest[4 + each : 4 + 2 * each]
    norm_scr, normt_scr, cot_scr, cotb_scr, acc_scr, pool_scr = rest[4 + 2 * each : 10 + 2 * each]
    w_scr = rest[10 + 2 * each :]
    up_w, down_w = w_scr if split else (uw_refs[0], dw_refs[0])
    chunk = pl.program_id(0)
    core = info[CORE]

    @pl.when(chunk == 0)
    def _():
        settle(uw_refs, w_scr and w_scr[0], info, False)
        settle(dw_refs, w_scr and w_scr[1], info, True)
        for slot in range(2):
            if slot == 0:
                edge = jnp.where(info[RANK] == ways - 1, edge_ref[1], high_ref[...])
            else:
                edge = low_ref[...]
            for piece, lanes in enumerate(LANES):
                spread(pool_scr, (slot, piece), dz_ref[CSPAN * slot : CSPAN * slot + CSPAN, lanes] * (1.0 / SHORT))
                pool_scr[slot, piece, SPAN:, :] = jnp.broadcast_to(edge[0:1, lanes] * (1.0 / SHORT), (8, 128))
                found = pool_scr[slot, piece, 2 : SPAN + 2, :]
                if slot == 1:
                    found = found + dh_ref[:, lanes]
                cot_scr[SPAN * slot : SPAN * slot + SPAN, lanes] = found
        cotb_scr[...] = cot_scr[...].astype(BF16)
        normed = (norm_parts(mid_ref[...])[0] * gain_ref[1:2, :]).astype(BF16)
        norm_scr[...] = normed
        normt_scr[...] = normed.T
        acc_scr[...] = jnp.zeros_like(acc_scr)

    down_in = cotb_scr[...]
    up_tile = up_w[:, pl.ds(pl.multiple_of(chunk * TILE, TILE), TILE), :].reshape(D, D)
    down_tile = down_w[pl.ds(chunk * 8, 8), : 4 * TILE, :].reshape(D, D)
    up = nn(norm_scr[...], up_tile)
    wave, gate = gelu_parts(up)
    hidden = (up * gate).astype(BF16)
    up_in = (nt(down_in, down_tile) * gelu_slope(up, wave, gate)).astype(BF16)
    put(down_refs, core, nn(hidden.T, down_in), rows=4 * TILE, chunk=chunk)
    put(up_refs, core, nn(normt_scr[...], up_in))
    acc_scr[...] += nt(up_in, up_tile)

    @pl.when(chunk == FF // D - 1)
    def _():
        hat, scale = norm_parts(mid_ref[...])
        pulled, dgain = norm_pull(hat, scale, gain_ref[1:2, :], acc_scr[...])
        dgain_ref[...] = dgain
        dmid = cot_scr[...] + pulled
        dmid_ref[...] = dmid
        out_in = dmid.astype(BF16)
        out_tile = tile_of(down_w, 4)
        put(down_refs, core, jnp.concatenate([nn(a0_ref[...].T, out_in), nn(a1_ref[...].T, out_in)], 0), at=4 * TILE)
        da0_ref[...] = nt(out_in, out_tile[:256]).astype(BF16)
        da1_ref[...] = nt(out_in, out_tile[256:]).astype(BF16)


def branch_back(info, dz, edge, high, low, dh, mid, parts, bundles, gains, ways, split):
    rows = mid.shape[0]
    ins = [info, dz, edge, high, low, dh, mid, *parts, *bundles[0], *bundles[1], gains]
    specs = [whole(i.shape) for i in ins[1:]]
    return call(
        partial(branch_back_body, ways=ways, split=split),
        "branch_back",
        [shape((rows, D)), shape((rows, 256), BF16), shape((rows, 256), BF16), shape((1, D))]
        + grad_shapes(4 * TILE, split)
        + grad_shapes(5 * TILE, split),
        ins,
        18,
        grid=(FF // D,),
        in_specs=specs,
        out_specs=[whole((rows, D)), whole((rows, 256)), whole((rows, 256)), whole((1, D))]
        + grad_specs(TILE, split, lambda i, _: (0, i, 0))
        + grad_specs(5 * TILE, split, lambda i, _: (0, 0, 0)),
        scratch=[
            pltpu.VMEM((rows, D), BF16),
            pltpu.VMEM((D, rows), BF16),
            pltpu.VMEM((rows, D), F32),
            pltpu.VMEM((rows, D), BF16),
            pltpu.VMEM((rows, D), F32),
            pltpu.VMEM((2, D // 128, SPAN + 8, 128), F32),
            *bundle_scratch(bundles, (4 * TILE, 5 * TILE)),
        ],
    )


def short_body(info, x_ref, a_ref, h_ref, *rest, split):
    each = 2 if split else 1
    parts = WEIGHT_PARTS if split else 1
    uw_refs, dw_refs = rest[:parts], rest[parts : 2 * parts]
    gain_ref, target_ref, counted_ref, rate_ref = rest[2 * parts : 2 * parts + 4]
    rest = rest[2 * parts + 4 :]
    loss_ref, dg4_ref, dg3_ref, dh_ref, dmid_ref, da_ref = rest[:6]
    up_refs, down_refs, head_refs = [rest[6 + each * i : 6 + each * i + each] for i in range(3)]
    mid_scr, norm_scr, normt_scr, cot_scr, acc_scr, up_scr = rest[6 + 3 * each : 12 + 3 * each]
    w_scr = rest[12 + 3 * each :]
    up_w, down_w = w_scr if split else (uw_refs[0], dw_refs[0])
    down_rows = slice(0, 4 * TILE)
    step = pl.program_id(0)
    core = info[CORE]

    @pl.when(step == 0)
    def _():
        settle(uw_refs, w_scr and w_scr[0], info, False)
        settle(dw_refs, w_scr and w_scr[1], info, True)
        middle = x_ref[...] + nn(a_ref[...], tile_of(up_w, 4))
        mid_scr[...] = middle
        normed = (norm_parts(middle)[0] * gain_ref[3:4, :]).astype(BF16)
        norm_scr[...] = normed
        normt_scr[...] = normed.T
        total = mid_scr[...]
        for chunk in range(FF // D):
            up = nn(normed, tile_of(up_w, chunk))
            hidden = (up * gelu_parts(up)[1]).astype(BF16)
            total = total + nn(hidden, down_w[8 * chunk : 8 * chunk + 8, down_rows, :].reshape(D, D))
        for piece, lanes in enumerate(LANES):
            spread(up_scr, (piece,), total[:, lanes])
        gain = gain_ref[4:5, :]
        hat, scale = norm_parts(h_ref[...] + jnp.concatenate([up_scr[piece] for piece in range(len(LANES))], 1))
        final = (hat * gain).astype(BF16)
        head = tile_of(down_w, 4)[:, :VOCAB]
        logits = nn(final, head)
        top = jnp.max(logits, -1, keepdims=True)
        log_total = top + jnp.log(jnp.sum(jnp.exp(logits - top), -1, keepdims=True))
        hot = target_ref[...] == lax.broadcasted_iota(jnp.int32, logits.shape, 1)
        picked = jnp.sum(jnp.where(hot, logits, 0.0), -1, keepdims=True)
        counted = counted_ref[...]
        loss = jnp.sum((log_total - picked) * counted, 0, keepdims=True) * (1.0 / LOG_TWO)
        loss_ref[...] = jnp.broadcast_to(loss, (1, 128))
        grad = ((jnp.exp(logits - log_total) - jnp.where(hot, 1.0, 0.0)) * (counted * rate_ref[0, 0])).astype(BF16)
        dhead = nn(final.T, grad)
        put(head_refs, core, jnp.concatenate([dhead, jnp.zeros((D, D - VOCAB), F32)], 1))
        pulled, dgain = norm_pull(hat, scale, gain, nt(grad, head))
        dg4_ref[...] = dgain
        dh_ref[...] = pulled
        for piece, lanes in enumerate(LANES):
            up_scr[piece] = pulled[:, lanes]
            cot_scr[:, lanes] = thirds(up_scr, (piece,), 0)
        acc_scr[...] = jnp.zeros_like(acc_scr)

    @pl.when(step > 0)
    def _():
        chunk = step - 1
        down_in = cot_scr[...].astype(BF16)
        up_tile = up_w[:, pl.ds(pl.multiple_of(chunk * TILE, TILE), TILE), :].reshape(D, D)
        up = nn(norm_scr[...], up_tile)
        wave, gate = gelu_parts(up)
        hidden = (up * gate).astype(BF16)
        up_in = (nt(down_in, down_w[pl.ds(chunk * 8, 8), down_rows, :].reshape(D, D)) * gelu_slope(up, wave, gate)).astype(BF16)
        put(down_refs, core, nn(hidden.T, down_in), rows=4 * TILE, chunk=chunk)
        put(up_refs, core, nn(normt_scr[...], up_in))
        acc_scr[...] += nt(up_in, up_tile)

    @pl.when(step == FF // D)
    def _():
        hat, scale = norm_parts(mid_scr[...])
        pulled, dgain = norm_pull(hat, scale, gain_ref[3:4, :], acc_scr[...])
        dg3_ref[...] = dgain
        dmid = cot_scr[...] + pulled
        dmid_ref[...] = dmid
        out_in = dmid.astype(BF16)
        put(down_refs, core, nn(a_ref[...].T, out_in), at=4 * TILE)
        da_ref[...] = nt(out_in, tile_of(up_w, 4)).astype(BF16)


def short_rest(info, z, a, h, bundles, gains, target, counted, rate, split):
    ins = [info, z, a, h, *bundles[0], *bundles[1], gains, target, counted, rate]
    specs = [whole(i.shape) for i in ins[1:]]
    specs[0] = pl.BlockSpec((CSPAN, D), lambda *_: (1, 0))
    specs[2] = pl.BlockSpec((SPAN, D), lambda *_: (1, 0))
    specs[-1] = pl.BlockSpec(memory_space=pltpu.SMEM)
    return call(
        partial(short_body, split=split),
        "short_rest",
        [shape((1, 128)), shape((1, D)), shape((1, D)), shape((SPAN, D)), shape((CSPAN, D)), shape((CSPAN, D), BF16)]
        + grad_shapes(4 * TILE, split)
        + grad_shapes(5 * TILE, split)
        + grad_shapes(TILE, split),
        ins,
        12,
        grid=(FF // D + 1,),
        in_specs=specs,
        out_specs=[whole((1, 128)), whole((1, D)), whole((1, D)), whole((SPAN, D)), whole((CSPAN, D)), whole((CSPAN, D))]
        + grad_specs(TILE, split, lambda i, _: (0, jnp.maximum(i - 1, 0), 0))
        + grad_specs(5 * TILE, split, lambda i, _: (0, 0, 0))
        + grad_specs(TILE, split, lambda i, _: (0, 0, 0)),
        scratch=[
            pltpu.VMEM((CSPAN, D), F32),
            pltpu.VMEM((CSPAN, D), BF16),
            pltpu.VMEM((D, CSPAN), BF16),
            pltpu.VMEM((CSPAN, D), F32),
            pltpu.VMEM((CSPAN, D), F32),
            pltpu.VMEM((D // 128, SPAN, 128), F32),
            *bundle_scratch(bundles, (5 * TILE, 5 * TILE)),
        ],
    )


def project_back_body(info, *refs, full, split, groups):
    refs = list(refs)
    take = lambda n: [refs.pop(0) for _ in range(n)]
    dqs, keeps, recvs = take(groups), take(groups), take(groups)
    dmid_ref, x_ref = take(2)
    if full:
        (token_ref,) = take(1)
        wa_refs, wb_refs = [take(WEIGHT_PARTS if split else 1) for _ in range(2)]
        dg_refs = take(4)
    else:
        wa_refs, wb_refs = [take(WEIGHT_PARTS if split else 1) for _ in range(2)]
    wa_ref = settle(wa_refs, refs[-2], info, False, 0 if full else 4 * TILE)
    wb_ref = settle(wb_refs, refs[-1], info, True, 0 if full else 5 * TILE)
    weight = [tile_of(wa_ref, 0), tile_of(wa_ref, 1), tile_of(wb_ref, 0)]
    gain_ref, cos_ref, sin_ref = take(3)
    each = 2 if split else 1
    first_refs = take(each)
    if full:
        second_refs = take(each)
    if not full or not split:
        dgain_ref, dx_ref = take(2)
    if not full:
        (edge_ref,) = take(1)
    core = info[CORE]
    gain = gain_ref[0:1, :] if full else gain_ref[2:3, :]
    hat, scale = norm_parts(x_ref[...].astype(F32))
    normed_t = (hat * gain).astype(BF16).T
    cosine, sine = cos_ref[...], sin_ref[...]
    rows = hat.shape[0]
    skip = rows - dqs[0].shape[0]
    total = jnp.zeros((rows, D), F32)
    for kind in range(3):
        if kind == 0:
            grad = jnp.concatenate([dq[...] for dq in dqs], 1) if groups > 1 else dqs[0][...]
            grad = rope_pull(grad * 0.125, cosine[skip:], sine[skip:]).astype(BF16)
            found = nn(normed_t[:, skip:], grad)
        else:
            both = [(keep[kind - 1] + recv[kind - 1].astype(F32)).T for keep, recv in zip(keeps, recvs)]
            grad = jnp.concatenate(both, 1) if groups > 1 else both[0]
            grad = (rope_pull(grad, cosine, sine) if kind == 1 else grad).astype(BF16)
            found = nn(normed_t, grad)
        if full and kind == 2:
            put(second_refs, core, found)
        else:
            put(first_refs, core, found, at=TILE * kind)
        back = nt(grad, weight[kind])
        if kind == 0 and skip:
            back = jnp.concatenate([jnp.zeros((skip, D), F32), back], 0)
        total = total + back
    pulled, dgain = norm_pull(hat, scale, gain, total)
    if not full:
        dgain_ref[...] = dgain
        dx = jnp.concatenate([pulled[:skip], dmid_ref[...] + pulled[skip:]], 0)
        dx_ref[...] = dx
        for slot in range(2):
            edge_ref[slot] = dx[CSPAN * slot : CSPAN * slot + 8]
        return
    back = (dmid_ref[...] + pulled).astype(BF16)
    hot = (token_ref[...] == lax.broadcasted_iota(jnp.int32, (VOCAB, rows), 0)).astype(BF16)
    dembed = nn(hot, back)
    if not split:
        dgain_ref[...] = dgain
        dx_ref[...] = dembed
        return
    dgains = jnp.concatenate([dgain] + [ref[...] for ref in dg_refs] + [jnp.zeros((3, D), F32)], 0)
    lane = lax.broadcasted_iota(jnp.int32, (8, D), 1)
    sides = [
        jnp.where(lane < TILE, dgains if j == 0 else pltpu.roll(dgains, D - TILE * j, 1), 0.0) for j in range(SHARDS)
    ]
    embeds = dembed.reshape(SHARDS, 8, D)
    for chip in range(SHARDS // 2):
        for part, values in ((slice(TILE, TILE + 8), embeds), (slice(TILE + 8, 2 * TILE), sides)):
            low, high = values[2 * chip], values[2 * chip + 1]
            second_refs[0][chip, part, :] = jnp.where(core == 0, low, high)
    second_refs[1][:, TILE:, :] = jnp.stack(
        [
            jnp.where(
                core == 0,
                jnp.concatenate([embeds[2 * chip + 1], sides[2 * chip + 1]], 0),
                jnp.concatenate([embeds[2 * chip], sides[2 * chip]], 0),
            ).astype(BF16)
            for chip in range(SHARDS // 2)
        ],
        0,
    )


def project_back(info, dqs, keeps, recvs, dmid, x, extra, bundles, dgs, gains, cosine, sine, full, split):
    groups = len(dqs)
    rows = cosine.shape[0]
    weights = [value for bundle in bundles for value in bundle]
    ins = [info, *dqs, *keeps, *recvs, dmid, x, *extra, *weights, *dgs, gains, cosine, sine]
    specs = [whole(i.shape) for i in ins[1:]]
    scratch = bundle_scratch(bundles, (2 * TILE, TILE))
    if full:
        outs = grad_shapes(2 * TILE, split)
        outs += grad_shapes(2 * TILE if split else TILE, split)
        if not split:
            outs += [shape((1, D)), shape((VOCAB, D))]
    else:
        outs = grad_shapes(3 * TILE, split) + [shape((1, D)), shape((rows, D)), shape((2, 8, D))]
    return call(
        partial(project_back_body, full=full, split=split, groups=groups),
        "project_back",
        outs,
        ins,
        10 if full else 5,
        in_specs=specs,
        scratch=scratch,
    )


def fold_body(info, *refs, layout):
    refs = list(refs)
    outs = refs[4 * sum(len(rows) for rows in layout) :]
    for order, rows in enumerate(layout):
        at = 0
        for count in rows:
            keep, far, recv, far_recv = [refs.pop(0) for _ in range(4)]
            lead = outs[2 * order].shape[0]
            part = slice(at, at + count)
            flat = lambda ref: ref[...].reshape(lead, count, D)
            outs[2 * order][:, part, :] = flat(keep) + flat(recv).astype(F32)
            outs[2 * order + 1][:, part, :] = (flat(far) + flat(far_recv).astype(F32)).astype(BF16)
            at += count


def fold(info, orders, steps, us):
    ins, specs, outs, out_specs, layout = [info], [], [], [], []
    for sources, pre, post, bit in orders:
        layout.append([keep.shape[-2] for keep, _ in sources])
        for keep, recv in sources:
            dims = (pre, 2, post, keep.shape[-2], D)
            for value in (keep, recv):
                for other in (0, 1):
                    ins.append(value.reshape(dims))
                    specs.append(
                        pl.BlockSpec(
                            (pre // steps, 1, post, keep.shape[-2], D),
                            lambda i, info, other=other, bit=bit: (i, jnp.abs(info[BITS + bit] - other), 0, 0, 0),
                        )
                    )
        total = sum(layout[-1])
        for kind in (F32, BF16):
            outs.append(shape((pre * post, total, D), kind))
            out_specs.append(pl.BlockSpec((pre * post // steps, total, D), lambda i, _: (i, 0, 0)))
    found = call(
        partial(fold_body, layout=layout), "fold", outs, ins, us, grid=(steps,), in_specs=specs, out_specs=out_specs
    )
    return [(found[2 * i], found[2 * i + 1]) for i in range(len(orders))]


CORE_BIT, Y_BIT, X_BIT, Z0_BIT, Z1_BIT = range(5)


class Scatter:
    def __init__(self, info, firsts, seconds):
        self.info = info
        self.values = [
            [(keep, swapped(send, CORE_BIT)) for keep, send in sources] for sources in (firsts, seconds)
        ]
        self.stage = 0

    def plan(self):
        first, second, steps = (
            ((X_BIT, 4, 2), (Y_BIT, 8, 1), 4),
            ((Y_BIT, 4, 1), (X_BIT, 4, 1), 4),
            ((Z0_BIT, 2, 1), None, 2),
            ((Z1_BIT, 1, 1), None, 1),
        )[self.stage]
        if second is None:
            self.values = [[pair for sources in self.values for pair in sources]]
        plans = [plan for plan in (first, second) if plan]
        orders = [(sources, pre, post, bit) for sources, (bit, pre, post) in zip(self.values, plans)]
        return orders, steps

    def folded(self, found, bits):
        self.values = [[(keep, swapped(send, bit))] for (keep, send), bit in zip(found, bits)]
        self.stage += 1

    def joined(self, other):
        found = Scatter(self.info, [], [])
        found.values = [mine + more for mine, more in zip(self.values, other.values)]
        found.stage = self.stage
        return found

    def kept(self):
        return [keep for sources in self.values for keep, _ in sources]

    def result(self):
        return [keep.reshape(-1, D) + recv.reshape(-1, D).astype(F32) for ((keep, recv),) in self.values]


def step_all(info, *needed):
    def step(*scatters):
        plans = [scatter.plan() for scatter in scatters]
        orders = [order for plan, _ in plans for order in plan]
        found = fold(after(info, needed) if needed else info, orders, min(steps for _, steps in plans), 0.05)
        for scatter, (plan, _) in zip(scatters, plans):
            scatter.folded([found.pop(0) for _ in plan], [bit for *_, bit in plan])

    return step


def after(value, *needed):
    leaves = jax.tree.leaves(needed)
    return lax.optimization_barrier((value, *leaves))[0]


DECAY = 1.0 - STEP ** (-0.8)
MATRICES = (
    [(VOCAB, 1, D), (D, 1, VOCAB)] + [(D, 3, 3 * D)] * 2 + [(D, 1, D)] * 2 + [(D, 4, FF)] * 2 + [(FF, 1, D)] * 2
)
TILES = sum(count for _, count, _ in MATRICES)
STAT_ROWS = 48


def as_column(row):
    return jnp.broadcast_to(row, (128, row.shape[1])).T[:, 0:1]


def as_row(column):
    return jnp.broadcast_to(column, (column.shape[0], 128)).T[0:1, :]


def tile_lanes(width, index):
    return slice(D * index, min(D * index + D, width))


def measure_body(info, *refs):
    refs = list(refs)
    take = lambda n: [refs.pop(0) for _ in range(n)]
    both, early = [keep[0] + recv[0].astype(F32) for keep, recv in [take(2) for _ in range(2)]]
    row_refs, weight_refs = take(6), take(6)
    gain_ref, sq_ref, loss_ref = take(3)
    grad_refs, new_row_refs = take(6), take(6)
    gain_grad_ref, new_sq_ref, stat_ref = take(3)
    both_a, both_b, early_a, early_b = both[: 11 * TILE], both[11 * TILE :], early[: 2 * TILE], early[2 * TILE :]
    cut = lambda value, start, count=1, size=TILE: [value[start + size * i : start + size * i + size] for i in range(count)]
    grads = [
        [early_b[TILE : TILE + 8]],
        [both_b[10 * TILE :, :VOCAB]],
        cut(early_a, 0, 2) + cut(early_b, 0),
        cut(both_a, 8 * TILE, 3),
        cut(both_b, 9 * TILE),
        cut(both_b, 4 * TILE),
        cut(both_a, 4 * TILE, 4),
        cut(both_a, 0, 4),
        cut(both_b, 5 * TILE, size=4 * TILE),
        cut(both_b, 0, size=4 * TILE),
    ]
    lane = lax.broadcasted_iota(jnp.int32, (1, D), 1)
    scalars = jnp.where(lane == 30, loss_ref[0:1, 0:1], 0.0)
    total = lambda value: jnp.sum(jnp.sum(value, 1, keepdims=True), 0, keepdims=True)
    stat_ref[...] = jnp.zeros_like(stat_ref)
    at = 0
    for index, (pieces, (_, _, width)) in enumerate(zip(grads, MATRICES)):
        kind, layer = (index, None) if index < 2 else (2 + (index - 2) // 2, index % 2)
        old = row_refs[kind][...] if layer is None else row_refs[kind][layer : layer + 1, :]
        weight = weight_refs[kind][...] if layer is None else weight_refs[kind][layer]
        squares = [piece * piece for piece in pieces]
        mean = sum(jnp.sum(square, 1, keepdims=True) for square in squares) * (1.0 / width)
        new_row = DECAY * as_column(old) + (1.0 - DECAY) * mean
        inverse = 1.0 / new_row
        new_rows = as_row(new_row)
        if layer is None:
            new_row_refs[kind][...] = new_rows
        else:
            new_row_refs[kind][layer : layer + 1, :] = new_rows
        for place, (piece, square) in enumerate(zip(pieces, squares)):
            lanes = tile_lanes(width, place)
            if layer is None:
                grad_refs[kind][:, lanes] = piece
            else:
                grad_refs[kind][layer, :, lanes] = piece
            own = slice(0, piece.shape[1])
            stat_ref[at : at + 1, own] = jnp.sum(square, 0, keepdims=True)
            stat_ref[TILES + at : TILES + at + 1, own] = jnp.sum(square * inverse, 0, keepdims=True)
            at += 1
        scalars = jnp.where(lane == 2 * index, total(new_row), scalars)
        scalars = jnp.where(lane == 2 * index + 1, total(weight * weight), scalars)
    gain_grad = early_b[TILE + 8 : TILE + 13, :TILE]
    gain_grad_ref[...] = gain_grad
    new_sq = DECAY * sq_ref[...] + (1.0 - DECAY) * gain_grad * gain_grad
    new_sq_ref[...] = new_sq
    gains = gain_ref[...]
    update = gain_grad / jnp.sqrt(new_sq)
    for value, start in ((update, 20), (gains, 25)):
        each = jnp.sum(value * value, 1, keepdims=True)
        for row in range(5):
            scalars = jnp.where(lane == start + row, each[row : row + 1], scalars)
    stat_ref[2 * TILES : 2 * TILES + 1, :] = scalars


def update_body(info, *refs):
    refs = list(refs)
    take = lambda n: [refs.pop(0) for _ in range(n)]
    (stat_ref,) = take(1)
    grad_refs, row_refs, col_refs, weight_refs = take(6), take(6), take(6), take(6)
    gain_ref, gain_grad_ref, sq_ref = take(3)
    new_col_refs, new_refs = take(6), take(6)
    gain_new_ref, loss_ref = take(2)
    scalars = stat_ref[2 * TILES : 2 * TILES + 1, :]
    scalar = lambda lane: scalars[:, lane : lane + 1]
    loss_ref[...] = scalar(30)
    at = 0
    for index, (rows, count, width) in enumerate(MATRICES):
        kind, layer = (index, None) if index < 2 else (2 + (index - 2) // 2, index % 2)
        mean_row = scalar(2 * index) * (1.0 / rows)
        size = rows * width
        new_row = as_column(row_refs[kind][...] if layer is None else row_refs[kind][layer : layer + 1, :])
        pieces, spread_sum = [], jnp.zeros((1, 1), F32)
        for place in range(count):
            lanes = tile_lanes(width, place)
            own = slice(0, lanes.stop - lanes.start)
            here = slice(0, 1) if layer is None else slice(layer, layer + 1)
            new_col = DECAY * col_refs[kind][here, lanes] + (1.0 - DECAY) * stat_ref[at : at + 1, own] * (1.0 / rows)
            new_col_refs[kind][here, lanes] = new_col
            spread_sum = spread_sum + jnp.sum(stat_ref[TILES + at : TILES + at + 1, own] / new_col, 1, keepdims=True)
            pieces.append((lanes, new_col))
            at += 1
        update_sum = mean_row * spread_sum
        rate = RATE_SCALE * jnp.sqrt(scalar(2 * index + 1) * (1.0 / size))
        rate = rate / jnp.maximum(1.0, jnp.sqrt(update_sum * (1.0 / size)))
        for lanes, new_col in pieces:
            if layer is None:
                grad, weight = grad_refs[kind][:, lanes], weight_refs[kind][:, lanes]
            else:
                grad, weight = grad_refs[kind][layer, :, lanes], weight_refs[kind][layer, :, lanes]
            found = weight - rate * (grad / jnp.sqrt(new_row * new_col / mean_row))
            if layer is None:
                new_refs[kind][:, lanes] = found
            else:
                new_refs[kind][layer, :, lanes] = found
    gains, gain_grad = gain_ref[...], gain_grad_ref[...]
    update = gain_grad / jnp.sqrt(sq_ref[...])
    for row in range(5):
        here = slice(row, row + 1)
        rate = RATE_SCALE * jnp.sqrt(scalar(25 + row) * (1.0 / D)) / jnp.maximum(1.0, jnp.sqrt(scalar(20 + row) * (1.0 / D)))
        gain_new_ref[here, :] = gains[here] - rate * update[here]


def optimize(info, sums, rows, cols, weights, gains, gains_sq, loss):
    flat = lambda values: [value[None] if value.ndim == 1 else value for value in values]
    rows, cols = flat(rows), flat(cols)
    same = lambda values: [shape(value.shape) for value in values]
    found = call(
        measure_body,
        "measure",
        same(weights) + same(rows) + [shape(gains.shape), shape(gains.shape), shape((STAT_ROWS, D))],
        [info, *[value for pair in sums for value in pair], *rows, *weights, gains, gains_sq, loss],
        0.05,
    )
    grads, new_rows, (gain_grad, new_sq, stats) = found[:6], found[6:12], found[12:]
    stats = sum_all(stats)
    found = call(
        update_body,
        "update",
        same(cols) + same(weights) + [shape(gains.shape), shape((1, 1))],
        [info, stats, *grads, *new_rows, *cols, *weights, gains, gain_grad, new_sq],
        0.05,
    )
    new_cols, new_weights, (gains_new, loss_sum) = found[:6], found[6:12], found[12:]
    outputs = []
    for index in range(6):
        plain = (lambda value: value[0]) if index < 2 else (lambda value: value)
        outputs += [grads[index], plain(new_rows[index]), plain(new_cols[index]), new_weights[index]]
    return [loss_sum[0, 0]], outputs + [gain_grad, new_sq, gains_new]


def flat_index():
    return lax.axis_index("dp") * lax.axis_size("seq") + lax.axis_index("seq")


def flat_count():
    return lax.axis_size("dp") * lax.axis_size("seq")


def swapped(value, bit):
    return lax.ppermute(value, BOTH, [(i, i ^ (1 << bit)) for i in range(flat_count())])


def bit_of(bit):
    return (flat_index() >> bit) & 1


def join_body(info, *refs):
    count = len(refs) // 3
    for index, out in enumerate(refs[2 * count :]):
        here, there = refs[2 * index : 2 * index + 2]
        rows = here.shape[0]
        out[:rows] = here[...]
        out[rows:] = there[...]


def join_pairs(info, pairs):
    outs = [shape((2 * here.shape[0], *here.shape[1:]), here.dtype) for here, _ in pairs]
    return call(join_body, "join", outs, [info, *[value for pair in pairs for value in pair]], 0.05)


class Gather:
    def __init__(self, packed):
        self.values = [packed[None]]
        self.near = None
        self.info = jnp.zeros((1,), jnp.int32)

    def send(self, *bits, needed=()):
        if needed:
            self.values = [after(value, *needed) for value in self.values]
        self.coming = [swapped(value, bit) for value, bit in zip(self.values, bits)]
        return self

    def pairs(self, needed):
        pairs = list(zip(self.values, self.coming))
        return lax.optimization_barrier((pairs, list(needed)))[0]

    def join(self, split=None, needed=()):
        pairs = self.pairs(needed)
        if split is not None:
            ((here, there),) = pairs
            pairs = [(here[:, :split], there[:, :split]), (here[:, split:], there[:, split:])]
        small = pairs[0][0].shape[0] * pairs[0][0].shape[1] < 256
        self.values = [jnp.concatenate(pair, 0) for pair in pairs] if small else join_pairs(self.info, pairs)
        return self

    def send_last(self, *bits, needed=()):
        self.send(*bits, needed=needed)
        self.near = [swapped(value, CORE_BIT) for value in self.values]
        return self

    def last(self, needed=()):
        self.values = self.pairs(needed)
        if self.near is None:
            self.near = [swapped(here, CORE_BIT) for here, _ in self.values]
        return [
            (here, there, near, swapped(there, CORE_BIT)) for (here, there), near in zip(self.values, self.near)
        ]


def group_perm(ways, links):
    count = lax.axis_size("seq")
    return [(base + a, base + b) for base in range(0, count, ways) for a, b in links]


def window_keys(kv, ways):
    if ways == 2:
        return [kv, lax.ppermute(kv, "seq", group_perm(2, ((0, 1), (1, 0))))]
    groups = [list(range(base, base + ways)) for base in range(0, lax.axis_size("seq"), ways)]
    found = []
    for value in (kv[0], kv[1]):
        every = lax.all_gather(value, "seq", axis=0, tiled=False, axis_index_groups=groups)
        rows = every.shape[1] // 2
        blocks = [every[w, :rows] for w in range(ways)] + [every[w, rows:] for w in reversed(range(ways))]
        found.append(jnp.concatenate(blocks, 0))
    return found


def window_sum(grads, ways):
    if ways == 2:
        keep, send = grads
        return keep, lax.ppermute(send, "seq", group_perm(2, ((0, 1), (1, 0))))
    groups = [list(range(base, base + ways)) for base in range(0, lax.axis_size("seq"), ways)]
    total = lax.psum_scatter(grads[0], "seq", scatter_dimension=0, tiled=False, axis_index_groups=groups)
    return total, jnp.zeros(total.shape, BF16)


def from_sides(first, second, ways):
    if ways == 2:
        rank = lax.axis_index("seq") % ways
        other = lax.ppermute(jnp.where(rank == 0, first, second), "seq", group_perm(2, ((0, 1), (1, 0))))
        zero = jnp.zeros_like(other)
        return jnp.where(rank == 0, zero, other), jnp.where(rank == 0, other, zero)
    up = [(i, i + 1) for i in range(ways - 1)]
    down = [(i + 1, i) for i in range(ways - 1)]
    return lax.ppermute(first, "seq", group_perm(ways, up)), lax.ppermute(second, "seq", group_perm(ways, down))


def sum_all(value):
    count = flat_count()
    for bit in range(count.bit_length() - 1):
        value = value + swapped(value, bit)
    return value


def tiles(weight):
    rows = weight.shape[0]
    return [weight[:, start : start + D] for start in range(0, weight.shape[1], D)] if rows else []


def pack_edge(embed, gains):
    rows = embed.shape[-2]
    pad = jnp.zeros((8, D - gains.shape[1]), gains.dtype)
    side = jnp.concatenate([jnp.concatenate([gains, jnp.zeros((3, gains.shape[1]), gains.dtype)], 0), pad], 1)
    return jnp.concatenate([embed, side], 0)


def gather_weights(embed, head, attn_in, attn_out, ffn_in, ffn_out, gains):
    full = [
        lax.all_gather(weight, BOTH, axis=axis, tiled=True)
        for weight, axis in ((embed, 0), (head, 0), (attn_in, 1), (attn_out, 1), (ffn_in, 1), (ffn_out, 1), (gains, 1))
    ]
    embed, head, attn_in, attn_out, ffn_in, ffn_out, gains = full
    fold_rows = lambda weight: weight.reshape(SHARDS, TILE, D)
    edge = jnp.zeros((SHARDS, TILE, D), BF16).at[:, :8].set(embed.reshape(SHARDS, 8, D))
    edge = edge.at[:, 8:13, :TILE].set(gains.reshape(5, SHARDS, TILE).transpose(1, 0, 2))
    head_tile = jnp.zeros((SHARDS, TILE, D), BF16).at[:, :, :VOCAB].set(head.reshape(SHARDS, TILE, VOCAB))
    down = ffn_out.reshape(2, SHARDS, 4 * TILE, D)
    side = [[fold_rows(t) for t in tiles(attn_in[i])] for i in range(2)]
    up = [[fold_rows(t) for t in tiles(ffn_in[i])] for i in range(2)]
    firsts = [jnp.concatenate(side[0][:2], 1), jnp.concatenate([side[0][2], edge], 1)]
    seconds = [
        jnp.concatenate(up[0] + side[1][:2], 1),
        jnp.concatenate([down[0], fold_rows(attn_out[0]), side[1][2]], 1),
    ]
    third = [jnp.concatenate(up[1] + [fold_rows(attn_out[1])], 1), jnp.concatenate([down[1], head_tile], 1)]
    return firsts, seconds, third


def reduce_natural(grad, axis):
    return lax.psum_scatter(grad, BOTH, scatter_dimension=axis, tiled=True)


def unfold(packed):
    parts = packed.shape[1] // TILE
    return jnp.concatenate([packed[:, TILE * i : TILE * i + TILE].reshape(D, D) for i in range(parts)], 1)


def local(
    stream, offsets, embed, head, attn_in, attn_out, ffn_in, ffn_out, gains,
    embed_row, embed_col, head_row, head_col, in_row, in_col, out_row, out_col, up_row, up_col, down_row, down_col, gains_sq,
):
    seq_rank = lax.axis_index("seq")
    dp_rank = lax.axis_index("dp")
    seq_count = lax.axis_size("seq")
    per_group = offsets.shape[0] // lax.axis_size("dp")
    ways = seq_count // per_group
    blocks = 2 * ways
    length = SPAN * blocks
    rank = seq_rank % ways
    split = flat_count() == SHARDS
    if split:
        low = lambda *values: [value.astype(BF16) for value in values]
        embed_low, gains_low, in_low = low(embed, gains, attn_in[0])
        one = Gather(jnp.concatenate(tiles(in_low) + [pack_edge(embed_low, gains_low)], 0))
        up_low, down_low, out_low, in_low = low(*after((ffn_in[0], ffn_out[0], attn_out[0], attn_in[1]), one.values))
        in_low = tiles(in_low)
        two = Gather(jnp.concatenate(tiles(up_low) + in_low[:2] + [down_low, out_low, in_low[2]], 0))
        one.send(Z1_BIT).join()
        two.send(Z1_BIT, needed=one.values)
        up_low, down_low, out_low, head_low = low(*after((ffn_in[1], ffn_out[1], attn_out[1], head), one.values))
        head_low = jnp.concatenate([head_low, jnp.zeros_like(head_low)], 1)
        three = Gather(jnp.concatenate(tiles(up_low) + [out_low, down_low, head_low], 0))
        one.send(Z0_BIT).join(2 * TILE)
        offsets_then, stream_then = after((offsets, stream), *one.values)
        two.join().send(Z0_BIT, needed=one.values)
        one.send(X_BIT, Y_BIT).join()
        two.join(6 * TILE)
        three.send(Z1_BIT, needed=one.values)
        one.send_last(Y_BIT, X_BIT)
        three.join()
        first = one.last()
        two.send(X_BIT, Y_BIT, needed=one.values)
    else:
        low = [w.astype(BF16) for w in (embed, head, attn_in, attn_out, ffn_in, ffn_out, gains)]
        first, second, third = gather_weights(*low)
        first, second, third = [[(value,) for value in pair] for pair in (first, second, third)]
        offsets_then, stream_then = offsets, stream

    window_start = offsets_then[dp_rank * per_group + seq_rank // ways]
    limits = jnp.minimum(length, STREAM - 1 - offsets_then) - (length - length // 2)
    count_real = jnp.sum(jnp.maximum(limits, 0)).astype(F32)
    own_blocks = jnp.stack([rank, blocks - 1 - rank]) + 0 * window_start
    positions = (own_blocks[:, None] * SPAN + jnp.arange(SPAN, dtype=jnp.int32)[None]).reshape(-1)
    coarse_pos = (own_blocks[:, None] * CSPAN + jnp.arange(CSPAN, dtype=jnp.int32)[None]).reshape(-1)
    reach = own_blocks + 1
    info = jnp.concatenate(
        [reach, jnp.stack([rank, flat_index() & 1] + [bit_of(bit) for bit in range(5)] + [flat_index() >> 1])], 0
    ).astype(jnp.int32)
    starts = window_start + own_blocks * SPAN
    padded = jnp.concatenate([stream_then, jnp.broadcast_to(stream_then[-1:], (length,))], 0)
    tokens = jnp.concatenate([lax.dynamic_slice_in_dim(padded, starts[s], SPAN, 0) for s in range(2)], 0)
    target = lax.dynamic_slice_in_dim(padded, starts[1] + 1, SPAN, 0)
    counted = (window_start + positions[SPAN:] + 1 < STREAM).astype(F32)
    rate = (1.0 / (LOG_TWO * count_real)).reshape(1, 1)

    def tables(at):
        frequency = 10000.0 ** (-jnp.arange(HD // 2, dtype=F32) / (HD // 2))
        angles = at.astype(F32)[:, None] * frequency[None, :]
        cosine, sine = jnp.cos(angles), jnp.sin(angles)
        return (jnp.concatenate([cosine] * 4, 1), jnp.concatenate([-sine, sine] * 2, 1))

    cos_0, sin_0 = tables(positions)
    cos_1, sin_1 = tables(coarse_pos)

    token_col, target_col, counted_col = tokens[:, None], target[:, None], counted[:, None]
    if split:
        token_col = after(token_col, target_col, counted_col, rate, cos_1, sin_1, three.values)
    h_0, q_0, kv_0, gain_rows = project(info, token_col, first, cos_0, sin_0)
    if split:
        two.join(needed=[q_0]).send_last(Y_BIT, X_BIT)
        three.send(Z0_BIT)
        kv_0 = after(kv_0, two.values)
    keys_0 = window_keys(kv_0, ways)
    a_lo, lse_lo = attend(info, q_0, keys_0, SPAN, 0, 1)
    if split:
        three.join(5 * TILE, needed=[a_lo]).send(X_BIT, Y_BIT)
    a_hi, lse_hi = attend(info, after(q_0, a_lo, three.values, two.near) if split else q_0, keys_0, SPAN, 1, 1)
    if split:
        three.join(needed=[a_hi])
        second = two.last([a_hi, *three.values])
        three.send(Y_BIT, X_BIT)
    m_0, h_1, tail = branch(info, after(h_0, three.values) if split else h_0, (a_lo, a_hi), second, gain_rows)

    z_0, q_1, kv_1 = project_short(
        info, h_1, tail, *from_sides(tail[0], tail[1], ways), second, gain_rows, cos_1, sin_1, ways
    )
    keys_1 = window_keys(kv_1, ways)
    a_1, lse_1 = attend(info, q_1, keys_1, CSPAN, 0, 2)
    if split:
        third = three.last([a_1])
    found = short_rest(info, z_0, a_1, h_1, third, gain_rows, target_col, counted_col, rate, split)
    loss, dg_4, dg_3, d_h2, d_m1, d_a1 = found[:6]
    each = 2 if split else 1
    d_up_1, d_down_1, d_head = [found[6 + each * i : 6 + each * i + each] for i in range(3)]
    if split:
        late = Scatter(info, [d_up_1], [d_down_1])
    d_q1, *d_kv1 = attend_back(info, q_1, keys_1, d_a1, lse_1, CSPAN, 0, 2)
    keep, recv = window_sum(d_kv1, ways)
    found = project_back(info, [d_q1], [keep], [recv], d_m1, z_0, [], second, [], gain_rows, cos_1, sin_1, False, split)
    d_in_1, (dg_2, d_z0, edge) = found[:each], found[each:]

    low_edge, high = from_sides(edge[1], edge[0], ways)
    found = branch_back(info, d_z0, edge, high, low_edge, d_h2, m_0, (a_lo, a_hi), second, gain_rows, ways, split)
    d_m0, da_lo, da_hi, dg_1 = found[:4]
    d_up_0, d_down_0 = [found[4 + each * i : 4 + each * i + each] for i in range(2)]
    if split:
        middle = Scatter(info, [d_up_0, d_in_1], [d_down_0, d_head])
        step_all(info, d_m0)(late)
        step_all(info, late.kept())(middle)
        both = late.joined(middle)
        da_lo = after(da_lo, both.kept())
    dq_lo, *dkv_lo = attend_back(info, q_0, keys_0, da_lo, lse_lo, SPAN, 0, 1)
    if split:
        da_hi = after(da_hi, dq_lo)
    sum_lo = window_sum(dkv_lo, ways)
    dq_hi, *dkv_hi = attend_back(info, q_0, keys_0, da_hi, lse_hi, SPAN, 1, 1)
    if split:
        step_all(info, dq_hi)(both)
        dkv_hi = after(tuple(dkv_hi), both.kept())
    sum_hi = window_sum(dkv_hi, ways)
    found = project_back(
        info, [dq_lo, dq_hi], [sum_lo[0], sum_hi[0]], [sum_lo[1], sum_hi[1]], d_m0, h_0, [tokens[None, :]], first,
        [dg_1, dg_2, dg_3, dg_4], gain_rows, cos_0, sin_0, True, split,
    )

    if split:
        early = Scatter(info, [found[:2]], [found[2:]])
        step_all(info, found[0])(both, early)
        step_all(info)(early)
        step_all(info)(both, early)
        step_all(info)(early)
        loss_sum, outputs = optimize(
            info,
            [sources[0] for sources in both.values + early.values],
            [embed_row, head_row, in_row, out_row, up_row, down_row],
            [embed_col, head_col, in_col, out_col, up_col, down_col],
            [embed, head, attn_in, attn_out, ffn_in, ffn_out],
            gains,
            gains_sq,
            loss,
        )
        return (*loss_sum, count_real, *outputs)
    d_qk, d_v, dg_0, d_embed = found
    if True:
        d_in_0 = jnp.concatenate([d_qk, d_v], 1)
        g_embed = reduce_natural(d_embed, 0)
        g_head = reduce_natural(d_head[0][:, :, :VOCAB].reshape(D, VOCAB), 0)
        g_in = reduce_natural(jnp.stack([unfold(d_in_0), unfold(d_in_1[0])]), 1)
        g_out = reduce_natural(jnp.stack([unfold(d) for d in (d_down_0[0][:, 4 * TILE :], d_down_1[0][:, 4 * TILE :])]), 1)
        g_up = reduce_natural(jnp.stack([unfold(d_up_0[0]), unfold(d_up_1[0])]), 1)
        g_down = reduce_natural(jnp.stack([d.reshape(FF, D) for d in (d_down_0[0][:, : 4 * TILE], d_down_1[0][:, : 4 * TILE])]), 1)
        gain_grad = reduce_natural(jnp.concatenate([dg_0, dg_1, dg_2, dg_3, dg_4], 0), 1)

    embed, head, attn_in, attn_out, ffn_in, ffn_out = after((embed, head, attn_in, attn_out, ffn_in, ffn_out), d_q1)
    decay = 1.0 - STEP ** (-0.8)
    matrices = [
        (g_embed, embed_row, embed_col, embed, VOCAB),
        (g_head, head_row, head_col, head, D),
        (g_in, in_row, in_col, attn_in, D),
        (g_out, out_row, out_col, attn_out, D),
        (g_up, up_row, up_col, ffn_in, D),
        (g_down, down_row, down_col, ffn_out, FF),
    ]
    new_rows, sums = [], []
    for grad, row, _, weight, _ in matrices:
        square = grad * grad
        new_row = decay * row + (1.0 - decay) * jnp.mean(square, -1)
        new_rows.append(new_row)
        sums += [
            jnp.sum(square, -2),
            jnp.sum(square / new_row[..., None], -2),
            jnp.sum(new_row, -1),
            jnp.sum(weight * weight, (-2, -1)),
        ]
    new_sq = decay * gains_sq + (1.0 - decay) * gain_grad * gain_grad
    gain_update = gain_grad / jnp.sqrt(new_sq)
    sums += [jnp.sum(gain_update * gain_update, -1), jnp.sum(gains * gains, -1), loss[0, :1]]
    flat = jnp.concatenate([s.reshape(-1) for s in sums], 0)
    size = flat.shape[0]
    flat = jnp.pad(flat, (0, -size % 1024)).reshape(-1, 128)
    flat = sum_all(flat).reshape(-1)
    totals, at = [], 0
    for s in sums:
        totals.append(flat[at : at + s.size].reshape(s.shape))
        at += s.size
    outputs = [totals[-1].reshape(()), count_real]
    for index, (grad, _, col, weight, full_rows) in enumerate(matrices):
        col_sum, ratio_sum, row_sum, weight_sum = totals[4 * index : 4 * index + 4]
        new_row = new_rows[index]
        new_col = decay * col + (1.0 - decay) * col_sum / full_rows
        mean_row = row_sum / full_rows
        size_all = full_rows * grad.shape[-1]
        update_sum = mean_row * jnp.sum(ratio_sum / new_col, -1)
        rate_now = RATE_SCALE * jnp.sqrt(weight_sum / size_all) / jnp.maximum(1.0, jnp.sqrt(update_sum / size_all))
        update = grad / jnp.sqrt(new_row[..., :, None] * new_col[..., None, :] / mean_row[..., None, None])
        outputs += [grad, new_row, new_col, weight - rate_now[..., None, None] * update]
    gain_rate = RATE_SCALE * jnp.sqrt(totals[-2] / D) / jnp.maximum(1.0, jnp.sqrt(totals[-3] / D))
    outputs += [gain_grad, new_sq, gains - gain_rate[:, None] * gain_update]
    return tuple(outputs)


def solution(mesh):
    row = P(BOTH, None)
    mid = P(None, BOTH, None)
    vec = P(BOTH)
    vec2 = P(None, BOTH)
    state = (vec, P(), vec, P(), vec2, P(), vec2, P(), vec2, P(), vec2, P(), vec2)
    return jax.shard_map(
        local,
        mesh=mesh,
        in_specs=(P(), P(), row, row, mid, mid, mid, mid, vec2) + state,
        out_specs=(P(), P())
        + (row, vec, P(), row) * 2
        + (mid, vec2, P(), mid) * 4
        + (vec2, vec2, vec2),
        check_vma=False,
    )
```

```python
from functools import partial
import math

import jax
import jax.numpy as jnp
from jax import lax
from jax.experimental import pallas as pl
from jax.experimental.pallas import tpu as pltpu
from jax.sharding import PartitionSpec as P

D = 512
HEADS = 8
FF = 2048
VOCAB = 256
SHORT = 3
HD = 64
SPAN = 384
CSPAN = SPAN // SHORT
STREAM = 65536
STEP = 10
SHARDS = 32
TILE = 16

EPSILON = 1e-05
RATE_SCALE = 0.5
LOG_TWO = math.log(2.0)
MASKED = -1e30
GELU_A = math.sqrt(2.0 / math.pi)
GELU_B = 0.044715
BOTH = ("dp", "seq")
F32 = jnp.float32
BF16 = jnp.bfloat16
ROOM = {
    "fold": 24, "join": 16, "measure": 20, "attend": 24, "attend_back": 36, "project": 28, "project_short": 28,
    "branch": 32, "branch_back": 44, "short_rest": 34, "project_back": 36,
}


def nn(left, right):
    return jnp.dot(left, right, preferred_element_type=F32)


def nt(left, right):
    return lax.dot_general(left, right, (((1,), (1,)), ((), ())), preferred_element_type=F32)


def call(body, name, outs, ins, us, grid=(1,), in_specs=None, out_specs=None, scratch=(), prefetch=1):
    room = ROOM.get(name, 56) * 2**20
    spec = pltpu.PrefetchScalarGridSpec(
        num_scalar_prefetch=prefetch,
        grid=grid,
        in_specs=in_specs or [held(i.shape) for i in ins[prefetch:]],
        out_specs=out_specs or [whole(o.shape) for o in outs],
        scratch_shapes=list(scratch),
    )
    return pl.pallas_call(
        body,
        grid_spec=spec,
        out_shape=list(outs),
        compiler_params=pltpu.CompilerParams(vmem_limit_bytes=room),
        cost_estimate=pl.CostEstimate(flops=int(us * 2e10), bytes_accessed=1 << 20, transcendentals=0),
        name=name,
    )(*ins)


def whole(dims):
    return pl.BlockSpec(dims, lambda *_: (0,) * len(dims))


def held(dims):
    return pl.BlockSpec(dims, lambda *_: (0,) * len(dims), pipeline_mode=pl.Buffered(1))


def shape(dims, kind=F32):
    return jax.ShapeDtypeStruct(dims, kind)


RANK, CORE, BITS, CHIP = 2, 3, 4, 9
WEIGHT_PARTS = 4


def norm_parts(values):
    center = values - jnp.mean(values, -1, keepdims=True)
    scale = lax.rsqrt(jnp.mean(center * center, -1, keepdims=True) + EPSILON)
    return center * scale, scale


def norm_pull(hat, scale, gain, cotangent):
    pulled = cotangent * gain
    inner = pulled - jnp.mean(pulled, -1, keepdims=True) - hat * jnp.mean(pulled * hat, -1, keepdims=True)
    return scale * inner, jnp.sum(cotangent * hat, 0, keepdims=True)


def swap_halves(values):
    lane = lax.broadcasted_iota(jnp.int32, values.shape, 1)
    return jnp.where(lane % HD < HD // 2, pltpu.roll(values, 128 - HD // 2, 1), pltpu.roll(values, HD // 2, 1))


def rope(values, cosine, sine):
    pieces = []
    for start in range(0, D, 128):
        piece = values[:, start : start + 128]
        pieces.append(piece * cosine + swap_halves(piece) * sine)
    return jnp.concatenate(pieces, 1)


def rope_pull(values, cosine, sine):
    pieces = []
    for start in range(0, D, 128):
        piece = values[:, start : start + 128]
        pieces.append(piece * cosine + swap_halves(piece * sine))
    return jnp.concatenate(pieces, 1)


def gelu_parts(values):
    inner = GELU_A * (values + GELU_B * (values * values * values))
    wave = jnp.tanh(inner)
    return wave, 0.5 * (1.0 + wave)


def gelu_slope(values, wave, gate):
    return gate + 0.5 * values * (1.0 - wave * wave) * (GELU_A * (1.0 + 3.0 * GELU_B * values * values))


def tile_of(ref, index):
    return ref[:, TILE * index : TILE * index + TILE, :].reshape(D, ref.shape[-1])


def settle(refs, scr, info, second, start=0):
    if len(refs) == 1:
        return refs[0].at[:, start:]
    rows = slice(start, start + scr.shape[1])
    last, next_last = (1, 0) if second else (0, 1)

    def place(r, carry):
        mask = ((r & 1) << 3) | (((r >> 1) & 1) << 2) | (((r >> 2) & 1) << next_last)
        for far in range(2):
            chip = info[CHIP] ^ (mask | (far << last))
            scr[2 * chip + info[CORE]] = refs[far][r, rows]
            scr[2 * chip + 1 - info[CORE]] = refs[2 + far][r, rows]
        return carry

    lax.fori_loop(0, SHARDS // 4, place, 0)
    return scr


def bundle_scratch(bundles, rows):
    return [pltpu.VMEM((SHARDS, count, D), BF16) for bundle, count in zip(bundles, rows) if len(bundle) > 1]


def thirds(ref, lead, start):
    found = ref[(*lead, pl.ds(start, CSPAN, stride=SHORT), slice(None))]
    for shift in range(1, SHORT):
        found = found + ref[(*lead, pl.ds(start + shift, CSPAN, stride=SHORT), slice(None))]
    return found


def spread(ref, lead, value):
    for shift in range(SHORT):
        ref[(*lead, pl.ds(shift, CSPAN, stride=SHORT), slice(None))] = value


LANES = [slice(start, start + 128) for start in range(0, D, 128)]


def grad_shapes(rows, split):
    if split:
        return [shape((SHARDS // 2, rows, D)), shape((SHARDS // 2, rows, D), BF16)]
    return [shape((SHARDS, rows, D))]


def grad_specs(rows, split, index, shards=SHARDS):
    if split:
        return [pl.BlockSpec((shards // 2, rows, D), index)] * 2
    return [pl.BlockSpec((shards, rows, D), index)]


def put(refs, core, value, at=0, rows=TILE, chunk=0):
    width = value.shape[-1]
    part = pl.ds(at, rows)
    shards = D // rows
    if len(refs) == 2:
        pairs = value.reshape(shards // 2, 2, rows, width)
        low, high = pairs[:, 0], pairs[:, 1]
        where = pl.ds(chunk * (shards // 2), shards // 2)
        refs[0][where, part, :width] = jnp.where(core == 0, low, high)
        refs[1][where, part, :width] = jnp.where(core == 0, high, low).astype(BF16)
    else:
        refs[0][pl.ds(chunk * shards, shards), part, :width] = value.reshape(shards, rows, width).astype(refs[0].dtype)


def project_body(info, token_ref, *rest, each):
    wa_refs, wb_refs = rest[:each], rest[each : 2 * each]
    cos_ref, sin_ref, h_ref, q_ref, kv_ref, gain_ref = rest[2 * each : 2 * each + 6]
    scr = rest[2 * each + 6 :]
    wa_ref, wb_ref = scr if each > 1 else (wa_refs[0], wb_refs[0])

    @pl.when(pl.program_id(0) == 0)
    def _():
        settle(wa_refs, scr and scr[0], info, False)
        settle(wb_refs, scr and scr[1], info, True)
        lane = lax.broadcasted_iota(jnp.int32, (8, D), 1)
        found = jnp.zeros((8, D), F32)
        for shard in range(SHARDS):
            side = wb_ref[shard, TILE : 2 * TILE, :].astype(F32)[8:]
            side = side if shard == 0 else pltpu.roll(side, TILE * shard, 1)
            found = jnp.where(lane // TILE == shard, side, found)
        gain_ref[...] = found

    token = token_ref[...]
    row = (token // 8) * TILE + token % 8
    hot = (row == lax.broadcasted_iota(jnp.int32, (token.shape[0], D), 1)).astype(BF16)
    values = nn(hot, tile_of(wb_ref, 1))
    h_ref[...] = values.astype(BF16)
    normed = (norm_parts(values)[0] * gain_ref[0:1, :]).astype(BF16)
    cosine, sine = cos_ref[...], sin_ref[...]
    q_ref[...] = (rope(nn(normed, tile_of(wa_ref, 0)), cosine, sine) * 0.125).astype(BF16)
    kv_ref[0] = rope(nn(normed, tile_of(wa_ref, 1)), cosine, sine).astype(BF16)
    kv_ref[1] = nn(normed, tile_of(wb_ref, 0)).astype(BF16)


def project(info, token, bundles, cosine, sine):
    rows = cosine.shape[0]
    step = SPAN
    weights = [*bundles[0], *bundles[1]]
    return call(
        partial(project_body, each=len(bundles[0])),
        "project",
        [shape((rows, D), BF16)] * 2 + [shape((2, rows, D), BF16), shape((8, D))],
        [info, token, *weights, cosine, sine],
        5,
        grid=(rows // step,),
        in_specs=[pl.BlockSpec((step, 1), lambda i, _: (i, 0))]
        + [held(w.shape) for w in weights]
        + [pl.BlockSpec((step, 128), lambda i, _: (i, 0))] * 2,
        out_specs=[pl.BlockSpec((step, D), lambda i, _: (i, 0))] * 2
        + [pl.BlockSpec((2, step, D), lambda i, _: (0, i, 0)), whole((8, D))],
        scratch=bundle_scratch(bundles, (2 * TILE, 2 * TILE)),
    )


def project_short_body(
    info, h_ref, tail_ref, low_ref, high_ref, *rest, ways, each
):
    wa_refs, wb_refs = rest[:each], rest[each : 2 * each]
    gain_ref, cos_ref, sin_ref, z_ref, q_ref, kv_ref, scr = rest[2 * each : 2 * each + 7]
    wa_ref = settle(wa_refs, rest[-2], info, False, 4 * TILE)
    wb_ref = settle(wb_refs, rest[-1], info, True, 5 * TILE)
    for slot in range(2):
        if slot == 0:
            halo = low_ref[...]
        else:
            halo = jnp.where(info[RANK] == ways - 1, tail_ref[0], high_ref[...])
        for piece, lanes in enumerate(LANES):
            scr[slot, piece, :8, :] = halo[:, lanes]
            scr[slot, piece, 8:, :] = h_ref[SPAN * slot : SPAN * slot + SPAN, lanes]
            total = thirds(scr, (slot, piece), 6)
            z_ref[CSPAN * slot : CSPAN * slot + CSPAN, lanes] = total * (1.0 / SHORT)
    normed = (norm_parts(z_ref[...])[0] * gain_ref[2:3, :]).astype(BF16)
    cosine, sine = cos_ref[...], sin_ref[...]
    query = nn(normed[CSPAN:], tile_of(wa_ref, 0))
    q_ref[...] = (rope(query, cosine[CSPAN:], sine[CSPAN:]) * 0.125).astype(BF16)
    kv_ref[0] = rope(nn(normed, tile_of(wa_ref, 1)), cosine, sine).astype(BF16)
    kv_ref[1] = nn(normed, tile_of(wb_ref, 0)).astype(BF16)


def project_short(info, h, tail, low, high, bundles, gains, cosine, sine, ways):
    outs = [shape((2 * CSPAN, D)), shape((CSPAN, D), BF16), shape((2, 2 * CSPAN, D), BF16)]
    ins = [info, h, tail, low, high, *bundles[0], *bundles[1], gains, cosine, sine]
    specs = [held(i.shape) for i in ins[1:]]
    return call(
        partial(project_short_body, ways=ways, each=len(bundles[0])),
        "project_short",
        outs,
        ins,
        0.05,
        in_specs=specs,
        scratch=[pltpu.VMEM((2, D // 128, SPAN + 8, 128), F32)] + bundle_scratch(bundles, (2 * TILE, TILE)),
    )


def order_keys(info, own, other, found, block, count):
    for at in range(count):
        owner = min(at, count - 1 - at)
        place = 0 if owner == at else 1
        part = slice(place * block, place * block + block)
        for kind, keys in enumerate(found):
            keys[at * block : at * block + block, :] = jnp.where(
                info[RANK] == owner, own[kind, part, :], other[kind, part, :]
            )


def each_rows(rows, steps, count):
    if count <= 4:
        for i in range(steps):
            rows(i)
    else:
        lax.fori_loop(0, steps, lambda i, carry: (rows(i), carry)[1], 0)


def each_head(head, together):
    if together == 4:
        for j in range(4):
            head(j)
        return

    def some(i, carry):
        for j in range(together):
            head(i * together + j)
        return carry

    lax.fori_loop(0, 4 // together, some, 0)


def masked_rows(s_scr, part, start, step, block, width):
    score = s_scr[part, :width]
    row = start + lax.broadcasted_iota(jnp.int32, (step, block), 0)
    key = lax.broadcasted_iota(jnp.int32, (step, block), 1)
    edge = jnp.where(row >= key, score[:, width - block :], MASKED)
    return jnp.concatenate([score[:, : width - block], edge], 1) if width > block else edge


def rows_part(i, step):
    return pl.ds(i * step if isinstance(i, int) else pl.multiple_of(i * step, step), step)


def attend_body(info, q_ref, *rest, count, block, step, pair, base):
    if pair:
        own, other, out_ref, lse_ref, s_scr, p_scr, k_ref, v_ref = rest
    else:
        k_ref, v_ref, out_ref, lse_ref, s_scr, p_scr = rest
    slot = pl.program_id(1)
    nk = info[slot + base]
    lane = lax.broadcasted_iota(jnp.int32, (1, 256), 1)
    column = lax.broadcasted_iota(jnp.int32, (step, 128), 1)
    zero = jnp.zeros((), BF16)
    if pair:

        @pl.when(slot == 0)
        def _():
            order_keys(info, own, other, (k_ref, v_ref), block, count)

    def variant(blocks):
        width = blocks * block

        def head(j):
            mine = lane // HD == j
            s_scr[:, :width] = nt(jnp.where(mine, q_ref[...], zero), k_ref[:width, :])

            def rows(i):
                part = rows_part(i, step)
                score = masked_rows(s_scr, part, i * step, step, block, width)
                top = jnp.max(score, -1, keepdims=True)
                raised = jnp.exp(score - top)
                total = jnp.sum(raised, -1, keepdims=True)
                p_scr[part, :width] = (raised * (1.0 / total)).astype(BF16)
                lse_ref[0, 0, part, :] = jnp.where(column == j, top + jnp.log(total), lse_ref[0, 0, part, :])

            each_rows(rows, block // step, count)
            found = nn(p_scr[:, :width], v_ref[:width, :]).astype(BF16)
            out_ref[...] = jnp.where(mine, found, out_ref[...])

        each_head(head, 4 if count <= 4 else 1)

    for blocks in range(1, count + 1):
        pl.when(nk == blocks)(partial(variant, blocks))


def key_spec(key, first):
    lead = key.shape[:-1]
    return pl.BlockSpec((*lead, 256), lambda h, s, _: (0,) * len(lead) + (h + first,))


def attend(info, q, keys, block, first, groups):
    slots = q.shape[0] // block
    pair = keys[0].ndim == 3
    total = keys[0].shape[-2] * (2 if pair else 1)
    count = total // block
    scratch = [pltpu.VMEM((block, total), F32), pltpu.VMEM((block, total), BF16)]
    if pair:
        scratch += [pltpu.VMEM((total, 256), BF16)] * 2
    return call(
        partial(attend_body, count=count, block=block, step=64, pair=pair, base=2 - slots),
        "attend",
        [shape((slots * block, 256 * groups), BF16), shape((groups, slots, block, 128))],
        [info, q, *keys],
        8 if block == SPAN else 0.05,
        grid=(groups, slots),
        in_specs=[pl.BlockSpec((block, 256), lambda h, s, _: (s, h + first))]
        + [key_spec(key, first) for key in keys],
        out_specs=[
            pl.BlockSpec((block, 256), lambda h, s, _: (s, h)),
            pl.BlockSpec((1, 1, block, 128), lambda h, s, _: (h, s, 0, 0)),
        ],
        scratch=scratch,
    )


def attend_back_body(info, q_ref, *rest, count, block, step, pair, base):
    if pair:
        own, other, back_ref, lse_ref, dq_ref, keep_ref, send_ref = rest[:7]
        s_scr, dp_scr, p_scr, ds_scr, dk_scr, dv_scr, qt_scr, bt_scr, k_ref, v_ref = rest[7:]
    else:
        k_ref, v_ref, back_ref, lse_ref, dq_ref, keep_ref = rest[:6]
        s_scr, dp_scr, p_scr, ds_scr, dk_scr, dv_scr, qt_scr, bt_scr = rest[6:]
    slot = pl.program_id(1)
    nk = info[slot + base]
    lane = lax.broadcasted_iota(jnp.int32, (1, 256), 1)
    column = lax.broadcasted_iota(jnp.int32, (step, 128), 1)
    zero = jnp.zeros((), BF16)

    qt_scr[...] = q_ref[...].T
    bt_scr[...] = back_ref[...].T

    @pl.when(slot == 0)
    def _():
        dk_scr[...] = jnp.zeros_like(dk_scr)
        dv_scr[...] = jnp.zeros_like(dv_scr)
        if pair:
            order_keys(info, own, other, (k_ref, v_ref), block, count)

    def variant(blocks):
        width = blocks * block

        def head(j):
            mine = lane // HD == j
            s_scr[:, :width] = nt(jnp.where(mine, q_ref[...], zero), k_ref[:width, :])
            dp_scr[:, :width] = nt(jnp.where(mine, back_ref[...], zero), v_ref[:width, :])

            def rows(i):
                part = rows_part(i, step)
                score = masked_rows(s_scr, part, i * step, step, block, width)
                lse = jnp.sum(jnp.where(column == j, lse_ref[0, 0, part, :], 0.0), -1, keepdims=True)
                prob = jnp.exp(score - lse)
                p_scr[part, :width] = prob.astype(BF16)
                prob_back = dp_scr[part, :width]
                delta = jnp.sum(prob * prob_back, -1, keepdims=True)
                ds_scr[part, :width] = (prob * (prob_back - delta)).astype(BF16)

            each_rows(rows, block // step, count)
            found = nn(ds_scr[:, :width], k_ref[:width, :])
            dq_ref[...] = jnp.where(mine, found, dq_ref[...])
            mine_rows = pl.ds(HD * j if isinstance(j, int) else pl.multiple_of(HD * j, HD), HD)
            dk_scr[mine_rows, :width] += nn(qt_scr[mine_rows, :], ds_scr[:, :width])
            dv_scr[mine_rows, :width] += nn(bt_scr[mine_rows, :], p_scr[:, :width])

        each_head(head, 2 if count <= 4 else 1)

    for blocks in range(1, count + 1):
        pl.when(nk == blocks)(partial(variant, blocks))

    @pl.when(slot == pl.num_programs(1) - 1)
    def _():
        for kind, scr in enumerate((dk_scr, dv_scr)):
            for place in range(2):
                to = slice(place * block, place * block + block)

                def from_owner(owner):
                    at = owner if place == 0 else count - 1 - owner
                    return scr[:, at * block : at * block + block]

                if pair:
                    low, high = from_owner(0), from_owner(1)
                    keep_ref[kind, :, to] = jnp.where(info[RANK] == 0, low, high)
                    send_ref[kind, :, to] = jnp.where(info[RANK] == 0, high, low).astype(BF16)
                else:
                    for owner in range(count // 2):
                        keep_ref[owner, kind, :, to] = from_owner(owner)


def attend_back(info, q, keys, back, lse, block, first, groups):
    slots = q.shape[0] // block
    pair = keys[0].ndim == 3
    total = keys[0].shape[-2] * (2 if pair else 1)
    count = total // block
    outs = [shape((slots * block, 256 * groups))]
    out_specs = [pl.BlockSpec((block, 256), lambda h, s, _: (s, h))]
    if pair:
        outs += [shape((2, 256 * groups, 2 * block)), shape((2, 256 * groups, 2 * block), BF16)]
        out_specs += [pl.BlockSpec((2, 256, 2 * block), lambda h, s, _: (0, h, 0))] * 2
    else:
        outs += [shape((count // 2, 2, 256 * groups, 2 * block))]
        out_specs += [pl.BlockSpec((count // 2, 2, 256, 2 * block), lambda h, s, _: (0, 0, h, 0))]
    scratch = [
        pltpu.VMEM((block, total), F32),
        pltpu.VMEM((block, total), F32),
        pltpu.VMEM((block, total), BF16),
        pltpu.VMEM((block, total), BF16),
        pltpu.VMEM((256, total), F32),
        pltpu.VMEM((256, total), F32),
        pltpu.VMEM((256, block), BF16),
        pltpu.VMEM((256, block), BF16),
    ]
    if pair:
        scratch += [pltpu.VMEM((total, 256), BF16)] * 2
    return call(
        partial(attend_back_body, count=count, block=block, step=64, pair=pair, base=2 - slots),
        "attend_back",
        outs,
        [info, q, *keys, back, lse],
        13 if block == SPAN else 7,
        grid=(groups, slots),
        in_specs=[pl.BlockSpec((block, 256), lambda h, s, _: (s, h + first))]
        + [key_spec(key, first) for key in keys]
        + [
            pl.BlockSpec((block, 256), lambda h, s, _: (s, h)),
            pl.BlockSpec((1, 1, block, 128), lambda h, s, _: (h, s, 0, 0)),
        ],
        out_specs=out_specs,
        scratch=scratch,
    )


def branch_body(info, x_ref, a0_ref, a1_ref, *rest, each):
    up_refs, down_refs = rest[:each], rest[each : 2 * each]
    gain_ref, mid_ref, res_ref, tail_ref = rest[2 * each : 2 * each + 4]
    scr = rest[2 * each + 4 :]
    up_w, down_w = scr if each > 1 else (up_refs[0], down_refs[0])

    @pl.when(pl.program_id(0) == 0)
    def _():
        settle(up_refs, scr and scr[0], info, False)
        settle(down_refs, scr and scr[1], info, True)

    out_tile = tile_of(down_w, 4)
    middle = x_ref[...].astype(F32) + nn(a0_ref[...], out_tile[:256]) + nn(a1_ref[...], out_tile[256:])
    mid_ref[...] = middle
    normed = (norm_parts(middle)[0] * gain_ref[1:2, :]).astype(BF16)
    total = mid_ref[...]
    for chunk in range(FF // D):
        up = nn(normed, tile_of(up_w, chunk))
        hidden = (up * gelu_parts(up)[1]).astype(BF16)
        total = total + nn(hidden, down_w[8 * chunk : 8 * chunk + 8, : 4 * TILE, :].reshape(D, D))
    res_ref[...] = total
    tail_ref[0] = total[total.shape[0] - 8 :]


def branch(info, x, parts, bundles, gains):
    rows = x.shape[0]
    row = lambda width: pl.BlockSpec((SPAN, width), lambda i, _: (i, 0))
    weights = [*bundles[0], *bundles[1]]
    return call(
        partial(branch_body, each=len(bundles[0])),
        "branch",
        [shape((rows, D)), shape((rows, D)), shape((2, 8, D))],
        [info, x, *parts, *weights, gains],
        9,
        grid=(rows // SPAN,),
        in_specs=[row(D), row(256), row(256), *[held(w.shape) for w in weights], held(gains.shape)],
        out_specs=[row(D), row(D), pl.BlockSpec((1, 8, D), lambda i, _: (i, 0, 0))],
        scratch=bundle_scratch(bundles, (4 * TILE, 5 * TILE)),
    )


def branch_back_body(info, dz_ref, edge_ref, high_ref, low_ref, dh_ref, mid_ref, a0_ref, a1_ref, *rest, ways, split):
    each = 2 if split else 1
    parts = WEIGHT_PARTS if split else 1
    uw_refs, dw_refs, gain_ref = rest[:parts], rest[parts : 2 * parts], rest[2 * parts]
    rest = rest[2 * parts + 1 :]
    dmid_ref, da0_ref, da1_ref, dgain_ref = rest[:4]
    up_refs, down_refs = rest[4 : 4 + each], rest[4 + each : 4 + 2 * each]
    norm_scr, normt_scr, cot_scr, cotb_scr, acc_scr, pool_scr = rest[4 + 2 * each : 10 + 2 * each]
    w_scr = rest[10 + 2 * each :]
    up_w, down_w = w_scr if split else (uw_refs[0], dw_refs[0])
    chunk = pl.program_id(0)
    core = info[CORE]

    @pl.when(chunk == 0)
    def _():
        settle(uw_refs, w_scr and w_scr[0], info, False)
        settle(dw_refs, w_scr and w_scr[1], info, True)
        for slot in range(2):
            if slot == 0:
                edge = jnp.where(info[RANK] == ways - 1, edge_ref[1], high_ref[...])
            else:
                edge = low_ref[...]
            for piece, lanes in enumerate(LANES):
                spread(pool_scr, (slot, piece), dz_ref[CSPAN * slot : CSPAN * slot + CSPAN, lanes] * (1.0 / SHORT))
                pool_scr[slot, piece, SPAN:, :] = jnp.broadcast_to(edge[0:1, lanes] * (1.0 / SHORT), (8, 128))
                found = pool_scr[slot, piece, 2 : SPAN + 2, :]
                if slot == 1:
                    found = found + dh_ref[:, lanes]
                cot_scr[SPAN * slot : SPAN * slot + SPAN, lanes] = found
        cotb_scr[...] = cot_scr[...].astype(BF16)
        normed = (norm_parts(mid_ref[...])[0] * gain_ref[1:2, :]).astype(BF16)
        norm_scr[...] = normed
        normt_scr[...] = normed.T
        acc_scr[...] = jnp.zeros_like(acc_scr)

    down_in = cotb_scr[...]
    up_tile = up_w[:, pl.ds(pl.multiple_of(chunk * TILE, TILE), TILE), :].reshape(D, D)
    down_tile = down_w[pl.ds(chunk * 8, 8), : 4 * TILE, :].reshape(D, D)
    up = nn(norm_scr[...], up_tile)
    wave, gate = gelu_parts(up)
    hidden = (up * gate).astype(BF16)
    up_in = (nt(down_in, down_tile) * gelu_slope(up, wave, gate)).astype(BF16)
    put(down_refs, core, nn(hidden.T, down_in), rows=4 * TILE, chunk=chunk)
    put(up_refs, core, nn(normt_scr[...], up_in))
    acc_scr[...] += nt(up_in, up_tile)

    @pl.when(chunk == FF // D - 1)
    def _():
        hat, scale = norm_parts(mid_ref[...])
        pulled, dgain = norm_pull(hat, scale, gain_ref[1:2, :], acc_scr[...])
        dgain_ref[...] = dgain
        dmid = cot_scr[...] + pulled
        dmid_ref[...] = dmid
        out_in = dmid.astype(BF16)
        out_tile = tile_of(down_w, 4)
        put(down_refs, core, jnp.concatenate([nn(a0_ref[...].T, out_in), nn(a1_ref[...].T, out_in)], 0), at=4 * TILE)
        da0_ref[...] = nt(out_in, out_tile[:256]).astype(BF16)
        da1_ref[...] = nt(out_in, out_tile[256:]).astype(BF16)


def branch_back(info, dz, edge, high, low, dh, mid, parts, bundles, gains, ways, split):
    rows = mid.shape[0]
    ins = [info, dz, edge, high, low, dh, mid, *parts, *bundles[0], *bundles[1], gains]
    specs = [held(i.shape) for i in ins[1:]]
    return call(
        partial(branch_back_body, ways=ways, split=split),
        "branch_back",
        [shape((rows, D)), shape((rows, 256), BF16), shape((rows, 256), BF16), shape((1, D))]
        + grad_shapes(4 * TILE, split)
        + grad_shapes(5 * TILE, split),
        ins,
        18,
        grid=(FF // D,),
        in_specs=specs,
        out_specs=[whole((rows, D)), whole((rows, 256)), whole((rows, 256)), whole((1, D))]
        + grad_specs(TILE, split, lambda i, _: (0, i, 0))
        + grad_specs(5 * TILE, split, lambda i, _: (0, 0, 0)),
        scratch=[
            pltpu.VMEM((rows, D), BF16),
            pltpu.VMEM((D, rows), BF16),
            pltpu.VMEM((rows, D), F32),
            pltpu.VMEM((rows, D), BF16),
            pltpu.VMEM((rows, D), F32),
            pltpu.VMEM((2, D // 128, SPAN + 8, 128), F32),
            *bundle_scratch(bundles, (4 * TILE, 5 * TILE)),
        ],
    )


def short_body(info, x_ref, a_ref, h_ref, *rest, split):
    each = 2 if split else 1
    parts = WEIGHT_PARTS if split else 1
    uw_refs, dw_refs = rest[:parts], rest[parts : 2 * parts]
    gain_ref, target_ref, counted_ref, rate_ref = rest[2 * parts : 2 * parts + 4]
    rest = rest[2 * parts + 4 :]
    loss_ref, dg4_ref, dg3_ref, dh_ref, dmid_ref, da_ref = rest[:6]
    up_refs, down_refs, head_refs = [rest[6 + each * i : 6 + each * i + each] for i in range(3)]
    mid_scr, norm_scr, normt_scr, cot_scr, acc_scr, up_scr = rest[6 + 3 * each : 12 + 3 * each]
    w_scr = rest[12 + 3 * each :]
    up_w, down_w = w_scr if split else (uw_refs[0], dw_refs[0])
    down_rows = slice(0, 4 * TILE)
    step = pl.program_id(0)
    core = info[CORE]

    @pl.when(step == 0)
    def _():
        settle(uw_refs, w_scr and w_scr[0], info, False)
        settle(dw_refs, w_scr and w_scr[1], info, True)
        middle = x_ref[...] + nn(a_ref[...], tile_of(up_w, 4))
        mid_scr[...] = middle
        normed = (norm_parts(middle)[0] * gain_ref[3:4, :]).astype(BF16)
        norm_scr[...] = normed
        normt_scr[...] = normed.T
        total = mid_scr[...]
        for chunk in range(FF // D):
            up = nn(normed, tile_of(up_w, chunk))
            hidden = (up * gelu_parts(up)[1]).astype(BF16)
            total = total + nn(hidden, down_w[8 * chunk : 8 * chunk + 8, down_rows, :].reshape(D, D))
        for piece, lanes in enumerate(LANES):
            spread(up_scr, (piece,), total[:, lanes])
        gain = gain_ref[4:5, :]
        hat, scale = norm_parts(h_ref[...] + jnp.concatenate([up_scr[piece] for piece in range(len(LANES))], 1))
        final = (hat * gain).astype(BF16)
        head = tile_of(down_w, 4)[:, :VOCAB]
        logits = nn(final, head)
        top = jnp.max(logits, -1, keepdims=True)
        log_total = top + jnp.log(jnp.sum(jnp.exp(logits - top), -1, keepdims=True))
        hot = target_ref[...] == lax.broadcasted_iota(jnp.int32, logits.shape, 1)
        picked = jnp.sum(jnp.where(hot, logits, 0.0), -1, keepdims=True)
        counted = counted_ref[...]
        loss = jnp.sum((log_total - picked) * counted, 0, keepdims=True) * (1.0 / LOG_TWO)
        loss_ref[...] = jnp.broadcast_to(loss, (1, 128))
        grad = ((jnp.exp(logits - log_total) - jnp.where(hot, 1.0, 0.0)) * (counted * rate_ref[0, 0])).astype(BF16)
        dhead = nn(final.T, grad)
        put(head_refs, core, jnp.concatenate([dhead, jnp.zeros((D, D - VOCAB), F32)], 1))
        pulled, dgain = norm_pull(hat, scale, gain, nt(grad, head))
        dg4_ref[...] = dgain
        dh_ref[...] = pulled
        for piece, lanes in enumerate(LANES):
            up_scr[piece] = pulled[:, lanes]
            cot_scr[:, lanes] = thirds(up_scr, (piece,), 0)
        acc_scr[...] = jnp.zeros_like(acc_scr)

    @pl.when(step > 0)
    def _():
        chunk = step - 1
        down_in = cot_scr[...].astype(BF16)
        up_tile = up_w[:, pl.ds(pl.multiple_of(chunk * TILE, TILE), TILE), :].reshape(D, D)
        up = nn(norm_scr[...], up_tile)
        wave, gate = gelu_parts(up)
        hidden = (up * gate).astype(BF16)
        up_in = (nt(down_in, down_w[pl.ds(chunk * 8, 8), down_rows, :].reshape(D, D)) * gelu_slope(up, wave, gate)).astype(BF16)
        put(down_refs, core, nn(hidden.T, down_in), rows=4 * TILE, chunk=chunk)
        put(up_refs, core, nn(normt_scr[...], up_in))
        acc_scr[...] += nt(up_in, up_tile)

    @pl.when(step == FF // D)
    def _():
        hat, scale = norm_parts(mid_scr[...])
        pulled, dgain = norm_pull(hat, scale, gain_ref[3:4, :], acc_scr[...])
        dg3_ref[...] = dgain
        dmid = cot_scr[...] + pulled
        dmid_ref[...] = dmid
        out_in = dmid.astype(BF16)
        put(down_refs, core, nn(a_ref[...].T, out_in), at=4 * TILE)
        da_ref[...] = nt(out_in, tile_of(up_w, 4)).astype(BF16)


def short_rest(info, z, a, h, bundles, gains, target, counted, rate, split):
    ins = [info, z, a, h, *bundles[0], *bundles[1], gains, target, counted, rate]
    specs = [held(i.shape) for i in ins[1:]]
    specs[0] = pl.BlockSpec((CSPAN, D), lambda *_: (1, 0))
    specs[2] = pl.BlockSpec((SPAN, D), lambda *_: (1, 0))
    specs[-1] = pl.BlockSpec(memory_space=pltpu.SMEM)
    return call(
        partial(short_body, split=split),
        "short_rest",
        [shape((1, 128)), shape((1, D)), shape((1, D)), shape((SPAN, D)), shape((CSPAN, D)), shape((CSPAN, D), BF16)]
        + grad_shapes(4 * TILE, split)
        + grad_shapes(5 * TILE, split)
        + grad_shapes(TILE, split),
        ins,
        12,
        grid=(FF // D + 1,),
        in_specs=specs,
        out_specs=[whole((1, 128)), whole((1, D)), whole((1, D)), whole((SPAN, D)), whole((CSPAN, D)), whole((CSPAN, D))]
        + grad_specs(TILE, split, lambda i, _: (0, jnp.maximum(i - 1, 0), 0))
        + grad_specs(5 * TILE, split, lambda i, _: (0, 0, 0))
        + grad_specs(TILE, split, lambda i, _: (0, 0, 0)),
        scratch=[
            pltpu.VMEM((CSPAN, D), F32),
            pltpu.VMEM((CSPAN, D), BF16),
            pltpu.VMEM((D, CSPAN), BF16),
            pltpu.VMEM((CSPAN, D), F32),
            pltpu.VMEM((CSPAN, D), F32),
            pltpu.VMEM((D // 128, SPAN, 128), F32),
            *bundle_scratch(bundles, (5 * TILE, 5 * TILE)),
        ],
    )


def project_back_body(info, *refs, full, split, groups):
    refs = list(refs)
    take = lambda n: [refs.pop(0) for _ in range(n)]
    dqs, keeps, recvs = take(groups), take(groups), take(groups)
    dmid_ref, x_ref = take(2)
    if full:
        (token_ref,) = take(1)
        wa_refs, wb_refs = [take(WEIGHT_PARTS if split else 1) for _ in range(2)]
        dg_refs = take(4)
    else:
        wa_refs, wb_refs = [take(WEIGHT_PARTS if split else 1) for _ in range(2)]
    wa_ref = settle(wa_refs, refs[-2], info, False, 0 if full else 4 * TILE)
    wb_ref = settle(wb_refs, refs[-1], info, True, 0 if full else 5 * TILE)
    weight = [tile_of(wa_ref, 0), tile_of(wa_ref, 1), tile_of(wb_ref, 0)]
    gain_ref, cos_ref, sin_ref = take(3)
    each = 2 if split else 1
    first_refs = take(each)
    if full:
        second_refs = take(each)
    if not full or not split:
        dgain_ref, dx_ref = take(2)
    if not full:
        (edge_ref,) = take(1)
    core = info[CORE]
    gain = gain_ref[0:1, :] if full else gain_ref[2:3, :]
    hat, scale = norm_parts(x_ref[...].astype(F32))
    normed_t = (hat * gain).astype(BF16).T
    cosine, sine = cos_ref[...], sin_ref[...]
    rows = hat.shape[0]
    skip = rows - dqs[0].shape[0]
    total = jnp.zeros((rows, D), F32)
    for kind in range(3):
        if kind == 0:
            grad = jnp.concatenate([dq[...] for dq in dqs], 1) if groups > 1 else dqs[0][...]
            grad = rope_pull(grad * 0.125, cosine[skip:], sine[skip:]).astype(BF16)
            found = nn(normed_t[:, skip:], grad)
        else:
            both = [(keep[kind - 1] + recv[kind - 1].astype(F32)).T for keep, recv in zip(keeps, recvs)]
            grad = jnp.concatenate(both, 1) if groups > 1 else both[0]
            grad = (rope_pull(grad, cosine, sine) if kind == 1 else grad).astype(BF16)
            found = nn(normed_t, grad)
        if full and kind == 2:
            put(second_refs, core, found)
        else:
            put(first_refs, core, found, at=TILE * kind)
        back = nt(grad, weight[kind])
        if kind == 0 and skip:
            back = jnp.concatenate([jnp.zeros((skip, D), F32), back], 0)
        total = total + back
    pulled, dgain = norm_pull(hat, scale, gain, total)
    if not full:
        dgain_ref[...] = dgain
        dx = jnp.concatenate([pulled[:skip], dmid_ref[...] + pulled[skip:]], 0)
        dx_ref[...] = dx
        for slot in range(2):
            edge_ref[slot] = dx[CSPAN * slot : CSPAN * slot + 8]
        return
    back = (dmid_ref[...] + pulled).astype(BF16)
    hot = (token_ref[...] == lax.broadcasted_iota(jnp.int32, (VOCAB, rows), 0)).astype(BF16)
    dembed = nn(hot, back)
    if not split:
        dgain_ref[...] = dgain
        dx_ref[...] = dembed
        return
    dgains = jnp.concatenate([dgain] + [ref[...] for ref in dg_refs] + [jnp.zeros((3, D), F32)], 0)
    lane = lax.broadcasted_iota(jnp.int32, (8, D), 1)
    sides = [
        jnp.where(lane < TILE, dgains if j == 0 else pltpu.roll(dgains, D - TILE * j, 1), 0.0) for j in range(SHARDS)
    ]
    embeds = dembed.reshape(SHARDS, 8, D)
    for chip in range(SHARDS // 2):
        for part, values in ((slice(TILE, TILE + 8), embeds), (slice(TILE + 8, 2 * TILE), sides)):
            low, high = values[2 * chip], values[2 * chip + 1]
            second_refs[0][chip, part, :] = jnp.where(core == 0, low, high)
    second_refs[1][:, TILE:, :] = jnp.stack(
        [
            jnp.where(
                core == 0,
                jnp.concatenate([embeds[2 * chip + 1], sides[2 * chip + 1]], 0),
                jnp.concatenate([embeds[2 * chip], sides[2 * chip]], 0),
            ).astype(BF16)
            for chip in range(SHARDS // 2)
        ],
        0,
    )


def project_back(info, dqs, keeps, recvs, dmid, x, extra, bundles, dgs, gains, cosine, sine, full, split):
    groups = len(dqs)
    rows = cosine.shape[0]
    weights = [value for bundle in bundles for value in bundle]
    ins = [info, *dqs, *keeps, *recvs, dmid, x, *extra, *weights, *dgs, gains, cosine, sine]
    specs = [held(i.shape) for i in ins[1:]]
    scratch = bundle_scratch(bundles, (2 * TILE, TILE))
    if full:
        outs = grad_shapes(2 * TILE, split)
        outs += grad_shapes(2 * TILE if split else TILE, split)
        if not split:
            outs += [shape((1, D)), shape((VOCAB, D))]
    else:
        outs = grad_shapes(3 * TILE, split) + [shape((1, D)), shape((rows, D)), shape((2, 8, D))]
    return call(
        partial(project_back_body, full=full, split=split, groups=groups),
        "project_back",
        outs,
        ins,
        10 if full else 5,
        in_specs=specs,
        scratch=scratch,
    )


def fold_body(info, *refs, layout):
    refs = list(refs)
    outs = refs[4 * sum(len(rows) for rows in layout) :]
    for order, rows in enumerate(layout):
        at = 0
        for count in rows:
            keep, far, recv, far_recv = [refs.pop(0) for _ in range(4)]
            lead = outs[2 * order].shape[0]
            part = slice(at, at + count)
            flat = lambda ref: ref[...].reshape(lead, count, D)
            outs[2 * order][:, part, :] = flat(keep) + flat(recv).astype(F32)
            outs[2 * order + 1][:, part, :] = (flat(far) + flat(far_recv).astype(F32)).astype(BF16)
            at += count


def fold(info, orders, steps, us):
    ins, specs, outs, out_specs, layout = [info], [], [], [], []
    for sources, pre, post, bit in orders:
        layout.append([keep.shape[-2] for keep, _ in sources])
        for keep, recv in sources:
            dims = (pre, 2, post, keep.shape[-2], D)
            for value in (keep, recv):
                for other in (0, 1):
                    ins.append(value.reshape(dims))
                    inner = max(steps // pre, 1)
                    specs.append(
                        pl.BlockSpec(
                            (max(pre // steps, 1), 1, post // inner, keep.shape[-2], D),
                            lambda i, info, other=other, bit=bit, inner=inner: (
                                i // inner, jnp.abs(info[BITS + bit] - other), i % inner, 0, 0
                            ),
                        )
                    )
        total = sum(layout[-1])
        for kind in (F32, BF16):
            outs.append(shape((pre * post, total, D), kind))
            out_specs.append(pl.BlockSpec((pre * post // steps, total, D), lambda i, _: (i, 0, 0)))
    found = call(
        partial(fold_body, layout=layout), "fold", outs, ins, us, grid=(steps,), in_specs=specs, out_specs=out_specs
    )
    return [(found[2 * i], found[2 * i + 1]) for i in range(len(orders))]


CORE_BIT, Y_BIT, X_BIT, Z0_BIT, Z1_BIT = range(5)


class Scatter:
    def __init__(self, info, firsts, seconds):
        self.info = info
        self.values = [
            [(keep, swapped(send, CORE_BIT)) for keep, send in sources] for sources in (firsts, seconds)
        ]
        self.stage = 0

    def plan(self):
        first, second, steps = (
            ((X_BIT, 4, 2), (Y_BIT, 8, 1), 8),
            ((Y_BIT, 4, 1), (X_BIT, 4, 1), 4),
            ((Z0_BIT, 2, 1), None, 2),
            ((Z1_BIT, 1, 1), None, 1),
        )[self.stage]
        if second is None:
            self.values = [[pair for sources in self.values for pair in sources]]
        plans = [plan for plan in (first, second) if plan]
        orders = [(sources, pre, post, bit) for sources, (bit, pre, post) in zip(self.values, plans)]
        return orders, steps

    def folded(self, found, bits):
        self.values = [[(keep, swapped(send, bit))] for (keep, send), bit in zip(found, bits)]
        self.stage += 1

    def joined(self, other):
        found = Scatter(self.info, [], [])
        found.values = [mine + more for mine, more in zip(self.values, other.values)]
        found.stage = self.stage
        return found

    def kept(self):
        return [keep for sources in self.values for keep, _ in sources]

    def result(self):
        return [keep.reshape(-1, D) + recv.reshape(-1, D).astype(F32) for ((keep, recv),) in self.values]


def step_all(info, *needed):
    def step(*scatters):
        plans = [scatter.plan() for scatter in scatters]
        orders = [order for plan, _ in plans for order in plan]
        found = fold(after(info, needed) if needed else info, orders, min(steps for _, steps in plans), 0.05)
        for scatter, (plan, _) in zip(scatters, plans):
            scatter.folded([found.pop(0) for _ in plan], [bit for *_, bit in plan])

    return step


def after(value, *needed):
    leaves = jax.tree.leaves(needed)
    return lax.optimization_barrier((value, *leaves))[0]


DECAY = 1.0 - STEP ** (-0.8)
MATRICES = (
    [(VOCAB, 1, D), (D, 1, VOCAB)] + [(D, 3, 3 * D)] * 2 + [(D, 1, D)] * 2 + [(D, 4, FF)] * 2 + [(FF, 1, D)] * 2
)
TILES = sum(count for _, count, _ in MATRICES)
STAT_ROWS = 48


def as_column(row):
    return jnp.broadcast_to(row, (128, row.shape[1])).T[:, 0:1]


def as_row(column):
    return jnp.broadcast_to(column, (column.shape[0], 128)).T[0:1, :]


def tile_lanes(width, index):
    return slice(D * index, min(D * index + D, width))


def measure_body(info, *refs):
    refs = list(refs)
    take = lambda n: [refs.pop(0) for _ in range(n)]
    both, early = [keep[0] + recv[0].astype(F32) for keep, recv in [take(2) for _ in range(2)]]
    row_refs, weight_refs = take(6), take(6)
    gain_ref, sq_ref, loss_ref = take(3)
    grad_refs, new_row_refs = take(6), take(6)
    gain_grad_ref, new_sq_ref, stat_ref = take(3)
    both_a, both_b, early_a, early_b = both[: 11 * TILE], both[11 * TILE :], early[: 2 * TILE], early[2 * TILE :]
    cut = lambda value, start, count=1, size=TILE: [value[start + size * i : start + size * i + size] for i in range(count)]
    grads = [
        [early_b[TILE : TILE + 8]],
        [both_b[10 * TILE :, :VOCAB]],
        cut(early_a, 0, 2) + cut(early_b, 0),
        cut(both_a, 8 * TILE, 3),
        cut(both_b, 9 * TILE),
        cut(both_b, 4 * TILE),
        cut(both_a, 4 * TILE, 4),
        cut(both_a, 0, 4),
        cut(both_b, 5 * TILE, size=4 * TILE),
        cut(both_b, 0, size=4 * TILE),
    ]
    lane = lax.broadcasted_iota(jnp.int32, (1, D), 1)
    scalars = jnp.where(lane == 30, loss_ref[0:1, 0:1], 0.0)
    total = lambda value: jnp.sum(jnp.sum(value, 1, keepdims=True), 0, keepdims=True)
    stat_ref[...] = jnp.zeros_like(stat_ref)
    at = 0
    for index, (pieces, (_, _, width)) in enumerate(zip(grads, MATRICES)):
        kind, layer = (index, None) if index < 2 else (2 + (index - 2) // 2, index % 2)
        old = row_refs[kind][...] if layer is None else row_refs[kind][layer : layer + 1, :]
        weight = weight_refs[kind][...] if layer is None else weight_refs[kind][layer]
        squares = [piece * piece for piece in pieces]
        mean = sum(jnp.sum(square, 1, keepdims=True) for square in squares) * (1.0 / width)
        new_row = DECAY * as_column(old) + (1.0 - DECAY) * mean
        inverse = 1.0 / new_row
        new_rows = as_row(new_row)
        if layer is None:
            new_row_refs[kind][...] = new_rows
        else:
            new_row_refs[kind][layer : layer + 1, :] = new_rows
        for place, (piece, square) in enumerate(zip(pieces, squares)):
            lanes = tile_lanes(width, place)
            if layer is None:
                grad_refs[kind][:, lanes] = piece
            else:
                grad_refs[kind][layer, :, lanes] = piece
            own = slice(0, piece.shape[1])
            stat_ref[at : at + 1, own] = jnp.sum(square, 0, keepdims=True)
            stat_ref[TILES + at : TILES + at + 1, own] = jnp.sum(square * inverse, 0, keepdims=True)
            at += 1
        scalars = jnp.where(lane == 2 * index, total(new_row), scalars)
        scalars = jnp.where(lane == 2 * index + 1, total(weight * weight), scalars)
    gain_grad = early_b[TILE + 8 : TILE + 13, :TILE]
    gain_grad_ref[...] = gain_grad
    new_sq = DECAY * sq_ref[...] + (1.0 - DECAY) * gain_grad * gain_grad
    new_sq_ref[...] = new_sq
    gains = gain_ref[...]
    update = gain_grad / jnp.sqrt(new_sq)
    for value, start in ((update, 20), (gains, 25)):
        each = jnp.sum(value * value, 1, keepdims=True)
        for row in range(5):
            scalars = jnp.where(lane == start + row, each[row : row + 1], scalars)
    stat_ref[2 * TILES : 2 * TILES + 1, :] = scalars


def update_body(info, *refs):
    refs = list(refs)
    take = lambda n: [refs.pop(0) for _ in range(n)]
    (stat_ref,) = take(1)
    grad_refs, row_refs, col_refs, weight_refs = take(6), take(6), take(6), take(6)
    gain_ref, gain_grad_ref, sq_ref = take(3)
    new_col_refs, new_refs = take(6), take(6)
    gain_new_ref, loss_ref = take(2)
    scalars = stat_ref[2 * TILES : 2 * TILES + 1, :]
    scalar = lambda lane: scalars[:, lane : lane + 1]
    loss_ref[...] = scalar(30)
    at = 0
    for index, (rows, count, width) in enumerate(MATRICES):
        kind, layer = (index, None) if index < 2 else (2 + (index - 2) // 2, index % 2)
        mean_row = scalar(2 * index) * (1.0 / rows)
        size = rows * width
        new_row = as_column(row_refs[kind][...] if layer is None else row_refs[kind][layer : layer + 1, :])
        pieces, spread_sum = [], jnp.zeros((1, 1), F32)
        for place in range(count):
            lanes = tile_lanes(width, place)
            own = slice(0, lanes.stop - lanes.start)
            here = slice(0, 1) if layer is None else slice(layer, layer + 1)
            new_col = DECAY * col_refs[kind][here, lanes] + (1.0 - DECAY) * stat_ref[at : at + 1, own] * (1.0 / rows)
            new_col_refs[kind][here, lanes] = new_col
            spread_sum = spread_sum + jnp.sum(stat_ref[TILES + at : TILES + at + 1, own] / new_col, 1, keepdims=True)
            pieces.append((lanes, new_col))
            at += 1
        update_sum = mean_row * spread_sum
        rate = RATE_SCALE * jnp.sqrt(scalar(2 * index + 1) * (1.0 / size))
        rate = rate / jnp.maximum(1.0, jnp.sqrt(update_sum * (1.0 / size)))
        for lanes, new_col in pieces:
            if layer is None:
                grad, weight = grad_refs[kind][:, lanes], weight_refs[kind][:, lanes]
            else:
                grad, weight = grad_refs[kind][layer, :, lanes], weight_refs[kind][layer, :, lanes]
            found = weight - rate * (grad / jnp.sqrt(new_row * new_col / mean_row))
            if layer is None:
                new_refs[kind][:, lanes] = found
            else:
                new_refs[kind][layer, :, lanes] = found
    gains, gain_grad = gain_ref[...], gain_grad_ref[...]
    update = gain_grad / jnp.sqrt(sq_ref[...])
    for row in range(5):
        here = slice(row, row + 1)
        rate = RATE_SCALE * jnp.sqrt(scalar(25 + row) * (1.0 / D)) / jnp.maximum(1.0, jnp.sqrt(scalar(20 + row) * (1.0 / D)))
        gain_new_ref[here, :] = gains[here] - rate * update[here]


def optimize(info, sums, rows, cols, weights, gains, gains_sq, loss):
    flat = lambda values: [value[None] if value.ndim == 1 else value for value in values]
    rows, cols = flat(rows), flat(cols)
    same = lambda values: [shape(value.shape) for value in values]
    found = call(
        measure_body,
        "measure",
        same(weights) + same(rows) + [shape(gains.shape), shape(gains.shape), shape((STAT_ROWS, D))],
        [info, *[value for pair in sums for value in pair], *rows, *weights, gains, gains_sq, loss],
        0.05,
    )
    grads, new_rows, (gain_grad, new_sq, stats) = found[:6], found[6:12], found[12:]
    stats = sum_all(stats)
    found = call(
        update_body,
        "update",
        same(cols) + same(weights) + [shape(gains.shape), shape((1, 1))],
        [info, stats, *grads, *new_rows, *cols, *weights, gains, gain_grad, new_sq],
        0.05,
    )
    new_cols, new_weights, (gains_new, loss_sum) = found[:6], found[6:12], found[12:]
    outputs = []
    for index in range(6):
        plain = (lambda value: value[0]) if index < 2 else (lambda value: value)
        outputs += [grads[index], plain(new_rows[index]), plain(new_cols[index]), new_weights[index]]
    return [loss_sum[0, 0]], outputs + [gain_grad, new_sq, gains_new]


def flat_index():
    return lax.axis_index("dp") * lax.axis_size("seq") + lax.axis_index("seq")


def flat_count():
    return lax.axis_size("dp") * lax.axis_size("seq")


def swapped(value, bit):
    return lax.ppermute(value, BOTH, [(i, i ^ (1 << bit)) for i in range(flat_count())])


def bit_of(bit):
    return (flat_index() >> bit) & 1


def join_body(info, *refs):
    count = len(refs) // 3
    for index, out in enumerate(refs[2 * count :]):
        here, there = refs[2 * index : 2 * index + 2]
        rows = here.shape[0]
        out[:rows] = here[...]
        out[rows:] = there[...]


def join_pairs(info, pairs):
    outs = [shape((2 * here.shape[0], *here.shape[1:]), here.dtype) for here, _ in pairs]
    return call(join_body, "join", outs, [info, *[value for pair in pairs for value in pair]], 0.05)


class Gather:
    def __init__(self, packed):
        self.values = [packed[None]]
        self.near = None
        self.info = jnp.zeros((1,), jnp.int32)

    def send(self, *bits, needed=()):
        if needed:
            self.values = [after(value, *needed) for value in self.values]
        self.coming = [swapped(value, bit) for value, bit in zip(self.values, bits)]
        return self

    def pairs(self, needed):
        pairs = list(zip(self.values, self.coming))
        return lax.optimization_barrier((pairs, list(needed)))[0]

    def join(self, split=None, needed=()):
        pairs = self.pairs(needed)
        if split is not None:
            ((here, there),) = pairs
            pairs = [(here[:, :split], there[:, :split]), (here[:, split:], there[:, split:])]
        small = pairs[0][0].shape[0] * pairs[0][0].shape[1] < 256
        self.values = [jnp.concatenate(pair, 0) for pair in pairs] if small else join_pairs(self.info, pairs)
        return self

    def send_last(self, *bits, needed=()):
        self.send(*bits, needed=needed)
        self.near = [swapped(value, CORE_BIT) for value in self.values]
        return self

    def last(self, needed=()):
        self.values = self.pairs(needed)
        if self.near is None:
            self.near = [swapped(here, CORE_BIT) for here, _ in self.values]
        return [
            (here, there, near, swapped(there, CORE_BIT)) for (here, there), near in zip(self.values, self.near)
        ]


def group_perm(ways, links):
    count = lax.axis_size("seq")
    return [(base + a, base + b) for base in range(0, count, ways) for a, b in links]


def window_keys(kv, ways):
    if ways == 2:
        return [kv, lax.ppermute(kv, "seq", group_perm(2, ((0, 1), (1, 0))))]
    groups = [list(range(base, base + ways)) for base in range(0, lax.axis_size("seq"), ways)]
    found = []
    for value in (kv[0], kv[1]):
        every = lax.all_gather(value, "seq", axis=0, tiled=False, axis_index_groups=groups)
        rows = every.shape[1] // 2
        blocks = [every[w, :rows] for w in range(ways)] + [every[w, rows:] for w in reversed(range(ways))]
        found.append(jnp.concatenate(blocks, 0))
    return found


def window_sum(grads, ways):
    if ways == 2:
        keep, send = grads
        return keep, lax.ppermute(send, "seq", group_perm(2, ((0, 1), (1, 0))))
    groups = [list(range(base, base + ways)) for base in range(0, lax.axis_size("seq"), ways)]
    total = lax.psum_scatter(grads[0], "seq", scatter_dimension=0, tiled=False, axis_index_groups=groups)
    return total, jnp.zeros(total.shape, BF16)


def from_sides(first, second, ways):
    if ways == 2:
        rank = lax.axis_index("seq") % ways
        other = lax.ppermute(jnp.where(rank == 0, first, second), "seq", group_perm(2, ((0, 1), (1, 0))))
        zero = jnp.zeros_like(other)
        return jnp.where(rank == 0, zero, other), jnp.where(rank == 0, other, zero)
    up = [(i, i + 1) for i in range(ways - 1)]
    down = [(i + 1, i) for i in range(ways - 1)]
    return lax.ppermute(first, "seq", group_perm(ways, up)), lax.ppermute(second, "seq", group_perm(ways, down))


def sum_all(value):
    count = flat_count()
    for bit in range(count.bit_length() - 1):
        value = value + swapped(value, bit)
    return value


def tiles(weight):
    rows = weight.shape[0]
    return [weight[:, start : start + D] for start in range(0, weight.shape[1], D)] if rows else []


def pack_edge(embed, gains):
    rows = embed.shape[-2]
    pad = jnp.zeros((8, D - gains.shape[1]), gains.dtype)
    side = jnp.concatenate([jnp.concatenate([gains, jnp.zeros((3, gains.shape[1]), gains.dtype)], 0), pad], 1)
    return jnp.concatenate([embed, side], 0)


def gather_weights(embed, head, attn_in, attn_out, ffn_in, ffn_out, gains):
    full = [
        lax.all_gather(weight, BOTH, axis=axis, tiled=True)
        for weight, axis in ((embed, 0), (head, 0), (attn_in, 1), (attn_out, 1), (ffn_in, 1), (ffn_out, 1), (gains, 1))
    ]
    embed, head, attn_in, attn_out, ffn_in, ffn_out, gains = full
    fold_rows = lambda weight: weight.reshape(SHARDS, TILE, D)
    edge = jnp.zeros((SHARDS, TILE, D), BF16).at[:, :8].set(embed.reshape(SHARDS, 8, D))
    edge = edge.at[:, 8:13, :TILE].set(gains.reshape(5, SHARDS, TILE).transpose(1, 0, 2))
    head_tile = jnp.zeros((SHARDS, TILE, D), BF16).at[:, :, :VOCAB].set(head.reshape(SHARDS, TILE, VOCAB))
    down = ffn_out.reshape(2, SHARDS, 4 * TILE, D)
    side = [[fold_rows(t) for t in tiles(attn_in[i])] for i in range(2)]
    up = [[fold_rows(t) for t in tiles(ffn_in[i])] for i in range(2)]
    firsts = [jnp.concatenate(side[0][:2], 1), jnp.concatenate([side[0][2], edge], 1)]
    seconds = [
        jnp.concatenate(up[0] + side[1][:2], 1),
        jnp.concatenate([down[0], fold_rows(attn_out[0]), side[1][2]], 1),
    ]
    third = [jnp.concatenate(up[1] + [fold_rows(attn_out[1])], 1), jnp.concatenate([down[1], head_tile], 1)]
    return firsts, seconds, third


def reduce_natural(grad, axis):
    return lax.psum_scatter(grad, BOTH, scatter_dimension=axis, tiled=True)


def unfold(packed):
    parts = packed.shape[1] // TILE
    return jnp.concatenate([packed[:, TILE * i : TILE * i + TILE].reshape(D, D) for i in range(parts)], 1)


def local(
    stream, offsets, embed, head, attn_in, attn_out, ffn_in, ffn_out, gains,
    embed_row, embed_col, head_row, head_col, in_row, in_col, out_row, out_col, up_row, up_col, down_row, down_col, gains_sq,
):
    seq_rank = lax.axis_index("seq")
    dp_rank = lax.axis_index("dp")
    seq_count = lax.axis_size("seq")
    per_group = offsets.shape[0] // lax.axis_size("dp")
    ways = seq_count // per_group
    blocks = 2 * ways
    length = SPAN * blocks
    rank = seq_rank % ways
    split = flat_count() == SHARDS
    if split:
        low = lambda *values: [value.astype(BF16) for value in values]
        embed_low, gains_low, in_low = low(embed, gains, attn_in[0])
        one = Gather(jnp.concatenate(tiles(in_low) + [pack_edge(embed_low, gains_low)], 0))
        up_low, down_low, out_low, in_low = low(*after((ffn_in[0], ffn_out[0], attn_out[0], attn_in[1]), one.values))
        in_low = tiles(in_low)
        two = Gather(jnp.concatenate(tiles(up_low) + in_low[:2] + [down_low, out_low, in_low[2]], 0))
        one.send(Z1_BIT).join()
        two.send(Z1_BIT, needed=one.values)
        up_low, down_low, out_low, head_low = low(*after((ffn_in[1], ffn_out[1], attn_out[1], head), one.values))
        head_low = jnp.concatenate([head_low, jnp.zeros_like(head_low)], 1)
        three = Gather(jnp.concatenate(tiles(up_low) + [out_low, down_low, head_low], 0))
        one.send(Z0_BIT).join(2 * TILE)
        two.join().send(Z0_BIT, needed=one.values)
        one.send(X_BIT, Y_BIT).join()
        offsets_then, stream_then = after((offsets, stream), two.values)
        two.join(6 * TILE)
        three.send(Z1_BIT, needed=one.values)
        one.send_last(Y_BIT, X_BIT)
        three.join()
        first = one.last()
        two.send(X_BIT, Y_BIT, needed=one.values)
    else:
        low = [w.astype(BF16) for w in (embed, head, attn_in, attn_out, ffn_in, ffn_out, gains)]
        first, second, third = gather_weights(*low)
        first, second, third = [[(value,) for value in pair] for pair in (first, second, third)]
        offsets_then, stream_then = offsets, stream

    window_start = offsets_then[dp_rank * per_group + seq_rank // ways]
    limits = jnp.minimum(length, STREAM - 1 - offsets_then) - (length - length // 2)
    count_real = jnp.sum(jnp.maximum(limits, 0)).astype(F32)
    own_blocks = jnp.stack([rank, blocks - 1 - rank]) + 0 * window_start
    positions = (own_blocks[:, None] * SPAN + jnp.arange(SPAN, dtype=jnp.int32)[None]).reshape(-1)
    coarse_pos = (own_blocks[:, None] * CSPAN + jnp.arange(CSPAN, dtype=jnp.int32)[None]).reshape(-1)
    reach = own_blocks + 1
    info = jnp.concatenate(
        [reach, jnp.stack([rank, flat_index() & 1] + [bit_of(bit) for bit in range(5)] + [flat_index() >> 1])], 0
    ).astype(jnp.int32)
    starts = window_start + own_blocks * SPAN
    padded = jnp.concatenate([stream_then, jnp.broadcast_to(stream_then[-1:], (length,))], 0)
    tokens = jnp.concatenate([lax.dynamic_slice_in_dim(padded, starts[s], SPAN, 0) for s in range(2)], 0)
    target = lax.dynamic_slice_in_dim(padded, starts[1] + 1, SPAN, 0)
    counted = (window_start + positions[SPAN:] + 1 < STREAM).astype(F32)
    rate = (1.0 / (LOG_TWO * count_real)).reshape(1, 1)

    def tables(at):
        frequency = 10000.0 ** (-jnp.arange(HD // 2, dtype=F32) / (HD // 2))
        angles = at.astype(F32)[:, None] * frequency[None, :]
        cosine, sine = jnp.cos(angles), jnp.sin(angles)
        return (jnp.concatenate([cosine] * 4, 1), jnp.concatenate([-sine, sine] * 2, 1))

    cos_0, sin_0 = tables(positions)
    cos_1, sin_1 = tables(coarse_pos)

    token_col, target_col, counted_col = tokens[:, None], target[:, None], counted[:, None]
    if split:
        token_col = after(token_col, target_col, counted_col, rate, cos_1, sin_1, three.values)
    h_0, q_0, kv_0, gain_rows = project(info, token_col, first, cos_0, sin_0)
    if split:
        two.join(needed=[q_0]).send_last(Y_BIT, X_BIT)
        three.send(Z0_BIT)
        kv_0 = after(kv_0, two.values)
    keys_0 = window_keys(kv_0, ways)
    a_lo, lse_lo = attend(info, q_0, keys_0, SPAN, 0, 1)
    if split:
        three.join(5 * TILE, needed=[a_lo]).send(X_BIT, Y_BIT)
    a_hi, lse_hi = attend(info, after(q_0, a_lo, three.values, two.near) if split else q_0, keys_0, SPAN, 1, 1)
    if split:
        three.join(needed=[a_hi])
        second = two.last([a_hi, *three.values])
        three.send(Y_BIT, X_BIT)
    m_0, h_1, tail = branch(info, after(h_0, three.values) if split else h_0, (a_lo, a_hi), second, gain_rows)

    z_0, q_1, kv_1 = project_short(
        info, h_1, tail, *from_sides(tail[0], tail[1], ways), second, gain_rows, cos_1, sin_1, ways
    )
    keys_1 = window_keys(kv_1, ways)
    a_1, lse_1 = attend(info, q_1, keys_1, CSPAN, 0, 2)
    if split:
        third = three.last([a_1])
    found = short_rest(info, z_0, a_1, h_1, third, gain_rows, target_col, counted_col, rate, split)
    loss, dg_4, dg_3, d_h2, d_m1, d_a1 = found[:6]
    each = 2 if split else 1
    d_up_1, d_down_1, d_head = [found[6 + each * i : 6 + each * i + each] for i in range(3)]
    if split:
        late = Scatter(info, [d_up_1], [d_down_1])
    d_q1, *d_kv1 = attend_back(info, q_1, keys_1, d_a1, lse_1, CSPAN, 0, 2)
    keep, recv = window_sum(d_kv1, ways)
    found = project_back(info, [d_q1], [keep], [recv], d_m1, z_0, [], second, [], gain_rows, cos_1, sin_1, False, split)
    d_in_1, (dg_2, d_z0, edge) = found[:each], found[each:]

    low_edge, high = from_sides(edge[1], edge[0], ways)
    found = branch_back(info, d_z0, edge, high, low_edge, d_h2, m_0, (a_lo, a_hi), second, gain_rows, ways, split)
    d_m0, da_lo, da_hi, dg_1 = found[:4]
    d_up_0, d_down_0 = [found[4 + each * i : 4 + each * i + each] for i in range(2)]
    if split:
        middle = Scatter(info, [d_up_0, d_in_1], [d_down_0, d_head])
        step_all(info, d_m0)(late)
        step_all(info, late.kept())(middle)
        both = late.joined(middle)
        da_lo = after(da_lo, both.kept())
    dq_lo, *dkv_lo = attend_back(info, q_0, keys_0, da_lo, lse_lo, SPAN, 0, 1)
    if split:
        da_hi = after(da_hi, dq_lo)
    sum_lo = window_sum(dkv_lo, ways)
    dq_hi, *dkv_hi = attend_back(info, q_0, keys_0, da_hi, lse_hi, SPAN, 1, 1)
    if split:
        step_all(info, dq_hi)(both)
        dkv_hi = after(tuple(dkv_hi), both.kept())
    sum_hi = window_sum(dkv_hi, ways)
    found = project_back(
        info, [dq_lo, dq_hi], [sum_lo[0], sum_hi[0]], [sum_lo[1], sum_hi[1]], d_m0, h_0, [tokens[None, :]], first,
        [dg_1, dg_2, dg_3, dg_4], gain_rows, cos_0, sin_0, True, split,
    )

    if split:
        early = Scatter(info, [found[:2]], [found[2:]])
        step_all(info, found[0])(both, early)
        step_all(info)(early)
        step_all(info)(both, early)
        step_all(info)(early)
        loss_sum, outputs = optimize(
            info,
            [sources[0] for sources in both.values + early.values],
            [embed_row, head_row, in_row, out_row, up_row, down_row],
            [embed_col, head_col, in_col, out_col, up_col, down_col],
            [embed, head, attn_in, attn_out, ffn_in, ffn_out],
            gains,
            gains_sq,
            loss,
        )
        return (*loss_sum, count_real, *outputs)
    d_qk, d_v, dg_0, d_embed = found
    if True:
        d_in_0 = jnp.concatenate([d_qk, d_v], 1)
        g_embed = reduce_natural(d_embed, 0)
        g_head = reduce_natural(d_head[0][:, :, :VOCAB].reshape(D, VOCAB), 0)
        g_in = reduce_natural(jnp.stack([unfold(d_in_0), unfold(d_in_1[0])]), 1)
        g_out = reduce_natural(jnp.stack([unfold(d) for d in (d_down_0[0][:, 4 * TILE :], d_down_1[0][:, 4 * TILE :])]), 1)
        g_up = reduce_natural(jnp.stack([unfold(d_up_0[0]), unfold(d_up_1[0])]), 1)
        g_down = reduce_natural(jnp.stack([d.reshape(FF, D) for d in (d_down_0[0][:, : 4 * TILE], d_down_1[0][:, : 4 * TILE])]), 1)
        gain_grad = reduce_natural(jnp.concatenate([dg_0, dg_1, dg_2, dg_3, dg_4], 0), 1)

    embed, head, attn_in, attn_out, ffn_in, ffn_out = after((embed, head, attn_in, attn_out, ffn_in, ffn_out), d_q1)
    decay = 1.0 - STEP ** (-0.8)
    matrices = [
        (g_embed, embed_row, embed_col, embed, VOCAB),
        (g_head, head_row, head_col, head, D),
        (g_in, in_row, in_col, attn_in, D),
        (g_out, out_row, out_col, attn_out, D),
        (g_up, up_row, up_col, ffn_in, D),
        (g_down, down_row, down_col, ffn_out, FF),
    ]
    new_rows, sums = [], []
    for grad, row, _, weight, _ in matrices:
        square = grad * grad
        new_row = decay * row + (1.0 - decay) * jnp.mean(square, -1)
        new_rows.append(new_row)
        sums += [
            jnp.sum(square, -2),
            jnp.sum(square / new_row[..., None], -2),
            jnp.sum(new_row, -1),
            jnp.sum(weight * weight, (-2, -1)),
        ]
    new_sq = decay * gains_sq + (1.0 - decay) * gain_grad * gain_grad
    gain_update = gain_grad / jnp.sqrt(new_sq)
    sums += [jnp.sum(gain_update * gain_update, -1), jnp.sum(gains * gains, -1), loss[0, :1]]
    flat = jnp.concatenate([s.reshape(-1) for s in sums], 0)
    size = flat.shape[0]
    flat = jnp.pad(flat, (0, -size % 1024)).reshape(-1, 128)
    flat = sum_all(flat).reshape(-1)
    totals, at = [], 0
    for s in sums:
        totals.append(flat[at : at + s.size].reshape(s.shape))
        at += s.size
    outputs = [totals[-1].reshape(()), count_real]
    for index, (grad, _, col, weight, full_rows) in enumerate(matrices):
        col_sum, ratio_sum, row_sum, weight_sum = totals[4 * index : 4 * index + 4]
        new_row = new_rows[index]
        new_col = decay * col + (1.0 - decay) * col_sum / full_rows
        mean_row = row_sum / full_rows
        size_all = full_rows * grad.shape[-1]
        update_sum = mean_row * jnp.sum(ratio_sum / new_col, -1)
        rate_now = RATE_SCALE * jnp.sqrt(weight_sum / size_all) / jnp.maximum(1.0, jnp.sqrt(update_sum / size_all))
        update = grad / jnp.sqrt(new_row[..., :, None] * new_col[..., None, :] / mean_row[..., None, None])
        outputs += [grad, new_row, new_col, weight - rate_now[..., None, None] * update]
    gain_rate = RATE_SCALE * jnp.sqrt(totals[-2] / D) / jnp.maximum(1.0, jnp.sqrt(totals[-3] / D))
    outputs += [gain_grad, new_sq, gains - gain_rate[:, None] * gain_update]
    return tuple(outputs)


def solution(mesh):
    row = P(BOTH, None)
    mid = P(None, BOTH, None)
    vec = P(BOTH)
    vec2 = P(None, BOTH)
    state = (vec, P(), vec, P(), vec2, P(), vec2, P(), vec2, P(), vec2, P(), vec2)
    return jax.shard_map(
        local,
        mesh=mesh,
        in_specs=(P(), P(), row, row, mid, mid, mid, mid, vec2) + state,
        out_specs=(P(), P())
        + (row, vec, P(), row) * 2
        + (mid, vec2, P(), mid) * 4
        + (vec2, vec2, vec2),
        check_vma=False,
    )
```

```python
from functools import partial
import math

import jax
import jax.numpy as jnp
from jax import lax
from jax.experimental import pallas as pl
from jax.experimental.pallas import tpu as pltpu
from jax.sharding import PartitionSpec as P

D = 512
HEADS = 8
FF = 2048
VOCAB = 256
SHORT = 3
HD = 64
SPAN = 384
CSPAN = SPAN // SHORT
STREAM = 65536
STEP = 10
SHARDS = 32
TILE = 16

EPSILON = 1e-05
RATE_SCALE = 0.5
LOG_TWO = math.log(2.0)
MASKED = -1e30
GELU_A = math.sqrt(2.0 / math.pi)
GELU_B = 0.044715
BOTH = ("dp", "seq")
F32 = jnp.float32
BF16 = jnp.bfloat16
ROOM = {
    "fold": 24, "join": 16, "measure": 20, "attend": 24, "attend_back": 36, "project": 28, "project_short": 28,
    "branch": 32, "branch_back": 44, "short_rest": 34, "project_back": 36,
}


def nn(left, right):
    return jnp.dot(left, right, preferred_element_type=F32)


def nt(left, right):
    return lax.dot_general(left, right, (((1,), (1,)), ((), ())), preferred_element_type=F32)


def call(body, name, outs, ins, us, grid=(1,), in_specs=None, out_specs=None, scratch=(), prefetch=1):
    room = ROOM.get(name, 56) * 2**20
    spec = pltpu.PrefetchScalarGridSpec(
        num_scalar_prefetch=prefetch,
        grid=grid,
        in_specs=in_specs or [held(i.shape) for i in ins[prefetch:]],
        out_specs=out_specs or [whole(o.shape) for o in outs],
        scratch_shapes=list(scratch),
    )
    return pl.pallas_call(
        body,
        grid_spec=spec,
        out_shape=list(outs),
        compiler_params=pltpu.CompilerParams(vmem_limit_bytes=room),
        cost_estimate=pl.CostEstimate(flops=int(us * 2e10), bytes_accessed=1 << 20, transcendentals=0),
        name=name,
    )(*ins)


def whole(dims):
    return pl.BlockSpec(dims, lambda *_: (0,) * len(dims))


def held(dims):
    return pl.BlockSpec(dims, lambda *_: (0,) * len(dims), pipeline_mode=pl.Buffered(1))


def shape(dims, kind=F32):
    return jax.ShapeDtypeStruct(dims, kind)


RANK, CORE, BITS, CHIP = 2, 3, 4, 9
WEIGHT_PARTS = 4


def norm_parts(values):
    center = values - jnp.mean(values, -1, keepdims=True)
    scale = lax.rsqrt(jnp.mean(center * center, -1, keepdims=True) + EPSILON)
    return center * scale, scale


def norm_pull(hat, scale, gain, cotangent):
    pulled = cotangent * gain
    inner = pulled - jnp.mean(pulled, -1, keepdims=True) - hat * jnp.mean(pulled * hat, -1, keepdims=True)
    return scale * inner, jnp.sum(cotangent * hat, 0, keepdims=True)


def swap_halves(values):
    lane = lax.broadcasted_iota(jnp.int32, values.shape, 1)
    return jnp.where(lane % HD < HD // 2, pltpu.roll(values, 128 - HD // 2, 1), pltpu.roll(values, HD // 2, 1))


def rope(values, cosine, sine):
    pieces = []
    for start in range(0, D, 128):
        piece = values[:, start : start + 128]
        pieces.append(piece * cosine + swap_halves(piece) * sine)
    return jnp.concatenate(pieces, 1)


def rope_pull(values, cosine, sine):
    pieces = []
    for start in range(0, D, 128):
        piece = values[:, start : start + 128]
        pieces.append(piece * cosine + swap_halves(piece * sine))
    return jnp.concatenate(pieces, 1)


def gelu_parts(values):
    inner = GELU_A * (values + GELU_B * (values * values * values))
    wave = jnp.tanh(inner)
    return wave, 0.5 * (1.0 + wave)


def gelu_slope(values, wave, gate):
    return gate + 0.5 * values * (1.0 - wave * wave) * (GELU_A * (1.0 + 3.0 * GELU_B * values * values))


def tile_of(ref, index):
    return ref[:, TILE * index : TILE * index + TILE, :].reshape(D, ref.shape[-1])


def settle(refs, scr, info, second, start=0):
    if len(refs) == 1:
        return refs[0].at[:, start:]
    rows = slice(start, start + scr.shape[1])
    last, next_last = (1, 0) if second else (0, 1)

    def place(r, carry):
        mask = ((r & 1) << 3) | (((r >> 1) & 1) << 2) | (((r >> 2) & 1) << next_last)
        for far in range(2):
            chip = info[CHIP] ^ (mask | (far << last))
            scr[2 * chip + info[CORE]] = refs[far][r, rows]
            scr[2 * chip + 1 - info[CORE]] = refs[2 + far][r, rows]
        return carry

    lax.fori_loop(0, SHARDS // 4, place, 0)
    return scr


def bundle_scratch(bundles, rows):
    return [pltpu.VMEM((SHARDS, count, D), BF16) for bundle, count in zip(bundles, rows) if len(bundle) > 1]


def thirds(ref, lead, start):
    found = ref[(*lead, pl.ds(start, CSPAN, stride=SHORT), slice(None))]
    for shift in range(1, SHORT):
        found = found + ref[(*lead, pl.ds(start + shift, CSPAN, stride=SHORT), slice(None))]
    return found


def spread(ref, lead, value):
    for shift in range(SHORT):
        ref[(*lead, pl.ds(shift, CSPAN, stride=SHORT), slice(None))] = value


LANES = [slice(start, start + 128) for start in range(0, D, 128)]


def grad_shapes(rows, split):
    if split:
        return [shape((SHARDS // 2, rows, D)), shape((SHARDS // 2, rows, D), BF16)]
    return [shape((SHARDS, rows, D))]


def grad_specs(rows, split, index, shards=SHARDS):
    if split:
        return [pl.BlockSpec((shards // 2, rows, D), index)] * 2
    return [pl.BlockSpec((shards, rows, D), index)]


def put(refs, core, value, at=0, rows=TILE, chunk=0):
    width = value.shape[-1]
    part = pl.ds(at, rows)
    shards = D // rows
    if len(refs) == 2:
        pairs = value.reshape(shards // 2, 2, rows, width)
        low, high = pairs[:, 0], pairs[:, 1]
        where = pl.ds(chunk * (shards // 2), shards // 2)
        refs[0][where, part, :width] = jnp.where(core == 0, low, high)
        refs[1][where, part, :width] = jnp.where(core == 0, high, low).astype(BF16)
    else:
        refs[0][pl.ds(chunk * shards, shards), part, :width] = value.reshape(shards, rows, width).astype(refs[0].dtype)


def project_body(info, token_ref, *rest, each):
    wa_refs, wb_refs = rest[:each], rest[each : 2 * each]
    cos_ref, sin_ref, h_ref, q_ref, kv_ref, gain_ref = rest[2 * each : 2 * each + 6]
    scr = rest[2 * each + 6 :]
    wa_ref, wb_ref = scr if each > 1 else (wa_refs[0], wb_refs[0])

    @pl.when(pl.program_id(0) == 0)
    def _():
        settle(wa_refs, scr and scr[0], info, False)
        settle(wb_refs, scr and scr[1], info, True)
        lane = lax.broadcasted_iota(jnp.int32, (8, D), 1)
        found = jnp.zeros((8, D), F32)
        for shard in range(SHARDS):
            side = wb_ref[shard, TILE : 2 * TILE, :].astype(F32)[8:]
            side = side if shard == 0 else pltpu.roll(side, TILE * shard, 1)
            found = jnp.where(lane // TILE == shard, side, found)
        gain_ref[...] = found

    token = token_ref[...]
    row = (token // 8) * TILE + token % 8
    hot = (row == lax.broadcasted_iota(jnp.int32, (token.shape[0], D), 1)).astype(BF16)
    values = nn(hot, tile_of(wb_ref, 1))
    h_ref[...] = values.astype(BF16)
    normed = (norm_parts(values)[0] * gain_ref[0:1, :]).astype(BF16)
    cosine, sine = cos_ref[...], sin_ref[...]
    q_ref[...] = (rope(nn(normed, tile_of(wa_ref, 0)), cosine, sine) * 0.125).astype(BF16)
    kv_ref[0] = rope(nn(normed, tile_of(wa_ref, 1)), cosine, sine).astype(BF16)
    kv_ref[1] = nn(normed, tile_of(wb_ref, 0)).astype(BF16)


def project(info, token, bundles, cosine, sine):
    rows = cosine.shape[0]
    step = SPAN
    weights = [*bundles[0], *bundles[1]]
    return call(
        partial(project_body, each=len(bundles[0])),
        "project",
        [shape((rows, D), BF16)] * 2 + [shape((2, rows, D), BF16), shape((8, D))],
        [info, token, *weights, cosine, sine],
        5,
        grid=(rows // step,),
        in_specs=[pl.BlockSpec((step, 1), lambda i, _: (i, 0))]
        + [held(w.shape) for w in weights]
        + [pl.BlockSpec((step, 128), lambda i, _: (i, 0))] * 2,
        out_specs=[pl.BlockSpec((step, D), lambda i, _: (i, 0))] * 2
        + [pl.BlockSpec((2, step, D), lambda i, _: (0, i, 0)), whole((8, D))],
        scratch=bundle_scratch(bundles, (2 * TILE, 2 * TILE)),
    )


def project_short_body(
    info, h_ref, tail_ref, low_ref, high_ref, *rest, ways, each
):
    wa_refs, wb_refs = rest[:each], rest[each : 2 * each]
    gain_ref, cos_ref, sin_ref, z_ref, q_ref, kv_ref, scr = rest[2 * each : 2 * each + 7]
    wa_ref = settle(wa_refs, rest[-2], info, False, 4 * TILE)
    wb_ref = settle(wb_refs, rest[-1], info, True, 5 * TILE)
    for slot in range(2):
        if slot == 0:
            halo = low_ref[...]
        else:
            halo = jnp.where(info[RANK] == ways - 1, tail_ref[0], high_ref[...])
        for piece, lanes in enumerate(LANES):
            scr[slot, piece, :8, :] = halo[:, lanes]
            scr[slot, piece, 8:, :] = h_ref[SPAN * slot : SPAN * slot + SPAN, lanes]
            total = thirds(scr, (slot, piece), 6)
            z_ref[CSPAN * slot : CSPAN * slot + CSPAN, lanes] = total * (1.0 / SHORT)
    normed = (norm_parts(z_ref[...])[0] * gain_ref[2:3, :]).astype(BF16)
    cosine, sine = cos_ref[...], sin_ref[...]
    query = nn(normed[CSPAN:], tile_of(wa_ref, 0))
    q_ref[...] = (rope(query, cosine[CSPAN:], sine[CSPAN:]) * 0.125).astype(BF16)
    kv_ref[0] = rope(nn(normed, tile_of(wa_ref, 1)), cosine, sine).astype(BF16)
    kv_ref[1] = nn(normed, tile_of(wb_ref, 0)).astype(BF16)


def project_short(info, h, tail, low, high, bundles, gains, cosine, sine, ways):
    outs = [shape((2 * CSPAN, D)), shape((CSPAN, D), BF16), shape((2, 2 * CSPAN, D), BF16)]
    ins = [info, h, tail, low, high, *bundles[0], *bundles[1], gains, cosine, sine]
    specs = [held(i.shape) for i in ins[1:]]
    return call(
        partial(project_short_body, ways=ways, each=len(bundles[0])),
        "project_short",
        outs,
        ins,
        0.05,
        in_specs=specs,
        scratch=[pltpu.VMEM((2, D // 128, SPAN + 8, 128), F32)] + bundle_scratch(bundles, (2 * TILE, TILE)),
    )


def order_keys(info, own, other, found, block, count):
    for at in range(count):
        owner = min(at, count - 1 - at)
        place = 0 if owner == at else 1
        part = slice(place * block, place * block + block)
        for kind, keys in enumerate(found):
            keys[at * block : at * block + block, :] = jnp.where(
                info[RANK] == owner, own[kind, part, :], other[kind, part, :]
            )


def each_rows(rows, steps, count):
    if count <= 4:
        for i in range(steps):
            rows(i)
    else:
        lax.fori_loop(0, steps, lambda i, carry: (rows(i), carry)[1], 0)


def each_head(head, together):
    if together == 4:
        for j in range(4):
            head(j)
        return

    def some(i, carry):
        for j in range(together):
            head(i * together + j)
        return carry

    lax.fori_loop(0, 4 // together, some, 0)


def masked_rows(s_scr, part, start, step, block, width):
    score = s_scr[part, :width]
    row = start + lax.broadcasted_iota(jnp.int32, (step, block), 0)
    key = lax.broadcasted_iota(jnp.int32, (step, block), 1)
    edge = jnp.where(row >= key, score[:, width - block :], MASKED)
    return jnp.concatenate([score[:, : width - block], edge], 1) if width > block else edge


def rows_part(i, step):
    return pl.ds(i * step if isinstance(i, int) else pl.multiple_of(i * step, step), step)


def attend_body(info, q_ref, *rest, count, block, step, pair, base):
    if pair:
        own, other, out_ref, lse_ref, s_scr, p_scr, k_ref, v_ref = rest
    else:
        k_ref, v_ref, out_ref, lse_ref, s_scr, p_scr = rest
    slot = pl.program_id(1)
    nk = info[slot + base]
    lane = lax.broadcasted_iota(jnp.int32, (1, 256), 1)
    column = lax.broadcasted_iota(jnp.int32, (step, 128), 1)
    zero = jnp.zeros((), BF16)
    if pair:

        @pl.when(slot == 0)
        def _():
            order_keys(info, own, other, (k_ref, v_ref), block, count)

    def variant(blocks):
        width = blocks * block

        def head(j):
            mine = lane // HD == j
            s_scr[:, :width] = nt(jnp.where(mine, q_ref[...], zero), k_ref[:width, :])

            def rows(i):
                part = rows_part(i, step)
                score = masked_rows(s_scr, part, i * step, step, block, width)
                top = jnp.max(score, -1, keepdims=True)
                raised = jnp.exp(score - top)
                total = jnp.sum(raised, -1, keepdims=True)
                p_scr[part, :width] = (raised * (1.0 / total)).astype(BF16)
                lse_ref[0, 0, part, :] = jnp.where(column == j, top + jnp.log(total), lse_ref[0, 0, part, :])

            each_rows(rows, block // step, count)
            found = nn(p_scr[:, :width], v_ref[:width, :]).astype(BF16)
            out_ref[...] = jnp.where(mine, found, out_ref[...])

        each_head(head, 4 if count <= 4 else 1)

    for blocks in range(1, count + 1):
        pl.when(nk == blocks)(partial(variant, blocks))


def key_spec(key, first):
    lead = key.shape[:-1]
    return pl.BlockSpec((*lead, 256), lambda h, s, _: (0,) * len(lead) + (h + first,))


def attend(info, q, keys, block, first, groups):
    slots = q.shape[0] // block
    pair = keys[0].ndim == 3
    total = keys[0].shape[-2] * (2 if pair else 1)
    count = total // block
    scratch = [pltpu.VMEM((block, total), F32), pltpu.VMEM((block, total), BF16)]
    if pair:
        scratch += [pltpu.VMEM((total, 256), BF16)] * 2
    return call(
        partial(attend_body, count=count, block=block, step=64, pair=pair, base=2 - slots),
        "attend",
        [shape((slots * block, 256 * groups), BF16), shape((groups, slots, block, 128))],
        [info, q, *keys],
        8 if block == SPAN else 0.05,
        grid=(groups, slots),
        in_specs=[pl.BlockSpec((block, 256), lambda h, s, _: (s, h + first))]
        + [key_spec(key, first) for key in keys],
        out_specs=[
            pl.BlockSpec((block, 256), lambda h, s, _: (s, h)),
            pl.BlockSpec((1, 1, block, 128), lambda h, s, _: (h, s, 0, 0)),
        ],
        scratch=scratch,
    )


def attend_back_body(info, q_ref, *rest, count, block, step, pair, base):
    if pair:
        own, other, back_ref, lse_ref, dq_ref, keep_ref, send_ref = rest[:7]
        s_scr, dp_scr, p_scr, ds_scr, dk_scr, dv_scr, qt_scr, bt_scr, k_ref, v_ref = rest[7:]
    else:
        k_ref, v_ref, back_ref, lse_ref, dq_ref, keep_ref = rest[:6]
        s_scr, dp_scr, p_scr, ds_scr, dk_scr, dv_scr, qt_scr, bt_scr = rest[6:]
    slot = pl.program_id(1)
    nk = info[slot + base]
    lane = lax.broadcasted_iota(jnp.int32, (1, 256), 1)
    column = lax.broadcasted_iota(jnp.int32, (step, 128), 1)
    zero = jnp.zeros((), BF16)

    qt_scr[...] = q_ref[...].T
    bt_scr[...] = back_ref[...].T

    @pl.when(slot == 0)
    def _():
        dk_scr[...] = jnp.zeros_like(dk_scr)
        dv_scr[...] = jnp.zeros_like(dv_scr)
        if pair:
            order_keys(info, own, other, (k_ref, v_ref), block, count)

    def variant(blocks):
        width = blocks * block

        def head(j):
            mine = lane // HD == j
            s_scr[:, :width] = nt(jnp.where(mine, q_ref[...], zero), k_ref[:width, :])
            dp_scr[:, :width] = nt(jnp.where(mine, back_ref[...], zero), v_ref[:width, :])

            def rows(i):
                part = rows_part(i, step)
                score = masked_rows(s_scr, part, i * step, step, block, width)
                lse = jnp.sum(jnp.where(column == j, lse_ref[0, 0, part, :], 0.0), -1, keepdims=True)
                prob = jnp.exp(score - lse)
                p_scr[part, :width] = prob.astype(BF16)
                prob_back = dp_scr[part, :width]
                delta = jnp.sum(prob * prob_back, -1, keepdims=True)
                ds_scr[part, :width] = (prob * (prob_back - delta)).astype(BF16)

            each_rows(rows, block // step, count)
            found = nn(ds_scr[:, :width], k_ref[:width, :])
            dq_ref[...] = jnp.where(mine, found, dq_ref[...])
            mine_rows = pl.ds(HD * j if isinstance(j, int) else pl.multiple_of(HD * j, HD), HD)
            dk_scr[mine_rows, :width] += nn(qt_scr[mine_rows, :], ds_scr[:, :width])
            dv_scr[mine_rows, :width] += nn(bt_scr[mine_rows, :], p_scr[:, :width])

        each_head(head, 2 if count <= 4 else 1)

    for blocks in range(1, count + 1):
        pl.when(nk == blocks)(partial(variant, blocks))

    @pl.when(slot == pl.num_programs(1) - 1)
    def _():
        for kind, scr in enumerate((dk_scr, dv_scr)):
            for place in range(2):
                to = slice(place * block, place * block + block)

                def from_owner(owner):
                    at = owner if place == 0 else count - 1 - owner
                    return scr[:, at * block : at * block + block]

                if pair:
                    low, high = from_owner(0), from_owner(1)
                    keep_ref[kind, :, to] = jnp.where(info[RANK] == 0, low, high)
                    send_ref[kind, :, to] = jnp.where(info[RANK] == 0, high, low).astype(BF16)
                else:
                    for owner in range(count // 2):
                        keep_ref[owner, kind, :, to] = from_owner(owner)


def attend_back(info, q, keys, back, lse, block, first, groups):
    slots = q.shape[0] // block
    pair = keys[0].ndim == 3
    total = keys[0].shape[-2] * (2 if pair else 1)
    count = total // block
    outs = [shape((slots * block, 256 * groups))]
    out_specs = [pl.BlockSpec((block, 256), lambda h, s, _: (s, h))]
    if pair:
        outs += [shape((2, 256 * groups, 2 * block)), shape((2, 256 * groups, 2 * block), BF16)]
        out_specs += [pl.BlockSpec((2, 256, 2 * block), lambda h, s, _: (0, h, 0))] * 2
    else:
        outs += [shape((count // 2, 2, 256 * groups, 2 * block))]
        out_specs += [pl.BlockSpec((count // 2, 2, 256, 2 * block), lambda h, s, _: (0, 0, h, 0))]
    scratch = [
        pltpu.VMEM((block, total), F32),
        pltpu.VMEM((block, total), F32),
        pltpu.VMEM((block, total), BF16),
        pltpu.VMEM((block, total), BF16),
        pltpu.VMEM((256, total), F32),
        pltpu.VMEM((256, total), F32),
        pltpu.VMEM((256, block), BF16),
        pltpu.VMEM((256, block), BF16),
    ]
    if pair:
        scratch += [pltpu.VMEM((total, 256), BF16)] * 2
    return call(
        partial(attend_back_body, count=count, block=block, step=64, pair=pair, base=2 - slots),
        "attend_back",
        outs,
        [info, q, *keys, back, lse],
        13 if block == SPAN else 7,
        grid=(groups, slots),
        in_specs=[pl.BlockSpec((block, 256), lambda h, s, _: (s, h + first))]
        + [key_spec(key, first) for key in keys]
        + [
            pl.BlockSpec((block, 256), lambda h, s, _: (s, h)),
            pl.BlockSpec((1, 1, block, 128), lambda h, s, _: (h, s, 0, 0)),
        ],
        out_specs=out_specs,
        scratch=scratch,
    )


def branch_body(info, x_ref, a0_ref, a1_ref, *rest, each):
    up_refs, down_refs = rest[:each], rest[each : 2 * each]
    gain_ref, mid_ref, res_ref, tail_ref = rest[2 * each : 2 * each + 4]
    scr = rest[2 * each + 4 :]
    up_w, down_w = scr if each > 1 else (up_refs[0], down_refs[0])

    @pl.when(pl.program_id(0) == 0)
    def _():
        settle(up_refs, scr and scr[0], info, False)
        settle(down_refs, scr and scr[1], info, True)

    out_tile = tile_of(down_w, 4)
    middle = x_ref[...].astype(F32) + nn(a0_ref[...], out_tile[:256]) + nn(a1_ref[...], out_tile[256:])
    mid_ref[...] = middle
    normed = (norm_parts(middle)[0] * gain_ref[1:2, :]).astype(BF16)
    total = mid_ref[...]
    for chunk in range(FF // D):
        up = nn(normed, tile_of(up_w, chunk))
        hidden = (up * gelu_parts(up)[1]).astype(BF16)
        total = total + nn(hidden, down_w[8 * chunk : 8 * chunk + 8, : 4 * TILE, :].reshape(D, D))
    res_ref[...] = total
    tail_ref[0] = total[total.shape[0] - 8 :]


def branch(info, x, parts, bundles, gains):
    rows = x.shape[0]
    row = lambda width: pl.BlockSpec((SPAN, width), lambda i, _: (i, 0))
    weights = [*bundles[0], *bundles[1]]
    return call(
        partial(branch_body, each=len(bundles[0])),
        "branch",
        [shape((rows, D)), shape((rows, D)), shape((2, 8, D))],
        [info, x, *parts, *weights, gains],
        9,
        grid=(rows // SPAN,),
        in_specs=[row(D), row(256), row(256), *[held(w.shape) for w in weights], held(gains.shape)],
        out_specs=[row(D), row(D), pl.BlockSpec((1, 8, D), lambda i, _: (i, 0, 0))],
        scratch=bundle_scratch(bundles, (4 * TILE, 5 * TILE)),
    )


def branch_back_body(info, dz_ref, edge_ref, high_ref, low_ref, dh_ref, mid_ref, a0_ref, a1_ref, *rest, ways, split):
    each = 2 if split else 1
    parts = WEIGHT_PARTS if split else 1
    uw_refs, dw_refs, gain_ref = rest[:parts], rest[parts : 2 * parts], rest[2 * parts]
    rest = rest[2 * parts + 1 :]
    dmid_ref, da0_ref, da1_ref, dgain_ref = rest[:4]
    up_refs, down_refs = rest[4 : 4 + each], rest[4 + each : 4 + 2 * each]
    norm_scr, normt_scr, cot_scr, cotb_scr, acc_scr, pool_scr = rest[4 + 2 * each : 10 + 2 * each]
    w_scr = rest[10 + 2 * each :]
    up_w, down_w = w_scr if split else (uw_refs[0], dw_refs[0])
    chunk = pl.program_id(0)
    core = info[CORE]

    @pl.when(chunk == 0)
    def _():
        settle(uw_refs, w_scr and w_scr[0], info, False)
        settle(dw_refs, w_scr and w_scr[1], info, True)
        for slot in range(2):
            if slot == 0:
                edge = jnp.where(info[RANK] == ways - 1, edge_ref[1], high_ref[...])
            else:
                edge = low_ref[...]
            for piece, lanes in enumerate(LANES):
                spread(pool_scr, (slot, piece), dz_ref[CSPAN * slot : CSPAN * slot + CSPAN, lanes] * (1.0 / SHORT))
                pool_scr[slot, piece, SPAN:, :] = jnp.broadcast_to(edge[0:1, lanes] * (1.0 / SHORT), (8, 128))
                found = pool_scr[slot, piece, 2 : SPAN + 2, :]
                if slot == 1:
                    found = found + dh_ref[:, lanes]
                cot_scr[SPAN * slot : SPAN * slot + SPAN, lanes] = found
        cotb_scr[...] = cot_scr[...].astype(BF16)
        normed = (norm_parts(mid_ref[...])[0] * gain_ref[1:2, :]).astype(BF16)
        norm_scr[...] = normed
        normt_scr[...] = normed.T
        acc_scr[...] = jnp.zeros_like(acc_scr)

    down_in = cotb_scr[...]
    up_tile = up_w[:, pl.ds(pl.multiple_of(chunk * TILE, TILE), TILE), :].reshape(D, D)
    down_tile = down_w[pl.ds(chunk * 8, 8), : 4 * TILE, :].reshape(D, D)
    up = nn(norm_scr[...], up_tile)
    wave, gate = gelu_parts(up)
    hidden = (up * gate).astype(BF16)
    up_in = (nt(down_in, down_tile) * gelu_slope(up, wave, gate)).astype(BF16)
    put(down_refs, core, nn(hidden.T, down_in), rows=4 * TILE, chunk=chunk)
    put(up_refs, core, nn(normt_scr[...], up_in))
    acc_scr[...] += nt(up_in, up_tile)

    @pl.when(chunk == FF // D - 1)
    def _():
        hat, scale = norm_parts(mid_ref[...])
        pulled, dgain = norm_pull(hat, scale, gain_ref[1:2, :], acc_scr[...])
        dgain_ref[...] = dgain
        dmid = cot_scr[...] + pulled
        dmid_ref[...] = dmid
        out_in = dmid.astype(BF16)
        out_tile = tile_of(down_w, 4)
        put(down_refs, core, jnp.concatenate([nn(a0_ref[...].T, out_in), nn(a1_ref[...].T, out_in)], 0), at=4 * TILE)
        da0_ref[...] = nt(out_in, out_tile[:256]).astype(BF16)
        da1_ref[...] = nt(out_in, out_tile[256:]).astype(BF16)


def branch_back(info, dz, edge, high, low, dh, mid, parts, bundles, gains, ways, split):
    rows = mid.shape[0]
    ins = [info, dz, edge, high, low, dh, mid, *parts, *bundles[0], *bundles[1], gains]
    specs = [held(i.shape) for i in ins[1:]]
    return call(
        partial(branch_back_body, ways=ways, split=split),
        "branch_back",
        [shape((rows, D)), shape((rows, 256), BF16), shape((rows, 256), BF16), shape((1, D))]
        + grad_shapes(4 * TILE, split)
        + grad_shapes(5 * TILE, split),
        ins,
        0.3,
        grid=(FF // D,),
        in_specs=specs,
        out_specs=[whole((rows, D)), whole((rows, 256)), whole((rows, 256)), whole((1, D))]
        + grad_specs(TILE, split, lambda i, _: (0, i, 0))
        + grad_specs(5 * TILE, split, lambda i, _: (0, 0, 0)),
        scratch=[
            pltpu.VMEM((rows, D), BF16),
            pltpu.VMEM((D, rows), BF16),
            pltpu.VMEM((rows, D), F32),
            pltpu.VMEM((rows, D), BF16),
            pltpu.VMEM((rows, D), F32),
            pltpu.VMEM((2, D // 128, SPAN + 8, 128), F32),
            *bundle_scratch(bundles, (4 * TILE, 5 * TILE)),
        ],
    )


def short_body(info, x_ref, a_ref, h_ref, *rest, split):
    each = 2 if split else 1
    parts = WEIGHT_PARTS if split else 1
    uw_refs, dw_refs = rest[:parts], rest[parts : 2 * parts]
    gain_ref, target_ref, counted_ref, rate_ref = rest[2 * parts : 2 * parts + 4]
    rest = rest[2 * parts + 4 :]
    loss_ref, dg4_ref, dg3_ref, dh_ref, dmid_ref, da_ref = rest[:6]
    up_refs, down_refs, head_refs = [rest[6 + each * i : 6 + each * i + each] for i in range(3)]
    mid_scr, norm_scr, normt_scr, cot_scr, acc_scr, up_scr = rest[6 + 3 * each : 12 + 3 * each]
    w_scr = rest[12 + 3 * each :]
    up_w, down_w = w_scr if split else (uw_refs[0], dw_refs[0])
    down_rows = slice(0, 4 * TILE)
    step = pl.program_id(0)
    core = info[CORE]

    @pl.when(step == 0)
    def _():
        settle(uw_refs, w_scr and w_scr[0], info, False)
        settle(dw_refs, w_scr and w_scr[1], info, True)
        middle = x_ref[...] + nn(a_ref[...], tile_of(up_w, 4))
        mid_scr[...] = middle
        normed = (norm_parts(middle)[0] * gain_ref[3:4, :]).astype(BF16)
        norm_scr[...] = normed
        normt_scr[...] = normed.T
        total = mid_scr[...]
        for chunk in range(FF // D):
            up = nn(normed, tile_of(up_w, chunk))
            hidden = (up * gelu_parts(up)[1]).astype(BF16)
            total = total + nn(hidden, down_w[8 * chunk : 8 * chunk + 8, down_rows, :].reshape(D, D))
        for piece, lanes in enumerate(LANES):
            spread(up_scr, (piece,), total[:, lanes])
        gain = gain_ref[4:5, :]
        hat, scale = norm_parts(h_ref[...] + jnp.concatenate([up_scr[piece] for piece in range(len(LANES))], 1))
        final = (hat * gain).astype(BF16)
        head = tile_of(down_w, 4)[:, :VOCAB]
        logits = nn(final, head)
        top = jnp.max(logits, -1, keepdims=True)
        log_total = top + jnp.log(jnp.sum(jnp.exp(logits - top), -1, keepdims=True))
        hot = target_ref[...] == lax.broadcasted_iota(jnp.int32, logits.shape, 1)
        picked = jnp.sum(jnp.where(hot, logits, 0.0), -1, keepdims=True)
        counted = counted_ref[...]
        loss = jnp.sum((log_total - picked) * counted, 0, keepdims=True) * (1.0 / LOG_TWO)
        loss_ref[...] = jnp.broadcast_to(loss, (1, 128))
        grad = ((jnp.exp(logits - log_total) - jnp.where(hot, 1.0, 0.0)) * (counted * rate_ref[0, 0])).astype(BF16)
        dhead = nn(final.T, grad)
        put(head_refs, core, jnp.concatenate([dhead, jnp.zeros((D, D - VOCAB), F32)], 1))
        pulled, dgain = norm_pull(hat, scale, gain, nt(grad, head))
        dg4_ref[...] = dgain
        dh_ref[...] = pulled
        for piece, lanes in enumerate(LANES):
            up_scr[piece] = pulled[:, lanes]
            cot_scr[:, lanes] = thirds(up_scr, (piece,), 0)
        acc_scr[...] = jnp.zeros_like(acc_scr)

    @pl.when(step > 0)
    def _():
        chunk = step - 1
        down_in = cot_scr[...].astype(BF16)
        up_tile = up_w[:, pl.ds(pl.multiple_of(chunk * TILE, TILE), TILE), :].reshape(D, D)
        up = nn(norm_scr[...], up_tile)
        wave, gate = gelu_parts(up)
        hidden = (up * gate).astype(BF16)
        up_in = (nt(down_in, down_w[pl.ds(chunk * 8, 8), down_rows, :].reshape(D, D)) * gelu_slope(up, wave, gate)).astype(BF16)
        put(down_refs, core, nn(hidden.T, down_in), rows=4 * TILE, chunk=chunk)
        put(up_refs, core, nn(normt_scr[...], up_in))
        acc_scr[...] += nt(up_in, up_tile)

    @pl.when(step == FF // D)
    def _():
        hat, scale = norm_parts(mid_scr[...])
        pulled, dgain = norm_pull(hat, scale, gain_ref[3:4, :], acc_scr[...])
        dg3_ref[...] = dgain
        dmid = cot_scr[...] + pulled
        dmid_ref[...] = dmid
        out_in = dmid.astype(BF16)
        put(down_refs, core, nn(a_ref[...].T, out_in), at=4 * TILE)
        da_ref[...] = nt(out_in, tile_of(up_w, 4)).astype(BF16)


def short_rest(info, z, a, h, bundles, gains, target, counted, rate, split):
    ins = [info, z, a, h, *bundles[0], *bundles[1], gains, target, counted, rate]
    specs = [held(i.shape) for i in ins[1:]]
    specs[0] = pl.BlockSpec((CSPAN, D), lambda *_: (1, 0))
    specs[2] = pl.BlockSpec((SPAN, D), lambda *_: (1, 0))
    specs[-1] = pl.BlockSpec(memory_space=pltpu.SMEM)
    return call(
        partial(short_body, split=split),
        "short_rest",
        [shape((1, 128)), shape((1, D)), shape((1, D)), shape((SPAN, D)), shape((CSPAN, D)), shape((CSPAN, D), BF16)]
        + grad_shapes(4 * TILE, split)
        + grad_shapes(5 * TILE, split)
        + grad_shapes(TILE, split),
        ins,
        12,
        grid=(FF // D + 1,),
        in_specs=specs,
        out_specs=[whole((1, 128)), whole((1, D)), whole((1, D)), whole((SPAN, D)), whole((CSPAN, D)), whole((CSPAN, D))]
        + grad_specs(TILE, split, lambda i, _: (0, jnp.maximum(i - 1, 0), 0))
        + grad_specs(5 * TILE, split, lambda i, _: (0, 0, 0))
        + grad_specs(TILE, split, lambda i, _: (0, 0, 0)),
        scratch=[
            pltpu.VMEM((CSPAN, D), F32),
            pltpu.VMEM((CSPAN, D), BF16),
            pltpu.VMEM((D, CSPAN), BF16),
            pltpu.VMEM((CSPAN, D), F32),
            pltpu.VMEM((CSPAN, D), F32),
            pltpu.VMEM((D // 128, SPAN, 128), F32),
            *bundle_scratch(bundles, (5 * TILE, 5 * TILE)),
        ],
    )


def project_back_body(info, *refs, full, split, groups):
    refs = list(refs)
    take = lambda n: [refs.pop(0) for _ in range(n)]
    dqs, keeps, recvs = take(groups), take(groups), take(groups)
    dmid_ref, x_ref = take(2)
    if full:
        (token_ref,) = take(1)
        wa_refs, wb_refs = [take(WEIGHT_PARTS if split else 1) for _ in range(2)]
        dg_refs = take(4)
    else:
        wa_refs, wb_refs = [take(WEIGHT_PARTS if split else 1) for _ in range(2)]
    wa_ref = settle(wa_refs, refs[-2], info, False, 0 if full else 4 * TILE)
    wb_ref = settle(wb_refs, refs[-1], info, True, 0 if full else 5 * TILE)
    weight = [tile_of(wa_ref, 0), tile_of(wa_ref, 1), tile_of(wb_ref, 0)]
    gain_ref, cos_ref, sin_ref = take(3)
    each = 2 if split else 1
    first_refs = take(each)
    if not full or not split:
        dgain_ref, dx_ref = take(2)
    if not full:
        (edge_ref,) = take(1)
    core = info[CORE]
    gain = gain_ref[0:1, :] if full else gain_ref[2:3, :]
    hat, scale = norm_parts(x_ref[...].astype(F32))
    normed_t = (hat * gain).astype(BF16).T
    cosine, sine = cos_ref[...], sin_ref[...]
    rows = hat.shape[0]
    skip = rows - dqs[0].shape[0]
    total = jnp.zeros((rows, D), F32)
    for kind in range(3):
        if kind == 0:
            grad = jnp.concatenate([dq[...] for dq in dqs], 1) if groups > 1 else dqs[0][...]
            grad = rope_pull(grad * 0.125, cosine[skip:], sine[skip:]).astype(BF16)
            found = nn(normed_t[:, skip:], grad)
        else:
            both = [(keep[kind - 1] + recv[kind - 1].astype(F32)).T for keep, recv in zip(keeps, recvs)]
            grad = jnp.concatenate(both, 1) if groups > 1 else both[0]
            grad = (rope_pull(grad, cosine, sine) if kind == 1 else grad).astype(BF16)
            found = nn(normed_t, grad)
        put(first_refs, core, found, at=TILE * kind)
        back = nt(grad, weight[kind])
        if kind == 0 and skip:
            back = jnp.concatenate([jnp.zeros((skip, D), F32), back], 0)
        total = total + back
    pulled, dgain = norm_pull(hat, scale, gain, total)
    if not full:
        dgain_ref[...] = dgain
        dx = jnp.concatenate([pulled[:skip], dmid_ref[...] + pulled[skip:]], 0)
        dx_ref[...] = dx
        for slot in range(2):
            edge_ref[slot] = dx[CSPAN * slot : CSPAN * slot + 8]
        return
    back = (dmid_ref[...] + pulled).astype(BF16)
    hot = (token_ref[...] == lax.broadcasted_iota(jnp.int32, (VOCAB, rows), 0)).astype(BF16)
    dembed = nn(hot, back)
    if not split:
        dgain_ref[...] = dgain
        dx_ref[...] = dembed
        return
    dgains = jnp.concatenate([dgain] + [ref[...] for ref in dg_refs] + [jnp.zeros((3, D), F32)], 0)
    lane = lax.broadcasted_iota(jnp.int32, (8, D), 1)
    sides = [
        jnp.where(lane < TILE, dgains if j == 0 else pltpu.roll(dgains, D - TILE * j, 1), 0.0) for j in range(SHARDS)
    ]
    embeds = dembed.reshape(SHARDS, 8, D)
    for chip in range(SHARDS // 2):
        for part, values in ((slice(3 * TILE, 3 * TILE + 8), embeds), (slice(3 * TILE + 8, 4 * TILE), sides)):
            low, high = values[2 * chip], values[2 * chip + 1]
            first_refs[0][chip, part, :] = jnp.where(core == 0, low, high)
    first_refs[1][:, 3 * TILE :, :] = jnp.stack(
        [
            jnp.where(
                core == 0,
                jnp.concatenate([embeds[2 * chip + 1], sides[2 * chip + 1]], 0),
                jnp.concatenate([embeds[2 * chip], sides[2 * chip]], 0),
            ).astype(BF16)
            for chip in range(SHARDS // 2)
        ],
        0,
    )


def project_back(info, dqs, keeps, recvs, dmid, x, extra, bundles, dgs, gains, cosine, sine, full, split):
    groups = len(dqs)
    rows = cosine.shape[0]
    weights = [value for bundle in bundles for value in bundle]
    ins = [info, *dqs, *keeps, *recvs, dmid, x, *extra, *weights, *dgs, gains, cosine, sine]
    specs = [held(i.shape) for i in ins[1:]]
    scratch = bundle_scratch(bundles, (2 * TILE, TILE))
    if full:
        outs = grad_shapes(4 * TILE if split else 3 * TILE, split)
        if not split:
            outs += [shape((1, D)), shape((VOCAB, D))]
    else:
        outs = grad_shapes(3 * TILE, split) + [shape((1, D)), shape((rows, D)), shape((2, 8, D))]
    return call(
        partial(project_back_body, full=full, split=split, groups=groups),
        "project_back",
        outs,
        ins,
        10 if full else 5,
        in_specs=specs,
        scratch=scratch,
    )


def fold_body(info, *refs, layout):
    refs = list(refs)
    outs = refs[4 * sum(len(rows) for rows in layout) :]
    for order, rows in enumerate(layout):
        at = 0
        for count in rows:
            keep, far, recv, far_recv = [refs.pop(0) for _ in range(4)]
            lead = outs[2 * order].shape[0]
            part = slice(at, at + count)
            flat = lambda ref: ref[...].reshape(lead, count, D)
            outs[2 * order][:, part, :] = flat(keep) + flat(recv).astype(F32)
            outs[2 * order + 1][:, part, :] = (flat(far) + flat(far_recv).astype(F32)).astype(BF16)
            at += count


def fold(info, orders, steps, us):
    ins, specs, outs, out_specs, layout = [info], [], [], [], []
    for sources, pre, post, bit in orders:
        sources = [source if len(source) == 4 else (0, *source, source[0].shape[-2]) for source in sources]
        layout.append([rows for *_, rows in sources])
        for place, keep, recv, rows in sources:
            dims = (pre, 2, post, keep.shape[-2], D)
            for value in (keep, recv):
                for other in (0, 1):
                    ins.append(value.reshape(dims))
                    inner = max(steps // pre, 1)
                    specs.append(
                        pl.BlockSpec(
                            (max(pre // steps, 1), 1, post // inner, rows, D),
                            lambda i, info, other=other, bit=bit, inner=inner, place=place: (
                                i // inner, jnp.abs(info[BITS + bit] - other), i % inner, place, 0
                            ),
                        )
                    )
        total = sum(layout[-1])
        for kind in (F32, BF16):
            outs.append(shape((pre * post, total, D), kind))
            out_specs.append(pl.BlockSpec((pre * post // steps, total, D), lambda i, _: (i, 0, 0)))
    found = call(
        partial(fold_body, layout=layout), "fold", outs, ins, us, grid=(steps,), in_specs=specs, out_specs=out_specs
    )
    return [(found[2 * i], found[2 * i + 1]) for i in range(len(orders))]


CORE_BIT, Y_BIT, X_BIT, Z0_BIT, Z1_BIT = range(5)


ALONG_XY_FIRST = (
    ((X_BIT, 4, 2), (Y_BIT, 8, 1), 8),
    ((Y_BIT, 4, 1), (X_BIT, 4, 1), 4),
    ((Z0_BIT, 2, 1), 2),
    ((Z1_BIT, 1, 1), 1),
)
ALONG_Z_FIRST = (((Z0_BIT, 2, 4), 8), ((Z1_BIT, 1, 4), 4), ((X_BIT, 1, 2), 2), ((Y_BIT, 1, 1), 1))


def across(keep, send):
    return keep, swapped(send, CORE_BIT)


class Scatter:
    def __init__(self, firsts, seconds=None):
        groups = (firsts,) if seconds is None else (firsts, seconds)
        self.values = [[across(*pair) if len(pair) == 2 else pair for pair in sources] for sources in groups]
        self.stages = list(ALONG_Z_FIRST if seconds is None else ALONG_XY_FIRST)

    def plan(self):
        *plans, steps = self.stages.pop(0)
        if len(plans) == 1:
            self.values = [[pair for sources in self.values for pair in sources]]
        orders = [(sources, pre, post, bit) for sources, (bit, pre, post) in zip(self.values, plans)]
        return orders, steps

    def folded(self, found, bits):
        self.values = [[(keep, swapped(send, bit))] for (keep, send), bit in zip(found, bits)]

    def kept(self):
        return [keep for sources in self.values for keep, _ in sources]


def step_all(info, *needed):
    def step(*scatters):
        plans = [scatter.plan() for scatter in scatters]
        orders = [order for plan, _ in plans for order in plan]
        found = fold(after(info, needed) if needed else info, orders, min(steps for _, steps in plans), 0.05)
        for scatter, (plan, _) in zip(scatters, plans):
            scatter.folded([found.pop(0) for _ in plan], [bit for *_, bit in plan])

    return step


def after(value, *needed):
    return lax.optimization_barrier((value, needed))[0]


DECAY = 1.0 - STEP ** (-0.8)
MATRICES = (
    [(VOCAB, 1, D), (D, 1, VOCAB)] + [(D, 3, 3 * D)] * 2 + [(D, 1, D)] * 2 + [(D, 4, FF)] * 2 + [(FF, 1, D)] * 2
)
TILES = sum(count for _, count, _ in MATRICES)
STAT_ROWS = 48


def as_column(row):
    return jnp.broadcast_to(row, (128, row.shape[1])).T[:, 0:1]


def as_row(column):
    return jnp.broadcast_to(column, (column.shape[0], 128)).T[0:1, :]


def tile_lanes(width, index):
    return slice(D * index, min(D * index + D, width))


def measure_body(info, *refs):
    refs = list(refs)
    take = lambda n: [refs.pop(0) for _ in range(n)]
    late, middle, early = [keep[0] + recv[0].astype(F32) for keep, recv in [take(2) for _ in range(3)]]
    row_refs, weight_refs = take(6), take(6)
    gain_ref, sq_ref, loss_ref = take(3)
    grad_refs, new_row_refs = take(6), take(6)
    gain_grad_ref, new_sq_ref, stat_ref = take(3)
    early_a, early_b = early[: 2 * TILE], early[2 * TILE :]
    cut = lambda value, start, count=1, size=TILE: [value[start + size * i : start + size * i + size] for i in range(count)]
    grads = [
        [early_b[TILE : TILE + 8]],
        [middle[12 * TILE :, :VOCAB]],
        cut(early_a, 0, 2) + cut(early_b, 0),
        cut(middle, 4 * TILE, 3),
        cut(middle, 11 * TILE),
        cut(late, 8 * TILE),
        cut(middle, 0, 4),
        cut(late, 0, 4),
        cut(middle, 7 * TILE, size=4 * TILE),
        cut(late, 4 * TILE, size=4 * TILE),
    ]
    lane = lax.broadcasted_iota(jnp.int32, (1, D), 1)
    scalars = jnp.where(lane == 30, loss_ref[0:1, 0:1], 0.0)
    total = lambda value: jnp.sum(jnp.sum(value, 1, keepdims=True), 0, keepdims=True)
    stat_ref[...] = jnp.zeros_like(stat_ref)
    at = 0
    for index, (pieces, (_, _, width)) in enumerate(zip(grads, MATRICES)):
        kind, layer = (index, None) if index < 2 else (2 + (index - 2) // 2, index % 2)
        old = row_refs[kind][...] if layer is None else row_refs[kind][layer : layer + 1, :]
        weight = weight_refs[kind][...] if layer is None else weight_refs[kind][layer]
        squares = [piece * piece for piece in pieces]
        mean = sum(jnp.sum(square, 1, keepdims=True) for square in squares) * (1.0 / width)
        new_row = DECAY * as_column(old) + (1.0 - DECAY) * mean
        inverse = 1.0 / new_row
        new_rows = as_row(new_row)
        if layer is None:
            new_row_refs[kind][...] = new_rows
        else:
            new_row_refs[kind][layer : layer + 1, :] = new_rows
        for place, (piece, square) in enumerate(zip(pieces, squares)):
            lanes = tile_lanes(width, place)
            if layer is None:
                grad_refs[kind][:, lanes] = piece
            else:
                grad_refs[kind][layer, :, lanes] = piece
            own = slice(0, piece.shape[1])
            stat_ref[at : at + 1, own] = jnp.sum(square, 0, keepdims=True)
            stat_ref[TILES + at : TILES + at + 1, own] = jnp.sum(square * inverse, 0, keepdims=True)
            at += 1
        scalars = jnp.where(lane == 2 * index, total(new_row), scalars)
        scalars = jnp.where(lane == 2 * index + 1, total(weight * weight), scalars)
    gain_grad = early_b[TILE + 8 : TILE + 13, :TILE]
    gain_grad_ref[...] = gain_grad
    new_sq = DECAY * sq_ref[...] + (1.0 - DECAY) * gain_grad * gain_grad
    new_sq_ref[...] = new_sq
    gains = gain_ref[...]
    update = gain_grad / jnp.sqrt(new_sq)
    for value, start in ((update, 20), (gains, 25)):
        each = jnp.sum(value * value, 1, keepdims=True)
        for row in range(5):
            scalars = jnp.where(lane == start + row, each[row : row + 1], scalars)
    stat_ref[2 * TILES : 2 * TILES + 1, :] = scalars


def update_body(info, *refs):
    refs = list(refs)
    take = lambda n: [refs.pop(0) for _ in range(n)]
    (stat_ref,) = take(1)
    grad_refs, row_refs, col_refs, weight_refs = take(6), take(6), take(6), take(6)
    gain_ref, gain_grad_ref, sq_ref = take(3)
    new_col_refs, new_refs = take(6), take(6)
    gain_new_ref, loss_ref = take(2)
    scalars = stat_ref[2 * TILES : 2 * TILES + 1, :]
    scalar = lambda lane: scalars[:, lane : lane + 1]
    loss_ref[...] = scalar(30)
    at = 0
    for index, (rows, count, width) in enumerate(MATRICES):
        kind, layer = (index, None) if index < 2 else (2 + (index - 2) // 2, index % 2)
        mean_row = scalar(2 * index) * (1.0 / rows)
        size = rows * width
        new_row = as_column(row_refs[kind][...] if layer is None else row_refs[kind][layer : layer + 1, :])
        pieces, spread_sum = [], jnp.zeros((1, 1), F32)
        for place in range(count):
            lanes = tile_lanes(width, place)
            own = slice(0, lanes.stop - lanes.start)
            here = slice(0, 1) if layer is None else slice(layer, layer + 1)
            new_col = DECAY * col_refs[kind][here, lanes] + (1.0 - DECAY) * stat_ref[at : at + 1, own] * (1.0 / rows)
            new_col_refs[kind][here, lanes] = new_col
            spread_sum = spread_sum + jnp.sum(stat_ref[TILES + at : TILES + at + 1, own] / new_col, 1, keepdims=True)
            pieces.append((lanes, new_col))
            at += 1
        update_sum = mean_row * spread_sum
        rate = RATE_SCALE * jnp.sqrt(scalar(2 * index + 1) * (1.0 / size))
        rate = rate / jnp.maximum(1.0, jnp.sqrt(update_sum * (1.0 / size)))
        for lanes, new_col in pieces:
            if layer is None:
                grad, weight = grad_refs[kind][:, lanes], weight_refs[kind][:, lanes]
            else:
                grad, weight = grad_refs[kind][layer, :, lanes], weight_refs[kind][layer, :, lanes]
            found = weight - rate * (grad / jnp.sqrt(new_row * new_col / mean_row))
            if layer is None:
                new_refs[kind][:, lanes] = found
            else:
                new_refs[kind][layer, :, lanes] = found
    gains, gain_grad = gain_ref[...], gain_grad_ref[...]
    update = gain_grad / jnp.sqrt(sq_ref[...])
    for row in range(5):
        here = slice(row, row + 1)
        rate = RATE_SCALE * jnp.sqrt(scalar(25 + row) * (1.0 / D)) / jnp.maximum(1.0, jnp.sqrt(scalar(20 + row) * (1.0 / D)))
        gain_new_ref[here, :] = gains[here] - rate * update[here]


def optimize(info, sums, rows, cols, weights, gains, gains_sq, loss):
    flat = lambda values: [value[None] if value.ndim == 1 else value for value in values]
    rows, cols = flat(rows), flat(cols)
    same = lambda values: [shape(value.shape) for value in values]
    found = call(
        measure_body,
        "measure",
        same(weights) + same(rows) + [shape(gains.shape), shape(gains.shape), shape((STAT_ROWS, D))],
        [info, *[value for pair in sums for value in pair], *rows, *weights, gains, gains_sq, loss],
        0.05,
    )
    grads, new_rows, (gain_grad, new_sq, stats) = found[:6], found[6:12], found[12:]
    stats = sum_all(stats)
    found = call(
        update_body,
        "update",
        same(cols) + same(weights) + [shape(gains.shape), shape((1, 1))],
        [info, stats, *grads, *new_rows, *cols, *weights, gains, gain_grad, new_sq],
        0.05,
    )
    new_cols, new_weights, (gains_new, loss_sum) = found[:6], found[6:12], found[12:]
    outputs = []
    for index in range(6):
        plain = (lambda value: value[0]) if index < 2 else (lambda value: value)
        outputs += [grads[index], plain(new_rows[index]), plain(new_cols[index]), new_weights[index]]
    return [loss_sum[0, 0]], outputs + [gain_grad, new_sq, gains_new]


def flat_index():
    return lax.axis_index("dp") * lax.axis_size("seq") + lax.axis_index("seq")


def flat_count():
    return lax.axis_size("dp") * lax.axis_size("seq")


def swapped(value, bit):
    return lax.ppermute(value, BOTH, [(i, i ^ (1 << bit)) for i in range(flat_count())])


def bit_of(bit):
    return (flat_index() >> bit) & 1


def join_body(info, *refs):
    count = len(refs) // 3
    for index, out in enumerate(refs[2 * count :]):
        here, there = refs[2 * index : 2 * index + 2]
        rows = here.shape[0]
        out[:rows] = here[...]
        out[rows:] = there[...]


def join_pairs(info, pairs):
    outs = [shape((2 * here.shape[0], *here.shape[1:]), here.dtype) for here, _ in pairs]
    return call(join_body, "join", outs, [info, *[value for pair in pairs for value in pair]], 0.05)


class Gather:
    def __init__(self, packed):
        self.values = [packed[None]]
        self.near = None
        self.info = jnp.zeros((1,), jnp.int32)

    def send(self, *bits, needed=()):
        if needed:
            self.values = [after(value, *needed) for value in self.values]
        self.coming = [swapped(value, bit) for value, bit in zip(self.values, bits)]
        return self

    def pairs(self, needed):
        pairs = list(zip(self.values, self.coming))
        return lax.optimization_barrier((pairs, list(needed)))[0]

    def join(self, split=None, needed=()):
        pairs = self.pairs(needed)
        if split is not None:
            ((here, there),) = pairs
            pairs = [(here[:, :split], there[:, :split]), (here[:, split:], there[:, split:])]
        small = pairs[0][0].shape[0] * pairs[0][0].shape[1] < 256
        self.values = [jnp.concatenate(pair, 0) for pair in pairs] if small else join_pairs(self.info, pairs)
        return self

    def send_last(self, *bits, needed=()):
        self.send(*bits, needed=needed)
        self.near = [swapped(value, CORE_BIT) for value in self.values]
        return self

    def last(self, needed=()):
        self.values = self.pairs(needed)
        if self.near is None:
            self.near = [swapped(here, CORE_BIT) for here, _ in self.values]
        return [
            (here, there, near, swapped(there, CORE_BIT)) for (here, there), near in zip(self.values, self.near)
        ]


def group_perm(ways, links):
    count = lax.axis_size("seq")
    return [(base + a, base + b) for base in range(0, count, ways) for a, b in links]


def window_keys(kv, ways):
    if ways == 2:
        return [kv, lax.ppermute(kv, "seq", group_perm(2, ((0, 1), (1, 0))))]
    groups = [list(range(base, base + ways)) for base in range(0, lax.axis_size("seq"), ways)]
    found = []
    for value in (kv[0], kv[1]):
        every = lax.all_gather(value, "seq", axis=0, tiled=False, axis_index_groups=groups)
        rows = every.shape[1] // 2
        blocks = [every[w, :rows] for w in range(ways)] + [every[w, rows:] for w in reversed(range(ways))]
        found.append(jnp.concatenate(blocks, 0))
    return found


def window_sum(grads, ways):
    if ways == 2:
        keep, send = grads
        return keep, lax.ppermute(send, "seq", group_perm(2, ((0, 1), (1, 0))))
    groups = [list(range(base, base + ways)) for base in range(0, lax.axis_size("seq"), ways)]
    total = lax.psum_scatter(grads[0], "seq", scatter_dimension=0, tiled=False, axis_index_groups=groups)
    return total, jnp.zeros(total.shape, BF16)


def from_sides(first, second, ways):
    if ways == 2:
        rank = lax.axis_index("seq") % ways
        other = lax.ppermute(jnp.where(rank == 0, first, second), "seq", group_perm(2, ((0, 1), (1, 0))))
        zero = jnp.zeros_like(other)
        return jnp.where(rank == 0, zero, other), jnp.where(rank == 0, other, zero)
    up = [(i, i + 1) for i in range(ways - 1)]
    down = [(i + 1, i) for i in range(ways - 1)]
    return lax.ppermute(first, "seq", group_perm(ways, up)), lax.ppermute(second, "seq", group_perm(ways, down))


def sum_all(value):
    count = flat_count()
    for bit in range(count.bit_length() - 1):
        value = value + swapped(value, bit)
    return value


def tiles(weight):
    rows = weight.shape[0]
    return [weight[:, start : start + D] for start in range(0, weight.shape[1], D)] if rows else []


def pack_edge(embed, gains):
    rows = embed.shape[-2]
    pad = jnp.zeros((8, D - gains.shape[1]), gains.dtype)
    side = jnp.concatenate([jnp.concatenate([gains, jnp.zeros((3, gains.shape[1]), gains.dtype)], 0), pad], 1)
    return jnp.concatenate([embed, side], 0)


def gather_weights(embed, head, attn_in, attn_out, ffn_in, ffn_out, gains):
    full = [
        lax.all_gather(weight, BOTH, axis=axis, tiled=True)
        for weight, axis in ((embed, 0), (head, 0), (attn_in, 1), (attn_out, 1), (ffn_in, 1), (ffn_out, 1), (gains, 1))
    ]
    embed, head, attn_in, attn_out, ffn_in, ffn_out, gains = full
    fold_rows = lambda weight: weight.reshape(SHARDS, TILE, D)
    edge = jnp.zeros((SHARDS, TILE, D), BF16).at[:, :8].set(embed.reshape(SHARDS, 8, D))
    edge = edge.at[:, 8:13, :TILE].set(gains.reshape(5, SHARDS, TILE).transpose(1, 0, 2))
    head_tile = jnp.zeros((SHARDS, TILE, D), BF16).at[:, :, :VOCAB].set(head.reshape(SHARDS, TILE, VOCAB))
    down = ffn_out.reshape(2, SHARDS, 4 * TILE, D)
    side = [[fold_rows(t) for t in tiles(attn_in[i])] for i in range(2)]
    up = [[fold_rows(t) for t in tiles(ffn_in[i])] for i in range(2)]
    firsts = [jnp.concatenate(side[0][:2], 1), jnp.concatenate([side[0][2], edge], 1)]
    seconds = [
        jnp.concatenate(up[0] + side[1][:2], 1),
        jnp.concatenate([down[0], fold_rows(attn_out[0]), side[1][2]], 1),
    ]
    third = [jnp.concatenate(up[1] + [fold_rows(attn_out[1])], 1), jnp.concatenate([down[1], head_tile], 1)]
    return firsts, seconds, third


def reduce_natural(grad, axis):
    return lax.psum_scatter(grad, BOTH, scatter_dimension=axis, tiled=True)


def unfold(packed):
    parts = packed.shape[1] // TILE
    return jnp.concatenate([packed[:, TILE * i : TILE * i + TILE].reshape(D, D) for i in range(parts)], 1)


def local(
    stream, offsets, embed, head, attn_in, attn_out, ffn_in, ffn_out, gains,
    embed_row, embed_col, head_row, head_col, in_row, in_col, out_row, out_col, up_row, up_col, down_row, down_col, gains_sq,
):
    seq_rank = lax.axis_index("seq")
    dp_rank = lax.axis_index("dp")
    seq_count = lax.axis_size("seq")
    per_group = offsets.shape[0] // lax.axis_size("dp")
    ways = seq_count // per_group
    blocks = 2 * ways
    length = SPAN * blocks
    rank = seq_rank % ways
    split = flat_count() == SHARDS
    if split:
        low = lambda *values: [value.astype(BF16) for value in values]
        embed_low, gains_low, in_low = low(embed, gains, attn_in[0])
        one = Gather(jnp.concatenate(tiles(in_low) + [pack_edge(embed_low, gains_low)], 0))
        up_low, down_low, out_low, in_low = low(*after((ffn_in[0], ffn_out[0], attn_out[0], attn_in[1]), one.values))
        in_low = tiles(in_low)
        two = Gather(jnp.concatenate(tiles(up_low) + in_low[:2] + [down_low, out_low, in_low[2]], 0))
        one.send(Z1_BIT).join()
        two.send(Z1_BIT, needed=one.values)
        up_low, down_low, out_low, head_low = low(*after((ffn_in[1], ffn_out[1], attn_out[1], head), one.values))
        head_low = jnp.concatenate([head_low, jnp.zeros_like(head_low)], 1)
        three = Gather(jnp.concatenate(tiles(up_low) + [out_low, down_low, head_low], 0))
        one.send(Z0_BIT).join(2 * TILE)
        two.join().send(Z0_BIT, needed=one.values)
        one.send(X_BIT, Y_BIT).join()
        offsets_then, stream_then = after((offsets, stream), two.values)
        two.join(6 * TILE)
        three.send(Z1_BIT, needed=one.values)
        one.send_last(Y_BIT, X_BIT)
        three.join()
        first = one.last()
        two.send(X_BIT, Y_BIT, needed=one.values)
    else:
        low = [w.astype(BF16) for w in (embed, head, attn_in, attn_out, ffn_in, ffn_out, gains)]
        first, second, third = gather_weights(*low)
        first, second, third = [[(value,) for value in pair] for pair in (first, second, third)]
        offsets_then, stream_then = offsets, stream

    window_start = offsets_then[dp_rank * per_group + seq_rank // ways]
    limits = jnp.minimum(length, STREAM - 1 - offsets_then) - (length - length // 2)
    count_real = jnp.sum(jnp.maximum(limits, 0)).astype(F32)
    own_blocks = jnp.stack([rank, blocks - 1 - rank]) + 0 * window_start
    positions = (own_blocks[:, None] * SPAN + jnp.arange(SPAN, dtype=jnp.int32)[None]).reshape(-1)
    coarse_pos = (own_blocks[:, None] * CSPAN + jnp.arange(CSPAN, dtype=jnp.int32)[None]).reshape(-1)
    reach = own_blocks + 1
    info = jnp.concatenate(
        [reach, jnp.stack([rank, flat_index() & 1] + [bit_of(bit) for bit in range(5)] + [flat_index() >> 1])], 0
    ).astype(jnp.int32)
    starts = window_start + own_blocks * SPAN
    padded = jnp.concatenate([stream_then, jnp.broadcast_to(stream_then[-1:], (length,))], 0)
    tokens = jnp.concatenate([lax.dynamic_slice_in_dim(padded, starts[s], SPAN, 0) for s in range(2)], 0)
    target = lax.dynamic_slice_in_dim(padded, starts[1] + 1, SPAN, 0)
    counted = (window_start + positions[SPAN:] + 1 < STREAM).astype(F32)
    rate = (1.0 / (LOG_TWO * count_real)).reshape(1, 1)

    def tables(at):
        frequency = 10000.0 ** (-jnp.arange(HD // 2, dtype=F32) / (HD // 2))
        angles = at.astype(F32)[:, None] * frequency[None, :]
        cosine, sine = jnp.cos(angles), jnp.sin(angles)
        return (jnp.concatenate([cosine] * 4, 1), jnp.concatenate([-sine, sine] * 2, 1))

    cos_0, sin_0 = tables(positions)
    cos_1, sin_1 = tables(coarse_pos)

    token_col, target_col, counted_col = tokens[:, None], target[:, None], counted[:, None]
    if split:
        token_col = after(token_col, target_col, counted_col, rate, cos_1, sin_1, three.values)
    h_0, q_0, kv_0, gain_rows = project(info, token_col, first, cos_0, sin_0)
    if split:
        two.join(needed=[q_0]).send_last(Y_BIT, X_BIT)
        three.send(Z0_BIT)
        kv_0 = after(kv_0, two.values)
    keys_0 = window_keys(kv_0, ways)
    a_lo, lse_lo = attend(info, q_0, keys_0, SPAN, 0, 1)
    if split:
        three.join(5 * TILE, needed=[a_lo]).send(X_BIT, Y_BIT)
    a_hi, lse_hi = attend(info, after(q_0, a_lo, three.values, two.near) if split else q_0, keys_0, SPAN, 1, 1)
    if split:
        three.join(needed=[a_hi])
        second = two.last([a_hi, *three.values])
        three.send(Y_BIT, X_BIT)
    m_0, h_1, tail = branch(info, after(h_0, three.values) if split else h_0, (a_lo, a_hi), second, gain_rows)

    z_0, q_1, kv_1 = project_short(
        info, h_1, tail, *from_sides(tail[0], tail[1], ways), second, gain_rows, cos_1, sin_1, ways
    )
    keys_1 = window_keys(kv_1, ways)
    a_1, lse_1 = attend(info, q_1, keys_1, CSPAN, 0, 2)
    if split:
        third = three.last([a_1])
    found = short_rest(info, z_0, a_1, h_1, third, gain_rows, target_col, counted_col, rate, split)
    loss, dg_4, dg_3, d_h2, d_m1, d_a1 = found[:6]
    each = 2 if split else 1
    d_up_1, d_down_1, d_head = [found[6 + each * i : 6 + each * i + each] for i in range(3)]
    if split:
        late = Scatter([d_up_1, d_down_1])
    d_q1, *d_kv1 = attend_back(info, q_1, keys_1, d_a1, lse_1, CSPAN, 0, 2)
    if split:
        step_all(info, d_q1)(late)
        d_m1 = after(d_m1, late.kept())
    keep, recv = window_sum(d_kv1, ways)
    found = project_back(info, [d_q1], [keep], [recv], d_m1, z_0, [], second, [], gain_rows, cos_1, sin_1, False, split)
    d_in_1, (dg_2, d_z0, edge) = found[:each], found[each:]

    low_edge, high = from_sides(edge[1], edge[0], ways)
    if split:
        in_pair, head_pair = across(*d_in_1), across(*d_head)
        d_h2 = after(d_h2, in_pair, head_pair)
    found = branch_back(info, d_z0, edge, high, low_edge, d_h2, m_0, (a_lo, a_hi), second, gain_rows, ways, split)
    d_m0, da_lo, da_hi, dg_1 = found[:4]
    d_up_0, d_down_0 = [found[4 + each * i : 4 + each * i + each] for i in range(2)]
    if split:
        step_all(info, d_m0)(late)
        d_up_0, d_down_0 = after((tuple(d_up_0), tuple(d_down_0)), late.kept())
        middle = Scatter([d_up_0, (0, *in_pair, 3 * TILE)], [d_down_0, (0, *head_pair, TILE)])
        step_all(info)(middle)
        da_lo = after(da_lo, middle.kept())
    dq_lo, *dkv_lo = attend_back(info, q_0, keys_0, da_lo, lse_lo, SPAN, 0, 1)
    if split:
        da_hi = after(da_hi, dq_lo)
    sum_lo = window_sum(dkv_lo, ways)
    dq_hi, *dkv_hi = attend_back(info, q_0, keys_0, da_hi, lse_hi, SPAN, 1, 1)
    if split:
        step_all(info, dq_hi, sum_lo, late.values)(middle)
        dkv_hi = after(tuple(dkv_hi), middle.kept())
    sum_hi = window_sum(dkv_hi, ways)
    found = project_back(
        info, [dq_lo, dq_hi], [sum_lo[0], sum_hi[0]], [sum_lo[1], sum_hi[1]], d_m0, h_0, [tokens[None, :]], first,
        [dg_1, dg_2, dg_3, dg_4], gain_rows, cos_0, sin_0, True, split,
    )

    if split:
        pair = across(*after(tuple(found[:2]), middle.values))
        early = Scatter([(0, *pair, 2 * TILE)], [(1, *pair, 2 * TILE)])
        step_all(info)(middle)
        step_all(info, middle.kept())(early, late)
        step_all(info, early.kept())(early)
        step_all(info, early.kept())(middle, late)
        step_all(info, middle.kept())(early)
        step_all(info)(early)
        loss_sum, outputs = optimize(
            info,
            [sources[0] for sources in late.values + middle.values + early.values],
            [embed_row, head_row, in_row, out_row, up_row, down_row],
            [embed_col, head_col, in_col, out_col, up_col, down_col],
            [embed, head, attn_in, attn_out, ffn_in, ffn_out],
            gains,
            gains_sq,
            loss,
        )
        return (*loss_sum, count_real, *outputs)
    d_in_0, dg_0, d_embed = found
    if True:
        g_embed = reduce_natural(d_embed, 0)
        g_head = reduce_natural(d_head[0][:, :, :VOCAB].reshape(D, VOCAB), 0)
        g_in = reduce_natural(jnp.stack([unfold(d_in_0), unfold(d_in_1[0])]), 1)
        g_out = reduce_natural(jnp.stack([unfold(d) for d in (d_down_0[0][:, 4 * TILE :], d_down_1[0][:, 4 * TILE :])]), 1)
        g_up = reduce_natural(jnp.stack([unfold(d_up_0[0]), unfold(d_up_1[0])]), 1)
        g_down = reduce_natural(jnp.stack([d.reshape(FF, D) for d in (d_down_0[0][:, : 4 * TILE], d_down_1[0][:, : 4 * TILE])]), 1)
        gain_grad = reduce_natural(jnp.concatenate([dg_0, dg_1, dg_2, dg_3, dg_4], 0), 1)

    embed, head, attn_in, attn_out, ffn_in, ffn_out = after((embed, head, attn_in, attn_out, ffn_in, ffn_out), d_q1)
    decay = 1.0 - STEP ** (-0.8)
    matrices = [
        (g_embed, embed_row, embed_col, embed, VOCAB),
        (g_head, head_row, head_col, head, D),
        (g_in, in_row, in_col, attn_in, D),
        (g_out, out_row, out_col, attn_out, D),
        (g_up, up_row, up_col, ffn_in, D),
        (g_down, down_row, down_col, ffn_out, FF),
    ]
    new_rows, sums = [], []
    for grad, row, _, weight, _ in matrices:
        square = grad * grad
        new_row = decay * row + (1.0 - decay) * jnp.mean(square, -1)
        new_rows.append(new_row)
        sums += [
            jnp.sum(square, -2),
            jnp.sum(square / new_row[..., None], -2),
            jnp.sum(new_row, -1),
            jnp.sum(weight * weight, (-2, -1)),
        ]
    new_sq = decay * gains_sq + (1.0 - decay) * gain_grad * gain_grad
    gain_update = gain_grad / jnp.sqrt(new_sq)
    sums += [jnp.sum(gain_update * gain_update, -1), jnp.sum(gains * gains, -1), loss[0, :1]]
    flat = jnp.concatenate([s.reshape(-1) for s in sums], 0)
    size = flat.shape[0]
    flat = jnp.pad(flat, (0, -size % 1024)).reshape(-1, 128)
    flat = sum_all(flat).reshape(-1)
    totals, at = [], 0
    for s in sums:
        totals.append(flat[at : at + s.size].reshape(s.shape))
        at += s.size
    outputs = [totals[-1].reshape(()), count_real]
    for index, (grad, _, col, weight, full_rows) in enumerate(matrices):
        col_sum, ratio_sum, row_sum, weight_sum = totals[4 * index : 4 * index + 4]
        new_row = new_rows[index]
        new_col = decay * col + (1.0 - decay) * col_sum / full_rows
        mean_row = row_sum / full_rows
        size_all = full_rows * grad.shape[-1]
        update_sum = mean_row * jnp.sum(ratio_sum / new_col, -1)
        rate_now = RATE_SCALE * jnp.sqrt(weight_sum / size_all) / jnp.maximum(1.0, jnp.sqrt(update_sum / size_all))
        update = grad / jnp.sqrt(new_row[..., :, None] * new_col[..., None, :] / mean_row[..., None, None])
        outputs += [grad, new_row, new_col, weight - rate_now[..., None, None] * update]
    gain_rate = RATE_SCALE * jnp.sqrt(totals[-2] / D) / jnp.maximum(1.0, jnp.sqrt(totals[-3] / D))
    outputs += [gain_grad, new_sq, gains - gain_rate[:, None] * gain_update]
    return tuple(outputs)


def solution(mesh):
    row = P(BOTH, None)
    mid = P(None, BOTH, None)
    vec = P(BOTH)
    vec2 = P(None, BOTH)
    state = (vec, P(), vec, P(), vec2, P(), vec2, P(), vec2, P(), vec2, P(), vec2)
    return jax.shard_map(
        local,
        mesh=mesh,
        in_specs=(P(), P(), row, row, mid, mid, mid, mid, vec2) + state,
        out_specs=(P(), P())
        + (row, vec, P(), row) * 2
        + (mid, vec2, P(), mid) * 4
        + (vec2, vec2, vec2),
        check_vma=False,
    )
```

```python
from functools import partial
import math

import jax
import jax.numpy as jnp
from jax import lax
from jax.experimental import pallas as pl
from jax.experimental.pallas import tpu as pltpu
from jax.sharding import PartitionSpec as P

D = 512
HEADS = 8
FF = 2048
VOCAB = 256
SHORT = 3
HD = 64
SPAN = 384
CSPAN = SPAN // SHORT
STREAM = 65536
STEP = 10
SHARDS = 32
TILE = 16

EPSILON = 1e-05
RATE_SCALE = 0.5
LOG_TWO = math.log(2.0)
MASKED = -1e30
GELU_A = math.sqrt(2.0 / math.pi)
GELU_B = 0.044715
BOTH = ("dp", "seq")
F32 = jnp.float32
BF16 = jnp.bfloat16
ROOM = {
    "fold": 24, "join": 16, "measure": 20, "attend": 24, "attend_back": 36, "project": 28, "project_short": 28,
    "branch": 32, "branch_back": 44, "short_rest": 34, "project_back": 36,
}


def nn(left, right):
    return jnp.dot(left, right, preferred_element_type=F32)


def nt(left, right):
    return lax.dot_general(left, right, (((1,), (1,)), ((), ())), preferred_element_type=F32)


def call(body, name, outs, ins, us, grid=(1,), in_specs=None, out_specs=None, scratch=(), prefetch=1):
    room = ROOM.get(name, 56) * 2**20
    spec = pltpu.PrefetchScalarGridSpec(
        num_scalar_prefetch=prefetch,
        grid=grid,
        in_specs=in_specs or [held(i.shape) for i in ins[prefetch:]],
        out_specs=out_specs or [whole(o.shape) for o in outs],
        scratch_shapes=list(scratch),
    )
    return pl.pallas_call(
        body,
        grid_spec=spec,
        out_shape=list(outs),
        compiler_params=pltpu.CompilerParams(vmem_limit_bytes=room),
        cost_estimate=pl.CostEstimate(flops=int(us * 2e10), bytes_accessed=1 << 20, transcendentals=0),
        name=name,
    )(*ins)


def whole(dims):
    return pl.BlockSpec(dims, lambda *_: (0,) * len(dims))


def held(dims):
    return pl.BlockSpec(dims, lambda *_: (0,) * len(dims), pipeline_mode=pl.Buffered(1))


def shape(dims, kind=F32):
    return jax.ShapeDtypeStruct(dims, kind)


RANK, CORE, BITS, CHIP = 2, 3, 4, 9
WEIGHT_PARTS = 4


def norm_parts(values):
    center = values - jnp.mean(values, -1, keepdims=True)
    scale = lax.rsqrt(jnp.mean(center * center, -1, keepdims=True) + EPSILON)
    return center * scale, scale


def norm_pull(hat, scale, gain, cotangent):
    pulled = cotangent * gain
    inner = pulled - jnp.mean(pulled, -1, keepdims=True) - hat * jnp.mean(pulled * hat, -1, keepdims=True)
    return scale * inner, jnp.sum(cotangent * hat, 0, keepdims=True)


def swap_halves(values):
    lane = lax.broadcasted_iota(jnp.int32, values.shape, 1)
    return jnp.where(lane % HD < HD // 2, pltpu.roll(values, 128 - HD // 2, 1), pltpu.roll(values, HD // 2, 1))


def rope(values, cosine, sine):
    pieces = []
    for start in range(0, D, 128):
        piece = values[:, start : start + 128]
        pieces.append(piece * cosine + swap_halves(piece) * sine)
    return jnp.concatenate(pieces, 1)


def rope_pull(values, cosine, sine):
    pieces = []
    for start in range(0, D, 128):
        piece = values[:, start : start + 128]
        pieces.append(piece * cosine + swap_halves(piece * sine))
    return jnp.concatenate(pieces, 1)


def gelu_parts(values):
    inner = GELU_A * (values + GELU_B * (values * values * values))
    wave = jnp.tanh(inner)
    return wave, 0.5 * (1.0 + wave)


def gelu_slope(values, wave, gate):
    return gate + 0.5 * values * (1.0 - wave * wave) * (GELU_A * (1.0 + 3.0 * GELU_B * values * values))


def tile_of(ref, index):
    return ref[:, TILE * index : TILE * index + TILE, :].reshape(D, ref.shape[-1])


def settle(refs, scr, info, second, start=0):
    if len(refs) == 1:
        return refs[0].at[:, start:]
    rows = slice(start, start + scr.shape[1])
    last, next_last = (1, 0) if second else (0, 1)

    def place(r, carry):
        mask = ((r & 1) << 3) | (((r >> 1) & 1) << 2) | (((r >> 2) & 1) << next_last)
        for far in range(2):
            chip = info[CHIP] ^ (mask | (far << last))
            scr[2 * chip + info[CORE]] = refs[far][r, rows]
            scr[2 * chip + 1 - info[CORE]] = refs[2 + far][r, rows]
        return carry

    lax.fori_loop(0, SHARDS // 4, place, 0)
    return scr


def bundle_scratch(bundles, rows):
    return [pltpu.VMEM((SHARDS, count, D), BF16) for bundle, count in zip(bundles, rows) if len(bundle) > 1]


def thirds(ref, lead, start):
    found = ref[(*lead, pl.ds(start, CSPAN, stride=SHORT), slice(None))]
    for shift in range(1, SHORT):
        found = found + ref[(*lead, pl.ds(start + shift, CSPAN, stride=SHORT), slice(None))]
    return found


def spread(ref, lead, value):
    for shift in range(SHORT):
        ref[(*lead, pl.ds(shift, CSPAN, stride=SHORT), slice(None))] = value


LANES = [slice(start, start + 128) for start in range(0, D, 128)]


def grad_shapes(rows, split):
    if split:
        return [shape((SHARDS // 2, rows, D)), shape((SHARDS // 2, rows, D), BF16)]
    return [shape((SHARDS, rows, D))]


def grad_specs(rows, split, index, shards=SHARDS):
    if split:
        return [pl.BlockSpec((shards // 2, rows, D), index)] * 2
    return [pl.BlockSpec((shards, rows, D), index)]


def put(refs, core, value, at=0, rows=TILE, chunk=0):
    width = value.shape[-1]
    part = pl.ds(at, rows)
    shards = D // rows
    if len(refs) == 2:
        pairs = value.reshape(shards // 2, 2, rows, width)
        low, high = pairs[:, 0], pairs[:, 1]
        where = pl.ds(chunk * (shards // 2), shards // 2)
        refs[0][where, part, :width] = jnp.where(core == 0, low, high)
        refs[1][where, part, :width] = jnp.where(core == 0, high, low).astype(BF16)
    else:
        refs[0][pl.ds(chunk * shards, shards), part, :width] = value.reshape(shards, rows, width).astype(refs[0].dtype)


def project_body(info, token_ref, *rest, each):
    wa_refs, wb_refs = rest[:each], rest[each : 2 * each]
    cos_ref, sin_ref, h_ref, q_ref, kv_ref, gain_ref = rest[2 * each : 2 * each + 6]
    scr = rest[2 * each + 6 :]
    wa_ref, wb_ref = scr if each > 1 else (wa_refs[0], wb_refs[0])

    @pl.when(pl.program_id(0) == 0)
    def _():
        settle(wa_refs, scr and scr[0], info, False)
        settle(wb_refs, scr and scr[1], info, True)
        lane = lax.broadcasted_iota(jnp.int32, (8, D), 1)
        found = jnp.zeros((8, D), F32)
        for shard in range(SHARDS):
            side = wb_ref[shard, TILE : 2 * TILE, :].astype(F32)[8:]
            side = side if shard == 0 else pltpu.roll(side, TILE * shard, 1)
            found = jnp.where(lane // TILE == shard, side, found)
        gain_ref[...] = found

    token = token_ref[...]
    row = (token // 8) * TILE + token % 8
    hot = (row == lax.broadcasted_iota(jnp.int32, (token.shape[0], D), 1)).astype(BF16)
    values = nn(hot, tile_of(wb_ref, 1))
    h_ref[...] = values.astype(BF16)
    normed = (norm_parts(values)[0] * gain_ref[0:1, :]).astype(BF16)
    cosine, sine = cos_ref[...], sin_ref[...]
    q_ref[...] = (rope(nn(normed, tile_of(wa_ref, 0)), cosine, sine) * 0.125).astype(BF16)
    kv_ref[0] = rope(nn(normed, tile_of(wa_ref, 1)), cosine, sine).astype(BF16)
    kv_ref[1] = nn(normed, tile_of(wb_ref, 0)).astype(BF16)


def project(info, token, bundles, cosine, sine):
    rows = cosine.shape[0]
    step = SPAN
    weights = [*bundles[0], *bundles[1]]
    return call(
        partial(project_body, each=len(bundles[0])),
        "project",
        [shape((rows, D), BF16)] * 2 + [shape((2, rows, D), BF16), shape((8, D))],
        [info, token, *weights, cosine, sine],
        5,
        grid=(rows // step,),
        in_specs=[pl.BlockSpec((step, 1), lambda i, _: (i, 0))]
        + [held(w.shape) for w in weights]
        + [pl.BlockSpec((step, 128), lambda i, _: (i, 0))] * 2,
        out_specs=[pl.BlockSpec((step, D), lambda i, _: (i, 0))] * 2
        + [pl.BlockSpec((2, step, D), lambda i, _: (0, i, 0)), whole((8, D))],
        scratch=bundle_scratch(bundles, (2 * TILE, 2 * TILE)),
    )


def project_short_body(
    info, h_ref, tail_ref, low_ref, high_ref, *rest, ways, each
):
    wa_refs, wb_refs = rest[:each], rest[each : 2 * each]
    gain_ref, cos_ref, sin_ref, z_ref, q_ref, kv_ref, scr = rest[2 * each : 2 * each + 7]
    wa_ref = settle(wa_refs, rest[-2], info, False, 4 * TILE)
    wb_ref = settle(wb_refs, rest[-1], info, True, 5 * TILE)
    for slot in range(2):
        if slot == 0:
            halo = low_ref[...]
        else:
            halo = jnp.where(info[RANK] == ways - 1, tail_ref[0], high_ref[...])
        for piece, lanes in enumerate(LANES):
            scr[slot, piece, :8, :] = halo[:, lanes]
            scr[slot, piece, 8:, :] = h_ref[SPAN * slot : SPAN * slot + SPAN, lanes]
            total = thirds(scr, (slot, piece), 6)
            z_ref[CSPAN * slot : CSPAN * slot + CSPAN, lanes] = total * (1.0 / SHORT)
    normed = (norm_parts(z_ref[...])[0] * gain_ref[2:3, :]).astype(BF16)
    cosine, sine = cos_ref[...], sin_ref[...]
    query = nn(normed[CSPAN:], tile_of(wa_ref, 0))
    q_ref[...] = (rope(query, cosine[CSPAN:], sine[CSPAN:]) * 0.125).astype(BF16)
    kv_ref[0] = rope(nn(normed, tile_of(wa_ref, 1)), cosine, sine).astype(BF16)
    kv_ref[1] = nn(normed, tile_of(wb_ref, 0)).astype(BF16)


def project_short(info, h, tail, low, high, bundles, gains, cosine, sine, ways):
    outs = [shape((2 * CSPAN, D)), shape((CSPAN, D), BF16), shape((2, 2 * CSPAN, D), BF16)]
    ins = [info, h, tail, low, high, *bundles[0], *bundles[1], gains, cosine, sine]
    specs = [held(i.shape) for i in ins[1:]]
    return call(
        partial(project_short_body, ways=ways, each=len(bundles[0])),
        "project_short",
        outs,
        ins,
        0.05,
        in_specs=specs,
        scratch=[pltpu.VMEM((2, D // 128, SPAN + 8, 128), F32)] + bundle_scratch(bundles, (2 * TILE, TILE)),
    )


def order_keys(info, own, other, found, block, count):
    for at in range(count):
        owner = min(at, count - 1 - at)
        place = 0 if owner == at else 1
        part = slice(place * block, place * block + block)
        for kind, keys in enumerate(found):
            keys[at * block : at * block + block, :] = jnp.where(
                info[RANK] == owner, own[kind, part, :], other[kind, part, :]
            )


def each_rows(rows, steps, count):
    if count <= 4:
        for i in range(steps):
            rows(i)
    else:
        lax.fori_loop(0, steps, lambda i, carry: (rows(i), carry)[1], 0)


def each_head(head, together):
    if together == 4:
        for j in range(4):
            head(j)
        return

    def some(i, carry):
        for j in range(together):
            head(i * together + j)
        return carry

    lax.fori_loop(0, 4 // together, some, 0)


def masked_rows(s_scr, part, start, step, block, width):
    score = s_scr[part, :width]
    row = start + lax.broadcasted_iota(jnp.int32, (step, block), 0)
    key = lax.broadcasted_iota(jnp.int32, (step, block), 1)
    edge = jnp.where(row >= key, score[:, width - block :], MASKED)
    return jnp.concatenate([score[:, : width - block], edge], 1) if width > block else edge


def rows_part(i, step):
    return pl.ds(i * step if isinstance(i, int) else pl.multiple_of(i * step, step), step)


def attend_body(info, q_ref, *rest, count, block, step, pair, base):
    if pair:
        own, other, out_ref, lse_ref, s_scr, p_scr, k_ref, v_ref = rest
    else:
        k_ref, v_ref, out_ref, lse_ref, s_scr, p_scr = rest
    slot = pl.program_id(1)
    nk = info[slot + base]
    lane = lax.broadcasted_iota(jnp.int32, (1, 256), 1)
    column = lax.broadcasted_iota(jnp.int32, (step, 128), 1)
    zero = jnp.zeros((), BF16)
    if pair:

        @pl.when(slot == 0)
        def _():
            order_keys(info, own, other, (k_ref, v_ref), block, count)

    def variant(blocks):
        width = blocks * block

        def head(j):
            mine = lane // HD == j
            s_scr[:, :width] = nt(jnp.where(mine, q_ref[...], zero), k_ref[:width, :])

            def rows(i):
                part = rows_part(i, step)
                score = masked_rows(s_scr, part, i * step, step, block, width)
                top = jnp.max(score, -1, keepdims=True)
                raised = jnp.exp(score - top)
                total = jnp.sum(raised, -1, keepdims=True)
                p_scr[part, :width] = (raised * (1.0 / total)).astype(BF16)
                lse_ref[0, 0, part, :] = jnp.where(column == j, top + jnp.log(total), lse_ref[0, 0, part, :])

            each_rows(rows, block // step, count)
            found = nn(p_scr[:, :width], v_ref[:width, :]).astype(BF16)
            out_ref[...] = jnp.where(mine, found, out_ref[...])

        each_head(head, 4 if count <= 4 else 1)

    for blocks in range(1, count + 1):
        pl.when(nk == blocks)(partial(variant, blocks))


def key_spec(key, first):
    lead = key.shape[:-1]
    return pl.BlockSpec((*lead, 256), lambda h, s, _: (0,) * len(lead) + (h + first,))


def attend(info, q, keys, block, first, groups):
    slots = q.shape[0] // block
    pair = keys[0].ndim == 3
    total = keys[0].shape[-2] * (2 if pair else 1)
    count = total // block
    scratch = [pltpu.VMEM((block, total), F32), pltpu.VMEM((block, total), BF16)]
    if pair:
        scratch += [pltpu.VMEM((total, 256), BF16)] * 2
    return call(
        partial(attend_body, count=count, block=block, step=64, pair=pair, base=2 - slots),
        "attend",
        [shape((slots * block, 256 * groups), BF16), shape((groups, slots, block, 128))],
        [info, q, *keys],
        8 if block == SPAN else 0.05,
        grid=(groups, slots),
        in_specs=[pl.BlockSpec((block, 256), lambda h, s, _: (s, h + first))]
        + [key_spec(key, first) for key in keys],
        out_specs=[
            pl.BlockSpec((block, 256), lambda h, s, _: (s, h)),
            pl.BlockSpec((1, 1, block, 128), lambda h, s, _: (h, s, 0, 0)),
        ],
        scratch=scratch,
    )


def attend_back_body(info, q_ref, *rest, count, block, step, pair, base):
    if pair:
        own, other, back_ref, lse_ref, dq_ref, keep_ref, send_ref = rest[:7]
        s_scr, dp_scr, p_scr, ds_scr, dk_scr, dv_scr, qt_scr, bt_scr, k_ref, v_ref = rest[7:]
    else:
        k_ref, v_ref, back_ref, lse_ref, dq_ref, keep_ref = rest[:6]
        s_scr, dp_scr, p_scr, ds_scr, dk_scr, dv_scr, qt_scr, bt_scr = rest[6:]
    slot = pl.program_id(1)
    nk = info[slot + base]
    lane = lax.broadcasted_iota(jnp.int32, (1, 256), 1)
    column = lax.broadcasted_iota(jnp.int32, (step, 128), 1)
    zero = jnp.zeros((), BF16)

    qt_scr[...] = q_ref[...].T
    bt_scr[...] = back_ref[...].T

    @pl.when(slot == 0)
    def _():
        dk_scr[...] = jnp.zeros_like(dk_scr)
        dv_scr[...] = jnp.zeros_like(dv_scr)
        if pair:
            order_keys(info, own, other, (k_ref, v_ref), block, count)

    def variant(blocks):
        width = blocks * block

        def head(j):
            mine = lane // HD == j
            s_scr[:, :width] = nt(jnp.where(mine, q_ref[...], zero), k_ref[:width, :])
            dp_scr[:, :width] = nt(jnp.where(mine, back_ref[...], zero), v_ref[:width, :])

            def rows(i):
                part = rows_part(i, step)
                score = masked_rows(s_scr, part, i * step, step, block, width)
                lse = jnp.sum(jnp.where(column == j, lse_ref[0, 0, part, :], 0.0), -1, keepdims=True)
                prob = jnp.exp(score - lse)
                p_scr[part, :width] = prob.astype(BF16)
                prob_back = dp_scr[part, :width]
                delta = jnp.sum(prob * prob_back, -1, keepdims=True)
                ds_scr[part, :width] = (prob * (prob_back - delta)).astype(BF16)

            each_rows(rows, block // step, count)
            found = nn(ds_scr[:, :width], k_ref[:width, :])
            dq_ref[...] = jnp.where(mine, found, dq_ref[...])
            mine_rows = pl.ds(HD * j if isinstance(j, int) else pl.multiple_of(HD * j, HD), HD)
            dk_scr[mine_rows, :width] += nn(qt_scr[mine_rows, :], ds_scr[:, :width])
            dv_scr[mine_rows, :width] += nn(bt_scr[mine_rows, :], p_scr[:, :width])

        each_head(head, 2 if count <= 4 else 1)

    for blocks in range(1, count + 1):
        pl.when(nk == blocks)(partial(variant, blocks))

    @pl.when(slot == pl.num_programs(1) - 1)
    def _():
        for kind, scr in enumerate((dk_scr, dv_scr)):
            for place in range(2):
                to = slice(place * block, place * block + block)

                def from_owner(owner):
                    at = owner if place == 0 else count - 1 - owner
                    return scr[:, at * block : at * block + block]

                if pair:
                    low, high = from_owner(0), from_owner(1)
                    keep_ref[kind, :, to] = jnp.where(info[RANK] == 0, low, high)
                    send_ref[kind, :, to] = jnp.where(info[RANK] == 0, high, low).astype(BF16)
                else:
                    for owner in range(count // 2):
                        keep_ref[owner, kind, :, to] = from_owner(owner)


def attend_back(info, q, keys, back, lse, block, first, groups):
    slots = q.shape[0] // block
    pair = keys[0].ndim == 3
    total = keys[0].shape[-2] * (2 if pair else 1)
    count = total // block
    outs = [shape((slots * block, 256 * groups))]
    out_specs = [pl.BlockSpec((block, 256), lambda h, s, _: (s, h))]
    if pair:
        outs += [shape((2, 256 * groups, 2 * block)), shape((2, 256 * groups, 2 * block), BF16)]
        out_specs += [pl.BlockSpec((2, 256, 2 * block), lambda h, s, _: (0, h, 0))] * 2
    else:
        outs += [shape((count // 2, 2, 256 * groups, 2 * block))]
        out_specs += [pl.BlockSpec((count // 2, 2, 256, 2 * block), lambda h, s, _: (0, 0, h, 0))]
    scratch = [
        pltpu.VMEM((block, total), F32),
        pltpu.VMEM((block, total), F32),
        pltpu.VMEM((block, total), BF16),
        pltpu.VMEM((block, total), BF16),
        pltpu.VMEM((256, total), F32),
        pltpu.VMEM((256, total), F32),
        pltpu.VMEM((256, block), BF16),
        pltpu.VMEM((256, block), BF16),
    ]
    if pair:
        scratch += [pltpu.VMEM((total, 256), BF16)] * 2
    return call(
        partial(attend_back_body, count=count, block=block, step=64, pair=pair, base=2 - slots),
        "attend_back",
        outs,
        [info, q, *keys, back, lse],
        13 if block == SPAN else 7,
        grid=(groups, slots),
        in_specs=[pl.BlockSpec((block, 256), lambda h, s, _: (s, h + first))]
        + [key_spec(key, first) for key in keys]
        + [
            pl.BlockSpec((block, 256), lambda h, s, _: (s, h)),
            pl.BlockSpec((1, 1, block, 128), lambda h, s, _: (h, s, 0, 0)),
        ],
        out_specs=out_specs,
        scratch=scratch,
    )


def branch_body(info, x_ref, a0_ref, a1_ref, *rest, each):
    up_refs, down_refs = rest[:each], rest[each : 2 * each]
    gain_ref, mid_ref, res_ref, tail_ref = rest[2 * each : 2 * each + 4]
    scr = rest[2 * each + 4 :]
    up_w, down_w = scr if each > 1 else (up_refs[0], down_refs[0])

    @pl.when(pl.program_id(0) == 0)
    def _():
        settle(up_refs, scr and scr[0], info, False)
        settle(down_refs, scr and scr[1], info, True)

    out_tile = tile_of(down_w, 4)
    middle = x_ref[...].astype(F32) + nn(a0_ref[...], out_tile[:256]) + nn(a1_ref[...], out_tile[256:])
    mid_ref[...] = middle
    normed = (norm_parts(middle)[0] * gain_ref[1:2, :]).astype(BF16)
    total = mid_ref[...]
    for chunk in range(FF // D):
        up = nn(normed, tile_of(up_w, chunk))
        hidden = (up * gelu_parts(up)[1]).astype(BF16)
        total = total + nn(hidden, down_w[8 * chunk : 8 * chunk + 8, : 4 * TILE, :].reshape(D, D))
    res_ref[...] = total
    tail_ref[0] = total[total.shape[0] - 8 :]


def branch(info, x, parts, bundles, gains):
    rows = x.shape[0]
    row = lambda width: pl.BlockSpec((SPAN, width), lambda i, _: (i, 0))
    weights = [*bundles[0], *bundles[1]]
    return call(
        partial(branch_body, each=len(bundles[0])),
        "branch",
        [shape((rows, D)), shape((rows, D)), shape((2, 8, D))],
        [info, x, *parts, *weights, gains],
        9,
        grid=(rows // SPAN,),
        in_specs=[row(D), row(256), row(256), *[held(w.shape) for w in weights], held(gains.shape)],
        out_specs=[row(D), row(D), pl.BlockSpec((1, 8, D), lambda i, _: (i, 0, 0))],
        scratch=bundle_scratch(bundles, (4 * TILE, 5 * TILE)),
    )


def branch_back_body(info, dz_ref, edge_ref, high_ref, low_ref, dh_ref, mid_ref, a0_ref, a1_ref, *rest, ways, split):
    each = 2 if split else 1
    parts = WEIGHT_PARTS if split else 1
    uw_refs, dw_refs, gain_ref = rest[:parts], rest[parts : 2 * parts], rest[2 * parts]
    rest = rest[2 * parts + 1 :]
    dmid_ref, da0_ref, da1_ref, dgain_ref = rest[:4]
    up_refs, down_refs = rest[4 : 4 + each], rest[4 + each : 4 + 2 * each]
    norm_scr, normt_scr, cot_scr, cotb_scr, acc_scr, pool_scr = rest[4 + 2 * each : 10 + 2 * each]
    w_scr = rest[10 + 2 * each :]
    up_w, down_w = w_scr if split else (uw_refs[0], dw_refs[0])
    chunk = pl.program_id(0)
    core = info[CORE]

    @pl.when(chunk == 0)
    def _():
        settle(uw_refs, w_scr and w_scr[0], info, False)
        settle(dw_refs, w_scr and w_scr[1], info, True)
        for slot in range(2):
            if slot == 0:
                edge = jnp.where(info[RANK] == ways - 1, edge_ref[1], high_ref[...])
            else:
                edge = low_ref[...]
            for piece, lanes in enumerate(LANES):
                spread(pool_scr, (slot, piece), dz_ref[CSPAN * slot : CSPAN * slot + CSPAN, lanes] * (1.0 / SHORT))
                pool_scr[slot, piece, SPAN:, :] = jnp.broadcast_to(edge[0:1, lanes] * (1.0 / SHORT), (8, 128))
                found = pool_scr[slot, piece, 2 : SPAN + 2, :]
                if slot == 1:
                    found = found + dh_ref[:, lanes]
                cot_scr[SPAN * slot : SPAN * slot + SPAN, lanes] = found
        cotb_scr[...] = cot_scr[...].astype(BF16)
        normed = (norm_parts(mid_ref[...])[0] * gain_ref[1:2, :]).astype(BF16)
        norm_scr[...] = normed
        normt_scr[...] = normed.T
        acc_scr[...] = jnp.zeros_like(acc_scr)

    down_in = cotb_scr[...]
    up_tile = up_w[:, pl.ds(pl.multiple_of(chunk * TILE, TILE), TILE), :].reshape(D, D)
    down_tile = down_w[pl.ds(chunk * 8, 8), : 4 * TILE, :].reshape(D, D)
    up = nn(norm_scr[...], up_tile)
    wave, gate = gelu_parts(up)
    hidden = (up * gate).astype(BF16)
    up_in = (nt(down_in, down_tile) * gelu_slope(up, wave, gate)).astype(BF16)
    put(down_refs, core, nn(hidden.T, down_in), rows=4 * TILE, chunk=chunk)
    put(up_refs, core, nn(normt_scr[...], up_in))
    acc_scr[...] += nt(up_in, up_tile)

    @pl.when(chunk == FF // D - 1)
    def _():
        hat, scale = norm_parts(mid_ref[...])
        pulled, dgain = norm_pull(hat, scale, gain_ref[1:2, :], acc_scr[...])
        dgain_ref[...] = dgain
        dmid = cot_scr[...] + pulled
        dmid_ref[...] = dmid
        out_in = dmid.astype(BF16)
        out_tile = tile_of(down_w, 4)
        put(down_refs, core, jnp.concatenate([nn(a0_ref[...].T, out_in), nn(a1_ref[...].T, out_in)], 0), at=4 * TILE)
        da0_ref[...] = nt(out_in, out_tile[:256]).astype(BF16)
        da1_ref[...] = nt(out_in, out_tile[256:]).astype(BF16)


def branch_back(info, dz, edge, high, low, dh, mid, parts, bundles, gains, ways, split):
    rows = mid.shape[0]
    ins = [info, dz, edge, high, low, dh, mid, *parts, *bundles[0], *bundles[1], gains]
    specs = [held(i.shape) for i in ins[1:]]
    return call(
        partial(branch_back_body, ways=ways, split=split),
        "branch_back",
        [shape((rows, D)), shape((rows, 256), BF16), shape((rows, 256), BF16), shape((1, D))]
        + grad_shapes(4 * TILE, split)
        + grad_shapes(5 * TILE, split),
        ins,
        0.3,
        grid=(FF // D,),
        in_specs=specs,
        out_specs=[whole((rows, D)), whole((rows, 256)), whole((rows, 256)), whole((1, D))]
        + grad_specs(TILE, split, lambda i, _: (0, i, 0))
        + grad_specs(5 * TILE, split, lambda i, _: (0, 0, 0)),
        scratch=[
            pltpu.VMEM((rows, D), BF16),
            pltpu.VMEM((D, rows), BF16),
            pltpu.VMEM((rows, D), F32),
            pltpu.VMEM((rows, D), BF16),
            pltpu.VMEM((rows, D), F32),
            pltpu.VMEM((2, D // 128, SPAN + 8, 128), F32),
            *bundle_scratch(bundles, (4 * TILE, 5 * TILE)),
        ],
    )


def short_body(info, x_ref, a_ref, h_ref, *rest, split):
    each = 2 if split else 1
    parts = WEIGHT_PARTS if split else 1
    uw_refs, dw_refs = rest[:parts], rest[parts : 2 * parts]
    gain_ref, target_ref, counted_ref, rate_ref = rest[2 * parts : 2 * parts + 4]
    rest = rest[2 * parts + 4 :]
    loss_ref, dg4_ref, dg3_ref, dh_ref, dmid_ref, da_ref = rest[:6]
    up_refs, down_refs, head_refs = [rest[6 + each * i : 6 + each * i + each] for i in range(3)]
    mid_scr, norm_scr, normt_scr, cot_scr, acc_scr, up_scr = rest[6 + 3 * each : 12 + 3 * each]
    w_scr = rest[12 + 3 * each :]
    up_w, down_w = w_scr if split else (uw_refs[0], dw_refs[0])
    down_rows = slice(0, 4 * TILE)
    step = pl.program_id(0)
    core = info[CORE]

    @pl.when(step == 0)
    def _():
        settle(uw_refs, w_scr and w_scr[0], info, False)
        settle(dw_refs, w_scr and w_scr[1], info, True)
        middle = x_ref[...] + nn(a_ref[...], tile_of(up_w, 4))
        mid_scr[...] = middle
        normed = (norm_parts(middle)[0] * gain_ref[3:4, :]).astype(BF16)
        norm_scr[...] = normed
        normt_scr[...] = normed.T
        total = mid_scr[...]
        for chunk in range(FF // D):
            up = nn(normed, tile_of(up_w, chunk))
            hidden = (up * gelu_parts(up)[1]).astype(BF16)
            total = total + nn(hidden, down_w[8 * chunk : 8 * chunk + 8, down_rows, :].reshape(D, D))
        for piece, lanes in enumerate(LANES):
            spread(up_scr, (piece,), total[:, lanes])
        gain = gain_ref[4:5, :]
        hat, scale = norm_parts(h_ref[...] + jnp.concatenate([up_scr[piece] for piece in range(len(LANES))], 1))
        final = (hat * gain).astype(BF16)
        head = tile_of(down_w, 4)[:, :VOCAB]
        logits = nn(final, head)
        top = jnp.max(logits, -1, keepdims=True)
        log_total = top + jnp.log(jnp.sum(jnp.exp(logits - top), -1, keepdims=True))
        hot = target_ref[...] == lax.broadcasted_iota(jnp.int32, logits.shape, 1)
        picked = jnp.sum(jnp.where(hot, logits, 0.0), -1, keepdims=True)
        counted = counted_ref[...]
        loss = jnp.sum((log_total - picked) * counted, 0, keepdims=True) * (1.0 / LOG_TWO)
        loss_ref[...] = jnp.broadcast_to(loss, (1, 128))
        grad = ((jnp.exp(logits - log_total) - jnp.where(hot, 1.0, 0.0)) * (counted * rate_ref[0, 0])).astype(BF16)
        dhead = nn(final.T, grad)
        put(head_refs, core, jnp.concatenate([dhead, jnp.zeros((D, D - VOCAB), F32)], 1))
        pulled, dgain = norm_pull(hat, scale, gain, nt(grad, head))
        dg4_ref[...] = dgain
        dh_ref[...] = pulled
        for piece, lanes in enumerate(LANES):
            up_scr[piece] = pulled[:, lanes]
            cot_scr[:, lanes] = thirds(up_scr, (piece,), 0)
        acc_scr[...] = jnp.zeros_like(acc_scr)

    @pl.when(step > 0)
    def _():
        chunk = step - 1
        down_in = cot_scr[...].astype(BF16)
        up_tile = up_w[:, pl.ds(pl.multiple_of(chunk * TILE, TILE), TILE), :].reshape(D, D)
        up = nn(norm_scr[...], up_tile)
        wave, gate = gelu_parts(up)
        hidden = (up * gate).astype(BF16)
        up_in = (nt(down_in, down_w[pl.ds(chunk * 8, 8), down_rows, :].reshape(D, D)) * gelu_slope(up, wave, gate)).astype(BF16)
        put(down_refs, core, nn(hidden.T, down_in), rows=4 * TILE, chunk=chunk)
        put(up_refs, core, nn(normt_scr[...], up_in))
        acc_scr[...] += nt(up_in, up_tile)

    @pl.when(step == FF // D)
    def _():
        hat, scale = norm_parts(mid_scr[...])
        pulled, dgain = norm_pull(hat, scale, gain_ref[3:4, :], acc_scr[...])
        dg3_ref[...] = dgain
        dmid = cot_scr[...] + pulled
        dmid_ref[...] = dmid
        out_in = dmid.astype(BF16)
        put(down_refs, core, nn(a_ref[...].T, out_in), at=4 * TILE)
        da_ref[...] = nt(out_in, tile_of(up_w, 4)).astype(BF16)


def short_rest(info, z, a, h, bundles, gains, target, counted, rate, split):
    ins = [info, z, a, h, *bundles[0], *bundles[1], gains, target, counted, rate]
    specs = [held(i.shape) for i in ins[1:]]
    specs[0] = pl.BlockSpec((CSPAN, D), lambda *_: (1, 0))
    specs[2] = pl.BlockSpec((SPAN, D), lambda *_: (1, 0))
    specs[-1] = pl.BlockSpec(memory_space=pltpu.SMEM)
    return call(
        partial(short_body, split=split),
        "short_rest",
        [shape((1, 128)), shape((1, D)), shape((1, D)), shape((SPAN, D)), shape((CSPAN, D)), shape((CSPAN, D), BF16)]
        + grad_shapes(4 * TILE, split)
        + grad_shapes(5 * TILE, split)
        + grad_shapes(TILE, split),
        ins,
        12,
        grid=(FF // D + 1,),
        in_specs=specs,
        out_specs=[whole((1, 128)), whole((1, D)), whole((1, D)), whole((SPAN, D)), whole((CSPAN, D)), whole((CSPAN, D))]
        + grad_specs(TILE, split, lambda i, _: (0, jnp.maximum(i - 1, 0), 0))
        + grad_specs(5 * TILE, split, lambda i, _: (0, 0, 0))
        + grad_specs(TILE, split, lambda i, _: (0, 0, 0)),
        scratch=[
            pltpu.VMEM((CSPAN, D), F32),
            pltpu.VMEM((CSPAN, D), BF16),
            pltpu.VMEM((D, CSPAN), BF16),
            pltpu.VMEM((CSPAN, D), F32),
            pltpu.VMEM((CSPAN, D), F32),
            pltpu.VMEM((D // 128, SPAN, 128), F32),
            *bundle_scratch(bundles, (5 * TILE, 5 * TILE)),
        ],
    )


def project_back_body(info, *refs, full, split, groups):
    refs = list(refs)
    take = lambda n: [refs.pop(0) for _ in range(n)]
    dqs, keeps, recvs = take(groups), take(groups), take(groups)
    dmid_ref, x_ref = take(2)
    if full:
        (token_ref,) = take(1)
        wa_refs, wb_refs = [take(WEIGHT_PARTS if split else 1) for _ in range(2)]
        dg_refs = take(4)
    else:
        wa_refs, wb_refs = [take(WEIGHT_PARTS if split else 1) for _ in range(2)]
    wa_ref = settle(wa_refs, refs[-2], info, False, 0 if full else 4 * TILE)
    wb_ref = settle(wb_refs, refs[-1], info, True, 0 if full else 5 * TILE)
    weight = [tile_of(wa_ref, 0), tile_of(wa_ref, 1), tile_of(wb_ref, 0)]
    gain_ref, cos_ref, sin_ref = take(3)
    each = 2 if split else 1
    first_refs = take(each)
    if not full or not split:
        dgain_ref, dx_ref = take(2)
    if not full:
        (edge_ref,) = take(1)
    core = info[CORE]
    gain = gain_ref[0:1, :] if full else gain_ref[2:3, :]
    hat, scale = norm_parts(x_ref[...].astype(F32))
    normed_t = (hat * gain).astype(BF16).T
    cosine, sine = cos_ref[...], sin_ref[...]
    rows = hat.shape[0]
    skip = rows - dqs[0].shape[0]
    total = jnp.zeros((rows, D), F32)
    for kind in range(3):
        if kind == 0:
            grad = jnp.concatenate([dq[...] for dq in dqs], 1) if groups > 1 else dqs[0][...]
            grad = rope_pull(grad * 0.125, cosine[skip:], sine[skip:]).astype(BF16)
            found = nn(normed_t[:, skip:], grad)
        else:
            both = [(keep[kind - 1] + recv[kind - 1].astype(F32)).T for keep, recv in zip(keeps, recvs)]
            grad = jnp.concatenate(both, 1) if groups > 1 else both[0]
            grad = (rope_pull(grad, cosine, sine) if kind == 1 else grad).astype(BF16)
            found = nn(normed_t, grad)
        put(first_refs, core, found, at=TILE * kind)
        back = nt(grad, weight[kind])
        if kind == 0 and skip:
            back = jnp.concatenate([jnp.zeros((skip, D), F32), back], 0)
        total = total + back
    pulled, dgain = norm_pull(hat, scale, gain, total)
    if not full:
        dgain_ref[...] = dgain
        dx = jnp.concatenate([pulled[:skip], dmid_ref[...] + pulled[skip:]], 0)
        dx_ref[...] = dx
        for slot in range(2):
            edge_ref[slot] = dx[CSPAN * slot : CSPAN * slot + 8]
        return
    back = (dmid_ref[...] + pulled).astype(BF16)
    hot = (token_ref[...] == lax.broadcasted_iota(jnp.int32, (VOCAB, rows), 0)).astype(BF16)
    dembed = nn(hot, back)
    if not split:
        dgain_ref[...] = dgain
        dx_ref[...] = dembed
        return
    dgains = jnp.concatenate([dgain] + [ref[...] for ref in dg_refs] + [jnp.zeros((3, D), F32)], 0)
    lane = lax.broadcasted_iota(jnp.int32, (8, D), 1)
    sides = [
        jnp.where(lane < TILE, dgains if j == 0 else pltpu.roll(dgains, D - TILE * j, 1), 0.0) for j in range(SHARDS)
    ]
    embeds = dembed.reshape(SHARDS, 8, D)
    for chip in range(SHARDS // 2):
        for part, values in ((slice(3 * TILE, 3 * TILE + 8), embeds), (slice(3 * TILE + 8, 4 * TILE), sides)):
            low, high = values[2 * chip], values[2 * chip + 1]
            first_refs[0][chip, part, :] = jnp.where(core == 0, low, high)
    first_refs[1][:, 3 * TILE :, :] = jnp.stack(
        [
            jnp.where(
                core == 0,
                jnp.concatenate([embeds[2 * chip + 1], sides[2 * chip + 1]], 0),
                jnp.concatenate([embeds[2 * chip], sides[2 * chip]], 0),
            ).astype(BF16)
            for chip in range(SHARDS // 2)
        ],
        0,
    )


def project_back(info, dqs, keeps, recvs, dmid, x, extra, bundles, dgs, gains, cosine, sine, full, split):
    groups = len(dqs)
    rows = cosine.shape[0]
    weights = [value for bundle in bundles for value in bundle]
    ins = [info, *dqs, *keeps, *recvs, dmid, x, *extra, *weights, *dgs, gains, cosine, sine]
    specs = [held(i.shape) for i in ins[1:]]
    scratch = bundle_scratch(bundles, (2 * TILE, TILE))
    if full:
        outs = grad_shapes(4 * TILE if split else 3 * TILE, split)
        if not split:
            outs += [shape((1, D)), shape((VOCAB, D))]
    else:
        outs = grad_shapes(3 * TILE, split) + [shape((1, D)), shape((rows, D)), shape((2, 8, D))]
    return call(
        partial(project_back_body, full=full, split=split, groups=groups),
        "project_back",
        outs,
        ins,
        10 if full else 5,
        in_specs=specs,
        scratch=scratch,
    )


def fold_body(info, *refs, layout):
    refs = list(refs)
    outs = refs[4 * sum(len(rows) for rows in layout) :]
    for order, rows in enumerate(layout):
        at = 0
        for count in rows:
            keep, far, recv, far_recv = [refs.pop(0) for _ in range(4)]
            lead = outs[2 * order].shape[0]
            part = slice(at, at + count)
            flat = lambda ref: ref[...].reshape(lead, count, D)
            outs[2 * order][:, part, :] = flat(keep) + flat(recv).astype(F32)
            outs[2 * order + 1][:, part, :] = (flat(far) + flat(far_recv).astype(F32)).astype(BF16)
            at += count


def fold(info, orders, steps, us):
    ins, specs, outs, out_specs, layout = [info], [], [], [], []
    for sources, pre, post, bit in orders:
        sources = [source if len(source) == 4 else (0, *source, source[0].shape[-2]) for source in sources]
        layout.append([rows for *_, rows in sources])
        for place, keep, recv, rows in sources:
            dims = (pre, 2, post, keep.shape[-2], D)
            for value in (keep, recv):
                for other in (0, 1):
                    ins.append(value.reshape(dims))
                    inner = max(steps // pre, 1)
                    specs.append(
                        pl.BlockSpec(
                            (max(pre // steps, 1), 1, post // inner, rows, D),
                            lambda i, info, other=other, bit=bit, inner=inner, place=place: (
                                i // inner, jnp.abs(info[BITS + bit] - other), i % inner, place, 0
                            ),
                        )
                    )
        total = sum(layout[-1])
        for kind in (F32, BF16):
            outs.append(shape((pre * post, total, D), kind))
            out_specs.append(pl.BlockSpec((pre * post // steps, total, D), lambda i, _: (i, 0, 0)))
    found = call(
        partial(fold_body, layout=layout), "fold", outs, ins, us, grid=(steps,), in_specs=specs, out_specs=out_specs
    )
    return [(found[2 * i], found[2 * i + 1]) for i in range(len(orders))]


CORE_BIT, Y_BIT, X_BIT, Z0_BIT, Z1_BIT = range(5)


ALONG_XY_FIRST = (
    ((X_BIT, 4, 2), (Y_BIT, 8, 1), 8),
    ((Y_BIT, 4, 1), (X_BIT, 4, 1), 4),
    ((Z0_BIT, 2, 1), 2),
    ((Z1_BIT, 1, 1), 1),
)
ALONG_Z_FIRST = (((Z0_BIT, 2, 4), 8), ((Z1_BIT, 1, 4), 4), ((X_BIT, 1, 2), 2), ((Y_BIT, 1, 1), 1))


def across(keep, send):
    return keep, swapped(send, CORE_BIT)


class Scatter:
    def __init__(self, firsts, seconds=None):
        groups = (firsts,) if seconds is None else (firsts, seconds)
        self.values = [[across(*pair) if len(pair) == 2 else pair for pair in sources] for sources in groups]
        self.stages = list(ALONG_Z_FIRST if seconds is None else ALONG_XY_FIRST)

    def plan(self):
        *plans, steps = self.stages.pop(0)
        if len(plans) == 1:
            self.values = [[pair for sources in self.values for pair in sources]]
        orders = [(sources, pre, post, bit) for sources, (bit, pre, post) in zip(self.values, plans)]
        return orders, steps

    def folded(self, found, bits):
        self.values = [[(keep, swapped(send, bit))] for (keep, send), bit in zip(found, bits)]

    def kept(self):
        return [keep for sources in self.values for keep, _ in sources]


def step_all(info, *needed):
    def step(*scatters):
        plans = [scatter.plan() for scatter in scatters]
        orders = [order for plan, _ in plans for order in plan]
        found = fold(after(info, needed) if needed else info, orders, min(steps for _, steps in plans), 0.05)
        for scatter, (plan, _) in zip(scatters, plans):
            scatter.folded([found.pop(0) for _ in plan], [bit for *_, bit in plan])

    return step


def after(value, *needed):
    return lax.optimization_barrier((value, needed))[0]


DECAY = 1.0 - STEP ** (-0.8)
MATRICES = (
    [(VOCAB, 1, D), (D, 1, VOCAB)] + [(D, 3, 3 * D)] * 2 + [(D, 1, D)] * 2 + [(D, 4, FF)] * 2 + [(FF, 1, D)] * 2
)
TILES = sum(count for _, count, _ in MATRICES)
STAT_ROWS = 48


def as_column(row):
    return jnp.broadcast_to(row, (128, row.shape[1])).T[:, 0:1]


def as_row(column):
    return jnp.broadcast_to(column, (column.shape[0], 128)).T[0:1, :]


def tile_lanes(width, index):
    return slice(D * index, min(D * index + D, width))


def measure_body(info, *refs):
    refs = list(refs)
    take = lambda n: [refs.pop(0) for _ in range(n)]
    late, middle, early = [keep[0] + recv[0].astype(F32) for keep, recv in [take(2) for _ in range(3)]]
    row_refs, weight_refs = take(6), take(6)
    gain_ref, sq_ref, loss_ref = take(3)
    grad_refs, new_row_refs = take(6), take(6)
    gain_grad_ref, new_sq_ref, stat_ref = take(3)
    early_a, early_b = early[: 2 * TILE], early[2 * TILE :]
    cut = lambda value, start, count=1, size=TILE: [value[start + size * i : start + size * i + size] for i in range(count)]
    grads = [
        [early_b[TILE : TILE + 8]],
        [middle[12 * TILE :, :VOCAB]],
        cut(early_a, 0, 2) + cut(early_b, 0),
        cut(middle, 4 * TILE, 3),
        cut(middle, 11 * TILE),
        cut(late, 8 * TILE),
        cut(middle, 0, 4),
        cut(late, 0, 4),
        cut(middle, 7 * TILE, size=4 * TILE),
        cut(late, 4 * TILE, size=4 * TILE),
    ]
    lane = lax.broadcasted_iota(jnp.int32, (1, D), 1)
    scalars = jnp.where(lane == 30, loss_ref[0:1, 0:1], 0.0)
    total = lambda value: jnp.sum(jnp.sum(value, 1, keepdims=True), 0, keepdims=True)
    stat_ref[...] = jnp.zeros_like(stat_ref)
    at = 0
    for index, (pieces, (_, _, width)) in enumerate(zip(grads, MATRICES)):
        kind, layer = (index, None) if index < 2 else (2 + (index - 2) // 2, index % 2)
        old = row_refs[kind][...] if layer is None else row_refs[kind][layer : layer + 1, :]
        weight = weight_refs[kind][...] if layer is None else weight_refs[kind][layer]
        squares = [piece * piece for piece in pieces]
        mean = sum(jnp.sum(square, 1, keepdims=True) for square in squares) * (1.0 / width)
        new_row = DECAY * as_column(old) + (1.0 - DECAY) * mean
        inverse = 1.0 / new_row
        new_rows = as_row(new_row)
        if layer is None:
            new_row_refs[kind][...] = new_rows
        else:
            new_row_refs[kind][layer : layer + 1, :] = new_rows
        for place, (piece, square) in enumerate(zip(pieces, squares)):
            lanes = tile_lanes(width, place)
            if layer is None:
                grad_refs[kind][:, lanes] = piece
            else:
                grad_refs[kind][layer, :, lanes] = piece
            own = slice(0, piece.shape[1])
            stat_ref[at : at + 1, own] = jnp.sum(square, 0, keepdims=True)
            stat_ref[TILES + at : TILES + at + 1, own] = jnp.sum(square * inverse, 0, keepdims=True)
            at += 1
        scalars = jnp.where(lane == 2 * index, total(new_row), scalars)
        scalars = jnp.where(lane == 2 * index + 1, total(weight * weight), scalars)
    gain_grad = early_b[TILE + 8 : TILE + 13, :TILE]
    gain_grad_ref[...] = gain_grad
    new_sq = DECAY * sq_ref[...] + (1.0 - DECAY) * gain_grad * gain_grad
    new_sq_ref[...] = new_sq
    gains = gain_ref[...]
    update = gain_grad / jnp.sqrt(new_sq)
    for value, start in ((update, 20), (gains, 25)):
        each = jnp.sum(value * value, 1, keepdims=True)
        for row in range(5):
            scalars = jnp.where(lane == start + row, each[row : row + 1], scalars)
    stat_ref[2 * TILES : 2 * TILES + 1, :] = scalars


def update_body(info, *refs):
    refs = list(refs)
    take = lambda n: [refs.pop(0) for _ in range(n)]
    (stat_ref,) = take(1)
    grad_refs, row_refs, col_refs, weight_refs = take(6), take(6), take(6), take(6)
    gain_ref, gain_grad_ref, sq_ref = take(3)
    new_col_refs, new_refs = take(6), take(6)
    gain_new_ref, loss_ref = take(2)
    scalars = stat_ref[2 * TILES : 2 * TILES + 1, :]
    scalar = lambda lane: scalars[:, lane : lane + 1]
    loss_ref[...] = scalar(30)
    at = 0
    for index, (rows, count, width) in enumerate(MATRICES):
        kind, layer = (index, None) if index < 2 else (2 + (index - 2) // 2, index % 2)
        mean_row = scalar(2 * index) * (1.0 / rows)
        size = rows * width
        new_row = as_column(row_refs[kind][...] if layer is None else row_refs[kind][layer : layer + 1, :])
        pieces, spread_sum = [], jnp.zeros((1, 1), F32)
        for place in range(count):
            lanes = tile_lanes(width, place)
            own = slice(0, lanes.stop - lanes.start)
            here = slice(0, 1) if layer is None else slice(layer, layer + 1)
            new_col = DECAY * col_refs[kind][here, lanes] + (1.0 - DECAY) * stat_ref[at : at + 1, own] * (1.0 / rows)
            new_col_refs[kind][here, lanes] = new_col
            spread_sum = spread_sum + jnp.sum(stat_ref[TILES + at : TILES + at + 1, own] / new_col, 1, keepdims=True)
            pieces.append((lanes, new_col))
            at += 1
        update_sum = mean_row * spread_sum
        rate = RATE_SCALE * jnp.sqrt(scalar(2 * index + 1) * (1.0 / size))
        rate = rate / jnp.maximum(1.0, jnp.sqrt(update_sum * (1.0 / size)))
        for lanes, new_col in pieces:
            if layer is None:
                grad, weight = grad_refs[kind][:, lanes], weight_refs[kind][:, lanes]
            else:
                grad, weight = grad_refs[kind][layer, :, lanes], weight_refs[kind][layer, :, lanes]
            found = weight - rate * (grad / jnp.sqrt(new_row * new_col / mean_row))
            if layer is None:
                new_refs[kind][:, lanes] = found
            else:
                new_refs[kind][layer, :, lanes] = found
    gains, gain_grad = gain_ref[...], gain_grad_ref[...]
    update = gain_grad / jnp.sqrt(sq_ref[...])
    for row in range(5):
        here = slice(row, row + 1)
        rate = RATE_SCALE * jnp.sqrt(scalar(25 + row) * (1.0 / D)) / jnp.maximum(1.0, jnp.sqrt(scalar(20 + row) * (1.0 / D)))
        gain_new_ref[here, :] = gains[here] - rate * update[here]


def optimize(info, sums, rows, cols, weights, gains, gains_sq, loss):
    flat = lambda values: [value[None] if value.ndim == 1 else value for value in values]
    rows, cols = flat(rows), flat(cols)
    same = lambda values: [shape(value.shape) for value in values]
    found = call(
        measure_body,
        "measure",
        same(weights) + same(rows) + [shape(gains.shape), shape(gains.shape), shape((STAT_ROWS, D))],
        [info, *[value for pair in sums for value in pair], *rows, *weights, gains, gains_sq, loss],
        0.05,
    )
    grads, new_rows, (gain_grad, new_sq, stats) = found[:6], found[6:12], found[12:]
    stats = sum_all(stats)
    found = call(
        update_body,
        "update",
        same(cols) + same(weights) + [shape(gains.shape), shape((1, 1))],
        [info, stats, *grads, *new_rows, *cols, *weights, gains, gain_grad, new_sq],
        0.05,
    )
    new_cols, new_weights, (gains_new, loss_sum) = found[:6], found[6:12], found[12:]
    outputs = []
    for index in range(6):
        plain = (lambda value: value[0]) if index < 2 else (lambda value: value)
        outputs += [grads[index], plain(new_rows[index]), plain(new_cols[index]), new_weights[index]]
    return [loss_sum[0, 0]], outputs + [gain_grad, new_sq, gains_new]


def flat_index():
    return lax.axis_index("dp") * lax.axis_size("seq") + lax.axis_index("seq")


def flat_count():
    return lax.axis_size("dp") * lax.axis_size("seq")


def swapped(value, bit):
    return lax.ppermute(value, BOTH, [(i, i ^ (1 << bit)) for i in range(flat_count())])


def bit_of(bit):
    return (flat_index() >> bit) & 1


def join_body(info, *refs):
    count = len(refs) // 3
    for index, out in enumerate(refs[2 * count :]):
        here, there = refs[2 * index : 2 * index + 2]
        rows = here.shape[0]
        out[:rows] = here[...]
        out[rows:] = there[...]


def join_pairs(info, pairs):
    outs = [shape((2 * here.shape[0], *here.shape[1:]), here.dtype) for here, _ in pairs]
    return call(join_body, "join", outs, [info, *[value for pair in pairs for value in pair]], 0.05)


def split_body(info, here, there, *outs):
    count, at = here.shape[0], 0
    for out in outs:
        part = slice(at, at + out.shape[1])
        out[:count] = here[:, part]
        out[count:] = there[:, part]
        at += out.shape[1]


def split_pair(info, here, there, split):
    count, rows = here.shape[:2]
    outs = [shape((2 * count, size, D), here.dtype) for size in (split, rows - split)]
    return list(call(split_body, "join", outs, [info, here, there], 0.05))


class Gather:
    def __init__(self, packed):
        self.values = [packed[None]]
        self.near = None
        self.info = jnp.zeros((1,), jnp.int32)

    def send(self, *bits, needed=()):
        if needed:
            self.values = [after(value, *needed) for value in self.values]
        self.coming = [swapped(value, bit) for value, bit in zip(self.values, bits)]
        return self

    def pairs(self, needed):
        pairs = list(zip(self.values, self.coming))
        return lax.optimization_barrier((pairs, list(needed)))[0]

    def join(self, split=None, needed=()):
        pairs = self.pairs(needed)
        if split is not None:
            ((here, there),) = pairs
            if here.shape[0] * here.shape[1] >= 256:
                self.values = split_pair(self.info, here, there, split)
                return self
            pairs = [(here[:, :split], there[:, :split]), (here[:, split:], there[:, split:])]
        small = pairs[0][0].shape[0] * pairs[0][0].shape[1] < 256
        self.values = [jnp.concatenate(pair, 0) for pair in pairs] if small else join_pairs(self.info, pairs)
        return self

    def send_last(self, *bits, needed=()):
        self.send(*bits, needed=needed)
        self.near = [swapped(value, CORE_BIT) for value in self.values]
        return self

    def last(self, needed=()):
        self.values = self.pairs(needed)
        if self.near is None:
            self.near = [swapped(here, CORE_BIT) for here, _ in self.values]
        return [
            (here, there, near, swapped(there, CORE_BIT)) for (here, there), near in zip(self.values, self.near)
        ]


def group_perm(ways, links):
    count = lax.axis_size("seq")
    return [(base + a, base + b) for base in range(0, count, ways) for a, b in links]


def window_keys(kv, ways):
    if ways == 2:
        return [kv, lax.ppermute(kv, "seq", group_perm(2, ((0, 1), (1, 0))))]
    groups = [list(range(base, base + ways)) for base in range(0, lax.axis_size("seq"), ways)]
    found = []
    for value in (kv[0], kv[1]):
        every = lax.all_gather(value, "seq", axis=0, tiled=False, axis_index_groups=groups)
        rows = every.shape[1] // 2
        blocks = [every[w, :rows] for w in range(ways)] + [every[w, rows:] for w in reversed(range(ways))]
        found.append(jnp.concatenate(blocks, 0))
    return found


def window_sum(grads, ways):
    if ways == 2:
        keep, send = grads
        return keep, lax.ppermute(send, "seq", group_perm(2, ((0, 1), (1, 0))))
    groups = [list(range(base, base + ways)) for base in range(0, lax.axis_size("seq"), ways)]
    total = lax.psum_scatter(grads[0], "seq", scatter_dimension=0, tiled=False, axis_index_groups=groups)
    return total, jnp.zeros(total.shape, BF16)


def from_sides(first, second, ways):
    if ways == 2:
        rank = lax.axis_index("seq") % ways
        other = lax.ppermute(jnp.where(rank == 0, first, second), "seq", group_perm(2, ((0, 1), (1, 0))))
        zero = jnp.zeros_like(other)
        return jnp.where(rank == 0, zero, other), jnp.where(rank == 0, other, zero)
    up = [(i, i + 1) for i in range(ways - 1)]
    down = [(i + 1, i) for i in range(ways - 1)]
    return lax.ppermute(first, "seq", group_perm(ways, up)), lax.ppermute(second, "seq", group_perm(ways, down))


def sum_all(value):
    count = flat_count()
    for bit in range(count.bit_length() - 1):
        value = value + swapped(value, bit)
    return value


def tiles(weight):
    rows = weight.shape[0]
    return [weight[:, start : start + D] for start in range(0, weight.shape[1], D)] if rows else []


def pack_edge(embed, gains):
    rows = embed.shape[-2]
    pad = jnp.zeros((8, D - gains.shape[1]), gains.dtype)
    side = jnp.concatenate([jnp.concatenate([gains, jnp.zeros((3, gains.shape[1]), gains.dtype)], 0), pad], 1)
    return jnp.concatenate([embed, side], 0)


def gather_weights(embed, head, attn_in, attn_out, ffn_in, ffn_out, gains):
    full = [
        lax.all_gather(weight, BOTH, axis=axis, tiled=True)
        for weight, axis in ((embed, 0), (head, 0), (attn_in, 1), (attn_out, 1), (ffn_in, 1), (ffn_out, 1), (gains, 1))
    ]
    embed, head, attn_in, attn_out, ffn_in, ffn_out, gains = full
    fold_rows = lambda weight: weight.reshape(SHARDS, TILE, D)
    edge = jnp.zeros((SHARDS, TILE, D), BF16).at[:, :8].set(embed.reshape(SHARDS, 8, D))
    edge = edge.at[:, 8:13, :TILE].set(gains.reshape(5, SHARDS, TILE).transpose(1, 0, 2))
    head_tile = jnp.zeros((SHARDS, TILE, D), BF16).at[:, :, :VOCAB].set(head.reshape(SHARDS, TILE, VOCAB))
    down = ffn_out.reshape(2, SHARDS, 4 * TILE, D)
    side = [[fold_rows(t) for t in tiles(attn_in[i])] for i in range(2)]
    up = [[fold_rows(t) for t in tiles(ffn_in[i])] for i in range(2)]
    firsts = [jnp.concatenate(side[0][:2], 1), jnp.concatenate([side[0][2], edge], 1)]
    seconds = [
        jnp.concatenate(up[0] + side[1][:2], 1),
        jnp.concatenate([down[0], fold_rows(attn_out[0]), side[1][2]], 1),
    ]
    third = [jnp.concatenate(up[1] + [fold_rows(attn_out[1])], 1), jnp.concatenate([down[1], head_tile], 1)]
    return firsts, seconds, third


def reduce_natural(grad, axis):
    return lax.psum_scatter(grad, BOTH, scatter_dimension=axis, tiled=True)


def unfold(packed):
    parts = packed.shape[1] // TILE
    return jnp.concatenate([packed[:, TILE * i : TILE * i + TILE].reshape(D, D) for i in range(parts)], 1)


def local(
    stream, offsets, embed, head, attn_in, attn_out, ffn_in, ffn_out, gains,
    embed_row, embed_col, head_row, head_col, in_row, in_col, out_row, out_col, up_row, up_col, down_row, down_col, gains_sq,
):
    seq_rank = lax.axis_index("seq")
    dp_rank = lax.axis_index("dp")
    seq_count = lax.axis_size("seq")
    per_group = offsets.shape[0] // lax.axis_size("dp")
    ways = seq_count // per_group
    blocks = 2 * ways
    length = SPAN * blocks
    rank = seq_rank % ways
    split = flat_count() == SHARDS
    if split:
        low = lambda *values: [value.astype(BF16) for value in values]
        embed_low, gains_low, in_low = low(embed, gains, attn_in[0])
        one = Gather(jnp.concatenate(tiles(in_low) + [pack_edge(embed_low, gains_low)], 0))
        up_low, down_low, out_low, in_low = low(*after((ffn_in[0], ffn_out[0], attn_out[0], attn_in[1]), one.values))
        in_low = tiles(in_low)
        two = Gather(jnp.concatenate(tiles(up_low) + in_low[:2] + [down_low, out_low, in_low[2]], 0))
        one.send(Z1_BIT).join()
        two.send(Z1_BIT, needed=one.values)
        up_low, down_low, out_low, head_low = low(*after((ffn_in[1], ffn_out[1], attn_out[1], head), one.values))
        head_low = jnp.concatenate([head_low, jnp.zeros_like(head_low)], 1)
        three = Gather(jnp.concatenate(tiles(up_low) + [out_low, down_low, head_low], 0))
        one.send(Z0_BIT).join(2 * TILE)
        two.join().send(Z0_BIT, needed=one.values)
        one.send(X_BIT, Y_BIT).join()
        offsets_then, stream_then = after((offsets, stream), two.values)
        two.join(6 * TILE)
        three.send(Z1_BIT, needed=one.values)
        one.send_last(Y_BIT, X_BIT)
        three.join()
        first = one.last()
        two.send(X_BIT, Y_BIT, needed=one.values)
    else:
        low = [w.astype(BF16) for w in (embed, head, attn_in, attn_out, ffn_in, ffn_out, gains)]
        first, second, third = gather_weights(*low)
        first, second, third = [[(value,) for value in pair] for pair in (first, second, third)]
        offsets_then, stream_then = offsets, stream

    window_start = offsets_then[dp_rank * per_group + seq_rank // ways]
    limits = jnp.minimum(length, STREAM - 1 - offsets_then) - (length - length // 2)
    count_real = jnp.sum(jnp.maximum(limits, 0)).astype(F32)
    own_blocks = jnp.stack([rank, blocks - 1 - rank]) + 0 * window_start
    positions = (own_blocks[:, None] * SPAN + jnp.arange(SPAN, dtype=jnp.int32)[None]).reshape(-1)
    coarse_pos = (own_blocks[:, None] * CSPAN + jnp.arange(CSPAN, dtype=jnp.int32)[None]).reshape(-1)
    reach = own_blocks + 1
    info = jnp.concatenate(
        [reach, jnp.stack([rank, flat_index() & 1] + [bit_of(bit) for bit in range(5)] + [flat_index() >> 1])], 0
    ).astype(jnp.int32)
    starts = window_start + own_blocks * SPAN
    padded = jnp.concatenate([stream_then, jnp.broadcast_to(stream_then[-1:], (length,))], 0)
    tokens = jnp.concatenate([lax.dynamic_slice_in_dim(padded, starts[s], SPAN, 0) for s in range(2)], 0)
    target = lax.dynamic_slice_in_dim(padded, starts[1] + 1, SPAN, 0)
    counted = (window_start + positions[SPAN:] + 1 < STREAM).astype(F32)
    rate = (1.0 / (LOG_TWO * count_real)).reshape(1, 1)

    def tables(at):
        frequency = 10000.0 ** (-jnp.arange(HD // 2, dtype=F32) / (HD // 2))
        angles = at.astype(F32)[:, None] * frequency[None, :]
        cosine, sine = jnp.cos(angles), jnp.sin(angles)
        return (jnp.concatenate([cosine] * 4, 1), jnp.concatenate([-sine, sine] * 2, 1))

    cos_0, sin_0 = tables(positions)
    cos_1, sin_1 = tables(coarse_pos)

    token_col, target_col, counted_col = tokens[:, None], target[:, None], counted[:, None]
    if split:
        token_col = after(token_col, target_col, counted_col, rate, cos_1, sin_1, three.values)
    h_0, q_0, kv_0, gain_rows = project(info, token_col, first, cos_0, sin_0)
    if split:
        two.join(needed=[q_0]).send_last(Y_BIT, X_BIT)
        three.send(Z0_BIT)
        kv_0 = after(kv_0, two.values)
    keys_0 = window_keys(kv_0, ways)
    a_lo, lse_lo = attend(info, q_0, keys_0, SPAN, 0, 1)
    if split:
        three.join(5 * TILE, needed=[a_lo]).send(X_BIT, Y_BIT)
    a_hi, lse_hi = attend(info, after(q_0, a_lo, three.values, two.near) if split else q_0, keys_0, SPAN, 1, 1)
    if split:
        three.join(needed=[a_hi])
        second = two.last([a_hi, *three.values])
        three.send(Y_BIT, X_BIT)
    m_0, h_1, tail = branch(info, after(h_0, three.values) if split else h_0, (a_lo, a_hi), second, gain_rows)

    z_0, q_1, kv_1 = project_short(
        info, h_1, tail, *from_sides(tail[0], tail[1], ways), second, gain_rows, cos_1, sin_1, ways
    )
    keys_1 = window_keys(kv_1, ways)
    a_1, lse_1 = attend(info, q_1, keys_1, CSPAN, 0, 2)
    if split:
        third = three.last([a_1])
    found = short_rest(info, z_0, a_1, h_1, third, gain_rows, target_col, counted_col, rate, split)
    loss, dg_4, dg_3, d_h2, d_m1, d_a1 = found[:6]
    each = 2 if split else 1
    d_up_1, d_down_1, d_head = [found[6 + each * i : 6 + each * i + each] for i in range(3)]
    if split:
        late = Scatter([d_up_1, d_down_1])
    d_q1, *d_kv1 = attend_back(info, q_1, keys_1, d_a1, lse_1, CSPAN, 0, 2)
    if split:
        step_all(info, d_q1)(late)
        d_m1 = after(d_m1, late.kept())
    keep, recv = window_sum(d_kv1, ways)
    found = project_back(info, [d_q1], [keep], [recv], d_m1, z_0, [], second, [], gain_rows, cos_1, sin_1, False, split)
    d_in_1, (dg_2, d_z0, edge) = found[:each], found[each:]

    low_edge, high = from_sides(edge[1], edge[0], ways)
    if split:
        in_pair, head_pair = across(*d_in_1), across(*d_head)
        d_h2 = after(d_h2, in_pair, head_pair)
    found = branch_back(info, d_z0, edge, high, low_edge, d_h2, m_0, (a_lo, a_hi), second, gain_rows, ways, split)
    d_m0, da_lo, da_hi, dg_1 = found[:4]
    d_up_0, d_down_0 = [found[4 + each * i : 4 + each * i + each] for i in range(2)]
    if split:
        step_all(info, d_m0)(late)
        d_up_0, d_down_0 = after((tuple(d_up_0), tuple(d_down_0)), late.kept())
        middle = Scatter([d_up_0, (0, *in_pair, 3 * TILE)], [d_down_0, (0, *head_pair, TILE)])
        step_all(info)(middle)
        da_lo = after(da_lo, middle.kept())
    dq_lo, *dkv_lo = attend_back(info, q_0, keys_0, da_lo, lse_lo, SPAN, 0, 1)
    if split:
        da_hi = after(da_hi, dq_lo)
    sum_lo = window_sum(dkv_lo, ways)
    dq_hi, *dkv_hi = attend_back(info, q_0, keys_0, da_hi, lse_hi, SPAN, 1, 1)
    if split:
        step_all(info, dq_hi, sum_lo, late.values)(middle)
        dkv_hi = after(tuple(dkv_hi), middle.kept())
    sum_hi = window_sum(dkv_hi, ways)
    found = project_back(
        info, [dq_lo, dq_hi], [sum_lo[0], sum_hi[0]], [sum_lo[1], sum_hi[1]], d_m0, h_0, [tokens[None, :]], first,
        [dg_1, dg_2, dg_3, dg_4], gain_rows, cos_0, sin_0, True, split,
    )

    if split:
        pair = across(*after(tuple(found[:2]), middle.values))
        early = Scatter([(0, *pair, 2 * TILE)], [(1, *pair, 2 * TILE)])
        step_all(info)(middle)
        step_all(info, middle.kept())(early, late)
        step_all(info, early.kept())(early)
        step_all(info, early.kept())(middle, late)
        step_all(info, middle.kept())(early)
        step_all(info)(early)
        loss_sum, outputs = optimize(
            info,
            [sources[0] for sources in late.values + middle.values + early.values],
            [embed_row, head_row, in_row, out_row, up_row, down_row],
            [embed_col, head_col, in_col, out_col, up_col, down_col],
            [embed, head, attn_in, attn_out, ffn_in, ffn_out],
            gains,
            gains_sq,
            loss,
        )
        return (*loss_sum, count_real, *outputs)
    d_in_0, dg_0, d_embed = found
    if True:
        g_embed = reduce_natural(d_embed, 0)
        g_head = reduce_natural(d_head[0][:, :, :VOCAB].reshape(D, VOCAB), 0)
        g_in = reduce_natural(jnp.stack([unfold(d_in_0), unfold(d_in_1[0])]), 1)
        g_out = reduce_natural(jnp.stack([unfold(d) for d in (d_down_0[0][:, 4 * TILE :], d_down_1[0][:, 4 * TILE :])]), 1)
        g_up = reduce_natural(jnp.stack([unfold(d_up_0[0]), unfold(d_up_1[0])]), 1)
        g_down = reduce_natural(jnp.stack([d.reshape(FF, D) for d in (d_down_0[0][:, : 4 * TILE], d_down_1[0][:, : 4 * TILE])]), 1)
        gain_grad = reduce_natural(jnp.concatenate([dg_0, dg_1, dg_2, dg_3, dg_4], 0), 1)

    embed, head, attn_in, attn_out, ffn_in, ffn_out = after((embed, head, attn_in, attn_out, ffn_in, ffn_out), d_q1)
    decay = 1.0 - STEP ** (-0.8)
    matrices = [
        (g_embed, embed_row, embed_col, embed, VOCAB),
        (g_head, head_row, head_col, head, D),
        (g_in, in_row, in_col, attn_in, D),
        (g_out, out_row, out_col, attn_out, D),
        (g_up, up_row, up_col, ffn_in, D),
        (g_down, down_row, down_col, ffn_out, FF),
    ]
    new_rows, sums = [], []
    for grad, row, _, weight, _ in matrices:
        square = grad * grad
        new_row = decay * row + (1.0 - decay) * jnp.mean(square, -1)
        new_rows.append(new_row)
        sums += [
            jnp.sum(square, -2),
            jnp.sum(square / new_row[..., None], -2),
            jnp.sum(new_row, -1),
            jnp.sum(weight * weight, (-2, -1)),
        ]
    new_sq = decay * gains_sq + (1.0 - decay) * gain_grad * gain_grad
    gain_update = gain_grad / jnp.sqrt(new_sq)
    sums += [jnp.sum(gain_update * gain_update, -1), jnp.sum(gains * gains, -1), loss[0, :1]]
    flat = jnp.concatenate([s.reshape(-1) for s in sums], 0)
    size = flat.shape[0]
    flat = jnp.pad(flat, (0, -size % 1024)).reshape(-1, 128)
    flat = sum_all(flat).reshape(-1)
    totals, at = [], 0
    for s in sums:
        totals.append(flat[at : at + s.size].reshape(s.shape))
        at += s.size
    outputs = [totals[-1].reshape(()), count_real]
    for index, (grad, _, col, weight, full_rows) in enumerate(matrices):
        col_sum, ratio_sum, row_sum, weight_sum = totals[4 * index : 4 * index + 4]
        new_row = new_rows[index]
        new_col = decay * col + (1.0 - decay) * col_sum / full_rows
        mean_row = row_sum / full_rows
        size_all = full_rows * grad.shape[-1]
        update_sum = mean_row * jnp.sum(ratio_sum / new_col, -1)
        rate_now = RATE_SCALE * jnp.sqrt(weight_sum / size_all) / jnp.maximum(1.0, jnp.sqrt(update_sum / size_all))
        update = grad / jnp.sqrt(new_row[..., :, None] * new_col[..., None, :] / mean_row[..., None, None])
        outputs += [grad, new_row, new_col, weight - rate_now[..., None, None] * update]
    gain_rate = RATE_SCALE * jnp.sqrt(totals[-2] / D) / jnp.maximum(1.0, jnp.sqrt(totals[-3] / D))
    outputs += [gain_grad, new_sq, gains - gain_rate[:, None] * gain_update]
    return tuple(outputs)


def solution(mesh):
    row = P(BOTH, None)
    mid = P(None, BOTH, None)
    vec = P(BOTH)
    vec2 = P(None, BOTH)
    state = (vec, P(), vec, P(), vec2, P(), vec2, P(), vec2, P(), vec2, P(), vec2)
    return jax.shard_map(
        local,
        mesh=mesh,
        in_specs=(P(), P(), row, row, mid, mid, mid, mid, vec2) + state,
        out_specs=(P(), P())
        + (row, vec, P(), row) * 2
        + (mid, vec2, P(), mid) * 4
        + (vec2, vec2, vec2),
        check_vma=False,
    )
```
